32 devices in a mesh: dom: 16 (over z, x, core), sub: 2 (over y).
Axes of the slice: x: 2, y: 2, z: 4, core: 2. Of those that a mesh axis runs over, the one named last changes fastest.
Arguments:
- rhs_local: float32 [128, 64, 128], P('dom', 'sub'), may hold values from -8 to 8
- coefficient: float32 [128, 64, 128], P('dom', 'sub'), may hold values from 0.3 to 3
Outputs:
- preconditioned: float32 [128, 64, 128], P('dom', 'sub')
- coarse_solution: float32 [32, 16, 32], P('dom', 'sub')
The draws below stay inside these ranges and needn't reach their ends.
All inputs are finite; a program needn't handle non-finite values.
Results may differ from the reference program's by a relative error of at most 0.0003.
Values sent between devices are 32-bit elements; how exact they have to be, the bound alone decides.
No kernel may reach another device: no remote copies, remote signals or barrier semaphores. Data moves between devices by JAX's collectives and lax.ppermute only.
A program may use at most 64 MiB of HBM per device.

```python
import math
import jax
import jax.numpy as jnp
import numpy as np
from jax import lax

EZ = 16
NX = 128
NY = 64
NZ = 128
MX = 32
MY = 16
MZ = 32
N_DOM = 16


def shard_levels(key, dims, shards, least, largest):
    loudness = 1.0
    for dim, blocks in shards:
        heights = jax.random.uniform(jax.random.fold_in(jax.random.fold_in(key, 6), dim), (blocks,), jnp.float32, least / len(shards), largest / len(shards))
        loudness = loudness * jnp.repeat(jnp.exp(heights), dims[dim] // blocks).reshape((-1,) + (1,) * (len(dims) - 1 - dim))
    return loudness


def gaussian(rng, shape, spread, reach, shards=(), kind=jnp.bfloat16):
    entries = jax.random.normal(rng, shape, jnp.float32) * spread
    if len(shards) > 0:
        entries = shard_levels(rng, shape, shards, -0.22, 0.18) * entries
    return jnp.clip(entries, min=-reach, max=reach).astype(kind)


def setup_inputs(seed: int = 0) -> dict:
    splits = jax.random.split(jax.random.key(seed), 3)
    rhs_local = gaussian(splits[0], (NX, NY, NZ), 1.0, 8.0, ((0, 16), (1, 2)), jnp.float32)
    coefficient = jnp.clip(jnp.exp(math.log(3.0) - 2.3025851 * jax.random.uniform(splits[1], (NX, NY, NZ), jnp.float32) ** shard_levels(splits[1], (NX, NY, NZ), ((0, 16), (1, 2)), -0.2, 0.2)), 0.3, 3.0)
    return dict(rhs_local=rhs_local, coefficient=coefficient)


def legendre_value(points, degree):
    previous = np.ones(points.shape)
    current = points.copy()
    for level in range(1, degree):
        following = ((2 * level + 1) * points * current - level * previous) / (level + 1)
        previous = current
        current = following
    return current


def tables():
    degree = 7
    points = np.array([-1.0, -0.8717401485096066, -0.5917001814331423, -0.2092992179024789,
                       0.2092992179024789, 0.5917001814331423, 0.8717401485096066, 1.0])
    values = legendre_value(points, degree)
    weights = 2.0 / (degree * (degree + 1) * values ** 2)
    derivative = np.zeros((8, 8))
    for row_at in range(8):
        for col_at in range(8):
            if row_at != col_at:
                derivative[row_at, col_at] = values[row_at] / (values[col_at] * (points[row_at] - points[col_at]))
    derivative[0, 0] = -degree * (degree + 1) / 4.0
    derivative[7, 7] = degree * (degree + 1) / 4.0
    interp = np.stack([(1.0 - points) / 2.0, (1.0 + points) / 2.0], axis=1)
    slopes = np.array([-0.5, 0.5])
    return derivative, weights, interp, slopes


def fold_local(field, axis_at, per_elem):
    dims_of = field.shape
    elements = dims_of[axis_at] // per_elem
    split = field.reshape(dims_of[:axis_at] + (elements, per_elem) + dims_of[axis_at + 1:])
    first_face = lax.index_in_dim(split, 0, axis_at + 1, keepdims=False)
    last_face = lax.index_in_dim(split, per_elem - 1, axis_at + 1, keepdims=False)
    empty_face = jnp.zeros_like(lax.slice_in_dim(first_face, 0, 1, axis=axis_at))
    from_left = jnp.concatenate([empty_face, lax.slice_in_dim(last_face, 0, elements - 1, axis=axis_at)], axis_at)
    from_right = jnp.concatenate([lax.slice_in_dim(first_face, 1, elements, axis=axis_at), empty_face], axis_at)
    middle = lax.slice_in_dim(split, 1, per_elem - 1, axis=axis_at + 1)
    joined = jnp.concatenate([jnp.expand_dims(first_face + from_left, axis_at + 1), middle,
                              jnp.expand_dims(last_face + from_right, axis_at + 1)], axis_at + 1)
    return joined.reshape(dims_of)


def assemble_all(stacked, per_elem):
    return fold_local(fold_local(fold_local(stacked, 1, per_elem), 2, per_elem), 3, per_elem)


def edge_mask(total):
    spots = jnp.arange(total)
    return ((spots > 0) & (spots < total - 1)).astype(jnp.float32)


def box_mask(size_x, size_y, size_z):
    return edge_mask(size_x)[:, None, None] * edge_mask(size_y)[None, :, None] * edge_mask(size_z)[None, None, :]


def weight_field(size_x, size_y, size_z, weights):
    wvec = jnp.asarray(weights, jnp.float32)
    along_x = jnp.tile(wvec, size_x // 8)
    along_y = jnp.tile(wvec, size_y // 8)
    along_z = jnp.tile(wvec, size_z // 8)
    return along_x[:, None, None] * along_y[None, :, None] * along_z[None, None, :]


def local_operator(field, weighted, derivative, z_matrix):
    size_x, size_y, size_z = field.shape
    precise = lax.Precision.HIGHEST
    z_block = z_matrix.shape[0]
    grad_x = jnp.einsum("ab,ebyz->eayz", derivative, field.reshape(size_x // 8, 8, size_y, size_z), precision=precise).reshape(field.shape)
    grad_y = jnp.einsum("ab,xebz->xeaz", derivative, field.reshape(size_x, size_y // 8, 8, size_z), precision=precise).reshape(field.shape)
    grad_z = jnp.dot(field.reshape(-1, z_block), z_matrix.T, precision=precise, preferred_element_type=jnp.float32).reshape(field.shape)
    flux_x = (weighted * grad_x).reshape(size_x // 8, 8, size_y, size_z)
    flux_y = (weighted * grad_y).reshape(size_x, size_y // 8, 8, size_z)
    flux_z = (weighted * grad_z).reshape(-1, z_block)
    back_x = jnp.einsum("ab,eayz->ebyz", derivative, flux_x, precision=precise).reshape(field.shape)
    back_y = jnp.einsum("ab,xeaz->xebz", derivative, flux_y, precision=precise).reshape(field.shape)
    back_z = jnp.dot(flux_z, z_matrix, precision=precise, preferred_element_type=jnp.float32).reshape(field.shape)
    return back_x + back_y + back_z


def diagonal_local(weighted, derivative, z_matrix):
    size_x, size_y, size_z = weighted.shape
    precise = lax.Precision.HIGHEST
    squared = derivative * derivative
    z_block = z_matrix.shape[0]
    part_x = jnp.einsum("ka,ekyz->eayz", squared, weighted.reshape(size_x // 8, 8, size_y, size_z), precision=precise).reshape(weighted.shape)
    part_y = jnp.einsum("ka,xekz->xeaz", squared, weighted.reshape(size_x, size_y // 8, 8, size_z), precision=precise).reshape(weighted.shape)
    part_z = jnp.dot(weighted.reshape(-1, z_block), z_matrix * z_matrix, precision=precise, preferred_element_type=jnp.float32).reshape(weighted.shape)
    return part_x + part_y + part_z


def restrict(field, interp):
    size_x, size_y, size_z = field.shape
    precise = lax.Precision.HIGHEST
    section_x = jnp.einsum("ai,eayz->eiyz", interp, field.reshape(size_x // 8, 8, size_y, size_z), precision=precise).reshape(size_x // 4, size_y, size_z)
    section_y = jnp.einsum("ai,xeaz->xeiz", interp, section_x.reshape(size_x // 4, size_y // 8, 8, size_z), precision=precise).reshape(size_x // 4, size_y // 4, size_z)
    section_z = jnp.einsum("ai,xyea->xyei", interp, section_y.reshape(size_x // 4, size_y // 4, size_z // 8, 8), precision=precise)
    return section_z.reshape(size_x // 4, size_y // 4, size_z // 4)


def prolong(coarse, interp):
    size_x, size_y, size_z = coarse.shape
    precise = lax.Precision.HIGHEST
    section_z = jnp.einsum("ai,xyei->xyea", interp, coarse.reshape(size_x, size_y, size_z // 2, 2), precision=precise).reshape(size_x, size_y, size_z * 4)
    section_y = jnp.einsum("ai,xeiz->xeaz", interp, section_z.reshape(size_x, size_y // 2, 2, size_z * 4), precision=precise).reshape(size_x, size_y * 4, size_z * 4)
    section_x = jnp.einsum("ai,eiyz->eayz", interp, section_y.reshape(size_x // 2, 2, size_y * 4, size_z * 4), precision=precise)
    return section_x.reshape(size_x * 4, size_y * 4, size_z * 4)


def coarse_matrices(weighted, interp, slopes):
    size_x, size_y, size_z = weighted.shape
    precise = lax.Precision.HIGHEST
    shaped = weighted.reshape(size_x // 8, 8, size_y // 8, 8, size_z // 8, 8)
    interp_t = interp.T
    mass_pair = jnp.asarray(interp_t[:, None, :] * interp_t[None, :, :], jnp.float32)
    grad_pair = jnp.asarray(slopes[:, None, None] * slopes[None, :, None] * np.ones((1, 1, 8)), jnp.float32)
    form = "xaybzc,ipa,jqb,krc->ijkpqrxyz"
    total = jnp.einsum(form, shaped, grad_pair, mass_pair, mass_pair, precision=precise)
    total = total + jnp.einsum(form, shaped, mass_pair, grad_pair, mass_pair, precision=precise)
    total = total + jnp.einsum(form, shaped, mass_pair, mass_pair, grad_pair, precision=precise)
    return total.reshape(8, 8, -1)


def coarse_diagonal(galerkin, ex_n, ey_n, ez_n):
    eye_table = jnp.eye(8, dtype=jnp.float32)
    flat = jnp.sum(galerkin * eye_table[:, :, None], axis=1)
    return flat.reshape(2, 2, 2, ex_n, ey_n, ez_n).transpose(3, 0, 4, 1, 5, 2).reshape(2 * ex_n, 2 * ey_n, 2 * ez_n)


def coarse_apply(galerkin, coarse):
    size_x, size_y, size_z = coarse.shape
    ex_n, ey_n, ez_n = size_x // 2, size_y // 2, size_z // 2
    flat = coarse.reshape(ex_n, 2, ey_n, 2, ez_n, 2).transpose(1, 3, 5, 0, 2, 4).reshape(8, -1)
    result = jnp.sum(galerkin * flat[None, :, :], axis=1)
    return result.reshape(2, 2, 2, ex_n, ey_n, ez_n).transpose(3, 0, 4, 1, 5, 2).reshape(coarse.shape)


def reference(rhs_local, coefficient):
    derivative_np, weights, interp_np, slopes = tables()
    derivative = jnp.asarray(derivative_np, jnp.float32)
    interp = jnp.asarray(interp_np, jnp.float32)
    z_block = min(EZ, 16)
    z_matrix = jnp.asarray(np.kron(np.eye(z_block), derivative_np), jnp.float32)
    size_x, size_y, size_z = rhs_local.shape
    weighted = coefficient * weight_field(size_x, size_y, size_z, weights)
    fmask = box_mask(size_x, size_y, size_z)
    w_blocks = weighted.reshape(N_DOM, size_x // N_DOM, size_y, size_z)

    def apply_block(pair_in):
        return local_operator(pair_in[0], pair_in[1], derivative, z_matrix)

    def operate(field):
        pieces = lax.map(apply_block, (field.reshape(w_blocks.shape), w_blocks))
        return fmask * assemble_all(pieces.reshape(field.shape)[None], 8)[0]

    def galerkin_block(block_in):
        return coarse_matrices(block_in, interp_np, slopes)

    summed = assemble_all(jnp.stack([rhs_local, diagonal_local(weighted, derivative, z_matrix)]), 8)
    residual = fmask * summed[0]
    inverse = fmask / summed[1]
    theta = 1.1
    delta = 0.9
    sigma_val = theta / delta
    rho_prev = 1.0 / sigma_val
    rho_next = 1.0 / (2.0 * sigma_val - rho_prev)
    step_one = inverse * residual / theta
    res_one = residual - operate(step_one)
    second = step_one + rho_next * rho_prev * step_one + (2.0 * rho_next / delta) * inverse * res_one
    res_two = residual - operate(second)
    galerkin = lax.map(galerkin_block, w_blocks)
    galerkin = galerkin.transpose(1, 2, 0, 3).reshape(8, 8, -1)
    coarse_stack = assemble_all(jnp.stack([restrict(res_two, interp), coarse_diagonal(galerkin, MX // 2, MY // 2, MZ // 2)]), 2)
    cmask = box_mask(MX, MY, MZ)
    coarse_rhs = cmask * coarse_stack[0]
    coarse_diag = coarse_stack[1]
    coarse_one = (2.0 / 3.0) * coarse_rhs / coarse_diag
    image_c = cmask * assemble_all(coarse_apply(galerkin, coarse_one)[None], 2)[0]
    coarse_solution = coarse_one + (2.0 / 3.0) * (coarse_rhs - image_c) / coarse_diag
    preconditioned = second + fmask * prolong(coarse_solution, interp)
    return preconditioned, coarse_solution
```

```python
import functools

import jax
import jax.numpy as jnp
import numpy as np
from jax import lax
from jax.experimental import pallas as pl
from jax.experimental.pallas import tpu as pltpu
from jax.sharding import PartitionSpec as P

N = 8
THETA = 1.1
DELTA = 0.9
SIGMA = THETA / DELTA
RHO0 = 1.0 / SIGMA
RHO1 = 1.0 / (2.0 * SIGMA - RHO0)
F32 = jnp.float32
BF16 = jnp.bfloat16
VMEM_LIMIT = 48 * 1024 * 1024


def legendre_value(points, degree):
    previous = np.ones(points.shape)
    current = points.copy()
    for level in range(1, degree):
        following = ((2 * level + 1) * points * current - level * previous) / (level + 1)
        previous = current
        current = following
    return current


def tables():
    degree = 7
    points = np.array(
        [
            -1.0,
            -0.8717401485096066,
            -0.5917001814331423,
            -0.2092992179024789,
            0.2092992179024789,
            0.5917001814331423,
            0.8717401485096066,
            1.0,
        ]
    )
    values = legendre_value(points, degree)
    weights = 2.0 / (degree * (degree + 1) * values**2)
    derivative = np.zeros((8, 8))
    for row_at in range(8):
        for col_at in range(8):
            if row_at != col_at:
                derivative[row_at, col_at] = values[row_at] / (
                    values[col_at] * (points[row_at] - points[col_at])
                )
    derivative[0, 0] = -degree * (degree + 1) / 4.0
    derivative[7, 7] = degree * (degree + 1) / 4.0
    interp = np.stack([(1.0 - points) / 2.0, (1.0 + points) / 2.0], axis=1)
    return derivative, weights, interp


DM, WEIGHTS, INTERP = tables()
MULT = np.array([2.0] + [1.0] * 6 + [2.0])
RHO = MULT[:, None] * INTERP
DRHO = DM @ RHO


def blockdiag(block, count):
    return np.kron(np.eye(count), block)


def hi_lo(matrix):
    hi = matrix.astype(jnp.bfloat16)
    lo = (matrix - hi.astype(np.float64)).astype(jnp.bfloat16)
    return hi, lo


def right_table(matrix):
    hi, lo = hi_lo(matrix)
    return np.concatenate([hi, hi, lo], axis=0)


def left_table(matrix):
    hi, lo = hi_lo(matrix)
    return np.concatenate([hi, hi, lo], axis=1)


def vertex_table(per_node, elements, columns, wrap):
    out = np.zeros((8 * elements, columns))
    for e in range(elements):
        for i in range(2):
            v = e + i
            if v >= columns:
                if not wrap:
                    continue
                v -= columns
            out[8 * e : 8 * e + 8, v] += per_node[:, i]
    return out


def moment_table(per_node, elements, columns):
    out = np.zeros((8 * elements, columns))
    for e in range(elements):
        out[8 * e : 8 * e + 8, e] = per_node
    return out


PAIRS = [(0, 0), (0, 1), (1, 1)]
MASS = [INTERP[:, i] * INTERP[:, j] for i, j in PAIRS]


def round_up(value, to):
    return -(-value // to) * to


def make_tables(ny, nz, own_y, wrap):
    ey, ez = ny // N, nz // N
    cr = round_up(ey, 8)
    t = {}
    t["z_d"] = right_table(blockdiag(DM, ez).T)
    t["z_dt"] = right_table(blockdiag(DM, ez))
    t["z_sq"] = right_table(blockdiag(DM * DM, ez))
    t["y_d"] = left_table(blockdiag(DM, ey))
    t["y_dt"] = left_table(blockdiag(DM, ey).T)
    t["y_sq"] = left_table(blockdiag(DM * DM, ey).T)
    py = vertex_table(RHO, ey, cr, wrap)
    dpy = blockdiag(DM, ey) @ py
    pz = vertex_table(RHO, ez, nz, False)
    dpz = blockdiag(DM, ez) @ pz
    t["ry"] = np.concatenate([py, dpy], axis=0).T.astype(np.float32)
    t["rz"] = np.concatenate([pz, dpz], axis=0).astype(np.float32)
    t["my"] = np.concatenate([moment_table(m, ey, cr) for m in MASS], axis=1).T.astype(np.float32)
    t["mz"] = np.concatenate([moment_table(m, ez, nz) for m in MASS], axis=1).astype(np.float32)
    t["py"] = vertex_table(INTERP, ey, cr, wrap).astype(np.float32)
    t["pz"] = vertex_table(INTERP, ez, nz, False).T.astype(np.float32)
    sy = np.zeros((2 * ey, cr))
    for e in range(ey):
        for i in range(2):
            v = e + i
            if v >= cr:
                v = v - cr if wrap else 0
            sy[2 * e + i, v] = 1.0
    t["sy"] = sy.astype(np.float32)
    sz = np.zeros((nz, 2 * ez))
    for e in range(ez):
        for i in range(2):
            sz[e + i, 2 * e + i] = 1.0
    t["sz"] = sz.astype(np.float32)
    w3 = WEIGHTS[:, None, None] * WEIGHTS[None, :, None] * np.ones((1, 1, nz))
    t["w3"] = (w3 * np.tile(WEIGHTS, ez)[None, None, :]).astype(np.float32)
    return t


def even_odd(matrix, values, sign):
    even = [values[b] + values[7 - b] for b in range(4)]
    odd = [values[b] - values[7 - b] for b in range(4)]
    out = [None] * 8
    for a in range(4):
        pe = po = None
        for b in range(4):
            ce = float((matrix[a, b] + matrix[a, 7 - b]) / 2.0)
            co = float((matrix[a, b] - matrix[a, 7 - b]) / 2.0)
            te = ce * even[b]
            to = co * odd[b]
            pe = te if pe is None else pe + te
            po = to if po is None else po + to
        out[a] = pe + po
        out[7 - a] = pe - po if sign > 0 else po - pe
    return out


def split(x):
    hi = x.astype(BF16)
    lo = (x - hi.astype(F32)).astype(BF16)
    return hi, lo


def dot(a, b):
    return jnp.dot(a, b, preferred_element_type=F32)


def exact_dot(a, b):
    return jnp.dot(a, b, preferred_element_type=F32, precision=lax.Precision.HIGHEST)


def z_apply(hi, lo, table):
    return dot(jnp.concatenate([hi, lo, hi], axis=1), table)


def y_apply(hi, lo, table):
    return dot(table, jnp.concatenate([hi, lo, hi], axis=0))


def assemble_yz(v):
    ny, nz = v.shape
    row = lax.broadcasted_iota(jnp.int32, (N, nz), 0)
    lane = lax.broadcasted_iota(jnp.int32, (1, nz), 1)
    top = (row == N - 1).astype(F32)
    bottom = (row == 0).astype(F32)
    blocks = [v[N * e : N * e + N] for e in range(ny // N)]
    ups = [pltpu.roll(b, N - 1, 0) for b in blocks]
    downs = [pltpu.roll(b, 1, 0) for b in blocks]
    out = []
    for e, b in enumerate(blocks):
        if e + 1 < len(blocks):
            b = b + top * ups[e + 1]
        if e > 0:
            b = b + bottom * downs[e - 1]
        out.append(b)
    v = jnp.concatenate(out, axis=0)
    last = ((lane % N == N - 1) & (lane < nz - 1)).astype(F32)
    first = ((lane % N == 0) & (lane > 0)).astype(F32)
    return v + last * pltpu.roll(v, nz - 1, 1) + first * pltpu.roll(v, 1, 1)


def yz_mask(ny, nz, start, total):
    row = lax.broadcasted_iota(jnp.int32, (ny, nz), 0) + start
    lane = lax.broadcasted_iota(jnp.int32, (ny, nz), 1)
    return (row > 0) & (row < total - 1) & (lane > 0) & (lane < nz - 1)


class Layout:
    def __init__(self, own_y, nz, dom, sub):
        self.own_y, self.nz, self.dom, self.sub = own_y, nz, dom, sub
        self.blocks = min(sub, 3)
        self.ny = own_y * self.blocks
        self.total_y = own_y * sub
        self.wrap = sub <= 2
        self.ey, self.ez = self.ny // N, nz // N
        self.cr = round_up(self.ey, 8)

    def where(self):
        d = lax.axis_index("dom")
        h = lax.axis_index("sub")
        parity = lax.rem(d, 2)
        pair = lax.div(d, 2)
        if self.sub <= 2:
            start = 0
            offset = h * self.own_y
        else:
            start = (h - 1) * self.own_y
            offset = self.own_y
        low = (pair > 0).astype(F32)
        high = (pair < self.dom // 2 - 1).astype(F32)
        return parity, h, start, offset, low, high


def gather_window(lay, own, others, h, store):
    y = lay.own_y
    if lay.sub == 1:
        store(pl.ds(0, y), own)
    elif lay.sub == 2:
        store(pl.ds(pl.multiple_of(h * y, y), y), own)
        store(pl.ds(pl.multiple_of((1 - h) * y, y), y), others[0])
    else:
        store(pl.ds(0, y), others[0])
        store(pl.ds(y, y), own)
        store(pl.ds(2 * y, y), others[1])


def first_kernel(lay, n_other, *refs):
    own_r, own_c, mate = refs[:3]
    other = refs[3 : 3 + n_other]
    mate_other = refs[3 + n_other : 3 + 2 * n_other]
    refs = refs[3 + 2 * n_other :]
    z_sq, y_sq, w3 = refs[:3]
    msg, w_out, rhs_out, u_out, inv_out, res_out = refs[3:9]
    d_s = refs[9]
    ny, nz = lay.ny, lay.nz
    parity, h, start, offset, low, high = lay.where()
    for side, k_own, k_mate, target in (
        (0, own_r[...], mate[0], rhs_out),
        (1, own_c[...], mate[1], w_out),
    ):
        def store(base):
            def put(rows, value):
                target[pl.ds(base, N), rows, :] = value
            return put
        gather_window(lay, k_own, [o[side] for o in other], h, store(parity * N))
        gather_window(lay, k_mate, [o[side] for o in mate_other], h, store((1 - parity) * N))
    table3 = w3[...]
    for el in range(2):
        for e in range(lay.ey):
            rows = pl.ds(N * e, N)
            w = [w_out[N * el + a, rows, :] * table3[a] for a in range(N)]
            dx = even_odd((DM * DM).T, w, 1)
            for a in range(N):
                w_out[N * el + a, rows, :] = w[a]
                d_s[N * el + a, rows, :] = dx[a]
    hi, lo = split(w_out[...].reshape(2 * N * ny, nz))
    dz = z_apply(hi, lo, z_sq[...])
    mask = yz_mask(ny, nz, start, lay.total_y)
    inside = mask.astype(F32)
    own_plane = 15 * parity
    sx_own = d_s[own_plane]
    msg[2] = assemble_yz(sx_own)
    msg[3] = w_out[own_plane]
    for p in range(2 * N):
        cut = slice(p * ny, (p + 1) * ny)
        dy = y_apply(hi[cut], lo[cut], y_sq[...])
        d_s[p] = assemble_yz(d_s[p] + dz[cut] + dy)
        res_out[p] = assemble_yz(rhs_out[p])
    for s in (d_s, res_out):
        both = s[N - 1] + s[N]
        s[N - 1] = both
        s[N] = both
    msg[0] = res_out[own_plane]
    msg[1] = d_s[own_plane]
    for p in range(2 * N):
        if p in (0, 2 * N - 1):
            u_out[p] = jnp.zeros((ny, nz), F32)
            inv_out[p] = d_s[p]
        else:
            inv = inside / jnp.where(mask, d_s[p], 1.0)
            res = inside * res_out[p]
            inv_out[p] = inv
            res_out[p] = res
            u_out[p] = inv * res * (1.0 / THETA)
    base = parity * N
    acc = []
    col = [jnp.where(parity == 0, float(DM[a, 0]), float(DM[a, N - 1])) for a in range(N)]
    for e in range(lay.ey):
        rows = pl.ds(N * e, N)
        u = [u_out[base + a, rows, :] for a in range(N)]
        g = even_odd(DM, u, -1)
        total = None
        for a in range(N):
            term = (w_out[base + a, rows, :] * g[a]) * col[a]
            total = term if total is None else total + term
        acc.append(total)
    msg[4] = assemble_yz(jnp.concatenate(acc, axis=0))


def coarse_tables_kernel(lay, w_ref, rhs_ref, my, mz, ry, rz, g_out, r_out):
    ny, nz, cr = lay.ny, lay.nz, lay.cr
    lhs = []
    for el in range(2):
        for m in MASS:
            total = None
            for a in range(N):
                term = float(m[a]) * w_ref[N * el + a]
                total = term if total is None else total + term
            lhs.append(total)
    along_z = exact_dot(jnp.concatenate(lhs, axis=0), mz[...])
    for el in range(2):
        mom = {}
        for alpha in range(3):
            at = (3 * el + alpha) * ny
            block = exact_dot(my[...], along_z[at : at + ny])
            for beta in range(3):
                for gamma in range(3):
                    mom[alpha, beta, gamma] = block[
                        beta * cr : (beta + 1) * cr, gamma * nz : (gamma + 1) * nz
                    ]
        x_sum, y_sum, z_sum = {}, {}, {}
        for i in range(3):
            for j in range(3):
                x_sum[i, j] = mom[0, i, j] + 2.0 * mom[1, i, j] + mom[2, i, j]
                y_sum[i, j] = mom[i, 0, j] + 2.0 * mom[i, 1, j] + mom[i, 2, j]
                z_sum[i, j] = mom[i, j, 0] + 2.0 * mom[i, j, 1] + mom[i, j, 2]
        sign = (1.0, -1.0, 1.0)
        for alpha in range(3):
            for beta in range(3):
                for gamma in range(3):
                    g_out[el, 9 * alpha + 3 * beta + gamma] = 0.25 * (
                        sign[alpha] * x_sum[beta, gamma]
                        + sign[beta] * y_sum[alpha, gamma]
                        + sign[gamma] * z_sum[alpha, beta]
                    )
    for el in range(2):
        for i in range(2):
            total = None
            for a in range(N):
                term = float(RHO[a, i]) * rhs_ref[N * el + a]
                total = term if total is None else total + term
            part = exact_dot(ry[:, :ny], total)
            r_out[el, i] = exact_dot(part, rz[:nz])


def gradient_flux(lay, u_ref, w_ref, w_low, w_high, z_d, y_d, fx, fy, fz):
    ny, nz = lay.ny, lay.nz
    for el in range(2):
        for e in range(lay.ey):
            rows = pl.ds(N * e, N)
            u = [u_ref[N * el + a, rows, :] for a in range(N)]
            g = even_odd(DM, u, -1)
            for a in range(N):
                fx[N * el + a, rows, :] = w_ref[N * el + a, rows, :] * g[a]
    hi, lo = split(u_ref[...].reshape(2 * N * ny, nz))
    gz = z_apply(hi, lo, z_d[...])
    for p in range(2 * N):
        cut = slice(p * ny, (p + 1) * ny)
        gy = y_apply(hi[cut], lo[cut], y_d[...])
        w = w_ref[p]
        if p == 0 and w_low is not None:
            w = w + w_low
        if p == 2 * N - 1 and w_high is not None:
            w = w + w_high
        fy[p] = w * gy
        fz[p] = w * gz[cut]


def pair_index(i, j):
    return i + j


def shifted(c, q, r):
    if q:
        c = pltpu.roll(c, c.shape[0] - 1, 0)
    if r:
        c = pltpu.roll(c, c.shape[1] - 1, 1)
    return c


def scatter(parts):
    cr, nz = parts[0, 0].shape
    first = parts[0, 0] + pltpu.roll(parts[0, 1], 1, 1)
    second = parts[1, 0] + pltpu.roll(parts[1, 1], 1, 1)
    return first + pltpu.roll(second, 1, 0)


def gathered(c):
    return {(q, r): shifted(c, q, r) for q in range(2) for r in range(2)}


def face_apply(entry, c, out=None):
    out = {} if out is None else out
    for j in range(2):
        for k in range(2):
            for q in range(2):
                for r in range(2):
                    term = entry(pair_index(j, q), pair_index(k, r)) * c[q, r]
                    out[j, k] = term if (j, k) not in out else out[j, k] + term
    return out


def coarse_diag(entry):
    return scatter({(j, k): entry(2 * j, 2 * k) for j in range(2) for k in range(2)})


def coarse_mask(lay, start):
    row = lax.broadcasted_iota(jnp.int32, (lay.cr, lay.nz), 0) + lax.div(start, N)
    lane = lax.broadcasted_iota(jnp.int32, (lay.cr, lay.nz), 1)
    return (row > 0) & (row < lay.total_y // N) & (lane > 0) & (lane < lay.ez)


def second_kernel(lay, *refs):
    own_msg, mate_msg, w_ref, u_in, inv_in, res_in, g_ref, r_ref = refs[:8]
    z_d, z_dt, y_d, y_dt, ry, rz = refs[8:14]
    out, msg, state = refs[14:17]
    u, inv_s, res_s, sec, fx, fy, fz, back = refs[17:]
    ny, nz, cr = lay.ny, lay.nz, lay.cr
    parity, h, start, offset, low, high = lay.where()
    mask = yz_mask(ny, nz, start, lay.total_y)
    inside = mask.astype(F32)
    is_even = parity == 0
    lo_msg = [jnp.where(is_even, own_msg[k], mate_msg[k]) for k in range(5)]
    hi_msg = [jnp.where(is_even, mate_msg[k], own_msg[k]) for k in range(5)]
    u[...] = u_in[...]
    inv_s[...] = inv_in[...]
    res_s[...] = res_in[...]
    for p, m, flag in ((0, lo_msg, low), (2 * N - 1, hi_msg, high)):
        inv = inside * flag / jnp.where(mask, inv_in[p] + m[1], 1.0)
        res = inside * flag * (res_in[p] + m[0])
        inv_s[p] = inv
        res_s[p] = res
        u[p] = inv * res * (1.0 / THETA)
    gradient_flux(lay, u, w_ref, lo_msg[3], hi_msg[3], z_d, y_d, fx, fy, fz)
    for el in range(2):
        for e in range(lay.ey):
            rows = pl.ds(N * e, N)
            b = even_odd(DM.T, [fx[N * el + a, rows, :] for a in range(N)], -1)
            for a in range(N):
                back[N * el + a, rows, :] = b[a]
    hi, lo = split(fz[...].reshape(2 * N * ny, nz))
    bz = z_apply(hi, lo, z_dt[...])
    for p in range(2 * N):
        hi, lo = split(fy[p])
        by = y_apply(hi, lo, y_dt[...])
        back[p] = assemble_yz(back[p] + by + bz[p * ny : (p + 1) * ny])
    both = back[N - 1] + back[N]
    back[N - 1] = both
    back[N] = both
    back[0] = back[0] + lo_msg[4] + lo_msg[2] * u[0]
    back[2 * N - 1] = back[2 * N - 1] + hi_msg[4] + hi_msg[2] * u[2 * N - 1]
    for p in range(2 * N):
        res_one = res_s[p] - inside * back[p]
        sec[p] = (1.0 + RHO1 * RHO0) * u[p] + (2.0 * RHO1 / DELTA) * inv_s[p] * res_one
    out[...] = sec[pl.ds(parity * N, N), pl.ds(pl.multiple_of(offset, N), lay.own_y), :]
    gradient_flux(lay, sec, w_ref, None, None, z_d, y_d, fx, fy, fz)
    r = {}
    for el in range(2):
        for i in range(2):
            sums = []
            for f, weight in ((fx, DRHO), (fy, RHO), (fz, RHO)):
                total = None
                for a in range(N):
                    term = float(weight[a, i]) * f[N * el + a]
                    total = term if total is None else total + term
                sums.append(total)
            first = exact_dot(ry[...], jnp.concatenate(sums[:2], axis=0))
            second = exact_dot(ry[:, :ny], sums[2])
            both = exact_dot(jnp.concatenate([first, second], axis=1), rz[...])
            r[el, i] = r_ref[el, i] - both
    planes = [r[0, 0], r[0, 1] + r[1, 0], r[1, 1]]
    cmask = coarse_mask(lay, start)

    def entry(el, alpha):
        return lambda beta, gamma: g_ref[el, 9 * alpha + 3 * beta + gamma]

    d = [
        coarse_diag(entry(0, 0)),
        coarse_diag(entry(0, 2)) + coarse_diag(entry(1, 0)),
        coarse_diag(entry(1, 2)),
    ]
    cin = cmask.astype(F32)
    mid = (2.0 / 3.0) * cin * planes[1] / jnp.where(cmask, d[1], 1.0)
    c = gathered(mid)
    g_low = scatter(face_apply(entry(0, 1), c))
    g_high = scatter(face_apply(entry(1, 1), c))
    g_mid = scatter(face_apply(entry(1, 0), c, face_apply(entry(0, 2), c)))
    state[0] = planes[0]
    state[1] = planes[1]
    state[2] = planes[2]
    state[3] = d[0]
    state[4] = d[1]
    state[5] = d[2]
    state[6] = g_low
    state[7] = g_mid
    state[8] = g_high
    state[9] = mid
    msg[0] = jnp.where(is_even, planes[0], planes[2])
    msg[1] = jnp.where(is_even, d[0], d[2])
    msg[2] = jnp.where(is_even, g_low, g_high)
    for k in range(9):
        msg[3 + k] = jnp.where(is_even, g_ref[0, k], g_ref[1, 18 + k])


def third_kernel(lay, *refs):
    own_msg, mate_msg, sec, state, g_ref, py, pz, sy, sz, out, coarse = refs
    ny, nz, cr = lay.ny, lay.nz, lay.cr
    parity, h, start, offset, low, high = lay.where()
    is_even = parity == 0
    cmask = coarse_mask(lay, start)
    cin = cmask.astype(F32)
    lo_msg = [jnp.where(is_even, own_msg[k], mate_msg[k]) for k in range(12)]
    hi_msg = [jnp.where(is_even, mate_msg[k], own_msg[k]) for k in range(12)]

    def entry(el, alpha):
        return lambda beta, gamma: g_ref[el, 9 * alpha + 3 * beta + gamma]

    def outer(at, m, flag, el, alpha):
        rhs = cin * flag * (state[at] + m[0])
        d = jnp.where(cmask, state[3 + at] + m[1], 1.0)
        one = (2.0 / 3.0) * rhs / d
        c = gathered(one)
        here = lambda beta, gamma: g_ref[el, 9 * alpha + 3 * beta + gamma] + m[3 + 3 * beta + gamma]
        image = scatter(face_apply(here, c)) + state[6 + at] + m[2]
        cross = face_apply(entry(el, 1), c)
        solution = one + (2.0 / 3.0) * (rhs - cin * flag * image) / d
        return solution, cross

    c_low, cross_low = outer(0, lo_msg, low, 0, 0)
    c_high, cross_high = outer(2, hi_msg, high, 1, 2)
    cross = scatter({k: cross_low[k] + cross_high[k] for k in cross_low})
    rhs = cin * state[1]
    d = jnp.where(cmask, state[4], 1.0)
    c_mid = state[9] + (2.0 / 3.0) * (rhs - cin * (state[7] + cross)) / d
    left = jnp.where(is_even, c_low, c_mid)
    right = jnp.where(is_even, c_mid, c_high)
    both = jnp.concatenate([left, right], axis=1)
    rows = pl.ds(pl.multiple_of(offset, N), lay.own_y)
    along_y = exact_dot(py[rows, :], both)
    q_left = exact_dot(along_y[:, :nz], pz[...])
    q_right = exact_dot(along_y[:, nz:], pz[...])
    inside = yz_mask(lay.own_y, nz, start + offset, lay.total_y).astype(F32)
    q_left = inside * q_left
    q_right = inside * q_right
    first_flag = jnp.where(is_even, low, 1.0)
    last_flag = jnp.where(is_even, 1.0, high)
    for a in range(N):
        add = float(INTERP[a, 0]) * q_left + float(INTERP[a, 1]) * q_right
        if a == 0:
            add = first_flag * add
        if a == N - 1:
            add = last_flag * add
        out[a] = sec[a] + add
    crows = pl.ds(pl.multiple_of(lax.div(offset, 4), lay.own_y // 4), lay.own_y // 4)
    picked = exact_dot(sy[crows, :], both)
    coarse[0] = exact_dot(picked[:, :nz], sz[...])
    coarse[1] = exact_dot(picked[:, nz:], sz[...])


def run(kernel, args, outs, scratch=()):
    vm = pl.BlockSpec(memory_space=pltpu.VMEM)
    return pl.pallas_call(
        kernel,
        out_shape=[jax.ShapeDtypeStruct(o, F32) for o in outs],
        in_specs=[vm] * len(args),
        out_specs=[vm] * len(outs),
        scratch_shapes=[pltpu.VMEM(s, F32) for s in scratch],
        compiler_params=pltpu.CompilerParams(vmem_limit_bytes=VMEM_LIMIT),
    )(*args)


def swap_pairs(count, first):
    pairs = []
    for i in range(first, count - 1, 2):
        pairs += [(i, i + 1), (i + 1, i)]
    return pairs


def shards(dom, sub, rhs_local, coefficient):
    size_x, own_y, nz = rhs_local.shape
    lay = Layout(own_y, nz, dom, sub)
    ny, cr = lay.ny, lay.cr
    t = {k: jnp.asarray(v) for k, v in make_tables(ny, nz, own_y, lay.wrap).items()}
    even = lambda v: lax.ppermute(v, "dom", swap_pairs(dom, 0))
    odd = lambda v: lax.ppermute(v, "dom", swap_pairs(dom, 1))
    raw = jnp.stack([rhs_local, coefficient])
    if sub == 1:
        others = []
    elif sub == 2:
        others = [lax.ppermute(raw, "sub", [(0, 1), (1, 0)])]
    else:
        up = [(i, i + 1) for i in range(sub - 1)]
        others = [
            lax.ppermute(raw, "sub", up),
            lax.ppermute(raw, "sub", [(b, a) for a, b in up]),
        ]
    mate = even(raw)
    mate_others = [even(o) for o in others]
    pair = (2 * N, ny, nz)
    plane = (ny, nz)
    msg, w, rhs, u, inv, res = run(
        functools.partial(first_kernel, lay, len(others)),
        [rhs_local, coefficient, mate, *others, *mate_others, t["z_sq"], t["y_sq"], t["w3"]],
        [(5,) + plane] + [pair] * 5,
        [pair],
    )
    from_odd = odd(msg)
    g, r = run(
        functools.partial(coarse_tables_kernel, lay),
        [w, rhs, t["my"], t["mz"], t["ry"], t["rz"]],
        [(2, 27, cr, nz), (2, 2, cr, nz)],
    )
    from_mate = even(from_odd)
    sec, msg, state = run(
        functools.partial(second_kernel, lay),
        [from_odd, from_mate, w, u, inv, res, g, r]
        + [t[k] for k in ("z_d", "z_dt", "y_d", "y_dt", "ry", "rz")],
        [(N, own_y, nz), (12, cr, nz), (10, cr, nz)],
        [pair] * 8,
    )
    from_odd = odd(msg)
    from_mate = even(from_odd)
    return tuple(
        run(
            functools.partial(third_kernel, lay),
            [from_odd, from_mate, sec, state, g, t["py"], t["pz"], t["sy"], t["sz"]],
            [(N, own_y, nz), (size_x // 4, own_y // 4, nz // 4)],
        )
    )


def solution(mesh):
    dom, sub = mesh.shape["dom"], mesh.shape["sub"]
    return jax.shard_map(
        functools.partial(shards, dom, sub),
        mesh=mesh,
        in_specs=(P("dom", "sub", None), P("dom", "sub", None)),
        out_specs=(P("dom", "sub", None), P("dom", "sub", None)),
        check_vma=False,
    )
```

```python
import functools

import jax
import jax.numpy as jnp
import numpy as np
from jax import lax
from jax.experimental import pallas as pl
from jax.experimental.pallas import tpu as pltpu
from jax.sharding import PartitionSpec as P

N = 8
THETA = 1.1
DELTA = 0.9
SIGMA = THETA / DELTA
RHO0 = 1.0 / SIGMA
RHO1 = 1.0 / (2.0 * SIGMA - RHO0)
F32 = jnp.float32
BF16 = jnp.bfloat16
VMEM_LIMIT = 48 * 1024 * 1024


def legendre_value(points, degree):
    previous = np.ones(points.shape)
    current = points.copy()
    for level in range(1, degree):
        following = ((2 * level + 1) * points * current - level * previous) / (level + 1)
        previous = current
        current = following
    return current


def tables():
    degree = 7
    points = np.array(
        [
            -1.0,
            -0.8717401485096066,
            -0.5917001814331423,
            -0.2092992179024789,
            0.2092992179024789,
            0.5917001814331423,
            0.8717401485096066,
            1.0,
        ]
    )
    values = legendre_value(points, degree)
    weights = 2.0 / (degree * (degree + 1) * values**2)
    derivative = np.zeros((8, 8))
    for row_at in range(8):
        for col_at in range(8):
            if row_at != col_at:
                derivative[row_at, col_at] = values[row_at] / (
                    values[col_at] * (points[row_at] - points[col_at])
                )
    derivative[0, 0] = -degree * (degree + 1) / 4.0
    derivative[7, 7] = degree * (degree + 1) / 4.0
    interp = np.stack([(1.0 - points) / 2.0, (1.0 + points) / 2.0], axis=1)
    return derivative, weights, interp


DM, WEIGHTS, INTERP = tables()
MULT = np.array([2.0] + [1.0] * 6 + [2.0])
RHO = MULT[:, None] * INTERP
DRHO = DM @ RHO


def blockdiag(block, count):
    return np.kron(np.eye(count), block)


def hi_lo(matrix):
    hi = matrix.astype(jnp.bfloat16)
    lo = (matrix - hi.astype(np.float64)).astype(jnp.bfloat16)
    return hi, lo


def right_table(matrix):
    hi, lo = hi_lo(matrix)
    return np.concatenate([hi, hi, lo], axis=0)


def left_table(matrix):
    hi, lo = hi_lo(matrix)
    return np.concatenate([hi, hi, lo], axis=1)


def vertex_table(per_node, elements, columns, wrap):
    out = np.zeros((8 * elements, columns))
    for e in range(elements):
        for i in range(2):
            v = e + i
            if v >= columns:
                if not wrap:
                    continue
                v -= columns
            out[8 * e : 8 * e + 8, v] += per_node[:, i]
    return out


def moment_table(per_node, elements, columns):
    out = np.zeros((8 * elements, columns))
    for e in range(elements):
        out[8 * e : 8 * e + 8, e] = per_node
    return out


PAIRS = [(0, 0), (0, 1), (1, 1)]
MASS = [INTERP[:, i] * INTERP[:, j] for i, j in PAIRS]


def round_up(value, to):
    return -(-value // to) * to


def make_tables(ny, nz, own_y, wrap):
    ey, ez = ny // N, nz // N
    cr = round_up(ey, 8)
    t = {}
    t["z_d"] = right_table(blockdiag(DM, ez).T)
    t["z_dt"] = right_table(blockdiag(DM, ez))
    t["z_sq"] = right_table(blockdiag(DM * DM, ez))
    t["y_d"] = left_table(blockdiag(DM, ey))
    t["y_dt"] = left_table(blockdiag(DM, ey).T)
    t["y_sq"] = left_table(blockdiag(DM * DM, ey).T)
    py = vertex_table(RHO, ey, cr, wrap)
    dpy = blockdiag(DM, ey) @ py
    pz = vertex_table(RHO, ez, nz, False)
    dpz = blockdiag(DM, ez) @ pz
    t["ry"] = np.concatenate([py, dpy], axis=0).T.astype(np.float32)
    t["rz"] = np.concatenate([pz, dpz], axis=0).astype(np.float32)
    t["my"] = np.concatenate([moment_table(m, ey, cr) for m in MASS], axis=1).T.astype(np.float32)
    t["mz"] = np.concatenate([moment_table(m, ez, nz) for m in MASS], axis=1).astype(np.float32)
    t["py"] = vertex_table(INTERP, ey, cr, wrap).astype(np.float32)
    t["pz"] = vertex_table(INTERP, ez, nz, False).T.astype(np.float32)
    sy = np.zeros((2 * ey, cr))
    for e in range(ey):
        for i in range(2):
            v = e + i
            if v >= cr:
                v = v - cr if wrap else 0
            sy[2 * e + i, v] = 1.0
    t["sy"] = sy.astype(np.float32)
    sz = np.zeros((nz, 2 * ez))
    for e in range(ez):
        for i in range(2):
            sz[e + i, 2 * e + i] = 1.0
    t["sz"] = sz.astype(np.float32)
    w3 = WEIGHTS[:, None, None] * WEIGHTS[None, :, None] * np.ones((1, 1, nz))
    t["w3"] = (w3 * np.tile(WEIGHTS, ez)[None, None, :]).astype(np.float32)
    return t


def even_odd(matrix, values, sign):
    even = [values[b] + values[7 - b] for b in range(4)]
    odd = [values[b] - values[7 - b] for b in range(4)]
    out = [None] * 8
    for a in range(4):
        pe = po = None
        for b in range(4):
            ce = float((matrix[a, b] + matrix[a, 7 - b]) / 2.0)
            co = float((matrix[a, b] - matrix[a, 7 - b]) / 2.0)
            te = ce * even[b]
            to = co * odd[b]
            pe = te if pe is None else pe + te
            po = to if po is None else po + to
        out[a] = pe + po
        out[7 - a] = pe - po if sign > 0 else po - pe
    return out


def split(x):
    hi = x.astype(BF16)
    lo = (x - hi.astype(F32)).astype(BF16)
    return hi, lo


def dot(a, b):
    return jnp.dot(a, b, preferred_element_type=F32)


def exact_dot(a, b):
    return jnp.dot(a, b, preferred_element_type=F32, precision=lax.Precision.HIGHEST)


def z_apply(hi, lo, table):
    return dot(jnp.concatenate([hi, lo, hi], axis=1), table)


def y_apply(hi, lo, table):
    return dot(table, jnp.concatenate([hi, lo, hi], axis=0))


def assemble_yz(v):
    ny, nz = v.shape
    row = lax.broadcasted_iota(jnp.int32, (N, nz), 0)
    lane = lax.broadcasted_iota(jnp.int32, (1, nz), 1)
    top = (row == N - 1).astype(F32)
    bottom = (row == 0).astype(F32)
    blocks = [v[N * e : N * e + N] for e in range(ny // N)]
    ups = [pltpu.roll(b, N - 1, 0) for b in blocks]
    downs = [pltpu.roll(b, 1, 0) for b in blocks]
    out = []
    for e, b in enumerate(blocks):
        if e + 1 < len(blocks):
            b = b + top * ups[e + 1]
        if e > 0:
            b = b + bottom * downs[e - 1]
        out.append(b)
    v = jnp.concatenate(out, axis=0)
    last = ((lane % N == N - 1) & (lane < nz - 1)).astype(F32)
    first = ((lane % N == 0) & (lane > 0)).astype(F32)
    return v + last * pltpu.roll(v, nz - 1, 1) + first * pltpu.roll(v, 1, 1)


def yz_mask(ny, nz, start, total):
    row = lax.broadcasted_iota(jnp.int32, (ny, nz), 0) + start
    lane = lax.broadcasted_iota(jnp.int32, (ny, nz), 1)
    return (row > 0) & (row < total - 1) & (lane > 0) & (lane < nz - 1)


class Layout:
    def __init__(self, own_y, nz, dom, sub):
        self.own_y, self.nz, self.dom, self.sub = own_y, nz, dom, sub
        self.blocks = min(sub, 3)
        self.ny = own_y * self.blocks
        self.total_y = own_y * sub
        self.wrap = sub <= 2
        self.ey, self.ez = self.ny // N, nz // N
        self.cr = round_up(self.ey, 8)

    def where(self):
        d = lax.axis_index("dom")
        h = lax.axis_index("sub")
        parity = lax.rem(d, 2)
        pair = lax.div(d, 2)
        if self.sub <= 2:
            start = 0
            offset = h * self.own_y
        else:
            start = (h - 1) * self.own_y
            offset = self.own_y
        low = (pair > 0).astype(F32)
        high = (pair < self.dom // 2 - 1).astype(F32)
        return parity, h, start, offset, low, high


def gather_window(lay, own, others, h, store):
    y = lay.own_y
    if lay.sub == 1:
        store(pl.ds(0, y), own)
    elif lay.sub == 2:
        store(pl.ds(pl.multiple_of(h * y, y), y), own)
        store(pl.ds(pl.multiple_of((1 - h) * y, y), y), others[0])
    else:
        store(pl.ds(0, y), others[0])
        store(pl.ds(y, y), own)
        store(pl.ds(2 * y, y), others[1])


def first_kernel(lay, n_other, *refs):
    own_r, own_c, mate = refs[:3]
    other = refs[3 : 3 + n_other]
    mate_other = refs[3 + n_other : 3 + 2 * n_other]
    refs = refs[3 + 2 * n_other :]
    z_sq, y_sq, w3 = refs[:3]
    msg, w_out, rhs_out, u_out, inv_out, res_out = refs[3:9]
    d_s = refs[9]
    ny, nz = lay.ny, lay.nz
    parity, h, start, offset, low, high = lay.where()
    for side, k_own, k_mate, target in (
        (0, own_r[...], mate[0], rhs_out),
        (1, own_c[...], mate[1], w_out),
    ):
        def store(base):
            def put(rows, value):
                target[pl.ds(base, N), rows, :] = value
            return put
        gather_window(lay, k_own, [o[side] for o in other], h, store(parity * N))
        gather_window(lay, k_mate, [o[side] for o in mate_other], h, store((1 - parity) * N))
    table3 = w3[...]
    for el in range(2):
        for e in range(lay.ey):
            rows = pl.ds(N * e, N)
            w = [w_out[N * el + a, rows, :] * table3[a] for a in range(N)]
            dx = even_odd((DM * DM).T, w, 1)
            for a in range(N):
                w_out[N * el + a, rows, :] = w[a]
                d_s[N * el + a, rows, :] = dx[a]
    hi, lo = split(w_out[...].reshape(2 * N * ny, nz))
    dz = z_apply(hi, lo, z_sq[...])
    mask = yz_mask(ny, nz, start, lay.total_y)
    inside = mask.astype(F32)
    own_plane = 15 * parity
    sx_own = d_s[own_plane]
    msg[2] = assemble_yz(sx_own)
    msg[3] = w_out[own_plane]
    for p in range(2 * N):
        cut = slice(p * ny, (p + 1) * ny)
        dy = y_apply(hi[cut], lo[cut], y_sq[...])
        d_s[p] = assemble_yz(d_s[p] + dz[cut] + dy)
        res_out[p] = assemble_yz(rhs_out[p])
    for s in (d_s, res_out):
        both = s[N - 1] + s[N]
        s[N - 1] = both
        s[N] = both
    msg[0] = res_out[own_plane]
    msg[1] = d_s[own_plane]
    for p in range(2 * N):
        if p in (0, 2 * N - 1):
            u_out[p] = jnp.zeros((ny, nz), F32)
            inv_out[p] = d_s[p]
        else:
            inv = inside / jnp.where(mask, d_s[p], 1.0)
            res = inside * res_out[p]
            inv_out[p] = inv
            res_out[p] = res
            u_out[p] = inv * res * (1.0 / THETA)
    base = parity * N
    acc = []
    col = [jnp.where(parity == 0, float(DM[a, 0]), float(DM[a, N - 1])) for a in range(N)]
    for e in range(lay.ey):
        rows = pl.ds(N * e, N)
        u = [u_out[base + a, rows, :] for a in range(N)]
        g = even_odd(DM, u, -1)
        total = None
        for a in range(N):
            term = (w_out[base + a, rows, :] * g[a]) * col[a]
            total = term if total is None else total + term
        acc.append(total)
    msg[4] = assemble_yz(jnp.concatenate(acc, axis=0))


def coarse_tables_kernel(lay, w_ref, rhs_ref, my, mz, ry, rz, g_out, r_out):
    ny, nz, cr = lay.ny, lay.nz, lay.cr
    lhs = []
    for el in range(2):
        for m in MASS:
            total = None
            for a in range(N):
                term = float(m[a]) * w_ref[N * el + a]
                total = term if total is None else total + term
            lhs.append(total)
    along_z = exact_dot(jnp.concatenate(lhs, axis=0), mz[...])
    for el in range(2):
        mom = {}
        for alpha in range(3):
            at = (3 * el + alpha) * ny
            block = exact_dot(my[...], along_z[at : at + ny])
            for beta in range(3):
                for gamma in range(3):
                    mom[alpha, beta, gamma] = block[
                        beta * cr : (beta + 1) * cr, gamma * nz : (gamma + 1) * nz
                    ]
        x_sum, y_sum, z_sum = {}, {}, {}
        for i in range(3):
            for j in range(3):
                x_sum[i, j] = mom[0, i, j] + 2.0 * mom[1, i, j] + mom[2, i, j]
                y_sum[i, j] = mom[i, 0, j] + 2.0 * mom[i, 1, j] + mom[i, 2, j]
                z_sum[i, j] = mom[i, j, 0] + 2.0 * mom[i, j, 1] + mom[i, j, 2]
        sign = (1.0, -1.0, 1.0)
        for alpha in range(3):
            for beta in range(3):
                for gamma in range(3):
                    g_out[el, 9 * alpha + 3 * beta + gamma] = 0.25 * (
                        sign[alpha] * x_sum[beta, gamma]
                        + sign[beta] * y_sum[alpha, gamma]
                        + sign[gamma] * z_sum[alpha, beta]
                    )
    for el in range(2):
        for i in range(2):
            total = None
            for a in range(N):
                term = float(RHO[a, i]) * rhs_ref[N * el + a]
                total = term if total is None else total + term
            part = exact_dot(ry[:, :ny], total)
            r_out[el, i] = exact_dot(part, rz[:nz])


def gradient_flux(lay, u_ref, w_ref, w_low, w_high, z_d, y_d, fx, fy, fz):
    ny, nz = lay.ny, lay.nz
    for el in range(2):
        for e in range(lay.ey):
            rows = pl.ds(N * e, N)
            u = [u_ref[N * el + a, rows, :] for a in range(N)]
            g = even_odd(DM, u, -1)
            for a in range(N):
                fx[N * el + a, rows, :] = w_ref[N * el + a, rows, :] * g[a]
    hi, lo = split(u_ref[...].reshape(2 * N * ny, nz))
    gz = z_apply(hi, lo, z_d[...])
    for p in range(2 * N):
        cut = slice(p * ny, (p + 1) * ny)
        gy = y_apply(hi[cut], lo[cut], y_d[...])
        w = w_ref[p]
        if p == 0 and w_low is not None:
            w = w + w_low
        if p == 2 * N - 1 and w_high is not None:
            w = w + w_high
        fy[p] = w * gy
        fz[p] = w * gz[cut]


def pair_index(i, j):
    return i + j


def shifted(c, q, r):
    if q:
        c = pltpu.roll(c, c.shape[0] - 1, 0)
    if r:
        c = pltpu.roll(c, c.shape[1] - 1, 1)
    return c


def scatter(parts):
    cr, nz = parts[0, 0].shape
    first = parts[0, 0] + pltpu.roll(parts[0, 1], 1, 1)
    second = parts[1, 0] + pltpu.roll(parts[1, 1], 1, 1)
    return first + pltpu.roll(second, 1, 0)


def gathered(c):
    return {(q, r): shifted(c, q, r) for q in range(2) for r in range(2)}


def face_apply(entry, c, out=None):
    out = {} if out is None else out
    for j in range(2):
        for k in range(2):
            for q in range(2):
                for r in range(2):
                    term = entry(pair_index(j, q), pair_index(k, r)) * c[q, r]
                    out[j, k] = term if (j, k) not in out else out[j, k] + term
    return out


def coarse_diag(entry):
    return scatter({(j, k): entry(2 * j, 2 * k) for j in range(2) for k in range(2)})


def coarse_mask(lay, start):
    row = lax.broadcasted_iota(jnp.int32, (lay.cr, lay.nz), 0) + lax.div(start, N)
    lane = lax.broadcasted_iota(jnp.int32, (lay.cr, lay.nz), 1)
    return (row > 0) & (row < lay.total_y // N) & (lane > 0) & (lane < lay.ez)


def second_kernel(lay, *refs):
    own_msg, mate_msg, w_ref, u_in, inv_in, res_in, g_ref, r_ref = refs[:8]
    z_d, z_dt, y_d, y_dt, ry, rz = refs[8:14]
    out, msg, state = refs[14:17]
    u, inv_s, res_s, sec, fx, fy, fz, back = refs[17:]
    ny, nz, cr = lay.ny, lay.nz, lay.cr
    parity, h, start, offset, low, high = lay.where()
    mask = yz_mask(ny, nz, start, lay.total_y)
    inside = mask.astype(F32)
    is_even = parity == 0
    lo_msg = [jnp.where(is_even, own_msg[k], mate_msg[k]) for k in range(5)]
    hi_msg = [jnp.where(is_even, mate_msg[k], own_msg[k]) for k in range(5)]
    u[...] = u_in[...]
    inv_s[...] = inv_in[...]
    res_s[...] = res_in[...]
    for p, m, flag in ((0, lo_msg, low), (2 * N - 1, hi_msg, high)):
        inv = inside * flag / jnp.where(mask, inv_in[p] + m[1], 1.0)
        res = inside * flag * (res_in[p] + m[0])
        inv_s[p] = inv
        res_s[p] = res
        u[p] = inv * res * (1.0 / THETA)
    gradient_flux(lay, u, w_ref, lo_msg[3], hi_msg[3], z_d, y_d, fx, fy, fz)
    for el in range(2):
        for e in range(lay.ey):
            rows = pl.ds(N * e, N)
            b = even_odd(DM.T, [fx[N * el + a, rows, :] for a in range(N)], -1)
            for a in range(N):
                back[N * el + a, rows, :] = b[a]
    hi, lo = split(fz[...].reshape(2 * N * ny, nz))
    bz = z_apply(hi, lo, z_dt[...])
    for p in range(2 * N):
        hi, lo = split(fy[p])
        by = y_apply(hi, lo, y_dt[...])
        back[p] = assemble_yz(back[p] + by + bz[p * ny : (p + 1) * ny])
    both = back[N - 1] + back[N]
    back[N - 1] = both
    back[N] = both
    back[0] = back[0] + lo_msg[4] + lo_msg[2] * u[0]
    back[2 * N - 1] = back[2 * N - 1] + hi_msg[4] + hi_msg[2] * u[2 * N - 1]
    for p in range(2 * N):
        res_one = res_s[p] - inside * back[p]
        sec[p] = (1.0 + RHO1 * RHO0) * u[p] + (2.0 * RHO1 / DELTA) * inv_s[p] * res_one
    out[...] = sec[pl.ds(parity * N, N), pl.ds(pl.multiple_of(offset, N), lay.own_y), :]
    gradient_flux(lay, sec, w_ref, None, None, z_d, y_d, fx, fy, fz)
    r = {}
    for el in range(2):
        for i in range(2):
            sums = []
            for f, weight in ((fx, DRHO), (fy, RHO), (fz, RHO)):
                total = None
                for a in range(N):
                    term = float(weight[a, i]) * f[N * el + a]
                    total = term if total is None else total + term
                sums.append(total)
            first = exact_dot(ry[...], jnp.concatenate(sums[:2], axis=0))
            second = exact_dot(ry[:, :ny], sums[2])
            both = exact_dot(jnp.concatenate([first, second], axis=1), rz[...])
            r[el, i] = r_ref[el, i] - both
    planes = [r[0, 0], r[0, 1] + r[1, 0], r[1, 1]]
    cmask = coarse_mask(lay, start)

    def entry(el, alpha):
        return lambda beta, gamma: g_ref[el, 9 * alpha + 3 * beta + gamma]

    d = [
        coarse_diag(entry(0, 0)),
        coarse_diag(entry(0, 2)) + coarse_diag(entry(1, 0)),
        coarse_diag(entry(1, 2)),
    ]
    cin = cmask.astype(F32)
    mid = (2.0 / 3.0) * cin * planes[1] / jnp.where(cmask, d[1], 1.0)
    c = gathered(mid)
    g_low = scatter(face_apply(entry(0, 1), c))
    g_high = scatter(face_apply(entry(1, 1), c))
    g_mid = scatter(face_apply(entry(1, 0), c, face_apply(entry(0, 2), c)))
    state[0] = planes[0]
    state[1] = planes[1]
    state[2] = planes[2]
    state[3] = d[0]
    state[4] = d[1]
    state[5] = d[2]
    state[6] = g_low
    state[7] = g_mid
    state[8] = g_high
    state[9] = mid
    msg[0] = jnp.where(is_even, planes[0], planes[2])
    msg[1] = jnp.where(is_even, d[0], d[2])
    msg[2] = jnp.where(is_even, g_low, g_high)
    for k in range(9):
        msg[3 + k] = jnp.where(is_even, g_ref[0, k], g_ref[1, 18 + k])


def third_kernel(lay, *refs):
    own_msg, mate_msg, sec, state, g_ref, py, pz, sy, sz, out, coarse = refs
    ny, nz, cr = lay.ny, lay.nz, lay.cr
    parity, h, start, offset, low, high = lay.where()
    is_even = parity == 0
    cmask = coarse_mask(lay, start)
    cin = cmask.astype(F32)
    lo_msg = [jnp.where(is_even, own_msg[k], mate_msg[k]) for k in range(12)]
    hi_msg = [jnp.where(is_even, mate_msg[k], own_msg[k]) for k in range(12)]

    def entry(el, alpha):
        return lambda beta, gamma: g_ref[el, 9 * alpha + 3 * beta + gamma]

    def outer(at, m, flag, el, alpha):
        rhs = cin * flag * (state[at] + m[0])
        d = jnp.where(cmask, state[3 + at] + m[1], 1.0)
        one = (2.0 / 3.0) * rhs / d
        c = gathered(one)
        here = lambda beta, gamma: g_ref[el, 9 * alpha + 3 * beta + gamma] + m[3 + 3 * beta + gamma]
        image = scatter(face_apply(here, c)) + state[6 + at] + m[2]
        cross = face_apply(entry(el, 1), c)
        solution = one + (2.0 / 3.0) * (rhs - cin * flag * image) / d
        return solution, cross

    c_low, cross_low = outer(0, lo_msg, low, 0, 0)
    c_high, cross_high = outer(2, hi_msg, high, 1, 2)
    cross = scatter({k: cross_low[k] + cross_high[k] for k in cross_low})
    rhs = cin * state[1]
    d = jnp.where(cmask, state[4], 1.0)
    c_mid = state[9] + (2.0 / 3.0) * (rhs - cin * (state[7] + cross)) / d
    left = jnp.where(is_even, c_low, c_mid)
    right = jnp.where(is_even, c_mid, c_high)
    both = jnp.concatenate([left, right], axis=1)
    rows = pl.ds(pl.multiple_of(offset, N), lay.own_y)
    along_y = exact_dot(py[rows, :], both)
    q_left = exact_dot(along_y[:, :nz], pz[...])
    q_right = exact_dot(along_y[:, nz:], pz[...])
    inside = yz_mask(lay.own_y, nz, start + offset, lay.total_y).astype(F32)
    q_left = inside * q_left
    q_right = inside * q_right
    first_flag = jnp.where(is_even, low, 1.0)
    last_flag = jnp.where(is_even, 1.0, high)
    for a in range(N):
        add = float(INTERP[a, 0]) * q_left + float(INTERP[a, 1]) * q_right
        if a == 0:
            add = first_flag * add
        if a == N - 1:
            add = last_flag * add
        out[a] = sec[a] + add
    crows = pl.ds(pl.multiple_of(lax.div(offset, 4), lay.own_y // 4), lay.own_y // 4)
    picked = exact_dot(sy[crows, :], both)
    coarse[0] = exact_dot(picked[:, :nz], sz[...])
    coarse[1] = exact_dot(picked[:, nz:], sz[...])


def run(kernel, args, outs, scratch=()):
    vm = pl.BlockSpec(memory_space=pltpu.VMEM)
    return pl.pallas_call(
        kernel,
        out_shape=[jax.ShapeDtypeStruct(o, F32) for o in outs],
        in_specs=[vm] * len(args),
        out_specs=[vm] * len(outs),
        scratch_shapes=[pltpu.VMEM(s, F32) for s in scratch],
        compiler_params=pltpu.CompilerParams(vmem_limit_bytes=VMEM_LIMIT),
    )(*args)


def swap_pairs(count, first):
    pairs = []
    for i in range(first, count - 1, 2):
        pairs += [(i, i + 1), (i + 1, i)]
    return pairs


def chip_pairs(dom, sub):
    pairs = []
    for a, b in swap_pairs(dom, 1):
        pairs += [(a * sub + q, b * sub + q) for q in range(sub)]
    for end in (0, dom - 1):
        pairs += [(end * sub + a, end * sub + b) for a, b in swap_pairs(sub, 0)]
    return pairs


def shards(dom, sub, rhs_local, coefficient):
    size_x, own_y, nz = rhs_local.shape
    lay = Layout(own_y, nz, dom, sub)
    ny, cr = lay.ny, lay.cr
    t = {k: jnp.asarray(v) for k, v in make_tables(ny, nz, own_y, lay.wrap).items()}
    even = lambda v: lax.ppermute(v, "dom", swap_pairs(dom, 0))
    odd = lambda v: lax.ppermute(v, ("dom", "sub"), chip_pairs(dom, sub))
    raw = jnp.stack([rhs_local, coefficient])
    if sub == 1:
        others = []
    elif sub == 2:
        others = [lax.ppermute(raw, "sub", [(0, 1), (1, 0)])]
    else:
        up = [(i, i + 1) for i in range(sub - 1)]
        others = [
            lax.ppermute(raw, "sub", up),
            lax.ppermute(raw, "sub", [(b, a) for a, b in up]),
        ]
    mate = even(raw)
    mate_others = [even(o) for o in others]
    pair = (2 * N, ny, nz)
    plane = (ny, nz)
    msg, w, rhs, u, inv, res = run(
        functools.partial(first_kernel, lay, len(others)),
        [rhs_local, coefficient, mate, *others, *mate_others, t["z_sq"], t["y_sq"], t["w3"]],
        [(5,) + plane] + [pair] * 5,
        [pair],
    )
    from_odd = odd(msg)
    g, r = run(
        functools.partial(coarse_tables_kernel, lay),
        [w, rhs, t["my"], t["mz"], t["ry"], t["rz"]],
        [(2, 27, cr, nz), (2, 2, cr, nz)],
    )
    from_odd, g, r = lax.optimization_barrier((from_odd, g, r))
    from_mate = even(from_odd)
    sec, msg, state = run(
        functools.partial(second_kernel, lay),
        [from_odd, from_mate, w, u, inv, res, g, r]
        + [t[k] for k in ("z_d", "z_dt", "y_d", "y_dt", "ry", "rz")],
        [(N, own_y, nz), (12, cr, nz), (10, cr, nz)],
        [pair] * 8,
    )
    from_odd = odd(msg)
    from_mate = even(from_odd)
    return tuple(
        run(
            functools.partial(third_kernel, lay),
            [from_odd, from_mate, sec, state, g, t["py"], t["pz"], t["sy"], t["sz"]],
            [(N, own_y, nz), (size_x // 4, own_y // 4, nz // 4)],
        )
    )


def solution(mesh):
    dom, sub = mesh.shape["dom"], mesh.shape["sub"]
    return jax.shard_map(
        functools.partial(shards, dom, sub),
        mesh=mesh,
        in_specs=(P("dom", "sub", None), P("dom", "sub", None)),
        out_specs=(P("dom", "sub", None), P("dom", "sub", None)),
        check_vma=False,
    )
```

```python
import functools

import jax
import jax.numpy as jnp
import numpy as np
from jax import lax
from jax.experimental import pallas as pl
from jax.experimental.pallas import tpu as pltpu
from jax.sharding import PartitionSpec as P

N = 8
SPARE = 3 * N
HALO = 3 * N
THETA = 1.1
DELTA = 0.9
SIGMA = THETA / DELTA
RHO0 = 1.0 / SIGMA
RHO1 = 1.0 / (2.0 * SIGMA - RHO0)
F32 = jnp.float32
BF16 = jnp.bfloat16
VMEM_LIMIT = 48 * 1024 * 1024


def legendre_value(points, degree):
    previous = np.ones(points.shape)
    current = points.copy()
    for level in range(1, degree):
        following = ((2 * level + 1) * points * current - level * previous) / (level + 1)
        previous = current
        current = following
    return current


def tables():
    degree = 7
    points = np.array(
        [
            -1.0,
            -0.8717401485096066,
            -0.5917001814331423,
            -0.2092992179024789,
            0.2092992179024789,
            0.5917001814331423,
            0.8717401485096066,
            1.0,
        ]
    )
    values = legendre_value(points, degree)
    weights = 2.0 / (degree * (degree + 1) * values**2)
    derivative = np.zeros((8, 8))
    for row_at in range(8):
        for col_at in range(8):
            if row_at != col_at:
                derivative[row_at, col_at] = values[row_at] / (
                    values[col_at] * (points[row_at] - points[col_at])
                )
    derivative[0, 0] = -degree * (degree + 1) / 4.0
    derivative[7, 7] = degree * (degree + 1) / 4.0
    interp = np.stack([(1.0 - points) / 2.0, (1.0 + points) / 2.0], axis=1)
    return derivative, weights, interp


DM, WEIGHTS, INTERP = tables()
MULT = np.array([2.0] + [1.0] * 6 + [2.0])
RHO = MULT[:, None] * INTERP
DRHO = DM @ RHO


def blockdiag(block, count):
    return np.kron(np.eye(count), block)


def hi_lo(matrix):
    hi = matrix.astype(jnp.bfloat16)
    lo = (matrix - hi.astype(np.float64)).astype(jnp.bfloat16)
    return hi, lo


def right_table(matrix):
    hi, lo = hi_lo(matrix)
    return np.concatenate([hi, hi, lo], axis=0).astype(np.float32)


def left_table(matrix):
    hi, lo = hi_lo(matrix)
    return np.concatenate([hi, hi, lo], axis=1).astype(np.float32)


def vertex_table(per_node, elements, columns, count=8):
    out = np.zeros((count * elements, columns))
    for e in range(elements):
        for i in range(2):
            out[count * e : count * (e + 1), e + i] += per_node[:, i]
    return out


def moment_table(per_node, elements, columns):
    out = np.zeros((8 * elements, columns))
    for e in range(elements):
        out[8 * e : 8 * e + 8, e] = per_node
    return out


PAIRS = [(0, 0), (0, 1), (1, 1)]
MASS = [INTERP[:, i] * INTERP[:, j] for i, j in PAIRS]


def round_up(value, to):
    return -(-value // to) * to


def make_tables(ny, nz, own_y):
    ey, ez = ny // N, nz // N
    cr = round_up(ey + 1, 8)
    t = {}
    t["z_d"] = right_table(blockdiag(DM, ez).T)
    t["z_dt"] = right_table(blockdiag(DM, ez))
    t["z_sq"] = right_table(blockdiag(DM * DM, ez))
    t["y_d"] = left_table(blockdiag(DM, ey))
    t["y_dt"] = left_table(blockdiag(DM, ey).T)
    t["y_sq"] = left_table(blockdiag(DM * DM, ey).T)
    t["y_sq_own"] = left_table(blockdiag(DM * DM, own_y // N).T)
    py = vertex_table(RHO, ey, cr)
    dpy = blockdiag(DM, ey) @ py
    pz = vertex_table(RHO, ez, nz)
    dpz = blockdiag(DM, ez) @ pz
    t["ry"] = left_table(np.concatenate([py, dpy], axis=0).T)
    t["ry_one"] = left_table(py.T)
    t["rz"] = right_table(np.concatenate([pz, dpz], axis=0))
    t["rz_one"] = right_table(pz)
    t["my"] = left_table(np.concatenate([moment_table(m, ey, cr) for m in MASS], axis=1).T)
    t["mz"] = right_table(np.concatenate([moment_table(m, ez, nz) for m in MASS], axis=1))
    own_ey = own_y // N
    py = vertex_table(INTERP, own_ey, cr)
    t["py"] = left_table(np.concatenate([py, vertex_table(np.eye(2), own_ey, cr, 2)], axis=0))
    pz = vertex_table(INTERP, ez, nz).T
    sz = vertex_table(np.eye(2), ez, nz, 2).T
    t["pz"] = right_table(np.concatenate([pz, sz], axis=1))
    cols = np.concatenate([DM.T, DM.T[[N - 1]], DM.T[[0]]], axis=0)
    t["line"] = np.broadcast_to(cols[:, :, None], (N + 2, N, nz)).astype(np.float32)
    w3 = WEIGHTS[:, None, None] * WEIGHTS[None, :, None] * np.ones((1, 1, nz))
    t["w3"] = (w3 * np.tile(WEIGHTS, ez)[None, None, :]).astype(np.float32)
    return t


def even_odd(matrix, values, sign):
    even = [values[b] + values[7 - b] for b in range(4)]
    odd = [values[b] - values[7 - b] for b in range(4)]
    out = [None] * 8
    for a in range(4):
        pe = po = None
        for b in range(4):
            ce = float((matrix[a, b] + matrix[a, 7 - b]) / 2.0)
            co = float((matrix[a, b] - matrix[a, 7 - b]) / 2.0)
            te = ce * even[b]
            to = co * odd[b]
            pe = te if pe is None else pe + te
            po = to if po is None else po + to
        out[a] = pe + po
        out[7 - a] = pe - po if sign > 0 else po - pe
    return out


def split(x):
    hi = x.astype(BF16)
    lo = (x - hi.astype(F32)).astype(BF16)
    return hi, lo


def dot(a, b):
    return jnp.dot(a, b, preferred_element_type=F32)


def z_apply(hi, lo, table):
    return dot(jnp.concatenate([hi, lo, hi], axis=1), table.astype(BF16))


def y_apply(hi, lo, table):
    return dot(table.astype(BF16), jnp.concatenate([hi, lo, hi], axis=0))


def assemble_yz(v):
    ny, nz = v.shape
    row = lax.broadcasted_iota(jnp.int32, (N, nz), 0)
    lane = lax.broadcasted_iota(jnp.int32, (1, nz), 1)
    top = (row == N - 1).astype(F32)
    bottom = (row == 0).astype(F32)
    blocks = [v[N * e : N * e + N] for e in range(ny // N)]
    ups = [pltpu.roll(b, N - 1, 0) for b in blocks]
    downs = [pltpu.roll(b, 1, 0) for b in blocks]
    out = []
    for e, b in enumerate(blocks):
        if e + 1 < len(blocks):
            b = b + top * ups[e + 1]
        if e > 0:
            b = b + bottom * downs[e - 1]
        out.append(b)
    v = jnp.concatenate(out, axis=0)
    last = ((lane % N == N - 1) & (lane < nz - 1)).astype(F32)
    first = ((lane % N == 0) & (lane > 0)).astype(F32)
    return v + last * pltpu.roll(v, nz - 1, 1) + first * pltpu.roll(v, 1, 1)


def yz_mask(ny, nz, start, total):
    row = lax.broadcasted_iota(jnp.int32, (ny, nz), 0) + start
    lane = lax.broadcasted_iota(jnp.int32, (ny, nz), 1)
    return (row > 0) & (row < total - 1) & (lane > 0) & (lane < nz - 1)


class Layout:
    def __init__(self, own_y, nz, dom, sub):
        self.own_y, self.nz, self.dom, self.sub = own_y, nz, dom, sub
        self.blocks = min(sub, 3)
        self.ny = own_y + HALO * (self.blocks - 1)
        self.total_y = own_y * sub
        self.ey, self.ez = self.ny // N, nz // N
        self.cr = round_up(self.ey + 1, 8)

    def where(self):
        d = lax.axis_index("dom")
        h = lax.axis_index("sub")
        parity = lax.rem(d, 2)
        pair = lax.div(d, 2)
        if self.sub == 1:
            start, offset = 0, 0
        elif self.sub == 2:
            start, offset = h * (self.own_y - HALO), h * HALO
        else:
            start, offset = h * self.own_y - HALO, HALO
        low = (pair > 0).astype(F32)
        high = (pair < self.dom // 2 - 1).astype(F32)
        return parity, h, start, offset, low, high

    def sent_rows(self, h):
        y = self.own_y
        down = (y - HALO, y - HALO)
        up = (0, HALO - 1)
        if self.sub == 1:
            return []
        if self.sub == 2:
            return [tuple(h * u + (1 - h) * v for u, v in zip(up, down))]
        return [down, up]

    def far_rows(self, h):
        if self.sub == 1:
            return []
        if self.sub == 2:
            return [(1 - h) * (self.ny - 1)]
        return [0, self.ny - 1]

    def used_rows(self, h):
        if self.sub == 1:
            return []
        if self.sub == 2:
            return [h * (self.own_y - HALO)]
        return [self.own_y - HALO, 0]

    def interfaces(self, h):
        if self.sub == 1:
            return []
        if self.sub == 2:
            return [self.own_y - h * (self.own_y - HALO)]
        return [HALO, HALO + self.own_y]


def aligned(start, size):
    return pl.ds(start if isinstance(start, int) else pl.multiple_of(start, N), size)


def gather_window(lay, own, others, h, store):
    y = lay.own_y
    if lay.sub == 1:
        store(pl.ds(0, y), own)
    elif lay.sub == 2:
        store(aligned(h * HALO, y), own)
        store(aligned((1 - h) * y, HALO), others[0])
    else:
        store(pl.ds(0, HALO), others[0])
        store(pl.ds(HALO, y), own)
        store(pl.ds(HALO + y, HALO), others[1])


def line_rows(lay, h):
    if lay.sub == 1:
        return []
    if lay.sub == 2:
        return [(lay.own_y - 1) * (1 - h)]
    return [0, lay.own_y - 1]


def line_count(lay):
    return 0 if lay.sub == 1 else 1 if lay.sub == 2 else 2


def own_kernel(lay, raw, z_sq, y_sq, w3, face, w_out, d_out, r_out, sx_out, *packs):
    rhs, coef = raw.at[0], raw.at[1]
    y, nz = lay.own_y, lay.nz
    parity, h = lay.where()[:2]
    table3 = w3[...]
    for e in range(y // N):
        rows = pl.ds(N * e, N)
        w = [coef[a, rows, :] * table3[a] for a in range(N)]
        dx = even_odd((DM * DM).T, w, 1)
        for a in range(N):
            w_out[a, rows, :] = w[a]
            d_out[a, rows, :] = dx[a]
    hi, lo = split(w_out[...].reshape(N * y, nz))
    dz = z_apply(hi, lo, z_sq[...])
    sx_out[...] = assemble_yz(d_out[(N - 1) * parity])
    for a in range(N):
        cut = slice(a * y, (a + 1) * y)
        dy = y_apply(hi[cut], lo[cut], y_sq[...])
        d_out[a] = assemble_yz(d_out[a] + dz[cut] + dy)
        r_out[a] = assemble_yz(rhs[a])
    inner = (N - 1) * (1 - parity)
    face[0] = r_out[inner]
    face[1] = d_out[inner]
    for pack, (first, far) in zip(packs, lay.sent_rows(h)):
        for side, field in ((0, r_out), (1, d_out)):
            for a in range(N):
                pack[side, pl.ds(a * HALO, HALO), :] = raw[side, a, aligned(first, HALO), :]
                pack[side, pl.ds(N * HALO + a, 1), :] = field[a, pl.ds(far, 1), :]


def message_kernel(lay, w, d, r, sx, face, msg, u_s, d_s, r_s):
    y, nz = lay.own_y, lay.nz
    parity, h, start, offset, low, high = lay.where()
    mask = yz_mask(y, nz, h * y, lay.total_y)
    scale = mask.astype(F32) * (1.0 / THETA)
    odd = parity.astype(F32)
    for a in range(N):
        dd, rr = d[a], r[a]
        keep = scale
        if a in (0, N - 1):
            inner = odd if a == 0 else 1.0 - odd
            dd = dd + inner * face[1]
            rr = rr + inner * face[0]
            keep = scale * inner
        d_s[a] = dd
        r_s[a] = rr
        u_s[a] = keep * rr / jnp.where(mask, dd, 1.0)
    col = [jnp.where(parity == 0, float(DM[a, 0]), float(DM[a, N - 1])) for a in range(N)]
    acc = []
    for e in range(y // N):
        rows = pl.ds(N * e, N)
        g = even_odd(DM, [u_s[a, rows, :] for a in range(N)], -1)
        total = None
        for a in range(N):
            term = (w[a, rows, :] * g[a]) * col[a]
            total = term if total is None else total + term
        acc.append(total)
    outer = (N - 1) * parity
    msg[pl.ds(0, y), :] = r[outer]
    msg[pl.ds(y, y), :] = d[outer]
    msg[pl.ds(2 * y, y), :] = sx[...]
    msg[pl.ds(3 * y, y), :] = w[outer]
    msg[pl.ds(4 * y, y), :] = assemble_yz(jnp.concatenate(acc, axis=0))
    base = 5 * y
    for row in line_rows(lay, h):
        for field in (r_s, d_s, w):
            for a in range(N):
                msg[pl.ds(base + a, 1), :] = field[a, pl.ds(row, 1), :]
            base += N
    msg[pl.ds(base, SPARE), :] = jnp.zeros((SPARE, nz), F32)


def gradient_flux(lay, u_ref, w_ref, planes, z_d, y_d, fx, fy, fz):
    ny, nz = lay.ny, lay.nz
    for el in range(2):
        for e in range(lay.ey):
            rows = pl.ds(N * e, N)
            u = [u_ref[N * el + a, rows, :] for a in range(N)]
            g = even_odd(DM, u, -1)
            for a in range(N):
                fx[N * el + a, rows, :] = w_ref[N * el + a, rows, :] * g[a]
    first, count = planes[0], len(planes)
    hi, lo = split(u_ref[pl.ds(first, count)].reshape(count * ny, nz))
    gz = z_apply(hi, lo, z_d[...])
    for p in planes:
        cut = slice((p - first) * ny, (p - first + 1) * ny)
        gy = y_apply(hi[cut], lo[cut], y_d[...])
        w = w_ref[p]
        fy[p] = w * gy
        fz[p] = w * gz[cut]


def deep_kernel(lay, n_other, *refs):
    own, mate = refs[:2]
    other = refs[2 : 2 + n_other]
    mate_other = [refs[2 + n_other + 2 * k :][:2] for k in range(n_other)]
    refs = refs[2 + 3 * n_other :]
    z_sq, y_sq, z_d, z_dt, y_d, y_dt, w3 = refs[:7]
    w_out, rhs_out, sec_out, lin_out, ends = refs[7:12]
    d_s, r_s, u_s, inv_s, fx, fy, fz, back = refs[12:]
    ny, nz = lay.ny, lay.nz
    last = 2 * N - 1
    parity, h, start, offset, low, high = lay.where()
    for side, target in ((0, rhs_out), (1, w_out)):
        for base, block, pieces in (
            (parity * N, own, [o.at[side] for o in other]),
            ((1 - parity) * N, mate, [o[side] for o in mate_other]),
        ):
            for a in range(N):

                def put(rows, value):
                    target[base + a, rows, :] = value

                cut = pl.ds(a * HALO, HALO)
                gather_window(lay, block[side, a], [o[cut, :] for o in pieces], h, put)
    table3 = w3[...]
    for el in range(2):
        outer = DM[:, 0] if el == 0 else DM[:, N - 1]
        for e in range(lay.ey):
            rows = pl.ds(N * e, N)
            w = [w_out[N * el + a, rows, :] * table3[a] for a in range(N)]
            dx = even_odd((DM * DM).T, w, 1)
            cx = even_odd(DM.T, [float(outer[a]) * w[a] for a in range(N)], -1)
            for a in range(N):
                w_out[N * el + a, rows, :] = w[a]
                d_s[N * el + a, rows, :] = dx[a]
                lin_out[N * el + a, rows, :] = cx[a]
    hi, lo = split(w_out[...].reshape(2 * N * ny, nz))
    dz = z_apply(hi, lo, z_sq[...])
    mask = yz_mask(ny, nz, start, lay.total_y)
    inside = mask.astype(F32)
    for p in range(2 * N):
        cut = slice(p * ny, (p + 1) * ny)
        dy = y_apply(hi[cut], lo[cut], y_sq[...])
        d_s[p] = assemble_yz(d_s[p] + dz[cut] + dy)
        r_s[p] = assemble_yz(rhs_out[p])
    for k, row in enumerate(lay.far_rows(h)):
        for side, target in ((0, r_s), (1, d_s)):
            for base, piece in (
                (parity * N, other[k].at[side]),
                ((1 - parity) * N, mate_other[k][side]),
            ):
                for a in range(N):
                    target[base + a, pl.ds(row, 1), :] = piece[pl.ds(N * HALO + a, 1), :]
    for s in (d_s, r_s):
        both = s[N - 1] + s[N]
        s[N - 1] = both
        s[N] = both
    ends[0, 0] = r_s[0]
    ends[0, 1] = d_s[0]
    ends[1, 0] = r_s[last]
    ends[1, 1] = d_s[last]
    zero = jnp.zeros((ny, nz), F32)
    u_s[0] = zero
    u_s[last] = zero
    for p in range(1, last):
        inv = inside / jnp.where(mask, d_s[p], 1.0)
        inv_s[p] = inv
        u_s[p] = inv * r_s[p] * (1.0 / THETA)
    middle = list(range(1, last))
    gradient_flux(lay, u_s, w_out, middle, z_d, y_d, fx, fy, fz)
    for el in range(2):
        for e in range(lay.ey):
            rows = pl.ds(N * e, N)
            b = even_odd(DM.T, [fx[N * el + a, rows, :] for a in range(N)], -1)
            for a in range(N):
                back[N * el + a, rows, :] = b[a]
    hi, lo = split(fz[pl.ds(1, last - 1)].reshape((last - 1) * ny, nz))
    bz = z_apply(hi, lo, z_dt[...])
    for p in middle:
        hi, lo = split(fy[p])
        by = y_apply(hi, lo, y_dt[...])
        back[p] = assemble_yz(back[p] + by + bz[(p - 1) * ny : p * ny])
    both = back[N - 1] + back[N]
    back[N - 1] = both
    back[N] = both
    for p in range(2 * N):
        linear = assemble_yz(lin_out[p])
        if p in (0, last):
            lin_out[p] = linear
            sec_out[p] = assemble_yz(back[p])
        else:
            inv = (2.0 * RHO1 / DELTA) * inv_s[p]
            lin_out[p] = -inv * linear
            sec_out[p] = (1.0 + RHO1 * RHO0) * u_s[p] + inv * (r_s[p] - back[p])


def coarse_tables_kernel(lay, w_ref, rhs_ref, my, mz, ry, rz, g_out, r_out):
    ny, nz, cr = lay.ny, lay.nz, lay.cr
    lhs = []
    for el in range(2):
        for m in MASS:
            total = None
            for a in range(N):
                term = float(m[a]) * w_ref[N * el + a]
                total = term if total is None else total + term
            lhs.append(total)
    along_z = z_apply(*split(jnp.concatenate(lhs, axis=0)), mz[...])
    for el in range(2):
        mom = {}
        for alpha in range(3):
            at = (3 * el + alpha) * ny
            block = y_apply(*split(along_z[at : at + ny]), my[...])
            for beta in range(3):
                for gamma in range(3):
                    mom[alpha, beta, gamma] = block[
                        beta * cr : (beta + 1) * cr, gamma * nz : (gamma + 1) * nz
                    ]
        x_sum, y_sum, z_sum = {}, {}, {}
        for i in range(3):
            for j in range(3):
                x_sum[i, j] = mom[0, i, j] + 2.0 * mom[1, i, j] + mom[2, i, j]
                y_sum[i, j] = mom[i, 0, j] + 2.0 * mom[i, 1, j] + mom[i, 2, j]
                z_sum[i, j] = mom[i, j, 0] + 2.0 * mom[i, j, 1] + mom[i, j, 2]
        sign = (1.0, -1.0, 1.0)
        for alpha in range(3):
            for beta in range(3):
                for gamma in range(3):
                    g_out[el, 9 * alpha + 3 * beta + gamma] = 0.25 * (
                        sign[alpha] * x_sum[beta, gamma]
                        + sign[beta] * y_sum[alpha, gamma]
                        + sign[gamma] * z_sum[alpha, beta]
                    )
    sums = []
    for el in range(2):
        for i in range(2):
            total = None
            for a in range(N):
                term = float(RHO[a, i]) * rhs_ref[N * el + a]
                total = term if total is None else total + term
            sums.append(total)
    part = y_apply(*split(jnp.concatenate(sums, axis=1)), ry[...])
    rows = jnp.concatenate([part[:, k * nz : (k + 1) * nz] for k in range(4)], axis=0)
    full = z_apply(*split(rows), rz[...])
    for k in range(4):
        r_out[k] = full[k * cr : (k + 1) * cr]


def pair_index(i, j):
    return i + j


def shifted(c, q, r):
    if q:
        c = pltpu.roll(c, c.shape[0] - 1, 0)
    if r:
        c = pltpu.roll(c, c.shape[1] - 1, 1)
    return c


def scatter(parts):
    cr, nz = parts[0, 0].shape
    first = parts[0, 0] + pltpu.roll(parts[0, 1], 1, 1)
    second = parts[1, 0] + pltpu.roll(parts[1, 1], 1, 1)
    return first + pltpu.roll(second, 1, 0)


def gathered(c):
    return {(q, r): shifted(c, q, r) for q in range(2) for r in range(2)}


def face_apply(entry, c, out=None):
    out = {} if out is None else out
    for j in range(2):
        for k in range(2):
            for q in range(2):
                for r in range(2):
                    term = entry(pair_index(j, q), pair_index(k, r)) * c[q, r]
                    out[j, k] = term if (j, k) not in out else out[j, k] + term
    return out


def coarse_diag(entry):
    return scatter({(j, k): entry(2 * j, 2 * k) for j in range(2) for k in range(2)})


def coarse_mask(lay, start):
    row = lax.broadcasted_iota(jnp.int32, (lay.cr, lay.nz), 0) + lax.div(start, N)
    lane = lax.broadcasted_iota(jnp.int32, (lay.cr, lay.nz), 1)
    return (row > 0) & (row < lay.total_y // N) & (lane > 0) & (lane < lay.ez)


def unpack_sides(lay, pieces, mate_pieces, line, parity, h, start, win):
    y, nz = lay.own_y, lay.nz
    for side, group in ((parity, pieces), (1 - parity, mate_pieces)):
        for k in range(5):

            def put(rows, value):
                win[side, k, rows, :] = value

            others = [
                g[aligned(k * y + first, HALO), :] for g, first in zip(group[1:], lay.used_rows(h))
            ]
            gather_window(lay, group[0][pl.ds(k * y, y), :], others, h, put)
    is_even = parity == 0
    lane = lax.broadcasted_iota(jnp.int32, (N, nz), 1)
    node = lax.broadcasted_iota(jnp.int32, (N, nz), 0)
    lane_in = (lane > 0) & (lane < nz - 1)
    flank = lax.broadcasted_iota(jnp.int32, (1, nz), 1)
    last = ((flank % N == N - 1) & (flank < nz - 1)).astype(F32)
    first = ((flank % N == 0) & (flank > 0)).astype(F32)
    for b, begin in enumerate(lay.interfaces(h), 1):
        above, below = pl.ds(begin - 1, 1), pl.ds(begin, 1)
        for side in range(2):
            for k in range(3):
                both = win[side, k, above, :] + win[side, k, below, :]
                win[side, k, above, :] = both
                win[side, k, below, :] = both
        for side in range(2):
            outer = N - 1 if side == 0 else 0

            def field(k):
                def of(group):
                    if lay.sub == 2:
                        one, two, at_one, at_two = group[0], group[1], 0, 0
                    else:
                        order = [group[1], group[0], group[2]]
                        one, two, at_one, at_two = order[b - 1], order[b], 1, 0
                    base = 5 * y + k * N
                    return (
                        one[pl.ds(base + 3 * N * at_one, N), :]
                        + two[pl.ds(base + 3 * N * at_two, N), :]
                    )
                mine, theirs = of(pieces), of(mate_pieces)
                if side == 0:
                    return jnp.where(is_even, mine, theirs)
                return jnp.where(is_even, theirs, mine)

            r, d, w = field(0), field(1), field(2)
            row = start + begin
            ok = lane_in & (node != outer) & (row > 0) & (row < lay.total_y)
            u = jnp.where(ok, r / jnp.where(ok, d, 1.0) * (1.0 / THETA), 0.0)
            g = None
            for a in range(N):
                term = line[a] * u[a : a + 1]
                g = term if g is None else g + term
            total = jnp.sum(line[N + side] * (w * g), axis=0, keepdims=True)
            total = total + last * pltpu.roll(total, nz - 1, 1) + first * pltpu.roll(total, 1, 1)
            win[side, 4, above, :] = total
            win[side, 4, below, :] = total


def second_kernel(lay, n_pieces, *refs):
    pieces, mate_pieces = refs[:n_pieces], refs[n_pieces : 2 * n_pieces]
    w_ref, sec_in, lin_in, ends, g_ref, r_ref = refs[2 * n_pieces : 2 * n_pieces + 6]
    refs = refs[2 * n_pieces + 6 :]
    z_d, z_dt, y_d, y_dt, ry, ry_one, rz, line = refs[:8]
    out, msg, state = refs[8:11]
    win, sec, fx, fy, fz = refs[11:]
    ny, nz, cr = lay.ny, lay.nz, lay.cr
    last = 2 * N - 1
    parity, h, start, offset, low, high = lay.where()
    mask = yz_mask(ny, nz, start, lay.total_y)
    inside = mask.astype(F32)
    is_even = parity == 0
    unpack_sides(lay, pieces, mate_pieces, line, parity, h, start, win)
    flags = (low, high)
    inv, res, u = [], [], []
    for side in range(2):
        valid = inside * flags[side]
        inv.append(valid / jnp.where(mask, ends[side, 1] + win[side, 1], 1.0))
        res.append(valid * (ends[side, 0] + win[side, 0]))
        u.append(inv[side] * res[side] * (1.0 / THETA))
    for p in range(1, last):
        value = sec_in[p]
        if p <= N:
            value = value + lin_in[min(p, N - 1)] * u[0]
        if p >= N - 1:
            value = value + lin_in[max(p, N)] * u[1]
        sec[p] = value
    weights = [w_ref[0] + win[0, 3], w_ref[last] + win[1, 3]]
    hi, lo = split(jnp.concatenate(u, axis=0))
    gz = z_apply(hi, lo, z_d[...])
    gy = y_apply(
        jnp.concatenate([hi[:ny], hi[ny:]], axis=1),
        jnp.concatenate([lo[:ny], lo[ny:]], axis=1),
        y_d[...],
    )
    weight_z = jnp.concatenate(weights, axis=0)
    weight_y = jnp.concatenate(weights, axis=1)
    bz = z_apply(*split(weight_z * gz), z_dt[...])
    by = y_apply(*split(weight_y * gy), y_dt[...])
    for side, p in ((0, 0), (1, last)):
        plane = assemble_yz(bz[side * ny : (side + 1) * ny] + by[:, side * nz : (side + 1) * nz])
        plane = plane + sec_in[p] + win[side, 4] + (lin_in[p] + win[side, 2]) * u[side]
        res_one = res[side] - inside * plane
        sec[p] = (1.0 + RHO1 * RHO0) * u[side] + (2.0 * RHO1 / DELTA) * inv[side] * res_one
    out[...] = sec[pl.ds(parity * N, N), pl.ds(pl.multiple_of(offset, N), lay.own_y), :]
    gradient_flux(lay, sec, w_ref, list(range(2 * N)), z_d, y_d, fx, fy, fz)
    sums = []
    for f, weight in ((fx, DRHO), (fy, RHO), (fz, RHO)):
        lanes = []
        for el in range(2):
            for i in range(2):
                total = None
                for a in range(N):
                    term = float(weight[a, i]) * f[N * el + a]
                    total = term if total is None else total + term
                lanes.append(total)
        sums.append(jnp.concatenate(lanes, axis=1))
    one = y_apply(*split(jnp.concatenate(sums[:2], axis=0)), ry[...])
    two = y_apply(*split(sums[2]), ry_one[...])
    rows = [
        jnp.concatenate([v[:, k * nz : (k + 1) * nz] for v in (one, two)], axis=1) for k in range(4)
    ]
    full = z_apply(*split(jnp.concatenate(rows, axis=0)), rz[...])
    r = {}
    for el in range(2):
        for i in range(2):
            k = 2 * el + i
            r[el, i] = r_ref[k] - full[k * cr : (k + 1) * cr]
    planes = [r[0, 0], r[0, 1] + r[1, 0], r[1, 1]]
    cmask = coarse_mask(lay, start)

    def entry(el, alpha):
        return lambda beta, gamma: g_ref[el, 9 * alpha + 3 * beta + gamma]

    d = [
        coarse_diag(entry(0, 0)),
        coarse_diag(entry(0, 2)) + coarse_diag(entry(1, 0)),
        coarse_diag(entry(1, 2)),
    ]
    cin = cmask.astype(F32)
    mid = (2.0 / 3.0) * cin * planes[1] / jnp.where(cmask, d[1], 1.0)
    c = gathered(mid)
    g_low = scatter(face_apply(entry(0, 1), c))
    g_high = scatter(face_apply(entry(1, 1), c))
    g_mid = scatter(face_apply(entry(1, 0), c, face_apply(entry(0, 2), c)))
    state[0] = planes[0]
    state[1] = planes[1]
    state[2] = planes[2]
    state[3] = d[0]
    state[4] = d[1]
    state[5] = d[2]
    state[6] = g_low
    state[7] = g_mid
    state[8] = g_high
    state[9] = mid
    send = [
        jnp.where(is_even, planes[0], planes[2]),
        jnp.where(is_even, d[0], d[2]),
        jnp.where(is_even, g_low, g_high),
    ]
    send += [jnp.where(is_even, g_ref[0, k], g_ref[1, 18 + k]) for k in range(9)]
    for k in range(3):
        packed = send[4 * k]
        for q in range(1, 4):
            packed = packed + pltpu.roll(send[4 * k + q], q * (nz // 4), 1)
        msg[k] = packed


def third_kernel(lay, *refs):
    own_msg, mate_msg, sec, state, g_ref, py, pz, out, coarse = refs
    ny, nz, cr = lay.ny, lay.nz, lay.cr
    parity, h, start, offset, low, high = lay.where()
    is_even = parity == 0
    cmask = coarse_mask(lay, start)
    cin = cmask.astype(F32)
    lo_msg, hi_msg = [], []
    for k in range(3):
        mine, theirs = own_msg[k], mate_msg[k]
        for target, packed in (
            (lo_msg, jnp.where(is_even, mine, theirs)),
            (hi_msg, jnp.where(is_even, theirs, mine)),
        ):
            target.append(packed)
            for q in range(1, 4):
                target.append(pltpu.roll(packed, nz - q * (nz // 4), 1))

    def entry(el, alpha):
        return lambda beta, gamma: g_ref[el, 9 * alpha + 3 * beta + gamma]

    def outer(at, m, flag, el, alpha):
        rhs = cin * flag * (state[at] + m[0])
        d = jnp.where(cmask, state[3 + at] + m[1], 1.0)
        one = (2.0 / 3.0) * rhs / d
        c = gathered(one)
        here = lambda beta, gamma: g_ref[el, 9 * alpha + 3 * beta + gamma] + m[3 + 3 * beta + gamma]
        image = scatter(face_apply(here, c)) + state[6 + at] + m[2]
        cross = face_apply(entry(el, 1), c)
        solution = one + (2.0 / 3.0) * (rhs - cin * flag * image) / d
        return solution, cross

    c_low, cross_low = outer(0, lo_msg, low, 0, 0)
    c_high, cross_high = outer(2, hi_msg, high, 1, 2)
    cross = scatter({k: cross_low[k] + cross_high[k] for k in cross_low})
    rhs = cin * state[1]
    d = jnp.where(cmask, state[4], 1.0)
    c_mid = state[9] + (2.0 / 3.0) * (rhs - cin * (state[7] + cross)) / d
    left = jnp.where(is_even, c_low, c_mid)
    right = jnp.where(is_even, c_mid, c_high)
    both = jnp.concatenate([left, right], axis=1)
    if lay.sub > 1:
        both = pltpu.roll(both, cr - lax.div(offset, N), 0)
    y, cy = lay.own_y, lay.own_y // 4
    along_y = y_apply(*split(both), py[...])
    along_y = jnp.concatenate([along_y[:, :nz], along_y[:, nz:]], axis=0)
    full = z_apply(*split(along_y), pz[...])
    inside = yz_mask(y, nz, start + offset, lay.total_y).astype(F32)
    q_left = inside * full[:y, :nz]
    q_right = inside * full[y + cy : 2 * y + cy, :nz]
    coarse[0] = full[y : y + cy, nz : nz + nz // 4]
    coarse[1] = full[2 * y + cy :, nz : nz + nz // 4]
    first_flag = jnp.where(is_even, low, 1.0)
    last_flag = jnp.where(is_even, 1.0, high)
    for a in range(N):
        add = float(INTERP[a, 0]) * q_left + float(INTERP[a, 1]) * q_right
        if a == 0:
            add = first_flag * add
        if a == N - 1:
            add = last_flag * add
        out[a] = sec[a] + add


def run(kernel, args, outs, scratch=()):
    return pl.pallas_call(
        kernel,
        out_shape=[jax.ShapeDtypeStruct(o, F32) for o in outs],
        in_specs=[pl.BlockSpec(memory_space=pltpu.VMEM)] * len(args),
        out_specs=[pl.BlockSpec(memory_space=pltpu.VMEM)] * len(outs),
        scratch_shapes=[pltpu.VMEM(s, F32) for s in scratch],
        compiler_params=pltpu.CompilerParams(vmem_limit_bytes=VMEM_LIMIT),
        cost_estimate=pl.CostEstimate(flops=1, bytes_accessed=1, transcendentals=0),
    )(*args)


def swap_pairs(count, first):
    pairs = []
    for i in range(first, count - 1, 2):
        pairs += [(i, i + 1), (i + 1, i)]
    return pairs


def chip_pairs(dom, sub, shift):
    pairs = []
    for a, b in swap_pairs(dom, 1):
        for q in range(sub):
            to = (q + shift) % sub if sub == 2 else q + shift
            if 0 <= to < sub:
                pairs.append((a * sub + q, b * sub + to))
    for end in (0, dom - 1):
        pairs += [(end * sub + a, end * sub + b) for a, b in swap_pairs(sub, 0)]
    return pairs


def shards(dom, sub, rhs_local, coefficient):
    size_x, own_y, nz = rhs_local.shape
    assert size_x == N and dom % 2 == 0 and (sub == 1 or own_y > HALO)
    lay = Layout(own_y, nz, dom, sub)
    ny, cr = lay.ny, lay.cr
    t = {k: jnp.asarray(v) for k, v in make_tables(ny, nz, own_y).items()}
    pick = lambda *names: [t[k] for k in names]
    even = lambda v: lax.ppermute(v, "dom", swap_pairs(dom, 0))
    odd = lambda v, k=0: lax.ppermute(v, ("dom", "sub"), chip_pairs(dom, sub, k))
    block = (N, own_y, nz)
    raw = jnp.stack([rhs_local, coefficient])
    n_other = 0 if sub == 1 else 1 if sub == 2 else 2
    face, w, d, r, sx, *packs = run(
        functools.partial(own_kernel, lay),
        [raw] + pick("z_sq", "y_sq_own", "w3"),
        [(2, own_y, nz), block, block, block, (own_y, nz)]
        + [(2, N * (HALO + 1), nz)] * n_other,
    )
    mate_face = even(face)
    if sub == 1:
        steps = []
    elif sub == 2:
        steps = [[(0, 1), (1, 0)]]
    else:
        up = [(i, i + 1) for i in range(sub - 1)]
        steps = [up, [(b, a) for a, b in up]]
    others = [lax.ppermute(pack, "sub", step) for pack, step in zip(packs, steps)]
    mate = even(raw)
    (msg,) = run(
        functools.partial(message_kernel, lay),
        [w, d, r, sx, mate_face],
        [(5 * own_y + 3 * N * line_count(lay) + SPARE, nz)],
        [block] * 3,
    )
    shifts = [0] if sub == 1 else [0, 1] if sub == 2 else [0, 1, -1]
    pieces = [odd(msg, k) for k in shifts]
    mate_others = [even(o[side]) for o in others for side in range(2)]
    pair = (2 * N, ny, nz)
    w, rhs, sec, lin, ends = run(
        functools.partial(deep_kernel, lay, n_other),
        [raw, mate, *others, *mate_others]
        + pick("z_sq", "y_sq", "z_d", "z_dt", "y_d", "y_dt", "w3"),
        [pair] * 4 + [(2, 2, ny, nz)],
        [pair] * 8,
    )
    pieces, sec = lax.optimization_barrier((pieces, sec))
    mate_pieces = [even(p) for p in pieces]
    g, r = run(
        functools.partial(coarse_tables_kernel, lay),
        [w, rhs] + pick("my", "mz", "ry_one", "rz_one"),
        [(2, 27, cr, nz), (4, cr, nz)],
    )
    sec, msg, state = run(
        functools.partial(second_kernel, lay, len(pieces)),
        [*pieces, *mate_pieces, w, sec, lin, ends, g, r]
        + pick("z_d", "z_dt", "y_d", "y_dt", "ry", "ry_one", "rz", "line"),
        [block, (3, cr, nz), (10, cr, nz)],
        [(2, 5, ny, nz)] + [pair] * 4,
    )
    from_odd = odd(msg)
    from_mate = even(from_odd)
    return tuple(
        run(
            functools.partial(third_kernel, lay),
            [from_odd, from_mate, sec, state, g] + pick("py", "pz"),
            [block, (size_x // 4, own_y // 4, nz // 4)],
        )
    )


def solution(mesh):
    dom, sub = mesh.shape["dom"], mesh.shape["sub"]
    return jax.shard_map(
        functools.partial(shards, dom, sub),
        mesh=mesh,
        in_specs=(P("dom", "sub", None), P("dom", "sub", None)),
        out_specs=(P("dom", "sub", None), P("dom", "sub", None)),
        check_vma=False,
    )
```

```python
import functools

import jax
import jax.numpy as jnp
import numpy as np
from jax import lax
from jax.experimental import pallas as pl
from jax.experimental.pallas import tpu as pltpu
from jax.sharding import PartitionSpec as P

N = 8
SPARE = N
HALO = 3 * N
THETA = 1.1
DELTA = 0.9
SIGMA = THETA / DELTA
RHO0 = 1.0 / SIGMA
RHO1 = 1.0 / (2.0 * SIGMA - RHO0)
F32 = jnp.float32
BF16 = jnp.bfloat16
VMEM_LIMIT = 48 * 1024 * 1024


def legendre_value(points, degree):
    previous = np.ones(points.shape)
    current = points.copy()
    for level in range(1, degree):
        following = ((2 * level + 1) * points * current - level * previous) / (level + 1)
        previous = current
        current = following
    return current


def tables():
    degree = 7
    points = np.array(
        [
            -1.0,
            -0.8717401485096066,
            -0.5917001814331423,
            -0.2092992179024789,
            0.2092992179024789,
            0.5917001814331423,
            0.8717401485096066,
            1.0,
        ]
    )
    values = legendre_value(points, degree)
    weights = 2.0 / (degree * (degree + 1) * values**2)
    derivative = np.zeros((8, 8))
    for row_at in range(8):
        for col_at in range(8):
            if row_at != col_at:
                derivative[row_at, col_at] = values[row_at] / (
                    values[col_at] * (points[row_at] - points[col_at])
                )
    derivative[0, 0] = -degree * (degree + 1) / 4.0
    derivative[7, 7] = degree * (degree + 1) / 4.0
    interp = np.stack([(1.0 - points) / 2.0, (1.0 + points) / 2.0], axis=1)
    return derivative, weights, interp


DM, WEIGHTS, INTERP = tables()
MULT = np.array([2.0] + [1.0] * 6 + [2.0])
RHO = MULT[:, None] * INTERP
DRHO = DM @ RHO


def blockdiag(block, count):
    return np.kron(np.eye(count), block)


def hi_lo(matrix):
    hi = matrix.astype(jnp.bfloat16)
    lo = (matrix - hi.astype(np.float64)).astype(jnp.bfloat16)
    return hi, lo


def right_table(matrix):
    hi, lo = hi_lo(matrix)
    return np.concatenate([hi, hi, lo], axis=0).astype(np.float32)


def left_table(matrix):
    hi, lo = hi_lo(matrix)
    return np.concatenate([hi, hi, lo], axis=1).astype(np.float32)


def vertex_table(per_node, elements, columns, count=8):
    out = np.zeros((count * elements, columns))
    for e in range(elements):
        for i in range(2):
            out[count * e : count * (e + 1), e + i] += per_node[:, i]
    return out


def moment_table(per_node, elements, columns):
    out = np.zeros((8 * elements, columns))
    for e in range(elements):
        out[8 * e : 8 * e + 8, e] = per_node
    return out


PAIRS = [(0, 0), (0, 1), (1, 1)]
MASS = [INTERP[:, i] * INTERP[:, j] for i, j in PAIRS]


def round_up(value, to):
    return -(-value // to) * to


def make_tables(ny, nz, own_y):
    ey, ez = ny // N, nz // N
    cr = round_up(ey + 1, 8)
    t = {}
    t["z_d"] = right_table(blockdiag(DM, ez).T)
    t["z_dt"] = right_table(blockdiag(DM, ez))
    t["z_sq"] = right_table(blockdiag(DM * DM, ez))
    t["y_d"] = left_table(blockdiag(DM, ey))
    t["y_dt"] = left_table(blockdiag(DM, ey).T)
    t["y_sq"] = left_table(blockdiag(DM * DM, ey).T)
    t["y_sq_own"] = left_table(blockdiag(DM * DM, own_y // N).T)
    py = vertex_table(RHO, ey, cr)
    dpy = blockdiag(DM, ey) @ py
    pz = vertex_table(RHO, ez, nz)
    dpz = blockdiag(DM, ez) @ pz
    t["ry"] = left_table(np.concatenate([py, dpy], axis=0).T)
    t["ry_one"] = left_table(py.T)
    t["rz"] = right_table(np.concatenate([pz, dpz], axis=0))
    t["rz_one"] = right_table(pz)
    t["my"] = left_table(np.concatenate([moment_table(m, ey, cr) for m in MASS], axis=1).T)
    t["mz"] = right_table(np.concatenate([moment_table(m, ez, nz) for m in MASS], axis=1))
    own_ey = own_y // N
    py = vertex_table(INTERP, own_ey, cr)
    t["py"] = left_table(np.concatenate([py, vertex_table(np.eye(2), own_ey, cr, 2)], axis=0))
    pz = vertex_table(INTERP, ez, nz).T
    sz = vertex_table(np.eye(2), ez, nz, 2).T
    t["pz"] = right_table(np.concatenate([pz, sz], axis=1))
    cols = np.concatenate([DM.T, DM.T[[N - 1]], DM.T[[0]]], axis=0)
    t["line"] = np.broadcast_to(cols[:, :, None], (N + 2, N, nz)).astype(np.float32)
    w3 = WEIGHTS[:, None, None] * WEIGHTS[None, :, None] * np.ones((1, 1, nz))
    t["w3"] = (w3 * np.tile(WEIGHTS, ez)[None, None, :]).astype(np.float32)
    return t


def even_odd(matrix, values, sign):
    even = [values[b] + values[7 - b] for b in range(4)]
    odd = [values[b] - values[7 - b] for b in range(4)]
    out = [None] * 8
    for a in range(4):
        pe = po = None
        for b in range(4):
            ce = float((matrix[a, b] + matrix[a, 7 - b]) / 2.0)
            co = float((matrix[a, b] - matrix[a, 7 - b]) / 2.0)
            te = ce * even[b]
            to = co * odd[b]
            pe = te if pe is None else pe + te
            po = to if po is None else po + to
        out[a] = pe + po
        out[7 - a] = pe - po if sign > 0 else po - pe
    return out


def split(x):
    hi = x.astype(BF16)
    lo = (x - hi.astype(F32)).astype(BF16)
    return hi, lo


def dot(a, b):
    return jnp.dot(a, b, preferred_element_type=F32)


def z_apply(hi, lo, table):
    return dot(jnp.concatenate([hi, lo, hi], axis=1), table.astype(BF16))


def y_apply(x, table):
    hi = x.astype(BF16).astype(F32)
    parts = jnp.concatenate([hi, x - hi, hi], axis=0).astype(BF16)
    return dot(table.astype(BF16), parts)


def y_planes(get, planes, table):
    table = table.astype(BF16)
    out = {}
    for p, q in zip(planes[::2], planes[1::2]):
        both = y_apply(jnp.concatenate([get(p), get(q)], axis=1), table)
        nz = both.shape[1] // 2
        out[p], out[q] = both[:, :nz], both[:, nz:]
    return out


def assemble_yz(v):
    ny, nz = v.shape
    row = lax.broadcasted_iota(jnp.int32, (N, nz), 0)
    lane = lax.broadcasted_iota(jnp.int32, (ny, nz), 1)
    is_top = row == 0
    flip = (N - 1) - row
    blocks = [v[N * e : N * e + N] for e in range(ny // N)]
    top = (row == N - 1).astype(F32)
    bottom = (row == 0).astype(F32)
    out = []
    for e, b in enumerate(blocks):
        if len(blocks) == 1:
            out.append(b)
            continue
        if e == 0:
            near, mask = blocks[1], top
        elif e + 1 == len(blocks):
            near, mask = blocks[e - 1], bottom
        else:
            near, mask = jnp.where(is_top, blocks[e + 1], blocks[e - 1]), top + bottom
        out.append(b + mask * jnp.take_along_axis(near, flip, axis=0))
    v = jnp.concatenate(out, axis=0)
    last = (lane % N == N - 1) & (lane < nz - 1)
    first = (lane % N == 0) & (lane > 0)
    other = lane + jnp.where(last, 1, 0) - jnp.where(first, 1, 0)
    mask = (last | first).astype(F32)
    return v + mask * jnp.take_along_axis(v, other, axis=1)


def yz_mask(ny, nz, start, total):
    row = lax.broadcasted_iota(jnp.int32, (ny, nz), 0) + start
    lane = lax.broadcasted_iota(jnp.int32, (ny, nz), 1)
    return (row > 0) & (row < total - 1) & (lane > 0) & (lane < nz - 1)


class Layout:
    def __init__(self, own_y, nz, dom, sub):
        self.own_y, self.nz, self.dom, self.sub = own_y, nz, dom, sub
        self.blocks = min(sub, 3)
        self.ny = own_y + HALO * (self.blocks - 1)
        self.total_y = own_y * sub
        self.ey, self.ez = self.ny // N, nz // N
        self.cr = round_up(self.ey + 1, 8)

    def where(self):
        d = lax.axis_index("dom")
        h = lax.axis_index("sub")
        parity = lax.rem(d, 2)
        pair = lax.div(d, 2)
        if self.sub == 1:
            start, offset = 0, 0
        elif self.sub == 2:
            start, offset = h * (self.own_y - HALO), h * HALO
        else:
            start, offset = h * self.own_y - HALO, HALO
        low = (pair > 0).astype(F32)
        high = (pair < self.dom // 2 - 1).astype(F32)
        return parity, h, start, offset, low, high

    def sent_rows(self, h):
        y = self.own_y
        down = (y - HALO, y - HALO)
        up = (0, HALO - 1)
        if self.sub == 1:
            return []
        if self.sub == 2:
            return [tuple(h * u + (1 - h) * v for u, v in zip(up, down))]
        return [down, up]

    def far_rows(self, h):
        if self.sub == 1:
            return []
        if self.sub == 2:
            return [(1 - h) * (self.ny - 1)]
        return [0, self.ny - 1]

    def interfaces(self, h):
        if self.sub == 1:
            return []
        if self.sub == 2:
            return [self.own_y - h * (self.own_y - HALO)]
        return [HALO, HALO + self.own_y]


def aligned(start, size):
    return pl.ds(start if isinstance(start, int) else pl.multiple_of(start, N), size)


def gather_window(lay, own, others, h, store):
    y = lay.own_y
    if lay.sub == 1:
        store(pl.ds(0, y), own)
    elif lay.sub == 2:
        store(aligned(h * HALO, y), own)
        store(aligned((1 - h) * y, HALO), others[0])
    else:
        store(pl.ds(0, HALO), others[0])
        store(pl.ds(HALO, y), own)
        store(pl.ds(HALO + y, HALO), others[1])


PACK = 2 * N + 2 * N * HALO
CUTS = [0, 2 * N + 5 * HALO, 2 * N + 10 * HALO, PACK]


def pack_rows(side, a):
    return pl.ds(2 * N + (side * N + a) * HALO, HALO)


class Pieces:
    def __init__(self, refs):
        self.refs = refs

    def __getitem__(self, rows):
        if len(self.refs) == 1:
            return self.refs[0][rows, :]
        k = max(i for i in range(len(self.refs)) if CUTS[i] <= rows.start)
        return self.refs[k][pl.ds(rows.start - CUTS[k], rows.size), :]


def line_rows(lay, h):
    if lay.sub == 1:
        return []
    if lay.sub == 2:
        return [(lay.own_y - 1) * (1 - h)]
    return [0, lay.own_y - 1]


def line_count(lay):
    return 0 if lay.sub == 1 else 1 if lay.sub == 2 else 2


def own_kernel(lay, raw, z_sq, y_sq, w3, face, w_out, d_out, r_out, sx_out, *packs):
    rhs, coef = raw.at[0], raw.at[1]
    y, nz = lay.own_y, lay.nz
    parity, h = lay.where()[:2]
    table3 = w3[...]
    for e in range(y // N):
        rows = pl.ds(N * e, N)
        w = [coef[a, rows, :] * table3[a] for a in range(N)]
        dx = even_odd((DM * DM).T, w, 1)
        for a in range(N):
            w_out[a, rows, :] = w[a]
            d_out[a, rows, :] = dx[a]
    hi, lo = split(w_out[...].reshape(N * y, nz))
    dz = z_apply(hi, lo, z_sq[...])
    sx_out[...] = assemble_yz(d_out[(N - 1) * parity])
    dy = y_planes(lambda a: w_out[a], list(range(N)), y_sq[...])
    for a in range(N):
        d_out[a] = assemble_yz(d_out[a] + dz[a * y : (a + 1) * y] + dy[a])
        r_out[a] = assemble_yz(rhs[a])
    inner = (N - 1) * (1 - parity)
    face[0] = r_out[inner]
    face[1] = d_out[inner]
    for pack, (first, far) in zip(packs, lay.sent_rows(h)):
        for side, field in ((0, r_out), (1, d_out)):
            for a in range(N):
                pack[pack_rows(side, a), :] = raw[side, a, aligned(first, HALO), :]
                pack[pl.ds(side * N + a, 1), :] = field[a, pl.ds(far, 1), :]


def message_kernel(lay, w, d, r, sx, face, *refs):
    msg, *side_msgs, u_s, d_s, r_s = refs
    y, nz = lay.own_y, lay.nz
    parity, h, start, offset, low, high = lay.where()
    mask = yz_mask(y, nz, h * y, lay.total_y)
    scale = mask.astype(F32) * (1.0 / THETA)
    odd = parity.astype(F32)
    for a in range(N):
        dd, rr = d[a], r[a]
        keep = scale
        if a in (0, N - 1):
            inner = odd if a == 0 else 1.0 - odd
            dd = dd + inner * face[1]
            rr = rr + inner * face[0]
            keep = scale * inner
        d_s[a] = dd
        r_s[a] = rr
        u_s[a] = keep * rr / jnp.where(mask, dd, 1.0)
    col = [jnp.where(parity == 0, float(DM[a, 0]), float(DM[a, N - 1])) for a in range(N)]
    acc = []
    for e in range(y // N):
        rows = pl.ds(N * e, N)
        g = even_odd(DM, [u_s[a, rows, :] for a in range(N)], -1)
        total = None
        for a in range(N):
            term = (w[a, rows, :] * g[a]) * col[a]
            total = term if total is None else total + term
        acc.append(total)
    outer = (N - 1) * parity
    msg[pl.ds(0, y), :] = r[outer]
    msg[pl.ds(y, y), :] = d[outer]
    msg[pl.ds(2 * y, y), :] = sx[...]
    msg[pl.ds(3 * y, y), :] = w[outer]
    msg[pl.ds(4 * y, y), :] = assemble_yz(jnp.concatenate(acc, axis=0))
    base = 5 * y
    for row in line_rows(lay, h):
        for field in (r_s, d_s, w):
            for a in range(N):
                msg[pl.ds(base + a, 1), :] = field[a, pl.ds(row, 1), :]
            base += N
    for out, (first, _) in zip(side_msgs, lay.sent_rows(h)):
        for k in range(5):
            out[pl.ds(k * HALO, HALO), :] = msg[aligned(k * y + first, HALO), :]
        lines = base - 5 * y
        out[pl.ds(5 * HALO, lines), :] = msg[pl.ds(5 * y, lines), :]
        out[pl.ds(5 * HALO + lines, SPARE), :] = jnp.zeros((SPARE, nz), F32)


def gradient_flux(lay, u_ref, w_ref, planes, z_d, y_d, fx, fy, fz):
    ny, nz = lay.ny, lay.nz
    for el in range(2):
        for e in range(lay.ey):
            rows = pl.ds(N * e, N)
            u = [u_ref[N * el + a, rows, :] for a in range(N)]
            g = even_odd(DM, u, -1)
            for a in range(N):
                fx[N * el + a, rows, :] = w_ref[N * el + a, rows, :] * g[a]
    first, count = planes[0], len(planes)
    hi, lo = split(u_ref[pl.ds(first, count)].reshape(count * ny, nz))
    gz = z_apply(hi, lo, z_d[...])
    gy = y_planes(lambda p: u_ref[p], planes, y_d[...])
    for p in planes:
        w = w_ref[p]
        fy[p] = w * gy[p]
        fz[p] = w * gz[(p - first) * ny : (p - first + 1) * ny]


def element_sums(lay, base, parity, h, block, pieces, tables, outs):
    z_sq, y_sq, w3 = tables
    w_out, rhs_out, d_s, r_s, lin = outs
    ny, nz = lay.ny, lay.nz
    for side, target in ((0, rhs_out), (1, w_out)):
        for a in range(N):

            def put(rows, value):
                target[base + a, rows, :] = value

            gather_window(lay, block[side, a], [o[pack_rows(side, a)] for o in pieces], h, put)
    table3 = w3[...]
    outer = [jnp.where(parity == 0, float(DM[a, 0]), float(DM[a, N - 1])) for a in range(N)]
    for e in range(lay.ey):
        rows = pl.ds(N * e, N)
        w = [w_out[base + a, rows, :] * table3[a] for a in range(N)]
        dx = even_odd((DM * DM).T, w, 1)
        cx = even_odd(DM.T, [outer[a] * w[a] for a in range(N)], -1)
        for a in range(N):
            w_out[base + a, rows, :] = w[a]
            d_s[base + a, rows, :] = dx[a]
            lin[base + a, rows, :] = cx[a]
    dz = z_apply(*split(w_out[pl.ds(base, N)].reshape(N * ny, nz)), z_sq[...])
    dy = y_planes(lambda a: w_out[base + a], list(range(N)), y_sq[...])
    for a in range(N):
        d_s[base + a] = assemble_yz(d_s[base + a] + dz[a * ny : (a + 1) * ny] + dy[a])
        r_s[base + a] = assemble_yz(rhs_out[base + a])
        lin[base + a] = assemble_yz(lin[base + a])
    for piece, row in zip(pieces, lay.far_rows(h)):
        for side, target in ((0, r_s), (1, d_s)):
            for a in range(N):
                target[base + a, pl.ds(row, 1), :] = piece[pl.ds(side * N + a, 1)]


def near_kernel(lay, own, *refs):
    n_other = len(refs) - 8
    other, tables, outs = refs[:n_other], refs[n_other : n_other + 3], refs[n_other + 3 :]
    parity, h = lay.where()[:2]
    pieces = [Pieces([o]) for o in other]
    element_sums(lay, parity * N, parity, h, own, pieces, tables, outs)


def deep_kernel(lay, n_other, mate, *refs):
    cuts = len(CUTS) - 1
    mate_other = [Pieces(refs[cuts * k : cuts * (k + 1)]) for k in range(n_other)]
    refs = refs[cuts * n_other + 5 :]
    z_sq, y_sq, z_d, z_dt, y_d, y_dt, w3 = refs[:7]
    w_out, rhs_out, d_s, r_s, lin_out, sec_out, ends = refs[7:14]
    u_s, inv_s, fx, fy, fz, back = refs[14:]
    ny, nz = lay.ny, lay.nz
    last = 2 * N - 1
    parity, h, start, offset, low, high = lay.where()
    element_sums(
        lay, (1 - parity) * N, 1 - parity, h, mate, mate_other, (z_sq, y_sq, w3),
        (w_out, rhs_out, d_s, r_s, lin_out),
    )
    for s in (d_s, r_s):
        both = s[N - 1] + s[N]
        s[N - 1] = both
        s[N] = both
    mask = yz_mask(ny, nz, start, lay.total_y)
    inside = mask.astype(F32)
    ends[0, 0] = r_s[0]
    ends[0, 1] = d_s[0]
    ends[1, 0] = r_s[last]
    ends[1, 1] = d_s[last]
    zero = jnp.zeros((ny, nz), F32)
    u_s[0] = zero
    u_s[last] = zero
    for p in range(1, last):
        inv = inside / jnp.where(mask, d_s[p], 1.0)
        inv_s[p] = inv
        u_s[p] = inv * r_s[p] * (1.0 / THETA)
    middle = list(range(1, last))
    gradient_flux(lay, u_s, w_out, middle, z_d, y_d, fx, fy, fz)
    for el in range(2):
        for e in range(lay.ey):
            rows = pl.ds(N * e, N)
            b = even_odd(DM.T, [fx[N * el + a, rows, :] for a in range(N)], -1)
            for a in range(N):
                back[N * el + a, rows, :] = b[a]
    hi, lo = split(fz[pl.ds(1, last - 1)].reshape((last - 1) * ny, nz))
    bz = z_apply(hi, lo, z_dt[...])
    by = y_planes(lambda p: fy[p], middle, y_dt[...])
    for p in middle:
        back[p] = assemble_yz(back[p] + by[p] + bz[(p - 1) * ny : p * ny])
    both = back[N - 1] + back[N]
    back[N - 1] = both
    back[N] = both
    for p in range(2 * N):
        if p in (0, last):
            sec_out[p] = assemble_yz(back[p])
        else:
            inv = (2.0 * RHO1 / DELTA) * inv_s[p]
            lin_out[p] = -inv * lin_out[p]
            sec_out[p] = (1.0 + RHO1 * RHO0) * u_s[p] + inv * (r_s[p] - back[p])


def coarse_tables_kernel(lay, w_ref, rhs_ref, my, mz, ry, rz, g_out, r_out):
    ny, nz, cr = lay.ny, lay.nz, lay.cr
    lhs = []
    for el in range(2):
        for m in MASS:
            total = None
            for a in range(N):
                term = float(m[a]) * w_ref[N * el + a]
                total = term if total is None else total + term
            lhs.append(total)
    along_z = z_apply(*split(jnp.concatenate(lhs, axis=0)), mz[...])
    for el in range(2):
        mom = {}
        for alpha in range(3):
            at = (3 * el + alpha) * ny
            block = y_apply(along_z[at : at + ny], my[...])
            for beta in range(3):
                for gamma in range(3):
                    mom[alpha, beta, gamma] = block[
                        beta * cr : (beta + 1) * cr, gamma * nz : (gamma + 1) * nz
                    ]
        x_sum, y_sum, z_sum = {}, {}, {}
        for i in range(3):
            for j in range(3):
                x_sum[i, j] = mom[0, i, j] + 2.0 * mom[1, i, j] + mom[2, i, j]
                y_sum[i, j] = mom[i, 0, j] + 2.0 * mom[i, 1, j] + mom[i, 2, j]
                z_sum[i, j] = mom[i, j, 0] + 2.0 * mom[i, j, 1] + mom[i, j, 2]
        sign = (1.0, -1.0, 1.0)
        for alpha in range(3):
            for beta in range(3):
                for gamma in range(3):
                    g_out[el, 9 * alpha + 3 * beta + gamma] = 0.25 * (
                        sign[alpha] * x_sum[beta, gamma]
                        + sign[beta] * y_sum[alpha, gamma]
                        + sign[gamma] * z_sum[alpha, beta]
                    )
    sums = []
    for el in range(2):
        for i in range(2):
            total = None
            for a in range(N):
                term = float(RHO[a, i]) * rhs_ref[N * el + a]
                total = term if total is None else total + term
            sums.append(total)
    part = y_apply(jnp.concatenate(sums, axis=1), ry[...])
    rows = jnp.concatenate([part[:, k * nz : (k + 1) * nz] for k in range(4)], axis=0)
    full = z_apply(*split(rows), rz[...])
    for k in range(4):
        r_out[k] = full[k * cr : (k + 1) * cr]


def pair_index(i, j):
    return i + j


def shifted(c, q, r):
    if q:
        c = pltpu.roll(c, c.shape[0] - 1, 0)
    if r:
        c = pltpu.roll(c, c.shape[1] - 1, 1)
    return c


def scatter(parts):
    cr, nz = parts[0, 0].shape
    first = parts[0, 0] + pltpu.roll(parts[0, 1], 1, 1)
    second = parts[1, 0] + pltpu.roll(parts[1, 1], 1, 1)
    return first + pltpu.roll(second, 1, 0)


def gathered(c):
    return {(q, r): shifted(c, q, r) for q in range(2) for r in range(2)}


def face_apply(entry, c, out=None):
    out = {} if out is None else out
    for j in range(2):
        for k in range(2):
            for q in range(2):
                for r in range(2):
                    term = entry(pair_index(j, q), pair_index(k, r)) * c[q, r]
                    out[j, k] = term if (j, k) not in out else out[j, k] + term
    return out


def coarse_diag(entry):
    return scatter({(j, k): entry(2 * j, 2 * k) for j in range(2) for k in range(2)})


def coarse_mask(lay, start):
    row = lax.broadcasted_iota(jnp.int32, (lay.cr, lay.nz), 0) + lax.div(start, N)
    lane = lax.broadcasted_iota(jnp.int32, (lay.cr, lay.nz), 1)
    return (row > 0) & (row < lay.total_y // N) & (lane > 0) & (lane < lay.ez)


def unpack_sides(lay, pieces, mate_pieces, line, parity, h, start, win):
    y, nz = lay.own_y, lay.nz
    for side, group in ((parity, pieces), (1 - parity, mate_pieces)):
        for k in range(5):

            def put(rows, value):
                win[side, k, rows, :] = value

            others = [g[pl.ds(k * HALO, HALO), :] for g in group[1:]]
            gather_window(lay, group[0][pl.ds(k * y, y), :], others, h, put)
    is_even = parity == 0
    lane = lax.broadcasted_iota(jnp.int32, (N, nz), 1)
    node = lax.broadcasted_iota(jnp.int32, (N, nz), 0)
    lane_in = (lane > 0) & (lane < nz - 1)
    flank = lax.broadcasted_iota(jnp.int32, (1, nz), 1)
    last = ((flank % N == N - 1) & (flank < nz - 1)).astype(F32)
    first = ((flank % N == 0) & (flank > 0)).astype(F32)
    for b, begin in enumerate(lay.interfaces(h), 1):
        above, below = pl.ds(begin - 1, 1), pl.ds(begin, 1)
        for side in range(2):
            for k in range(3):
                both = win[side, k, above, :] + win[side, k, below, :]
                win[side, k, above, :] = both
                win[side, k, below, :] = both
        for side in range(2):
            outer = N - 1 if side == 0 else 0

            def field(k):
                def of(group):
                    own_lines, other_lines = 5 * y + k * N, 5 * HALO + k * N
                    if lay.sub == 2:
                        mine, theirs = own_lines, other_lines
                        near = group[1]
                    else:
                        mine = own_lines + 3 * N * (b - 1)
                        theirs = other_lines + 3 * N * (2 - b)
                        near = group[b]
                    return group[0][pl.ds(mine, N), :] + near[pl.ds(theirs, N), :]
                mine, theirs = of(pieces), of(mate_pieces)
                if side == 0:
                    return jnp.where(is_even, mine, theirs)
                return jnp.where(is_even, theirs, mine)

            r, d, w = field(0), field(1), field(2)
            row = start + begin
            ok = lane_in & (node != outer) & (row > 0) & (row < lay.total_y)
            u = jnp.where(ok, r / jnp.where(ok, d, 1.0) * (1.0 / THETA), 0.0)
            g = None
            for a in range(N):
                term = line[a] * u[a : a + 1]
                g = term if g is None else g + term
            total = jnp.sum(line[N + side] * (w * g), axis=0, keepdims=True)
            total = total + last * pltpu.roll(total, nz - 1, 1) + first * pltpu.roll(total, 1, 1)
            win[side, 4, above, :] = total
            win[side, 4, below, :] = total


def second_kernel(lay, n_pieces, *refs):
    pieces, mate_pieces = refs[:n_pieces], refs[n_pieces : 2 * n_pieces]
    w_ref, sec_in, lin_in, ends, g_ref, r_ref = refs[2 * n_pieces : 2 * n_pieces + 6]
    refs = refs[2 * n_pieces + 6 :]
    z_d, z_dt, y_d, y_dt, ry, ry_one, rz, line = refs[:8]
    out, msg, state = refs[8:11]
    win, sec, fx, fy, fz = refs[11:]
    ny, nz, cr = lay.ny, lay.nz, lay.cr
    last = 2 * N - 1
    parity, h, start, offset, low, high = lay.where()
    mask = yz_mask(ny, nz, start, lay.total_y)
    inside = mask.astype(F32)
    is_even = parity == 0
    unpack_sides(lay, pieces, mate_pieces, line, parity, h, start, win)
    flags = (low, high)
    inv, res, u = [], [], []
    for side in range(2):
        valid = inside * flags[side]
        inv.append(valid / jnp.where(mask, ends[side, 1] + win[side, 1], 1.0))
        res.append(valid * (ends[side, 0] + win[side, 0]))
        u.append(inv[side] * res[side] * (1.0 / THETA))
    for p in range(1, last):
        value = sec_in[p]
        if p <= N:
            value = value + lin_in[min(p, N - 1)] * u[0]
        if p >= N - 1:
            value = value + lin_in[max(p, N)] * u[1]
        sec[p] = value
    weights = [w_ref[0] + win[0, 3], w_ref[last] + win[1, 3]]
    hi, lo = split(jnp.concatenate(u, axis=0))
    gz = z_apply(hi, lo, z_d[...])
    gy = y_apply(jnp.concatenate(u, axis=1), y_d[...])
    weight_z = jnp.concatenate(weights, axis=0)
    weight_y = jnp.concatenate(weights, axis=1)
    bz = z_apply(*split(weight_z * gz), z_dt[...])
    by = y_apply(weight_y * gy, y_dt[...])
    for side, p in ((0, 0), (1, last)):
        plane = assemble_yz(bz[side * ny : (side + 1) * ny] + by[:, side * nz : (side + 1) * nz])
        plane = plane + sec_in[p] + win[side, 4] + (lin_in[p] + win[side, 2]) * u[side]
        res_one = res[side] - inside * plane
        sec[p] = (1.0 + RHO1 * RHO0) * u[side] + (2.0 * RHO1 / DELTA) * inv[side] * res_one
    out[...] = sec[pl.ds(parity * N, N), pl.ds(pl.multiple_of(offset, N), lay.own_y), :]
    gradient_flux(lay, sec, w_ref, list(range(2 * N)), z_d, y_d, fx, fy, fz)
    sums = []
    for f, weight in ((fx, DRHO), (fy, RHO), (fz, RHO)):
        lanes = []
        for el in range(2):
            for i in range(2):
                total = None
                for a in range(N):
                    term = float(weight[a, i]) * f[N * el + a]
                    total = term if total is None else total + term
                lanes.append(total)
        sums.append(jnp.concatenate(lanes, axis=1))
    one = y_apply(jnp.concatenate(sums[:2], axis=0), ry[...])
    two = y_apply(sums[2], ry_one[...])
    rows = [
        jnp.concatenate([v[:, k * nz : (k + 1) * nz] for v in (one, two)], axis=1) for k in range(4)
    ]
    full = z_apply(*split(jnp.concatenate(rows, axis=0)), rz[...])
    r = {}
    for el in range(2):
        for i in range(2):
            k = 2 * el + i
            r[el, i] = r_ref[k] - full[k * cr : (k + 1) * cr]
    planes = [r[0, 0], r[0, 1] + r[1, 0], r[1, 1]]
    cmask = coarse_mask(lay, start)

    def entry(el, alpha):
        return lambda beta, gamma: g_ref[el, 9 * alpha + 3 * beta + gamma]

    d = [
        coarse_diag(entry(0, 0)),
        coarse_diag(entry(0, 2)) + coarse_diag(entry(1, 0)),
        coarse_diag(entry(1, 2)),
    ]
    cin = cmask.astype(F32)
    mid = (2.0 / 3.0) * cin * planes[1] / jnp.where(cmask, d[1], 1.0)
    c = gathered(mid)
    g_low = scatter(face_apply(entry(0, 1), c))
    g_high = scatter(face_apply(entry(1, 1), c))
    g_mid = scatter(face_apply(entry(1, 0), c, face_apply(entry(0, 2), c)))
    state[0] = planes[0]
    state[1] = planes[1]
    state[2] = planes[2]
    state[3] = d[0]
    state[4] = d[1]
    state[5] = d[2]
    state[6] = g_low
    state[7] = g_mid
    state[8] = g_high
    state[9] = mid
    send = [
        jnp.where(is_even, planes[0], planes[2]),
        jnp.where(is_even, d[0], d[2]),
        jnp.where(is_even, g_low, g_high),
    ]
    send += [jnp.where(is_even, g_ref[0, k], g_ref[1, 18 + k]) for k in range(9)]
    for k in range(3):
        packed = send[4 * k]
        for q in range(1, 4):
            packed = packed + pltpu.roll(send[4 * k + q], q * (nz // 4), 1)
        msg[k] = packed


def third_kernel(lay, *refs):
    own_msg, mate_msg, sec, state, g_ref, py, pz, out, coarse = refs
    ny, nz, cr = lay.ny, lay.nz, lay.cr
    parity, h, start, offset, low, high = lay.where()
    is_even = parity == 0
    cmask = coarse_mask(lay, start)
    cin = cmask.astype(F32)
    lo_msg, hi_msg = [], []
    for k in range(3):
        mine, theirs = own_msg[k], mate_msg[k]
        for target, packed in (
            (lo_msg, jnp.where(is_even, mine, theirs)),
            (hi_msg, jnp.where(is_even, theirs, mine)),
        ):
            target.append(packed)
            for q in range(1, 4):
                target.append(pltpu.roll(packed, nz - q * (nz // 4), 1))

    def entry(el, alpha):
        return lambda beta, gamma: g_ref[el, 9 * alpha + 3 * beta + gamma]

    def outer(at, m, flag, el, alpha):
        rhs = cin * flag * (state[at] + m[0])
        d = jnp.where(cmask, state[3 + at] + m[1], 1.0)
        one = (2.0 / 3.0) * rhs / d
        c = gathered(one)
        here = lambda beta, gamma: g_ref[el, 9 * alpha + 3 * beta + gamma] + m[3 + 3 * beta + gamma]
        image = scatter(face_apply(here, c)) + state[6 + at] + m[2]
        cross = face_apply(entry(el, 1), c)
        solution = one + (2.0 / 3.0) * (rhs - cin * flag * image) / d
        return solution, cross

    c_low, cross_low = outer(0, lo_msg, low, 0, 0)
    c_high, cross_high = outer(2, hi_msg, high, 1, 2)
    cross = scatter({k: cross_low[k] + cross_high[k] for k in cross_low})
    rhs = cin * state[1]
    d = jnp.where(cmask, state[4], 1.0)
    c_mid = state[9] + (2.0 / 3.0) * (rhs - cin * (state[7] + cross)) / d
    left = jnp.where(is_even, c_low, c_mid)
    right = jnp.where(is_even, c_mid, c_high)
    both = jnp.concatenate([left, right], axis=1)
    if lay.sub > 1:
        both = pltpu.roll(both, cr - lax.div(offset, N), 0)
    y, cy = lay.own_y, lay.own_y // 4
    along_y = y_apply(both, py[...])
    along_y = jnp.concatenate([along_y[:, :nz], along_y[:, nz:]], axis=0)
    full = z_apply(*split(along_y), pz[...])
    inside = yz_mask(y, nz, start + offset, lay.total_y).astype(F32)
    q_left = inside * full[:y, :nz]
    q_right = inside * full[y + cy : 2 * y + cy, :nz]
    coarse[0] = full[y : y + cy, nz : nz + nz // 4]
    coarse[1] = full[2 * y + cy :, nz : nz + nz // 4]
    first_flag = jnp.where(is_even, low, 1.0)
    last_flag = jnp.where(is_even, 1.0, high)
    for a in range(N):
        add = float(INTERP[a, 0]) * q_left + float(INTERP[a, 1]) * q_right
        if a == 0:
            add = first_flag * add
        if a == N - 1:
            add = last_flag * add
        out[a] = sec[a] + add


def run(kernel, args, outs, scratch=(), aliases={}):
    return pl.pallas_call(
        kernel,
        out_shape=[jax.ShapeDtypeStruct(o, F32) for o in outs],
        in_specs=[pl.BlockSpec(memory_space=pltpu.VMEM)] * len(args),
        out_specs=[pl.BlockSpec(memory_space=pltpu.VMEM)] * len(outs),
        scratch_shapes=[pltpu.VMEM(s, F32) for s in scratch],
        compiler_params=pltpu.CompilerParams(vmem_limit_bytes=VMEM_LIMIT),
        input_output_aliases=aliases,
        cost_estimate=pl.CostEstimate(flops=1, bytes_accessed=1, transcendentals=0),
    )(*args)


def swap_pairs(count, first):
    pairs = []
    for i in range(first, count - 1, 2):
        pairs += [(i, i + 1), (i + 1, i)]
    return pairs


def chip_pairs(dom, sub, shift):
    pairs = []
    for a, b in swap_pairs(dom, 1):
        for q in range(sub):
            to = (q + shift) % sub if sub == 2 else q + shift
            if 0 <= to < sub:
                pairs.append((a * sub + q, b * sub + to))
    for end in (0, dom - 1):
        pairs += [(end * sub + a, end * sub + b) for a, b in swap_pairs(sub, 0)]
    return pairs


def shards(dom, sub, rhs_local, coefficient):
    size_x, own_y, nz = rhs_local.shape
    assert size_x == N and dom % 2 == 0 and (sub == 1 or own_y > HALO)
    lay = Layout(own_y, nz, dom, sub)
    ny, cr = lay.ny, lay.cr
    t = {k: jnp.asarray(v) for k, v in make_tables(ny, nz, own_y).items()}
    pick = lambda *names: [t[k] for k in names]
    even = lambda v: lax.ppermute(v, "dom", swap_pairs(dom, 0))
    odd = lambda v, k=0: lax.ppermute(v, ("dom", "sub"), chip_pairs(dom, sub, k))
    block = (N, own_y, nz)
    raw = jnp.stack([rhs_local, coefficient])
    n_other = 0 if sub == 1 else 1 if sub == 2 else 2
    face, w, d, r, sx, *packs = run(
        functools.partial(own_kernel, lay),
        [raw] + pick("z_sq", "y_sq_own", "w3"),
        [(2, own_y, nz), block, block, block, (own_y, nz)]
        + [(PACK, nz)] * n_other,
    )
    mate_face = even(face)
    if sub == 1:
        steps = []
    elif sub == 2:
        steps = [[(0, 1), (1, 0)]]
    else:
        up = [(i, i + 1) for i in range(sub - 1)]
        steps = [up, [(b, a) for a, b in up]]
    others = [lax.ppermute(pack, "sub", step) for pack, step in zip(packs, steps)]
    mate = even(raw)
    lines = 3 * N * line_count(lay)
    msgs = run(
        functools.partial(message_kernel, lay),
        [w, d, r, sx, mate_face],
        [(5 * own_y + lines, nz)] + [(5 * HALO + lines + SPARE, nz)] * n_other,
        [block] * 3,
    )
    shifts = [0] if sub == 1 else [0, 1] if sub == 2 else [0, 1, -1]
    pieces = [odd(msg, k) for msg, k in zip(msgs, shifts)]
    mate_others = [even(o[a:b]) for o in others for a, b in zip(CUTS, CUTS[1:])]
    pair = (2 * N, ny, nz)
    arrays = run(
        functools.partial(near_kernel, lay),
        [raw, *others] + pick("z_sq", "y_sq", "w3"),
        [pair] * 5,
    )
    w, rhs, _, _, lin, sec, ends = run(
        functools.partial(deep_kernel, lay, n_other),
        [mate, *mate_others, *arrays] + pick("z_sq", "y_sq", "z_d", "z_dt", "y_d", "y_dt", "w3"),
        [pair] * 6 + [(2, 2, ny, nz)],
        [pair] * 6,
        {1 + len(mate_others) + k: k for k in range(5)},
    )
    pieces, sec = lax.optimization_barrier((pieces, sec))
    mate_pieces = [even(p) for p in pieces]
    g, r = run(
        functools.partial(coarse_tables_kernel, lay),
        [w, rhs] + pick("my", "mz", "ry_one", "rz_one"),
        [(2, 27, cr, nz), (4, cr, nz)],
    )
    sec, msg, state = run(
        functools.partial(second_kernel, lay, len(pieces)),
        [*pieces, *mate_pieces, w, sec, lin, ends, g, r]
        + pick("z_d", "z_dt", "y_d", "y_dt", "ry", "ry_one", "rz", "line"),
        [block, (3, cr, nz), (10, cr, nz)],
        [(2, 5, ny, nz)] + [pair] * 4,
    )
    from_odd = odd(msg)
    from_mate = even(from_odd)
    return tuple(
        run(
            functools.partial(third_kernel, lay),
            [from_odd, from_mate, sec, state, g] + pick("py", "pz"),
            [block, (size_x // 4, own_y // 4, nz // 4)],
        )
    )


def solution(mesh):
    dom, sub = mesh.shape["dom"], mesh.shape["sub"]
    return jax.shard_map(
        functools.partial(shards, dom, sub),
        mesh=mesh,
        in_specs=(P("dom", "sub", None), P("dom", "sub", None)),
        out_specs=(P("dom", "sub", None), P("dom", "sub", None)),
        check_vma=False,
    )
```

```python
import functools

import jax
import jax.numpy as jnp
import numpy as np
from jax import lax
from jax.experimental import pallas as pl
from jax.experimental.pallas import tpu as pltpu
from jax.sharding import PartitionSpec as P

N = 8
SPARE = N
HALO = 3 * N
THETA = 1.1
DELTA = 0.9
SIGMA = THETA / DELTA
RHO0 = 1.0 / SIGMA
RHO1 = 1.0 / (2.0 * SIGMA - RHO0)
F32 = jnp.float32
BF16 = jnp.bfloat16
VMEM_LIMIT = 48 * 1024 * 1024


def legendre_value(points, degree):
    previous = np.ones(points.shape)
    current = points.copy()
    for level in range(1, degree):
        following = ((2 * level + 1) * points * current - level * previous) / (level + 1)
        previous = current
        current = following
    return current


def tables():
    degree = 7
    points = np.array(
        [
            -1.0,
            -0.8717401485096066,
            -0.5917001814331423,
            -0.2092992179024789,
            0.2092992179024789,
            0.5917001814331423,
            0.8717401485096066,
            1.0,
        ]
    )
    values = legendre_value(points, degree)
    weights = 2.0 / (degree * (degree + 1) * values**2)
    derivative = np.zeros((8, 8))
    for row_at in range(8):
        for col_at in range(8):
            if row_at != col_at:
                derivative[row_at, col_at] = values[row_at] / (
                    values[col_at] * (points[row_at] - points[col_at])
                )
    derivative[0, 0] = -degree * (degree + 1) / 4.0
    derivative[7, 7] = degree * (degree + 1) / 4.0
    interp = np.stack([(1.0 - points) / 2.0, (1.0 + points) / 2.0], axis=1)
    return derivative, weights, interp


DM, WEIGHTS, INTERP = tables()
MULT = np.array([2.0] + [1.0] * 6 + [2.0])
RHO = MULT[:, None] * INTERP
DRHO = DM @ RHO


def blockdiag(block, count):
    return np.kron(np.eye(count), block)


def hi_lo(matrix):
    hi = matrix.astype(jnp.bfloat16)
    lo = (matrix - hi.astype(np.float64)).astype(jnp.bfloat16)
    return hi, lo


def right_table(matrix):
    hi, lo = hi_lo(matrix)
    top = np.concatenate([hi, lo], axis=1)
    return np.concatenate([top, np.concatenate([hi, 0 * lo], axis=1)], axis=0).astype(np.float32)


def left_table(matrix):
    hi, lo = hi_lo(matrix)
    return np.concatenate([hi, hi, lo], axis=1).astype(np.float32)


def vertex_table(per_node, elements, columns, count=8):
    out = np.zeros((count * elements, columns))
    for e in range(elements):
        for i in range(2):
            out[count * e : count * (e + 1), e + i] += per_node[:, i]
    return out


def moment_table(per_node, elements, columns):
    out = np.zeros((8 * elements, columns))
    for e in range(elements):
        out[8 * e : 8 * e + 8, e] = per_node
    return out


PAIRS = [(0, 0), (0, 1), (1, 1)]
MASS = [INTERP[:, i] * INTERP[:, j] for i, j in PAIRS]


def round_up(value, to):
    return -(-value // to) * to


def make_tables(ny, nz, own_y):
    ey, ez = ny // N, nz // N
    cr = round_up(ey + 1, 8)
    t = {}
    t["z_d"] = right_table(blockdiag(DM, ez).T)
    t["z_dt"] = right_table(blockdiag(DM, ez))
    t["z_sq"] = right_table(blockdiag(DM * DM, ez))
    t["y_d"] = left_table(blockdiag(DM, ey))
    t["y_dt"] = left_table(blockdiag(DM, ey).T)
    for count in range(1, own_y // N + 1):
        t["y_sq", count] = left_table(blockdiag(DM * DM, count).T)
        t["y_d", count] = left_table(blockdiag(DM, count))
        t["y_dt", count] = left_table(blockdiag(DM, count).T)
    py = vertex_table(RHO, ey, cr)
    dpy = blockdiag(DM, ey) @ py
    pz = vertex_table(RHO, ez, nz)
    dpz = blockdiag(DM, ez) @ pz
    zero = np.zeros_like(py)
    ry = np.concatenate([np.concatenate([py, dpy, zero]), np.concatenate([zero, zero, py])], axis=1)
    t["ry"] = np.concatenate(hi_lo(ry.T), axis=0).astype(np.float32)
    t["ry_one"] = left_table(py.T)
    t["rz"] = right_table(np.concatenate([pz, dpz], axis=0))
    t["rz_one"] = right_table(pz)
    t["my"] = left_table(np.concatenate([moment_table(m, ey, cr) for m in MASS], axis=1).T)
    t["mz"] = right_table(np.concatenate([moment_table(m, ez, nz) for m in MASS], axis=1))
    own_ey = own_y // N
    py = vertex_table(INTERP, own_ey, cr)
    t["py"] = left_table(np.concatenate([py, vertex_table(np.eye(2), own_ey, cr, 2)], axis=0))
    pz = vertex_table(INTERP, ez, nz).T
    sz = vertex_table(np.eye(2), ez, nz, 2).T
    t["pz"] = right_table(np.concatenate([pz, sz], axis=1))
    cols = np.concatenate([DM.T, DM.T[[N - 1]], DM.T[[0]]], axis=0)
    t["line"] = np.broadcast_to(cols[:, :, None], (N + 2, N, nz)).astype(np.float32)
    w3 = WEIGHTS[:, None, None] * WEIGHTS[None, :, None] * np.ones((1, 1, nz))
    t["w3"] = (w3 * np.tile(WEIGHTS, ez)[None, None, :]).astype(np.float32)
    return t


def even_odd(matrix, values, sign):
    even = [values[b] + values[7 - b] for b in range(4)]
    odd = [values[b] - values[7 - b] for b in range(4)]
    out = [None] * 8
    for a in range(4):
        pe = po = None
        for b in range(4):
            ce = float((matrix[a, b] + matrix[a, 7 - b]) / 2.0)
            co = float((matrix[a, b] - matrix[a, 7 - b]) / 2.0)
            te = ce * even[b]
            to = co * odd[b]
            pe = te if pe is None else pe + te
            po = to if po is None else po + to
        out[a] = pe + po
        out[7 - a] = pe - po if sign > 0 else po - pe
    return out


def split(x):
    hi = x.astype(BF16)
    lo = (x - hi.astype(F32)).astype(BF16)
    return hi, lo


def dot(a, b):
    return jnp.dot(a, b, preferred_element_type=F32)


def z_apply(hi, lo, table):
    both = dot(jnp.concatenate([hi, lo], axis=1), table.astype(BF16))
    half = both.shape[1] // 2
    return both[:, :half] + both[:, half:]


def y_apply(x, table):
    hi = x.astype(BF16).astype(F32)
    parts = jnp.concatenate([hi, x - hi, hi], axis=0).astype(BF16)
    return dot(table.astype(BF16), parts)


def y_planes(get, planes, table):
    table = table.astype(BF16)
    out = {}
    for p, q in zip(planes[::2], planes[1::2]):
        both = y_apply(jnp.concatenate([get(p), get(q)], axis=1), table)
        nz = both.shape[1] // 2
        out[p], out[q] = both[:, :nz], both[:, nz:]
    return out


def assemble_yz(v):
    ny, nz = v.shape
    row = lax.broadcasted_iota(jnp.int32, (N, nz), 0)
    lane = lax.broadcasted_iota(jnp.int32, (ny, nz), 1)
    is_top = row == 0
    flip = (N - 1) - row
    blocks = [v[N * e : N * e + N] for e in range(ny // N)]
    top = (row == N - 1).astype(F32)
    bottom = (row == 0).astype(F32)
    out = []
    for e, b in enumerate(blocks):
        if len(blocks) == 1:
            out.append(b)
            continue
        if e == 0:
            near, mask = blocks[1], top
        elif e + 1 == len(blocks):
            near, mask = blocks[e - 1], bottom
        else:
            near, mask = jnp.where(is_top, blocks[e + 1], blocks[e - 1]), top + bottom
        out.append(b + mask * jnp.take_along_axis(near, flip, axis=0))
    v = jnp.concatenate(out, axis=0)
    last = (lane % N == N - 1) & (lane < nz - 1)
    first = (lane % N == 0) & (lane > 0)
    other = lane + jnp.where(last, 1, 0) - jnp.where(first, 1, 0)
    mask = (last | first).astype(F32)
    return v + mask * jnp.take_along_axis(v, other, axis=1)


def yz_mask(ny, nz, start, total):
    row = lax.broadcasted_iota(jnp.int32, (ny, nz), 0) + start
    lane = lax.broadcasted_iota(jnp.int32, (ny, nz), 1)
    return (row > 0) & (row < total - 1) & (lane > 0) & (lane < nz - 1)


class Layout:
    def __init__(self, own_y, nz, dom, sub):
        self.own_y, self.nz, self.dom, self.sub = own_y, nz, dom, sub
        self.blocks = min(sub, 3)
        self.ny = own_y + HALO * (self.blocks - 1)
        self.total_y = own_y * sub
        self.ey, self.ez = self.ny // N, nz // N
        self.cr = round_up(self.ey + 1, 8)

    def where(self):
        d = lax.axis_index("dom")
        h = lax.axis_index("sub")
        parity = lax.rem(d, 2)
        pair = lax.div(d, 2)
        if self.sub == 1:
            start, offset = 0, 0
        elif self.sub == 2:
            start, offset = h * (self.own_y - HALO), h * HALO
        else:
            start, offset = h * self.own_y - HALO, HALO
        low = (pair > 0).astype(F32)
        high = (pair < self.dom // 2 - 1).astype(F32)
        return parity, h, start, offset, low, high

    def sent_rows(self, h):
        y = self.own_y
        down = (y - HALO, y - HALO)
        up = (0, HALO - 1)
        if self.sub == 1:
            return []
        if self.sub == 2:
            return [tuple(h * u + (1 - h) * v for u, v in zip(up, down))]
        return [down, up]

    def far_rows(self, h):
        if self.sub == 1:
            return []
        if self.sub == 2:
            return [(1 - h) * (self.ny - 1)]
        return [0, self.ny - 1]

    def other_starts(self, h):
        if self.sub == 1:
            return []
        if self.sub == 2:
            return [(1 - h) * self.own_y]
        return [0, HALO + self.own_y]

    def early_rows(self, h):
        if self.sub == 1:
            return 0, self.own_y
        if self.sub == 2:
            return h * (HALO + N), self.own_y - N
        return HALO + N, self.own_y - 2 * N

    def late_starts(self, h):
        if self.sub == 1:
            return []
        if self.sub == 2:
            return [(1 - h) * (self.own_y - N)]
        return [0, self.own_y + HALO - N]

    def interfaces(self, h):
        if self.sub == 1:
            return []
        if self.sub == 2:
            return [self.own_y - h * (self.own_y - HALO)]
        return [HALO, HALO + self.own_y]


def aligned(start, size):
    return pl.ds(start if isinstance(start, int) else pl.multiple_of(start, N), size)


def gather_window(lay, own, others, h, store):
    y = lay.own_y
    if lay.sub == 1:
        store(pl.ds(0, y), own)
    elif lay.sub == 2:
        store(aligned(h * HALO, y), own)
        store(aligned((1 - h) * y, HALO), others[0])
    else:
        store(pl.ds(0, HALO), others[0])
        store(pl.ds(HALO, y), own)
        store(pl.ds(HALO + y, HALO), others[1])


PACK = 2 * N + 2 * N * HALO
CUTS = [0, 2 * N + 5 * HALO, 2 * N + 10 * HALO, PACK]


def pack_rows(side, a):
    return pl.ds(2 * N + (side * N + a) * HALO, HALO)


class Pieces:
    def __init__(self, refs):
        self.refs = refs

    def __getitem__(self, rows):
        if len(self.refs) == 1:
            return self.refs[0][rows, :]
        k = max(i for i in range(len(self.refs)) if CUTS[i] <= rows.start)
        return self.refs[k][pl.ds(rows.start - CUTS[k], rows.size), :]


def line_rows(lay, h):
    if lay.sub == 1:
        return []
    if lay.sub == 2:
        return [(lay.own_y - 1) * (1 - h)]
    return [0, lay.own_y - 1]


def line_count(lay):
    return 0 if lay.sub == 1 else 1 if lay.sub == 2 else 2


def own_kernel(lay, raw, z_sq, y_sq, w3, face, w_out, d_out, r_out, sx_out, *packs):
    rhs, coef = raw.at[0], raw.at[1]
    y, nz = lay.own_y, lay.nz
    parity, h = lay.where()[:2]
    table3 = w3[...]
    for e in range(y // N):
        rows = pl.ds(N * e, N)
        w = [coef[a, rows, :] * table3[a] for a in range(N)]
        dx = even_odd((DM * DM).T, w, 1)
        for a in range(N):
            w_out[a, rows, :] = w[a]
            d_out[a, rows, :] = dx[a]
    hi, lo = split(w_out[...].reshape(N * y, nz))
    dz = z_apply(hi, lo, z_sq[...])
    sx_out[...] = assemble_yz(d_out[(N - 1) * parity])
    dy = y_planes(lambda a: w_out[a], list(range(N)), y_sq[...])
    for a in range(N):
        d_out[a] = assemble_yz(d_out[a] + dz[a * y : (a + 1) * y] + dy[a])
        r_out[a] = assemble_yz(rhs[a])
    inner = (N - 1) * (1 - parity)
    face[0] = r_out[inner]
    face[1] = d_out[inner]
    for pack, (first, far) in zip(packs, lay.sent_rows(h)):
        for side, field in ((0, r_out), (1, d_out)):
            for a in range(N):
                pack[pack_rows(side, a), :] = raw[side, a, aligned(first, HALO), :]
                pack[pl.ds(side * N + a, 1), :] = field[a, pl.ds(far, 1), :]


def message_kernel(lay, w, d, r, sx, face, *refs):
    msg, *side_msgs, u_s, d_s, r_s = refs
    y, nz = lay.own_y, lay.nz
    parity, h, start, offset, low, high = lay.where()
    mask = yz_mask(y, nz, h * y, lay.total_y)
    scale = mask.astype(F32) * (1.0 / THETA)
    odd = parity.astype(F32)
    for a in range(N):
        dd, rr = d[a], r[a]
        keep = scale
        if a in (0, N - 1):
            inner = odd if a == 0 else 1.0 - odd
            dd = dd + inner * face[1]
            rr = rr + inner * face[0]
            keep = scale * inner
        d_s[a] = dd
        r_s[a] = rr
        u_s[a] = keep * rr / jnp.where(mask, dd, 1.0)
    col = [jnp.where(parity == 0, float(DM[a, 0]), float(DM[a, N - 1])) for a in range(N)]
    acc = []
    for e in range(y // N):
        rows = pl.ds(N * e, N)
        g = even_odd(DM, [u_s[a, rows, :] for a in range(N)], -1)
        total = None
        for a in range(N):
            term = (w[a, rows, :] * g[a]) * col[a]
            total = term if total is None else total + term
        acc.append(total)
    outer = (N - 1) * parity
    msg[pl.ds(0, y), :] = r[outer]
    msg[pl.ds(y, y), :] = d[outer]
    msg[pl.ds(2 * y, y), :] = sx[...]
    msg[pl.ds(3 * y, y), :] = w[outer]
    msg[pl.ds(4 * y, y), :] = assemble_yz(jnp.concatenate(acc, axis=0))
    base = 5 * y
    for row in line_rows(lay, h):
        for field in (r_s, d_s, w):
            for a in range(N):
                msg[pl.ds(base + a, 1), :] = field[a, pl.ds(row, 1), :]
            base += N
    for out, (first, _) in zip(side_msgs, lay.sent_rows(h)):
        for k in range(5):
            out[pl.ds(k * HALO, HALO), :] = msg[aligned(k * y + first, HALO), :]
        lines = base - 5 * y
        out[pl.ds(5 * HALO, lines), :] = msg[pl.ds(5 * y, lines), :]
        out[pl.ds(5 * HALO + lines, SPARE), :] = jnp.zeros((SPARE, nz), F32)


def flux_x(lay, u_ref, w_ref, first, count, fx):
    for el in range(2):
        for e in range(count // N):
            rows, to = aligned(first + N * e, N), pl.ds(N * e, N)
            u = [u_ref[N * el + a, rows, :] for a in range(N)]
            g = even_odd(DM, u, -1)
            for a in range(N):
                fx[N * el + a, to, :] = w_ref[N * el + a, rows, :] * g[a]


def flux_yz(lay, u_ref, w_ref, planes, first, count, z_d, y_d, fy, fz):
    part, to = aligned(first, count), pl.ds(0, count)
    u = jnp.concatenate([u_ref[p, part, :] for p in planes], axis=0)
    gz = z_apply(*split(u), z_d[...])
    gy = y_planes(lambda p: u_ref[p, part, :], planes, y_d[...])
    for k, p in enumerate(planes):
        w = w_ref[p, part, :]
        fy[p, to, :] = w * gy[p]
        fz[p, to, :] = w * gz[k * count : (k + 1) * count]


def operate(lay, u_ref, w_ref, back, first, count, tables, fx, fy, fz):
    z_d, z_dt, y_d, y_dt = tables
    nz = lay.nz
    middle = list(range(1, 2 * N - 1))
    flux_x(lay, u_ref, w_ref, first, count, fx)
    flux_yz(lay, u_ref, w_ref, middle, first, count, z_d, y_d, fy, fz)
    to, part = pl.ds(0, count), aligned(first, count)
    for el in range(2):
        for e in range(count // N):
            rows, here = aligned(first + N * e, N), pl.ds(N * e, N)
            b = even_odd(DM.T, [fx[N * el + a, here, :] for a in range(N)], -1)
            for a in range(N):
                back[N * el + a, rows, :] = b[a]
    n = len(middle)
    bz = z_apply(*split(fz[pl.ds(1, n), to, :].reshape(n * count, nz)), z_dt[...])
    by = y_planes(lambda p: fy[p, to, :], middle, y_dt[...])
    for p in middle:
        back[p, part, :] = back[p, part, :] + by[p] + bz[(p - 1) * count : p * count]


def smooth_start(lay, d, r, inv, u, first, count, start):
    part = aligned(first, count)
    mask = yz_mask(count, lay.nz, start + first, lay.total_y)
    inside = mask.astype(F32)
    zero = jnp.zeros((count, lay.nz), F32)
    for p in range(2 * N):
        if p in (0, 2 * N - 1):
            u[p, part, :] = zero
        else:
            i = inside / jnp.where(mask, d[p, part, :], 1.0)
            inv[p, part, :] = i
            u[p, part, :] = i * r[p, part, :] * (1.0 / THETA)


def sum_middle(fields, first, count):
    part = aligned(first, count)
    for s in fields:
        both = s[N - 1, part, :] + s[N, part, :]
        s[N - 1, part, :] = both
        s[N, part, :] = both


def element_sums(lay, base, parity, first, count, source, tables, outs):
    z_sq, y_sq, w3 = tables
    w_out, rhs_out, d_s, r_s, lin = outs[:5]
    nz = lay.nz
    part = aligned(first, count)
    for side, target in ((0, rhs_out), (1, w_out)):
        for a in range(N):
            target[base + a, part, :] = source(side, a)
    table3 = w3[...]
    outer = [jnp.where(parity == 0, float(DM[a, 0]), float(DM[a, N - 1])) for a in range(N)]
    for e in range(count // N):
        rows = aligned(first + N * e, N)
        w = [w_out[base + a, rows, :] * table3[a] for a in range(N)]
        dx = even_odd((DM * DM).T, w, 1)
        cx = even_odd(DM.T, [outer[a] * w[a] for a in range(N)], -1)
        for a in range(N):
            w_out[base + a, rows, :] = w[a]
            d_s[base + a, rows, :] = dx[a]
            lin[base + a, rows, :] = cx[a]
    dz = z_apply(*split(w_out[pl.ds(base, N), part, :].reshape(N * count, nz)), z_sq[...])
    dy = y_planes(lambda a: w_out[base + a, part, :], list(range(N)), y_sq[...])
    for a in range(N):
        d_local = d_s[base + a, part, :] + dz[a * count : (a + 1) * count] + dy[a]
        d_s[base + a, part, :] = assemble_yz(d_local)
        r_s[base + a, part, :] = assemble_yz(rhs_out[base + a, part, :])
        lin[base + a, part, :] = assemble_yz(lin[base + a, part, :])


def other_sums(lay, base, parity, h, pieces, tables, outs):
    d_s, r_s = outs[2:4]
    for piece, first, row in zip(pieces, lay.other_starts(h), lay.far_rows(h)):
        source = lambda side, a, piece=piece: piece[pack_rows(side, a)]
        element_sums(lay, base, parity, first, HALO, source, tables, outs)
        for side, target in ((0, r_s), (1, d_s)):
            for a in range(N):
                target[base + a, pl.ds(row, 1), :] = piece[pl.ds(side * N + a, 1)]


ARRAYS = 8


def early_kernel(lay, own, mate, *refs):
    z_sq, y_sq, w3 = refs[:3]
    tables, outs, scratch = refs[3:7], refs[7 : 7 + ARRAYS], refs[7 + ARRAYS :]
    w, _, d, r, _, inv, u, back = outs
    parity, h, start, offset, low, high = lay.where()
    for base, el, block in ((parity * N, parity, own), ((1 - parity) * N, 1 - parity, mate)):
        source = lambda side, a, block=block: block[side, a]
        element_sums(lay, base, el, offset, lay.own_y, source, (z_sq, y_sq, w3), outs)
    sum_middle((d, r), offset, lay.own_y)
    smooth_start(lay, d, r, inv, u, offset, lay.own_y, start)
    first, count = lay.early_rows(h)
    operate(lay, u, w, back, first, count, tables, *scratch)


def near_kernel(lay, n_other, *refs):
    other, tables = refs[:n_other], refs[n_other : n_other + 3]
    outs = refs[n_other + 3 + ARRAYS :]
    parity, h = lay.where()[:2]
    other_sums(lay, parity * N, parity, h, [Pieces([o]) for o in other], tables, outs)


def deep_kernel(lay, n_other, *refs):
    cuts = len(CUTS) - 1
    mate_other = [Pieces(refs[cuts * k : cuts * (k + 1)]) for k in range(n_other)]
    refs = refs[cuts * n_other :]
    z_sq, y_sq, w3 = refs[:3]
    tables = refs[3:7]
    refs = refs[7 + ARRAYS :]
    outs, sec_out, ends = refs[:ARRAYS], refs[ARRAYS], refs[ARRAYS + 1]
    scratch = refs[ARRAYS + 2 :]
    w, _, d, r, lin, inv, u, back = outs
    last = 2 * N - 1
    parity, h, start, offset, low, high = lay.where()
    other_sums(lay, (1 - parity) * N, 1 - parity, h, mate_other, (z_sq, y_sq, w3), outs)
    for first in lay.other_starts(h):
        sum_middle((d, r), first, HALO)
    for begin in lay.interfaces(h):
        above, below = pl.ds(begin - 1, 1), pl.ds(begin, 1)
        for s in (d, r, lin):
            for p in range(2 * N):
                both = s[p, above, :] + s[p, below, :]
                s[p, above, :] = both
                s[p, below, :] = both
    for side, p in ((0, 0), (1, last)):
        ends[side, 0] = r[p]
        ends[side, 1] = d[p]
    for first in lay.late_starts(h):
        smooth_start(lay, d, r, inv, u, first, HALO + N, start)
        operate(lay, u, w, back, first, HALO + N, tables, *scratch)
    for p in range(1, last):
        back[p] = assemble_yz(back[p])
    sum_middle((back,), 0, lay.ny)
    for p in range(2 * N):
        if p in (0, last):
            sec_out[p] = assemble_yz(back[p])
        else:
            i = (2.0 * RHO1 / DELTA) * inv[p]
            lin[p] = -i * lin[p]
            sec_out[p] = (1.0 + RHO1 * RHO0) * u[p] + i * (r[p] - back[p])


def coarse_tables_kernel(lay, w_ref, rhs_ref, my, mz, ry, rz, g_out, r_out):
    ny, nz, cr = lay.ny, lay.nz, lay.cr
    lhs = []
    for el in range(2):
        for m in MASS:
            total = None
            for a in range(N):
                term = float(m[a]) * w_ref[N * el + a]
                total = term if total is None else total + term
            lhs.append(total)
    along_z = z_apply(*split(jnp.concatenate(lhs, axis=0)), mz[...])
    for el in range(2):
        mom = {}
        for alpha in range(3):
            at = (3 * el + alpha) * ny
            block = y_apply(along_z[at : at + ny], my[...])
            for beta in range(3):
                for gamma in range(3):
                    mom[alpha, beta, gamma] = block[
                        beta * cr : (beta + 1) * cr, gamma * nz : (gamma + 1) * nz
                    ]
        x_sum, y_sum, z_sum = {}, {}, {}
        for i in range(3):
            for j in range(3):
                x_sum[i, j] = mom[0, i, j] + 2.0 * mom[1, i, j] + mom[2, i, j]
                y_sum[i, j] = mom[i, 0, j] + 2.0 * mom[i, 1, j] + mom[i, 2, j]
                z_sum[i, j] = mom[i, j, 0] + 2.0 * mom[i, j, 1] + mom[i, j, 2]
        sign = (1.0, -1.0, 1.0)
        for alpha in range(3):
            for beta in range(3):
                for gamma in range(3):
                    g_out[el, 9 * alpha + 3 * beta + gamma] = 0.25 * (
                        sign[alpha] * x_sum[beta, gamma]
                        + sign[beta] * y_sum[alpha, gamma]
                        + sign[gamma] * z_sum[alpha, beta]
                    )
    sums = []
    for el in range(2):
        for i in range(2):
            total = None
            for a in range(N):
                term = float(RHO[a, i]) * rhs_ref[N * el + a]
                total = term if total is None else total + term
            sums.append(total)
    part = y_apply(jnp.concatenate(sums, axis=1), ry[...])
    rows = jnp.concatenate([part[:, k * nz : (k + 1) * nz] for k in range(4)], axis=0)
    full = z_apply(*split(rows), rz[...])
    for k in range(4):
        r_out[k] = full[k * cr : (k + 1) * cr]


def pair_index(i, j):
    return i + j


def shifted(c, q, r):
    if q:
        c = pltpu.roll(c, c.shape[0] - 1, 0)
    if r:
        c = pltpu.roll(c, c.shape[1] - 1, 1)
    return c


def scatter(parts):
    cr, nz = parts[0, 0].shape
    first = parts[0, 0] + pltpu.roll(parts[0, 1], 1, 1)
    second = parts[1, 0] + pltpu.roll(parts[1, 1], 1, 1)
    return first + pltpu.roll(second, 1, 0)


def gathered(c):
    return {(q, r): shifted(c, q, r) for q in range(2) for r in range(2)}


def face_apply(entry, c, out=None):
    out = {} if out is None else out
    for j in range(2):
        for k in range(2):
            for q in range(2):
                for r in range(2):
                    term = entry(pair_index(j, q), pair_index(k, r)) * c[q, r]
                    out[j, k] = term if (j, k) not in out else out[j, k] + term
    return out


def coarse_diag(entry):
    return scatter({(j, k): entry(2 * j, 2 * k) for j in range(2) for k in range(2)})


def coarse_mask(lay, start):
    row = lax.broadcasted_iota(jnp.int32, (lay.cr, lay.nz), 0) + lax.div(start, N)
    lane = lax.broadcasted_iota(jnp.int32, (lay.cr, lay.nz), 1)
    return (row > 0) & (row < lay.total_y // N) & (lane > 0) & (lane < lay.ez)


def unpack_sides(lay, pieces, mate_pieces, line, parity, h, start, win):
    y, nz = lay.own_y, lay.nz
    for side, group in ((parity, pieces), (1 - parity, mate_pieces)):
        for k in range(5):

            def put(rows, value):
                win[side, k, rows, :] = value

            others = [g[pl.ds(k * HALO, HALO), :] for g in group[1:]]
            gather_window(lay, group[0][pl.ds(k * y, y), :], others, h, put)
    is_even = parity == 0
    lane = lax.broadcasted_iota(jnp.int32, (N, nz), 1)
    node = lax.broadcasted_iota(jnp.int32, (N, nz), 0)
    lane_in = (lane > 0) & (lane < nz - 1)
    flank = lax.broadcasted_iota(jnp.int32, (1, nz), 1)
    last = ((flank % N == N - 1) & (flank < nz - 1)).astype(F32)
    first = ((flank % N == 0) & (flank > 0)).astype(F32)
    for b, begin in enumerate(lay.interfaces(h), 1):
        above, below = pl.ds(begin - 1, 1), pl.ds(begin, 1)
        for side in range(2):
            for k in range(3):
                both = win[side, k, above, :] + win[side, k, below, :]
                win[side, k, above, :] = both
                win[side, k, below, :] = both
        for side in range(2):
            outer = N - 1 if side == 0 else 0

            def field(k):
                def of(group):
                    own_lines, other_lines = 5 * y + k * N, 5 * HALO + k * N
                    if lay.sub == 2:
                        mine, theirs = own_lines, other_lines
                        near = group[1]
                    else:
                        mine = own_lines + 3 * N * (b - 1)
                        theirs = other_lines + 3 * N * (2 - b)
                        near = group[b]
                    return group[0][pl.ds(mine, N), :] + near[pl.ds(theirs, N), :]
                mine, theirs = of(pieces), of(mate_pieces)
                if side == 0:
                    return jnp.where(is_even, mine, theirs)
                return jnp.where(is_even, theirs, mine)

            r, d, w = field(0), field(1), field(2)
            row = start + begin
            ok = lane_in & (node != outer) & (row > 0) & (row < lay.total_y)
            u = jnp.where(ok, r / jnp.where(ok, d, 1.0) * (1.0 / THETA), 0.0)
            g = None
            for a in range(N):
                term = line[a] * u[a : a + 1]
                g = term if g is None else g + term
            total = jnp.sum(line[N + side] * (w * g), axis=0, keepdims=True)
            total = total + last * pltpu.roll(total, nz - 1, 1) + first * pltpu.roll(total, 1, 1)
            win[side, 4, above, :] = total
            win[side, 4, below, :] = total


def second_kernel(lay, n_pieces, *refs):
    pieces, mate_pieces = refs[:n_pieces], refs[n_pieces : 2 * n_pieces]
    w_ref, sec_in, lin_in, ends, g_ref, r_ref = refs[2 * n_pieces : 2 * n_pieces + 6]
    refs = refs[2 * n_pieces + 6 :]
    z_d, z_dt, y_d, y_dt, ry, ry_one, rz, line = refs[:8]
    out, msg, state = refs[8:11]
    win, sec, fx, fy, fz = refs[11:]
    ny, nz, cr = lay.ny, lay.nz, lay.cr
    last = 2 * N - 1
    parity, h, start, offset, low, high = lay.where()
    mask = yz_mask(ny, nz, start, lay.total_y)
    inside = mask.astype(F32)
    is_even = parity == 0
    unpack_sides(lay, pieces, mate_pieces, line, parity, h, start, win)
    flags = (low, high)
    inv, res, u = [], [], []
    for side in range(2):
        valid = inside * flags[side]
        inv.append(valid / jnp.where(mask, ends[side, 1] + win[side, 1], 1.0))
        res.append(valid * (ends[side, 0] + win[side, 0]))
        u.append(inv[side] * res[side] * (1.0 / THETA))
    for p in range(1, last):
        value = sec_in[p]
        if p <= N:
            value = value + lin_in[min(p, N - 1)] * u[0]
        if p >= N - 1:
            value = value + lin_in[max(p, N)] * u[1]
        sec[p] = value
    flux_yz(lay, sec, w_ref, list(range(1, last)), 0, ny, z_d, y_d, fy, fz)
    weights = [w_ref[0] + win[0, 3], w_ref[last] + win[1, 3]]
    hi, lo = split(jnp.concatenate(u, axis=0))
    gz = z_apply(hi, lo, z_d[...])
    gy = y_apply(jnp.concatenate(u, axis=1), y_d[...])
    weight_z = jnp.concatenate(weights, axis=0)
    weight_y = jnp.concatenate(weights, axis=1)
    bz = z_apply(*split(weight_z * gz), z_dt[...])
    by = y_apply(weight_y * gy, y_dt[...])
    for side, p in ((0, 0), (1, last)):
        plane = assemble_yz(bz[side * ny : (side + 1) * ny] + by[:, side * nz : (side + 1) * nz])
        plane = plane + sec_in[p] + win[side, 4] + (lin_in[p] + win[side, 2]) * u[side]
        res_one = res[side] - inside * plane
        sec[p] = (1.0 + RHO1 * RHO0) * u[side] + (2.0 * RHO1 / DELTA) * inv[side] * res_one
    out[...] = sec[pl.ds(parity * N, N), pl.ds(pl.multiple_of(offset, N), lay.own_y), :]
    flux_yz(lay, sec, w_ref, [0, last], 0, ny, z_d, y_d, fy, fz)
    flux_x(lay, sec, w_ref, 0, ny, fx)
    sums = []
    for f, weight in ((fx, DRHO), (fy, RHO), (fz, RHO)):
        lanes = []
        for el in range(2):
            for i in range(2):
                total = None
                for a in range(N):
                    term = float(weight[a, i]) * f[N * el + a]
                    total = term if total is None else total + term
                lanes.append(total)
        sums.append(jnp.concatenate(lanes, axis=1))
    data = jnp.concatenate(sums, axis=0)
    hi = data.astype(BF16).astype(F32)
    parts = jnp.concatenate([hi, data - hi], axis=1).astype(BF16)
    both = dot(ry[...].astype(BF16), parts)
    both = both[: 2 * cr, : 4 * nz] + both[2 * cr :, : 4 * nz] + both[: 2 * cr, 4 * nz :]
    rows = [
        jnp.concatenate([v[:, k * nz : (k + 1) * nz] for v in (both[:cr], both[cr:])], axis=1)
        for k in range(4)
    ]
    full = z_apply(*split(jnp.concatenate(rows, axis=0)), rz[...])
    r = {}
    for el in range(2):
        for i in range(2):
            k = 2 * el + i
            r[el, i] = r_ref[k] - full[k * cr : (k + 1) * cr]
    planes = [r[0, 0], r[0, 1] + r[1, 0], r[1, 1]]
    cmask = coarse_mask(lay, start)

    def entry(el, alpha):
        return lambda beta, gamma: g_ref[el, 9 * alpha + 3 * beta + gamma]

    d = [
        coarse_diag(entry(0, 0)),
        coarse_diag(entry(0, 2)) + coarse_diag(entry(1, 0)),
        coarse_diag(entry(1, 2)),
    ]
    cin = cmask.astype(F32)
    mid = (2.0 / 3.0) * cin * planes[1] / jnp.where(cmask, d[1], 1.0)
    c = gathered(mid)
    g_low = scatter(face_apply(entry(0, 1), c))
    g_high = scatter(face_apply(entry(1, 1), c))
    g_mid = scatter(face_apply(entry(1, 0), c, face_apply(entry(0, 2), c)))
    state[0] = planes[0]
    state[1] = planes[1]
    state[2] = planes[2]
    state[3] = d[0]
    state[4] = d[1]
    state[5] = d[2]
    state[6] = g_low
    state[7] = g_mid
    state[8] = g_high
    state[9] = mid
    send = [
        jnp.where(is_even, planes[0], planes[2]),
        jnp.where(is_even, d[0], d[2]),
        jnp.where(is_even, g_low, g_high),
    ]
    send += [jnp.where(is_even, g_ref[0, k], g_ref[1, 18 + k]) for k in range(9)]
    for k in range(3):
        packed = send[4 * k]
        for q in range(1, 4):
            packed = packed + pltpu.roll(send[4 * k + q], q * (nz // 4), 1)
        msg[k] = packed


def third_kernel(lay, *refs):
    own_msg, mate_msg, sec, state, g_ref, py, pz, out, coarse = refs
    ny, nz, cr = lay.ny, lay.nz, lay.cr
    parity, h, start, offset, low, high = lay.where()
    is_even = parity == 0
    cmask = coarse_mask(lay, start)
    cin = cmask.astype(F32)
    lo_msg, hi_msg = [], []
    for k in range(3):
        mine, theirs = own_msg[k], mate_msg[k]
        for target, packed in (
            (lo_msg, jnp.where(is_even, mine, theirs)),
            (hi_msg, jnp.where(is_even, theirs, mine)),
        ):
            target.append(packed)
            for q in range(1, 4):
                target.append(pltpu.roll(packed, nz - q * (nz // 4), 1))

    def entry(el, alpha):
        return lambda beta, gamma: g_ref[el, 9 * alpha + 3 * beta + gamma]

    def outer(at, m, flag, el, alpha):
        rhs = cin * flag * (state[at] + m[0])
        d = jnp.where(cmask, state[3 + at] + m[1], 1.0)
        one = (2.0 / 3.0) * rhs / d
        c = gathered(one)
        here = lambda beta, gamma: g_ref[el, 9 * alpha + 3 * beta + gamma] + m[3 + 3 * beta + gamma]
        image = scatter(face_apply(here, c)) + state[6 + at] + m[2]
        cross = face_apply(entry(el, 1), c)
        solution = one + (2.0 / 3.0) * (rhs - cin * flag * image) / d
        return solution, cross

    c_low, cross_low = outer(0, lo_msg, low, 0, 0)
    c_high, cross_high = outer(2, hi_msg, high, 1, 2)
    cross = scatter({k: cross_low[k] + cross_high[k] for k in cross_low})
    rhs = cin * state[1]
    d = jnp.where(cmask, state[4], 1.0)
    c_mid = state[9] + (2.0 / 3.0) * (rhs - cin * (state[7] + cross)) / d
    left = jnp.where(is_even, c_low, c_mid)
    right = jnp.where(is_even, c_mid, c_high)
    both = jnp.concatenate([left, right], axis=1)
    if lay.sub > 1:
        both = pltpu.roll(both, cr - lax.div(offset, N), 0)
    y, cy = lay.own_y, lay.own_y // 4
    along_y = y_apply(both, py[...])
    along_y = jnp.concatenate([along_y[:, :nz], along_y[:, nz:]], axis=0)
    full = z_apply(*split(along_y), pz[...])
    inside = yz_mask(y, nz, start + offset, lay.total_y).astype(F32)
    q_left = inside * full[:y, :nz]
    q_right = inside * full[y + cy : 2 * y + cy, :nz]
    coarse[0] = full[y : y + cy, nz : nz + nz // 4]
    coarse[1] = full[2 * y + cy :, nz : nz + nz // 4]
    first_flag = jnp.where(is_even, low, 1.0)
    last_flag = jnp.where(is_even, 1.0, high)
    for a in range(N):
        add = float(INTERP[a, 0]) * q_left + float(INTERP[a, 1]) * q_right
        if a == 0:
            add = first_flag * add
        if a == N - 1:
            add = last_flag * add
        out[a] = sec[a] + add


def run(kernel, args, outs, scratch=(), aliases={}):
    return pl.pallas_call(
        kernel,
        out_shape=[jax.ShapeDtypeStruct(o, F32) for o in outs],
        in_specs=[pl.BlockSpec(memory_space=pltpu.VMEM)] * len(args),
        out_specs=[pl.BlockSpec(memory_space=pltpu.VMEM)] * len(outs),
        scratch_shapes=[pltpu.VMEM(s, F32) for s in scratch],
        compiler_params=pltpu.CompilerParams(vmem_limit_bytes=VMEM_LIMIT),
        input_output_aliases=aliases,
        cost_estimate=pl.CostEstimate(flops=1, bytes_accessed=1, transcendentals=0),
    )(*args)


def swap_pairs(count, first):
    pairs = []
    for i in range(first, count - 1, 2):
        pairs += [(i, i + 1), (i + 1, i)]
    return pairs


def chip_pairs(dom, sub, shift):
    pairs = []
    for a, b in swap_pairs(dom, 1):
        for q in range(sub):
            to = (q + shift) % sub if sub == 2 else q + shift
            if 0 <= to < sub:
                pairs.append((a * sub + q, b * sub + to))
    for end in (0, dom - 1):
        pairs += [(end * sub + a, end * sub + b) for a, b in swap_pairs(sub, 0)]
    return pairs


def shards(dom, sub, rhs_local, coefficient):
    size_x, own_y, nz = rhs_local.shape
    assert size_x == N and dom % 2 == 0 and (sub == 1 or own_y > HALO)
    lay = Layout(own_y, nz, dom, sub)
    ny, cr = lay.ny, lay.cr
    t = {k: jnp.asarray(v) for k, v in make_tables(ny, nz, own_y).items()}
    pick = lambda *names: [t[k] for k in names]
    even = lambda v: lax.ppermute(v, "dom", swap_pairs(dom, 0))
    odd = lambda v, k=0: lax.ppermute(v, ("dom", "sub"), chip_pairs(dom, sub, k))
    block = (N, own_y, nz)
    raw = jnp.stack([rhs_local, coefficient])
    n_other = 0 if sub == 1 else 1 if sub == 2 else 2
    face, w, d, r, sx, *packs = run(
        functools.partial(own_kernel, lay),
        [raw, t["z_sq"], t["y_sq", own_y // N], t["w3"]],
        [(2, own_y, nz), block, block, block, (own_y, nz)]
        + [(PACK, nz)] * n_other,
    )
    mate_face = even(face)
    if sub == 1:
        steps = []
    elif sub == 2:
        steps = [[(0, 1), (1, 0)]]
    else:
        up = [(i, i + 1) for i in range(sub - 1)]
        steps = [up, [(b, a) for a, b in up]]
    others = [lax.ppermute(pack, "sub", step) for pack, step in zip(packs, steps)]
    mate = even(raw)
    lines = 3 * N * line_count(lay)
    msgs = run(
        functools.partial(message_kernel, lay),
        [w, d, r, sx, mate_face],
        [(5 * own_y + lines, nz)] + [(5 * HALO + lines + SPARE, nz)] * n_other,
        [block] * 3,
    )
    shifts = [0] if sub == 1 else [0, 1] if sub == 2 else [0, 1, -1]
    pieces = [odd(msg, k) for msg, k in zip(msgs, shifts)]
    pair = (2 * N, ny, nz)
    count = lay.early_rows(0)[1] // N
    arrays = run(
        functools.partial(early_kernel, lay),
        [raw, mate, t["z_sq"], t["y_sq", own_y // N], t["w3"]]
        + [t["z_d"], t["z_dt"], t["y_d", count], t["y_dt", count]],
        [pair] * ARRAYS,
        [(2 * N, count * N, nz)] * 3,
    )
    others, arrays = lax.optimization_barrier((others, arrays))
    mate_others = [even(o[a:b]) for o in others for a, b in zip(CUTS, CUTS[1:])]
    arrays = run(
        functools.partial(near_kernel, lay, n_other),
        [*others, t["z_sq"], t["y_sq", HALO // N], t["w3"], *arrays],
        [pair] * ARRAYS,
        (),
        {n_other + 3 + k: k for k in range(ARRAYS)},
    )
    pieces[0], arrays = lax.optimization_barrier((pieces[0], arrays))
    late = lambda *names: [t[k, HALO // N + 1] for k in names]
    sums = [t["z_sq"], t["y_sq", HALO // N], t["w3"]]
    w, rhs, _, _, lin, _, _, _, sec, ends = run(
        functools.partial(deep_kernel, lay, n_other),
        [*mate_others, *sums, t["z_d"], t["z_dt"], *late("y_d", "y_dt"), *arrays],
        [pair] * (ARRAYS + 1) + [(2, 2, ny, nz)],
        [(2 * N, HALO + N, nz)] * 3,
        {len(mate_others) + 7 + k: k for k in range(ARRAYS)},
    )
    later, sec = lax.optimization_barrier((pieces[1:], sec))
    pieces = pieces[:1] + later
    mate_pieces = [even(p) for p in pieces]
    g, r = run(
        functools.partial(coarse_tables_kernel, lay),
        [w, rhs] + pick("my", "mz", "ry_one", "rz_one"),
        [(2, 27, cr, nz), (4, cr, nz)],
    )
    sec, msg, state = run(
        functools.partial(second_kernel, lay, len(pieces)),
        [*pieces, *mate_pieces, w, sec, lin, ends, g, r]
        + pick("z_d", "z_dt", "y_d", "y_dt", "ry", "ry_one", "rz", "line"),
        [block, (3, cr, nz), (10, cr, nz)],
        [(2, 5, ny, nz)] + [pair] * 4,
    )
    from_odd = odd(msg)
    from_mate = even(from_odd)
    return tuple(
        run(
            functools.partial(third_kernel, lay),
            [from_odd, from_mate, sec, state, g] + pick("py", "pz"),
            [block, (size_x // 4, own_y // 4, nz // 4)],
        )
    )


def solution(mesh):
    dom, sub = mesh.shape["dom"], mesh.shape["sub"]
    return jax.shard_map(
        functools.partial(shards, dom, sub),
        mesh=mesh,
        in_specs=(P("dom", "sub", None), P("dom", "sub", None)),
        out_specs=(P("dom", "sub", None), P("dom", "sub", None)),
        check_vma=False,
    )
```

```python
import functools

import jax
import jax.numpy as jnp
import numpy as np
from jax import lax
from jax.experimental import pallas as pl
from jax.experimental.pallas import tpu as pltpu
from jax.sharding import PartitionSpec as P

N = 8
SPARE = N
HALO = 3 * N
THETA = 1.1
DELTA = 0.9
SIGMA = THETA / DELTA
RHO0 = 1.0 / SIGMA
RHO1 = 1.0 / (2.0 * SIGMA - RHO0)
LANES = 128
F32 = jnp.float32
BF16 = jnp.bfloat16
VMEM_LIMIT = 48 * 1024 * 1024


def legendre_value(points, degree):
    previous = np.ones(points.shape)
    current = points.copy()
    for level in range(1, degree):
        following = ((2 * level + 1) * points * current - level * previous) / (level + 1)
        previous = current
        current = following
    return current


def tables():
    degree = 7
    points = np.array(
        [
            -1.0,
            -0.8717401485096066,
            -0.5917001814331423,
            -0.2092992179024789,
            0.2092992179024789,
            0.5917001814331423,
            0.8717401485096066,
            1.0,
        ]
    )
    values = legendre_value(points, degree)
    weights = 2.0 / (degree * (degree + 1) * values**2)
    derivative = np.zeros((8, 8))
    for row_at in range(8):
        for col_at in range(8):
            if row_at != col_at:
                derivative[row_at, col_at] = values[row_at] / (
                    values[col_at] * (points[row_at] - points[col_at])
                )
    derivative[0, 0] = -degree * (degree + 1) / 4.0
    derivative[7, 7] = degree * (degree + 1) / 4.0
    interp = np.stack([(1.0 - points) / 2.0, (1.0 + points) / 2.0], axis=1)
    return derivative, weights, interp


DM, WEIGHTS, INTERP = tables()
MULT = np.array([2.0] + [1.0] * 6 + [2.0])
RHO = MULT[:, None] * INTERP
DRHO = DM @ RHO


def blockdiag(block, count):
    return np.kron(np.eye(count), block)


def hi_lo(matrix):
    hi = matrix.astype(jnp.bfloat16)
    lo = (matrix - hi.astype(np.float64)).astype(jnp.bfloat16)
    return hi, lo


def right_table(matrix):
    hi, lo = hi_lo(matrix)
    full = np.concatenate([np.concatenate([hi, hi]), np.concatenate([lo, 0 * lo])], axis=1)
    return np.stack(np.split(full, full.shape[1] // LANES, axis=1))


def left_table(matrix):
    hi, lo = hi_lo(matrix)
    return np.concatenate([hi, hi, lo], axis=1).astype(np.float32)


def vertex_table(per_node, elements, columns, count=8):
    out = np.zeros((count * elements, columns))
    for e in range(elements):
        for i in range(2):
            out[count * e : count * (e + 1), e + i] += per_node[:, i]
    return out


def moment_table(per_node, elements, columns):
    out = np.zeros((8 * elements, columns))
    for e in range(elements):
        out[8 * e : 8 * e + 8, e] = per_node
    return out


PAIRS = [(0, 0), (0, 1), (1, 1)]
MASS = [INTERP[:, i] * INTERP[:, j] for i, j in PAIRS]


def round_up(value, to):
    return -(-value // to) * to


def make_tables(ny, nz, own_y):
    ey, ez = ny // N, nz // N
    cr = round_up(ey + 1, 8)
    t = {}
    t["z_d"] = right_table(blockdiag(DM, ez).T)
    t["z_dt"] = right_table(blockdiag(DM, ez))
    t["z_sq"] = right_table(blockdiag(DM * DM, ez))
    t["y_d"] = left_table(blockdiag(DM, ey))
    t["y_dt"] = left_table(blockdiag(DM, ey).T)
    for count in range(1, own_y // N + 1):
        t["y_sq", count] = left_table(blockdiag(DM * DM, count).T)
        t["y_d", count] = left_table(blockdiag(DM, count))
        t["y_dt", count] = left_table(blockdiag(DM, count).T)
    py = vertex_table(RHO, ey, cr)
    dpy = blockdiag(DM, ey) @ py
    pz = vertex_table(RHO, ez, nz)
    dpz = blockdiag(DM, ez) @ pz
    zero = np.zeros_like(py)
    ry = np.concatenate([np.concatenate([py, dpy, zero]), np.concatenate([zero, zero, py])], axis=1)
    t["ry"] = np.concatenate(hi_lo(ry.T), axis=0).astype(np.float32)
    t["ry_one"] = left_table(py.T)
    t["rz"] = right_table(np.concatenate([pz, dpz], axis=0))
    t["rz_one"] = right_table(pz)
    t["my"] = left_table(np.concatenate([moment_table(m, ey, cr) for m in MASS], axis=1).T)
    t["mz"] = right_table(np.concatenate([moment_table(m, ez, nz) for m in MASS], axis=1))
    t["py"] = np.broadcast_to(INTERP.T[:, :, None], (2, N, nz)).astype(np.float32)
    pz = vertex_table(INTERP, ez, nz).T
    sz = vertex_table(np.eye(2), ez, nz, 2).T
    t["pz"] = right_table(np.concatenate([pz, sz], axis=1))
    cols = np.concatenate([DM.T, DM.T[[N - 1]], DM.T[[0]]], axis=0)
    t["line"] = np.broadcast_to(cols[:, :, None], (N + 2, N, nz)).astype(np.float32)
    w3 = WEIGHTS[:, None, None] * WEIGHTS[None, :, None] * np.ones((1, 1, nz))
    t["w3"] = (w3 * np.tile(WEIGHTS, ez)[None, None, :]).astype(np.float32)
    return t


def even_odd(matrix, values, sign):
    even = [values[b] + values[7 - b] for b in range(4)]
    odd = [values[b] - values[7 - b] for b in range(4)]
    out = [None] * 8
    for a in range(4):
        pe = po = None
        for b in range(4):
            ce = float((matrix[a, b] + matrix[a, 7 - b]) / 2.0)
            co = float((matrix[a, b] - matrix[a, 7 - b]) / 2.0)
            te = ce * even[b]
            to = co * odd[b]
            pe = te if pe is None else pe + te
            po = to if po is None else po + to
        out[a] = pe + po
        out[7 - a] = pe - po if sign > 0 else po - pe
    return out


def split(x):
    hi = x.astype(BF16)
    lo = (x - hi.astype(F32)).astype(BF16)
    return hi, lo


def dot(a, b):
    return jnp.dot(a, b, preferred_element_type=F32)


def z_apply(hi, lo, table):
    table = jnp.concatenate([table[k] for k in range(table.shape[0])], axis=1)
    both = dot(jnp.concatenate([hi, lo], axis=1), table)
    half = both.shape[1] // 2
    return both[:, :half] + both[:, half:]


def y_apply(x, table):
    hi = x.astype(BF16).astype(F32)
    parts = jnp.concatenate([hi, x - hi, hi], axis=0).astype(BF16)
    return dot(table.astype(BF16), parts)


def y_planes(get, planes, table):
    table = table.astype(BF16)
    out = {}
    for p, q in zip(planes[::2], planes[1::2]):
        both = y_apply(jnp.concatenate([get(p), get(q)], axis=1), table)
        nz = both.shape[1] // 2
        out[p], out[q] = both[:, :nz], both[:, nz:]
    return out


def assemble_yz(v):
    ny, nz = v.shape
    row = lax.broadcasted_iota(jnp.int32, (N, nz), 0)
    lane = lax.broadcasted_iota(jnp.int32, (ny, nz), 1)
    is_top = row == 0
    flip = (N - 1) - row
    blocks = [v[N * e : N * e + N] for e in range(ny // N)]
    top = (row == N - 1).astype(F32)
    bottom = (row == 0).astype(F32)
    out = []
    for e, b in enumerate(blocks):
        if len(blocks) == 1:
            out.append(b)
            continue
        if e == 0:
            near, mask = blocks[1], top
        elif e + 1 == len(blocks):
            near, mask = blocks[e - 1], bottom
        else:
            near, mask = jnp.where(is_top, blocks[e + 1], blocks[e - 1]), top + bottom
        out.append(b + mask * jnp.take_along_axis(near, flip, axis=0))
    v = jnp.concatenate(out, axis=0)
    last = (lane % N == N - 1) & (lane < nz - 1)
    first = (lane % N == 0) & (lane > 0)
    other = lane + jnp.where(last, 1, 0) - jnp.where(first, 1, 0)
    mask = (last | first).astype(F32)
    return v + mask * jnp.take_along_axis(v, other, axis=1)


def yz_mask(ny, nz, start, total):
    row = lax.broadcasted_iota(jnp.int32, (ny, nz), 0) + start
    lane = lax.broadcasted_iota(jnp.int32, (ny, nz), 1)
    return (row > 0) & (row < total - 1) & (lane > 0) & (lane < nz - 1)


class Layout:
    def __init__(self, own_y, nz, dom, sub):
        self.own_y, self.nz, self.dom, self.sub = own_y, nz, dom, sub
        self.blocks = min(sub, 3)
        self.ny = own_y + HALO * (self.blocks - 1)
        self.total_y = own_y * sub
        self.ey, self.ez = self.ny // N, nz // N
        self.cr = round_up(self.ey + 1, 8)

    def where(self):
        d = lax.axis_index("dom")
        h = lax.axis_index("sub")
        parity = lax.rem(d, 2)
        pair = lax.div(d, 2)
        if self.sub == 1:
            start, offset = 0, 0
        elif self.sub == 2:
            start, offset = h * (self.own_y - HALO), h * HALO
        else:
            start, offset = h * self.own_y - HALO, HALO
        low = (pair > 0).astype(F32)
        high = (pair < self.dom // 2 - 1).astype(F32)
        return parity, h, start, offset, low, high

    def sent_rows(self, h):
        y = self.own_y
        down = (y - HALO, y - HALO)
        up = (0, HALO - 1)
        if self.sub == 1:
            return []
        if self.sub == 2:
            return [tuple(h * u + (1 - h) * v for u, v in zip(up, down))]
        return [down, up]

    def far_rows(self, h):
        if self.sub == 1:
            return []
        if self.sub == 2:
            return [(1 - h) * (self.ny - 1)]
        return [0, self.ny - 1]

    def other_starts(self, h):
        if self.sub == 1:
            return []
        if self.sub == 2:
            return [(1 - h) * self.own_y]
        return [0, HALO + self.own_y]

    def early_rows(self, h):
        if self.sub == 1:
            return 0, self.own_y
        if self.sub == 2:
            return h * (HALO + N), self.own_y - N
        return HALO + N, self.own_y - 2 * N

    def late_starts(self, h):
        if self.sub == 1:
            return []
        if self.sub == 2:
            return [(1 - h) * (self.own_y - N)]
        return [0, self.own_y + HALO - N]

    def interfaces(self, h):
        if self.sub == 1:
            return []
        if self.sub == 2:
            return [self.own_y - h * (self.own_y - HALO)]
        return [HALO, HALO + self.own_y]


def aligned(start, size):
    return pl.ds(start if isinstance(start, int) else pl.multiple_of(start, N), size)


def gather_window(lay, own, others, h, store):
    y = lay.own_y
    if lay.sub == 1:
        store(pl.ds(0, y), own)
    elif lay.sub == 2:
        store(aligned(h * HALO, y), own)
        store(aligned((1 - h) * y, HALO), others[0])
    else:
        store(pl.ds(0, HALO), others[0])
        store(pl.ds(HALO, y), own)
        store(pl.ds(HALO + y, HALO), others[1])


PACK = 2 * N + 2 * N * HALO
CUTS = [0, 2 * N + 5 * HALO, 2 * N + 10 * HALO, PACK]


def pack_rows(side, a):
    return pl.ds(2 * N + (side * N + a) * HALO, HALO)


class Pieces:
    def __init__(self, refs):
        self.refs = refs

    def __getitem__(self, rows):
        if len(self.refs) == 1:
            return self.refs[0][rows, :]
        k = max(i for i in range(len(self.refs)) if CUTS[i] <= rows.start)
        return self.refs[k][pl.ds(rows.start - CUTS[k], rows.size), :]


def line_rows(lay, h):
    if lay.sub == 1:
        return []
    if lay.sub == 2:
        return [(lay.own_y - 1) * (1 - h)]
    return [0, lay.own_y - 1]


def line_count(lay):
    return 0 if lay.sub == 1 else 1 if lay.sub == 2 else 2


def own_kernel(lay, raw, z_sq, y_sq, w3, face, w_out, d_out, r_out, sx_out, *packs):
    rhs, coef = raw.at[0], raw.at[1]
    y, nz = lay.own_y, lay.nz
    parity, h = lay.where()[:2]
    table3 = w3[...]
    for e in range(y // N):
        rows = pl.ds(N * e, N)
        w = [coef[a, rows, :] * table3[a] for a in range(N)]
        dx = even_odd((DM * DM).T, w, 1)
        for a in range(N):
            w_out[a, rows, :] = w[a]
            d_out[a, rows, :] = dx[a]
    hi, lo = split(w_out[...].reshape(N * y, nz))
    dz = z_apply(hi, lo, z_sq[...])
    sx_out[...] = assemble_yz(d_out[(N - 1) * parity])
    dy = y_planes(lambda a: w_out[a], list(range(N)), y_sq[...])
    for a in range(N):
        d_out[a] = assemble_yz(d_out[a] + dz[a * y : (a + 1) * y] + dy[a])
        r_out[a] = assemble_yz(rhs[a])
    inner = (N - 1) * (1 - parity)
    face[0] = r_out[inner]
    face[1] = d_out[inner]
    for pack, (first, far) in zip(packs, lay.sent_rows(h)):
        for side, field in ((0, r_out), (1, d_out)):
            for a in range(N):
                pack[pack_rows(side, a), :] = raw[side, a, aligned(first, HALO), :]
                pack[pl.ds(side * N + a, 1), :] = field[a, pl.ds(far, 1), :]


def message_kernel(lay, w, d, r, sx, face, *refs):
    msg, *side_msgs, u_s, d_s, r_s = refs
    y, nz = lay.own_y, lay.nz
    parity, h, start, offset, low, high = lay.where()
    mask = yz_mask(y, nz, h * y, lay.total_y)
    scale = mask.astype(F32) * (1.0 / THETA)
    odd = parity.astype(F32)
    for a in range(N):
        dd, rr = d[a], r[a]
        keep = scale
        if a in (0, N - 1):
            inner = odd if a == 0 else 1.0 - odd
            dd = dd + inner * face[1]
            rr = rr + inner * face[0]
            keep = scale * inner
        d_s[a] = dd
        r_s[a] = rr
        u_s[a] = keep * rr / jnp.where(mask, dd, 1.0)
    col = [jnp.where(parity == 0, float(DM[a, 0]), float(DM[a, N - 1])) for a in range(N)]
    acc = []
    for e in range(y // N):
        rows = pl.ds(N * e, N)
        g = even_odd(DM, [u_s[a, rows, :] for a in range(N)], -1)
        total = None
        for a in range(N):
            term = (w[a, rows, :] * g[a]) * col[a]
            total = term if total is None else total + term
        acc.append(total)
    outer = (N - 1) * parity
    msg[pl.ds(0, y), :] = r[outer]
    msg[pl.ds(y, y), :] = d[outer]
    msg[pl.ds(2 * y, y), :] = sx[...]
    msg[pl.ds(3 * y, y), :] = w[outer]
    msg[pl.ds(4 * y, y), :] = assemble_yz(jnp.concatenate(acc, axis=0))
    base = 5 * y
    for row in line_rows(lay, h):
        for field in (r_s, d_s, w):
            for a in range(N):
                msg[pl.ds(base + a, 1), :] = field[a, pl.ds(row, 1), :]
            base += N
    for out, (first, _) in zip(side_msgs, lay.sent_rows(h)):
        for k in range(5):
            out[pl.ds(k * HALO, HALO), :] = msg[aligned(k * y + first, HALO), :]
        lines = base - 5 * y
        out[pl.ds(5 * HALO, lines), :] = msg[pl.ds(5 * y, lines), :]
        out[pl.ds(5 * HALO + lines, SPARE), :] = jnp.zeros((SPARE, nz), F32)


def flux_x(lay, u_ref, w_ref, first, count, fx):
    for el in range(2):
        for e in range(count // N):
            rows, to = aligned(first + N * e, N), pl.ds(N * e, N)
            u = [u_ref[N * el + a, rows, :] for a in range(N)]
            g = even_odd(DM, u, -1)
            for a in range(N):
                fx[N * el + a, to, :] = w_ref[N * el + a, rows, :] * g[a]


def flux_yz(lay, u_ref, w_ref, planes, first, count, z_d, y_d, fy, fz):
    part, to = aligned(first, count), pl.ds(0, count)
    u = jnp.concatenate([u_ref[p, part, :] for p in planes], axis=0)
    gz = z_apply(*split(u), z_d[...])
    gy = y_planes(lambda p: u_ref[p, part, :], planes, y_d[...])
    for k, p in enumerate(planes):
        w = w_ref[p, part, :]
        fy[p, to, :] = w * gy[p]
        fz[p, to, :] = w * gz[k * count : (k + 1) * count]


def operate(lay, u_ref, w_ref, back, first, count, tables, fx, fy, fz):
    z_d, z_dt, y_d, y_dt = tables
    nz = lay.nz
    middle = list(range(1, 2 * N - 1))
    flux_x(lay, u_ref, w_ref, first, count, fx)
    flux_yz(lay, u_ref, w_ref, middle, first, count, z_d, y_d, fy, fz)
    to, part = pl.ds(0, count), aligned(first, count)
    for el in range(2):
        for e in range(count // N):
            rows, here = aligned(first + N * e, N), pl.ds(N * e, N)
            b = even_odd(DM.T, [fx[N * el + a, here, :] for a in range(N)], -1)
            for a in range(N):
                back[N * el + a, rows, :] = b[a]
    n = len(middle)
    bz = z_apply(*split(fz[pl.ds(1, n), to, :].reshape(n * count, nz)), z_dt[...])
    by = y_planes(lambda p: fy[p, to, :], middle, y_dt[...])
    for p in middle:
        back[p, part, :] = back[p, part, :] + by[p] + bz[(p - 1) * count : p * count]


def smooth_start(lay, d, r, inv, u, first, count, start):
    part = aligned(first, count)
    mask = yz_mask(count, lay.nz, start + first, lay.total_y)
    inside = mask.astype(F32)
    zero = jnp.zeros((count, lay.nz), F32)
    for p in range(2 * N):
        if p in (0, 2 * N - 1):
            u[p, part, :] = zero
        else:
            i = inside / jnp.where(mask, d[p, part, :], 1.0)
            inv[p, part, :] = i
            u[p, part, :] = i * r[p, part, :] * (1.0 / THETA)


def sum_middle(fields, first, count):
    part = aligned(first, count)
    for s in fields:
        both = s[N - 1, part, :] + s[N, part, :]
        s[N - 1, part, :] = both
        s[N, part, :] = both


def element_sums(lay, base, parity, first, count, source, tables, outs):
    z_sq, y_sq, w3 = tables
    w_out, rhs_out, d_s, r_s, lin = outs[:5]
    nz = lay.nz
    part = aligned(first, count)
    for side, target in ((0, rhs_out), (1, w_out)):
        for a in range(N):
            target[base + a, part, :] = source(side, a)
    table3 = w3[...]
    outer = [jnp.where(parity == 0, float(DM[a, 0]), float(DM[a, N - 1])) for a in range(N)]
    for e in range(count // N):
        rows = aligned(first + N * e, N)
        w = [w_out[base + a, rows, :] * table3[a] for a in range(N)]
        dx = even_odd((DM * DM).T, w, 1)
        cx = even_odd(DM.T, [outer[a] * w[a] for a in range(N)], -1)
        for a in range(N):
            w_out[base + a, rows, :] = w[a]
            d_s[base + a, rows, :] = dx[a]
            lin[base + a, rows, :] = cx[a]
    dz = z_apply(*split(w_out[pl.ds(base, N), part, :].reshape(N * count, nz)), z_sq[...])
    dy = y_planes(lambda a: w_out[base + a, part, :], list(range(N)), y_sq[...])
    for a in range(N):
        d_local = d_s[base + a, part, :] + dz[a * count : (a + 1) * count] + dy[a]
        d_s[base + a, part, :] = assemble_yz(d_local)
        r_s[base + a, part, :] = assemble_yz(rhs_out[base + a, part, :])
        lin[base + a, part, :] = assemble_yz(lin[base + a, part, :])


def other_sums(lay, base, parity, h, pieces, tables, outs):
    d_s, r_s = outs[2:4]
    for piece, first, row in zip(pieces, lay.other_starts(h), lay.far_rows(h)):
        source = lambda side, a, piece=piece: piece[pack_rows(side, a)]
        element_sums(lay, base, parity, first, HALO, source, tables, outs)
        for side, target in ((0, r_s), (1, d_s)):
            for a in range(N):
                target[base + a, pl.ds(row, 1), :] = piece[pl.ds(side * N + a, 1)]


ARRAYS = 8


def early_kernel(lay, own, mate, *refs):
    z_sq, y_sq, w3 = refs[:3]
    tables, outs, scratch = refs[3:7], refs[7 : 7 + ARRAYS], refs[7 + ARRAYS :]
    w, _, d, r, _, inv, u, back = outs
    parity, h, start, offset, low, high = lay.where()
    for base, el, block in ((parity * N, parity, own), ((1 - parity) * N, 1 - parity, mate)):
        source = lambda side, a, block=block: block[side, a]
        element_sums(lay, base, el, offset, lay.own_y, source, (z_sq, y_sq, w3), outs)
    sum_middle((d, r), offset, lay.own_y)
    smooth_start(lay, d, r, inv, u, offset, lay.own_y, start)
    first, count = lay.early_rows(h)
    operate(lay, u, w, back, first, count, tables, *scratch)


def near_kernel(lay, n_other, *refs):
    other, tables = refs[:n_other], refs[n_other : n_other + 3]
    outs = refs[n_other + 3 + ARRAYS :]
    parity, h = lay.where()[:2]
    other_sums(lay, parity * N, parity, h, [Pieces([o]) for o in other], tables, outs)


def deep_kernel(lay, n_other, *refs):
    cuts = len(CUTS) - 1
    mate_other = [Pieces(refs[cuts * k : cuts * (k + 1)]) for k in range(n_other)]
    refs = refs[cuts * n_other :]
    z_sq, y_sq, w3 = refs[:3]
    tables = refs[3:7]
    refs = refs[7 + ARRAYS :]
    outs, sec_out, ends = refs[:ARRAYS], refs[ARRAYS], refs[ARRAYS + 1]
    scratch = refs[ARRAYS + 2 :]
    w, _, d, r, lin, inv, u, back = outs
    last = 2 * N - 1
    parity, h, start, offset, low, high = lay.where()
    other_sums(lay, (1 - parity) * N, 1 - parity, h, mate_other, (z_sq, y_sq, w3), outs)
    for first in lay.other_starts(h):
        sum_middle((d, r), first, HALO)
    for begin in lay.interfaces(h):
        above, below = pl.ds(begin - 1, 1), pl.ds(begin, 1)
        for s in (d, r, lin):
            for p in range(2 * N):
                both = s[p, above, :] + s[p, below, :]
                s[p, above, :] = both
                s[p, below, :] = both
    for side, p in ((0, 0), (1, last)):
        ends[side, 0] = r[p]
        ends[side, 1] = d[p]
    for first in lay.late_starts(h):
        smooth_start(lay, d, r, inv, u, first, HALO + N, start)
        operate(lay, u, w, back, first, HALO + N, tables, *scratch)
    for p in range(1, last):
        back[p] = assemble_yz(back[p])
    sum_middle((back,), 0, lay.ny)
    for p in range(2 * N):
        if p in (0, last):
            sec_out[p] = assemble_yz(back[p])
        else:
            i = (2.0 * RHO1 / DELTA) * inv[p]
            lin[p] = -i * lin[p]
            sec_out[p] = (1.0 + RHO1 * RHO0) * u[p] + i * (r[p] - back[p])


def coarse_tables_kernel(lay, w_ref, rhs_ref, my, mz, ry, rz, g_out, r_out):
    ny, nz, cr = lay.ny, lay.nz, lay.cr
    lhs = []
    for el in range(2):
        for m in MASS:
            total = None
            for a in range(N):
                term = float(m[a]) * w_ref[N * el + a]
                total = term if total is None else total + term
            lhs.append(total)
    along_z = z_apply(*split(jnp.concatenate(lhs, axis=0)), mz[...])
    for el in range(2):
        mom = {}
        for alpha in range(3):
            at = (3 * el + alpha) * ny
            block = y_apply(along_z[at : at + ny], my[...])
            for beta in range(3):
                for gamma in range(3):
                    mom[alpha, beta, gamma] = block[
                        beta * cr : (beta + 1) * cr, gamma * nz : (gamma + 1) * nz
                    ]
        x_sum, y_sum, z_sum = {}, {}, {}
        for i in range(3):
            for j in range(3):
                x_sum[i, j] = mom[0, i, j] + 2.0 * mom[1, i, j] + mom[2, i, j]
                y_sum[i, j] = mom[i, 0, j] + 2.0 * mom[i, 1, j] + mom[i, 2, j]
                z_sum[i, j] = mom[i, j, 0] + 2.0 * mom[i, j, 1] + mom[i, j, 2]
        sign = (1.0, -1.0, 1.0)
        for alpha in range(3):
            for beta in range(3):
                for gamma in range(3):
                    g_out[el, 9 * alpha + 3 * beta + gamma] = 0.25 * (
                        sign[alpha] * x_sum[beta, gamma]
                        + sign[beta] * y_sum[alpha, gamma]
                        + sign[gamma] * z_sum[alpha, beta]
                    )
    sums = []
    for el in range(2):
        for i in range(2):
            total = None
            for a in range(N):
                term = float(RHO[a, i]) * rhs_ref[N * el + a]
                total = term if total is None else total + term
            sums.append(total)
    part = y_apply(jnp.concatenate(sums, axis=1), ry[...])
    rows = jnp.concatenate([part[:, k * nz : (k + 1) * nz] for k in range(4)], axis=0)
    full = z_apply(*split(rows), rz[...])
    for k in range(4):
        r_out[k] = full[k * cr : (k + 1) * cr]


def pair_index(i, j):
    return i + j


def shifted(c, q, r):
    if q:
        c = pltpu.roll(c, c.shape[0] - 1, 0)
    if r:
        c = pltpu.roll(c, c.shape[1] - 1, 1)
    return c


def scatter(parts):
    cr, nz = parts[0, 0].shape
    first = parts[0, 0] + pltpu.roll(parts[0, 1], 1, 1)
    second = parts[1, 0] + pltpu.roll(parts[1, 1], 1, 1)
    return first + pltpu.roll(second, 1, 0)


def gathered(c):
    return {(q, r): shifted(c, q, r) for q in range(2) for r in range(2)}


def face_apply(entry, c, out=None):
    out = {} if out is None else out
    for j in range(2):
        for k in range(2):
            for q in range(2):
                for r in range(2):
                    term = entry(pair_index(j, q), pair_index(k, r)) * c[q, r]
                    out[j, k] = term if (j, k) not in out else out[j, k] + term
    return out


def coarse_diag(entry):
    return scatter({(j, k): entry(2 * j, 2 * k) for j in range(2) for k in range(2)})


def coarse_mask(lay, start):
    row = lax.broadcasted_iota(jnp.int32, (lay.cr, lay.nz), 0) + lax.div(start, N)
    lane = lax.broadcasted_iota(jnp.int32, (lay.cr, lay.nz), 1)
    return (row > 0) & (row < lay.total_y // N) & (lane > 0) & (lane < lay.ez)


def unpack_sides(lay, pieces, mate_pieces, line, parity, h, start, win):
    y, nz = lay.own_y, lay.nz
    for side, group in ((parity, pieces), (1 - parity, mate_pieces)):
        for k in range(5):

            def put(rows, value):
                win[side, k, rows, :] = value

            others = [g[pl.ds(k * HALO, HALO), :] for g in group[1:]]
            gather_window(lay, group[0][pl.ds(k * y, y), :], others, h, put)
    is_even = parity == 0
    lane = lax.broadcasted_iota(jnp.int32, (N, nz), 1)
    node = lax.broadcasted_iota(jnp.int32, (N, nz), 0)
    lane_in = (lane > 0) & (lane < nz - 1)
    flank = lax.broadcasted_iota(jnp.int32, (1, nz), 1)
    last = ((flank % N == N - 1) & (flank < nz - 1)).astype(F32)
    first = ((flank % N == 0) & (flank > 0)).astype(F32)
    for b, begin in enumerate(lay.interfaces(h), 1):
        above, below = pl.ds(begin - 1, 1), pl.ds(begin, 1)
        for side in range(2):
            for k in range(3):
                both = win[side, k, above, :] + win[side, k, below, :]
                win[side, k, above, :] = both
                win[side, k, below, :] = both
        for side in range(2):
            outer = N - 1 if side == 0 else 0

            def field(k):
                def of(group):
                    own_lines, other_lines = 5 * y + k * N, 5 * HALO + k * N
                    if lay.sub == 2:
                        mine, theirs = own_lines, other_lines
                        near = group[1]
                    else:
                        mine = own_lines + 3 * N * (b - 1)
                        theirs = other_lines + 3 * N * (2 - b)
                        near = group[b]
                    return group[0][pl.ds(mine, N), :] + near[pl.ds(theirs, N), :]
                mine, theirs = of(pieces), of(mate_pieces)
                if side == 0:
                    return jnp.where(is_even, mine, theirs)
                return jnp.where(is_even, theirs, mine)

            r, d, w = field(0), field(1), field(2)
            row = start + begin
            ok = lane_in & (node != outer) & (row > 0) & (row < lay.total_y)
            u = jnp.where(ok, r / jnp.where(ok, d, 1.0) * (1.0 / THETA), 0.0)
            g = None
            for a in range(N):
                term = line[a] * u[a : a + 1]
                g = term if g is None else g + term
            total = jnp.sum(line[N + side] * (w * g), axis=0, keepdims=True)
            total = total + last * pltpu.roll(total, nz - 1, 1) + first * pltpu.roll(total, 1, 1)
            win[side, 4, above, :] = total
            win[side, 4, below, :] = total


def second_kernel(lay, n_pieces, *refs):
    pieces, mate_pieces = refs[:n_pieces], refs[n_pieces : 2 * n_pieces]
    w_ref, sec_in, lin_in, ends, g_ref, r_ref = refs[2 * n_pieces : 2 * n_pieces + 6]
    refs = refs[2 * n_pieces + 6 :]
    z_d, z_dt, y_d, y_dt, ry, ry_one, rz, line = refs[:8]
    out, msg, state = refs[8:11]
    win, sec, fx, fy, fz = refs[11:]
    ny, nz, cr = lay.ny, lay.nz, lay.cr
    last = 2 * N - 1
    parity, h, start, offset, low, high = lay.where()
    mask = yz_mask(ny, nz, start, lay.total_y)
    inside = mask.astype(F32)
    is_even = parity == 0
    unpack_sides(lay, pieces, mate_pieces, line, parity, h, start, win)
    flags = (low, high)
    inv, res, u = [], [], []
    for side in range(2):
        valid = inside * flags[side]
        inv.append(valid / jnp.where(mask, ends[side, 1] + win[side, 1], 1.0))
        res.append(valid * (ends[side, 0] + win[side, 0]))
        u.append(inv[side] * res[side] * (1.0 / THETA))
    for p in range(1, last):
        value = sec_in[p]
        if p <= N:
            value = value + lin_in[min(p, N - 1)] * u[0]
        if p >= N - 1:
            value = value + lin_in[max(p, N)] * u[1]
        sec[p] = value
    flux_yz(lay, sec, w_ref, list(range(1, last)), 0, ny, z_d, y_d, fy, fz)
    weights = [w_ref[0] + win[0, 3], w_ref[last] + win[1, 3]]
    hi, lo = split(jnp.concatenate(u, axis=0))
    gz = z_apply(hi, lo, z_d[...])
    gy = y_apply(jnp.concatenate(u, axis=1), y_d[...])
    weight_z = jnp.concatenate(weights, axis=0)
    weight_y = jnp.concatenate(weights, axis=1)
    bz = z_apply(*split(weight_z * gz), z_dt[...])
    by = y_apply(weight_y * gy, y_dt[...])
    for side, p in ((0, 0), (1, last)):
        plane = assemble_yz(bz[side * ny : (side + 1) * ny] + by[:, side * nz : (side + 1) * nz])
        plane = plane + sec_in[p] + win[side, 4] + (lin_in[p] + win[side, 2]) * u[side]
        res_one = res[side] - inside * plane
        sec[p] = (1.0 + RHO1 * RHO0) * u[side] + (2.0 * RHO1 / DELTA) * inv[side] * res_one
    out[...] = sec[pl.ds(parity * N, N), pl.ds(pl.multiple_of(offset, N), lay.own_y), :]
    flux_yz(lay, sec, w_ref, [0, last], 0, ny, z_d, y_d, fy, fz)
    flux_x(lay, sec, w_ref, 0, ny, fx)
    sums = []
    for f, weight in ((fx, DRHO), (fy, RHO), (fz, RHO)):
        lanes = []
        for el in range(2):
            for i in range(2):
                total = None
                for a in range(N):
                    term = float(weight[a, i]) * f[N * el + a]
                    total = term if total is None else total + term
                lanes.append(total)
        sums.append(jnp.concatenate(lanes, axis=1))
    data = jnp.concatenate(sums, axis=0)
    hi = data.astype(BF16).astype(F32)
    parts = jnp.concatenate([hi, data - hi], axis=1).astype(BF16)
    both = dot(ry[...].astype(BF16), parts)
    both = both[: 2 * cr, : 4 * nz] + both[2 * cr :, : 4 * nz] + both[: 2 * cr, 4 * nz :]
    rows = [
        jnp.concatenate([v[:, k * nz : (k + 1) * nz] for v in (both[:cr], both[cr:])], axis=1)
        for k in range(4)
    ]
    full = z_apply(*split(jnp.concatenate(rows, axis=0)), rz[...])
    r = {}
    for el in range(2):
        for i in range(2):
            k = 2 * el + i
            r[el, i] = r_ref[k] - full[k * cr : (k + 1) * cr]
    planes = [r[0, 0], r[0, 1] + r[1, 0], r[1, 1]]
    cmask = coarse_mask(lay, start)

    def entry(el, alpha):
        return lambda beta, gamma: g_ref[el, 9 * alpha + 3 * beta + gamma]

    d = [
        coarse_diag(entry(0, 0)),
        coarse_diag(entry(0, 2)) + coarse_diag(entry(1, 0)),
        coarse_diag(entry(1, 2)),
    ]
    cin = cmask.astype(F32)
    mid = (2.0 / 3.0) * cin * planes[1] / jnp.where(cmask, d[1], 1.0)
    c = gathered(mid)
    g_low = scatter(face_apply(entry(0, 1), c))
    g_high = scatter(face_apply(entry(1, 1), c))
    g_mid = scatter(face_apply(entry(1, 0), c, face_apply(entry(0, 2), c)))
    state[0] = planes[0]
    state[1] = planes[1]
    state[2] = planes[2]
    state[3] = d[0]
    state[4] = d[1]
    state[5] = d[2]
    state[6] = g_low
    state[7] = g_mid
    state[8] = g_high
    state[9] = mid
    send = [
        jnp.where(is_even, planes[0], planes[2]),
        jnp.where(is_even, d[0], d[2]),
        jnp.where(is_even, g_low, g_high),
    ]
    send += [jnp.where(is_even, g_ref[0, k], g_ref[1, 18 + k]) for k in range(9)]
    for k in range(3):
        packed = send[4 * k]
        for q in range(1, 4):
            packed = packed + pltpu.roll(send[4 * k + q], q * (nz // 4), 1)
        msg[k] = packed


def third_kernel(lay, *refs):
    own_msg, mate_msg, sec, state, g_ref, py, pz, out, coarse = refs
    ny, nz, cr = lay.ny, lay.nz, lay.cr
    parity, h, start, offset, low, high = lay.where()
    is_even = parity == 0
    cmask = coarse_mask(lay, start)
    cin = cmask.astype(F32)
    lo_msg, hi_msg = [], []
    for k in range(3):
        mine, theirs = own_msg[k], mate_msg[k]
        for target, packed in (
            (lo_msg, jnp.where(is_even, mine, theirs)),
            (hi_msg, jnp.where(is_even, theirs, mine)),
        ):
            target.append(packed)
            for q in range(1, 4):
                target.append(pltpu.roll(packed, nz - q * (nz // 4), 1))

    def entry(el, alpha):
        return lambda beta, gamma: g_ref[el, 9 * alpha + 3 * beta + gamma]

    def outer(at, m, flag, el, alpha):
        rhs = cin * flag * (state[at] + m[0])
        d = jnp.where(cmask, state[3 + at] + m[1], 1.0)
        one = (2.0 / 3.0) * rhs / d
        c = gathered(one)
        here = lambda beta, gamma: g_ref[el, 9 * alpha + 3 * beta + gamma] + m[3 + 3 * beta + gamma]
        image = scatter(face_apply(here, c)) + state[6 + at] + m[2]
        cross = face_apply(entry(el, 1), c)
        solution = one + (2.0 / 3.0) * (rhs - cin * flag * image) / d
        return solution, cross

    c_low, cross_low = outer(0, lo_msg, low, 0, 0)
    c_high, cross_high = outer(2, hi_msg, high, 1, 2)
    cross = scatter({k: cross_low[k] + cross_high[k] for k in cross_low})
    rhs = cin * state[1]
    d = jnp.where(cmask, state[4], 1.0)
    c_mid = state[9] + (2.0 / 3.0) * (rhs - cin * (state[7] + cross)) / d
    left = jnp.where(is_even, c_low, c_mid)
    right = jnp.where(is_even, c_mid, c_high)
    both = jnp.concatenate([left, right], axis=0)
    full = z_apply(*split(both), pz[...])
    y = lay.own_y
    mask = yz_mask(y, nz, start + offset, lay.total_y).astype(F32)
    weight = [jnp.broadcast_to(py[i], (N, nz)) for i in range(2)]
    q = []
    for side in range(2):
        rows = full[side * cr : (side + 1) * cr]
        if lay.sub > 1:
            rows = pltpu.roll(rows, cr - lax.div(offset, N), 0)
        blocks = []
        for e in range(y // N):
            at = [rows[e + i : e + i + 1] for i in range(2)]
            blocks.append(weight[0] * at[0][:, :nz] + weight[1] * at[1][:, :nz])
            for i in range(2):
                coarse[side, pl.ds(2 * e + i, 1), :] = at[i][:, nz : nz + nz // 4]
        q.append(mask * jnp.concatenate(blocks, axis=0))
    q_left, q_right = q
    first_flag = jnp.where(is_even, low, 1.0)
    last_flag = jnp.where(is_even, 1.0, high)
    for a in range(N):
        add = float(INTERP[a, 0]) * q_left + float(INTERP[a, 1]) * q_right
        if a == 0:
            add = first_flag * add
        if a == N - 1:
            add = last_flag * add
        out[a] = sec[a] + add


def run(kernel, args, outs, scratch=(), aliases={}):
    return pl.pallas_call(
        kernel,
        out_shape=[jax.ShapeDtypeStruct(o, F32) for o in outs],
        in_specs=[pl.BlockSpec(memory_space=pltpu.VMEM)] * len(args),
        out_specs=[pl.BlockSpec(memory_space=pltpu.VMEM)] * len(outs),
        scratch_shapes=[pltpu.VMEM(s, F32) for s in scratch],
        compiler_params=pltpu.CompilerParams(vmem_limit_bytes=VMEM_LIMIT),
        input_output_aliases=aliases,
        cost_estimate=pl.CostEstimate(flops=1, bytes_accessed=1, transcendentals=0),
    )(*args)


def swap_pairs(count, first):
    pairs = []
    for i in range(first, count - 1, 2):
        pairs += [(i, i + 1), (i + 1, i)]
    return pairs


def chip_pairs(dom, sub, shift):
    pairs = []
    for a, b in swap_pairs(dom, 1):
        for q in range(sub):
            to = (q + shift) % sub if sub == 2 else q + shift
            if 0 <= to < sub:
                pairs.append((a * sub + q, b * sub + to))
    for end in (0, dom - 1):
        pairs += [(end * sub + a, end * sub + b) for a, b in swap_pairs(sub, 0)]
    return pairs


def shards(dom, sub, rhs_local, coefficient):
    size_x, own_y, nz = rhs_local.shape
    assert size_x == N and dom % 2 == 0 and (sub == 1 or own_y > HALO)
    lay = Layout(own_y, nz, dom, sub)
    ny, cr = lay.ny, lay.cr
    t = {k: jnp.asarray(v) for k, v in make_tables(ny, nz, own_y).items()}
    pick = lambda *names: [t[k] for k in names]
    even = lambda v: lax.ppermute(v, "dom", swap_pairs(dom, 0))
    odd = lambda v, k=0: lax.ppermute(v, ("dom", "sub"), chip_pairs(dom, sub, k))
    block = (N, own_y, nz)
    raw = jnp.stack([rhs_local, coefficient])
    n_other = 0 if sub == 1 else 1 if sub == 2 else 2
    face, w, d, r, sx, *packs = run(
        functools.partial(own_kernel, lay),
        [raw, t["z_sq"], t["y_sq", own_y // N], t["w3"]],
        [(2, own_y, nz), block, block, block, (own_y, nz)]
        + [(PACK, nz)] * n_other,
    )
    mate_face = even(face)
    if sub == 1:
        steps = []
    elif sub == 2:
        steps = [[(0, 1), (1, 0)]]
    else:
        up = [(i, i + 1) for i in range(sub - 1)]
        steps = [up, [(b, a) for a, b in up]]
    others = [lax.ppermute(pack, "sub", step) for pack, step in zip(packs, steps)]
    mate = even(lax.optimization_barrier((raw, face))[0])
    lines = 3 * N * line_count(lay)
    msgs = run(
        functools.partial(message_kernel, lay),
        [w, d, r, sx, mate_face],
        [(5 * own_y + lines, nz)] + [(5 * HALO + lines + SPARE, nz)] * n_other,
        [block] * 3,
    )
    shifts = [0] if sub == 1 else [0, 1] if sub == 2 else [0, 1, -1]
    pieces = [odd(msg, k) for msg, k in zip(msgs, shifts)]
    pair = (2 * N, ny, nz)
    count = lay.early_rows(0)[1] // N
    arrays = run(
        functools.partial(early_kernel, lay),
        [raw, mate, t["z_sq"], t["y_sq", own_y // N], t["w3"]]
        + [t["z_d"], t["z_dt"], t["y_d", count], t["y_dt", count]],
        [pair] * ARRAYS,
        [(2 * N, count * N, nz)] * 3,
    )
    others, arrays = lax.optimization_barrier((others, arrays))
    mate_others = [even(o[a:b]) for o in others for a, b in zip(CUTS, CUTS[1:])]
    arrays = run(
        functools.partial(near_kernel, lay, n_other),
        [*others, t["z_sq"], t["y_sq", HALO // N], t["w3"], *arrays],
        [pair] * ARRAYS,
        (),
        {n_other + 3 + k: k for k in range(ARRAYS)},
    )
    pieces[0], arrays = lax.optimization_barrier((pieces[0], arrays))
    late = lambda *names: [t[k, HALO // N + 1] for k in names]
    sums = [t["z_sq"], t["y_sq", HALO // N], t["w3"]]
    w, rhs, _, _, lin, _, _, _, sec, ends = run(
        functools.partial(deep_kernel, lay, n_other),
        [*mate_others, *sums, t["z_d"], t["z_dt"], *late("y_d", "y_dt"), *arrays],
        [pair] * (ARRAYS + 1) + [(2, 2, ny, nz)],
        [(2 * N, HALO + N, nz)] * 3,
        {len(mate_others) + 7 + k: k for k in range(ARRAYS)},
    )
    later, sec = lax.optimization_barrier((pieces[1:], sec))
    pieces = pieces[:1] + later
    mate_pieces = [even(p) for p in pieces]
    g, r = run(
        functools.partial(coarse_tables_kernel, lay),
        [w, rhs] + pick("my", "mz", "ry_one", "rz_one"),
        [(2, 27, cr, nz), (4, cr, nz)],
    )
    sec, msg, state = run(
        functools.partial(second_kernel, lay, len(pieces)),
        [*pieces, *mate_pieces, w, sec, lin, ends, g, r]
        + pick("z_d", "z_dt", "y_d", "y_dt", "ry", "ry_one", "rz", "line"),
        [block, (3, cr, nz), (10, cr, nz)],
        [(2, 5, ny, nz)] + [pair] * 4,
    )
    from_odd = odd(msg)
    from_mate = even(from_odd)
    return tuple(
        run(
            functools.partial(third_kernel, lay),
            [from_odd, from_mate, sec, state, g] + pick("py", "pz"),
            [block, (size_x // 4, own_y // 4, nz // 4)],
        )
    )


def solution(mesh):
    dom, sub = mesh.shape["dom"], mesh.shape["sub"]
    return jax.shard_map(
        functools.partial(shards, dom, sub),
        mesh=mesh,
        in_specs=(P("dom", "sub", None), P("dom", "sub", None)),
        out_specs=(P("dom", "sub", None), P("dom", "sub", None)),
        check_vma=False,
    )
```

```python
import functools

import jax
import jax.numpy as jnp
import numpy as np
from jax import lax
from jax.experimental import pallas as pl
from jax.experimental.pallas import tpu as pltpu
from jax.sharding import PartitionSpec as P

N = 8
SPARE = 4 * N
PLANES = 4
HALO = 3 * N
THETA = 1.1
DELTA = 0.9
SIGMA = THETA / DELTA
RHO0 = 1.0 / SIGMA
RHO1 = 1.0 / (2.0 * SIGMA - RHO0)
LANES = 128
F32 = jnp.float32
BF16 = jnp.bfloat16
VMEM_LIMIT = 48 * 1024 * 1024


def legendre_value(points, degree):
    previous = np.ones(points.shape)
    current = points.copy()
    for level in range(1, degree):
        following = ((2 * level + 1) * points * current - level * previous) / (level + 1)
        previous = current
        current = following
    return current


def tables():
    degree = 7
    points = np.array(
        [
            -1.0,
            -0.8717401485096066,
            -0.5917001814331423,
            -0.2092992179024789,
            0.2092992179024789,
            0.5917001814331423,
            0.8717401485096066,
            1.0,
        ]
    )
    values = legendre_value(points, degree)
    weights = 2.0 / (degree * (degree + 1) * values**2)
    derivative = np.zeros((8, 8))
    for row_at in range(8):
        for col_at in range(8):
            if row_at != col_at:
                derivative[row_at, col_at] = values[row_at] / (
                    values[col_at] * (points[row_at] - points[col_at])
                )
    derivative[0, 0] = -degree * (degree + 1) / 4.0
    derivative[7, 7] = degree * (degree + 1) / 4.0
    interp = np.stack([(1.0 - points) / 2.0, (1.0 + points) / 2.0], axis=1)
    return derivative, weights, interp


DM, WEIGHTS, INTERP = tables()
MULT = np.array([2.0] + [1.0] * 6 + [2.0])
RHO = MULT[:, None] * INTERP
DRHO = DM @ RHO


def blockdiag(block, count):
    return np.kron(np.eye(count), block)


def hi_lo(matrix):
    hi = matrix.astype(jnp.bfloat16)
    lo = (matrix - hi.astype(np.float64)).astype(jnp.bfloat16)
    return hi, lo


def right_table(matrix):
    hi, lo = hi_lo(matrix)
    full = np.concatenate([np.concatenate([hi, hi]), np.concatenate([lo, 0 * lo])], axis=1)
    return np.stack(np.split(full, full.shape[1] // LANES, axis=1))


def left_table(matrix):
    hi, lo = hi_lo(matrix)
    return np.concatenate([hi, hi, lo], axis=1).astype(np.float32)


def vertex_table(per_node, elements, columns, count=8):
    out = np.zeros((count * elements, columns))
    for e in range(elements):
        for i in range(2):
            out[count * e : count * (e + 1), e + i] += per_node[:, i]
    return out


def moment_table(per_node, elements, columns):
    out = np.zeros((8 * elements, columns))
    for e in range(elements):
        out[8 * e : 8 * e + 8, e] = per_node
    return out


PAIRS = [(0, 0), (0, 1), (1, 1)]
MASS = [INTERP[:, i] * INTERP[:, j] for i, j in PAIRS]


def round_up(value, to):
    return -(-value // to) * to


def make_tables(ny, nz, own_y):
    ey, ez = ny // N, nz // N
    cr = round_up(ey + 1, 8)
    t = {}
    t["z_d"] = right_table(blockdiag(DM, ez).T)
    t["z_dt"] = right_table(blockdiag(DM, ez))
    t["z_sq"] = right_table(blockdiag(DM * DM, ez))
    t["y_d"] = left_table(blockdiag(DM, ey))
    t["y_dt"] = left_table(blockdiag(DM, ey).T)
    for count in [*range(1, own_y // N + 1), ey]:
        t["y_sq", count] = left_table(blockdiag(DM * DM, count).T)
        t["y_d", count] = left_table(blockdiag(DM, count))
        t["y_dt", count] = left_table(blockdiag(DM, count).T)
    py = vertex_table(RHO, ey, cr)
    dpy = blockdiag(DM, ey) @ py
    pz = vertex_table(RHO, ez, nz)
    dpz = blockdiag(DM, ez) @ pz
    zero = np.zeros_like(py)
    ry = np.concatenate([np.concatenate([py, dpy, zero]), np.concatenate([zero, zero, py])], axis=1)
    t["ry"] = np.concatenate(hi_lo(ry.T), axis=0).astype(np.float32)
    t["ry_one"] = left_table(py.T)
    t["rz"] = right_table(np.concatenate([pz, dpz], axis=0))
    t["rz_one"] = right_table(pz)
    t["my"] = left_table(np.concatenate([moment_table(m, ey, cr) for m in MASS], axis=1).T)
    t["mz"] = right_table(np.concatenate([moment_table(m, ez, nz) for m in MASS], axis=1))
    t["py"] = np.broadcast_to(INTERP.T[:, :, None], (2, N, nz)).astype(np.float32)
    pz = vertex_table(INTERP, ez, nz).T
    sz = vertex_table(np.eye(2), ez, nz, 2).T
    t["pz"] = right_table(np.concatenate([pz, sz], axis=1))
    cols = np.concatenate([DM.T, DM.T[[N - 1]], DM.T[[0]]], axis=0)
    t["line"] = np.broadcast_to(cols[:, :, None], (N + 2, N, nz)).astype(np.float32)
    w3 = WEIGHTS[:, None, None] * WEIGHTS[None, :, None] * np.ones((1, 1, nz))
    t["w3"] = (w3 * np.tile(WEIGHTS, ez)[None, None, :]).astype(np.float32)
    return t


def even_odd(matrix, values, sign):
    even = [values[b] + values[7 - b] for b in range(4)]
    odd = [values[b] - values[7 - b] for b in range(4)]
    out = [None] * 8
    for a in range(4):
        pe = po = None
        for b in range(4):
            ce = float((matrix[a, b] + matrix[a, 7 - b]) / 2.0)
            co = float((matrix[a, b] - matrix[a, 7 - b]) / 2.0)
            te = ce * even[b]
            to = co * odd[b]
            pe = te if pe is None else pe + te
            po = to if po is None else po + to
        out[a] = pe + po
        out[7 - a] = pe - po if sign > 0 else po - pe
    return out


def split(x):
    hi = x.astype(BF16)
    lo = (x - hi.astype(F32)).astype(BF16)
    return hi, lo


def dot(a, b):
    return jnp.dot(a, b, preferred_element_type=F32)


def z_apply(hi, lo, table):
    table = jnp.concatenate([table[k] for k in range(table.shape[0])], axis=1)
    both = dot(jnp.concatenate([hi, lo], axis=1), table)
    half = both.shape[1] // 2
    return both[:, :half] + both[:, half:]


def y_apply(x, table):
    hi = x.astype(BF16).astype(F32)
    parts = jnp.concatenate([hi, x - hi, hi], axis=0).astype(BF16)
    return dot(table.astype(BF16), parts)


def y_planes(get, planes, table):
    table = table.astype(BF16)
    out = {}
    for p, q in zip(planes[::2], planes[1::2]):
        both = y_apply(jnp.concatenate([get(p), get(q)], axis=1), table)
        nz = both.shape[1] // 2
        out[p], out[q] = both[:, :nz], both[:, nz:]
    return out


def assemble_yz(v):
    ny, nz = v.shape
    row = lax.broadcasted_iota(jnp.int32, (N, nz), 0)
    lane = lax.broadcasted_iota(jnp.int32, (ny, nz), 1)
    is_top = row == 0
    flip = (N - 1) - row
    blocks = [v[N * e : N * e + N] for e in range(ny // N)]
    top = (row == N - 1).astype(F32)
    bottom = (row == 0).astype(F32)
    out = []
    for e, b in enumerate(blocks):
        if len(blocks) == 1:
            out.append(b)
            continue
        if e == 0:
            near, mask = blocks[1], top
        elif e + 1 == len(blocks):
            near, mask = blocks[e - 1], bottom
        else:
            near, mask = jnp.where(is_top, blocks[e + 1], blocks[e - 1]), top + bottom
        out.append(b + mask * jnp.take_along_axis(near, flip, axis=0))
    v = jnp.concatenate(out, axis=0)
    last = (lane % N == N - 1) & (lane < nz - 1)
    first = (lane % N == 0) & (lane > 0)
    other = lane + jnp.where(last, 1, 0) - jnp.where(first, 1, 0)
    mask = (last | first).astype(F32)
    return v + mask * jnp.take_along_axis(v, other, axis=1)


def yz_mask(ny, nz, start, total):
    row = lax.broadcasted_iota(jnp.int32, (ny, nz), 0) + start
    lane = lax.broadcasted_iota(jnp.int32, (ny, nz), 1)
    return (row > 0) & (row < total - 1) & (lane > 0) & (lane < nz - 1)


class Layout:
    def __init__(self, own_y, nz, dom, sub):
        self.own_y, self.nz, self.dom, self.sub = own_y, nz, dom, sub
        self.blocks = min(sub, 3)
        self.ny = own_y + HALO * (self.blocks - 1)
        self.total_y = own_y * sub
        self.ey, self.ez = self.ny // N, nz // N
        self.cr = round_up(self.ey + 1, 8)

    def where(self):
        d = lax.axis_index("dom")
        h = lax.axis_index("sub")
        parity = lax.rem(d, 2)
        pair = lax.div(d, 2)
        if self.sub == 1:
            start, offset = 0, 0
        elif self.sub == 2:
            start, offset = h * (self.own_y - HALO), h * HALO
        else:
            start, offset = h * self.own_y - HALO, HALO
        low = (pair > 0).astype(F32)
        high = (pair < self.dom // 2 - 1).astype(F32)
        return parity, h, start, offset, low, high

    def sent_rows(self, h):
        y = self.own_y
        down = (y - HALO, y - HALO)
        up = (0, HALO - 1)
        if self.sub == 1:
            return []
        if self.sub == 2:
            return [tuple(h * u + (1 - h) * v for u, v in zip(up, down))]
        return [down, up]

    def far_rows(self, h):
        if self.sub == 1:
            return []
        if self.sub == 2:
            return [(1 - h) * (self.ny - 1)]
        return [0, self.ny - 1]

    def other_starts(self, h):
        if self.sub == 1:
            return []
        if self.sub == 2:
            return [(1 - h) * self.own_y]
        return [0, HALO + self.own_y]

    def early_rows(self, h):
        if self.sub == 1:
            return 0, self.own_y
        if self.sub == 2:
            return h * (HALO + N), self.own_y - N
        return HALO + N, self.own_y - 2 * N

    def late_starts(self, h):
        if self.sub == 1:
            return []
        if self.sub == 2:
            return [(1 - h) * (self.own_y - N)]
        return [0, self.own_y + HALO - N]

    def interfaces(self, h):
        if self.sub == 1:
            return []
        if self.sub == 2:
            return [self.own_y - h * (self.own_y - HALO)]
        return [HALO, HALO + self.own_y]


def aligned(start, size):
    return pl.ds(start if isinstance(start, int) else pl.multiple_of(start, N), size)


def gather_window(lay, own, others, h, store):
    y = lay.own_y
    if lay.sub == 1:
        store(pl.ds(0, y), own)
    elif lay.sub == 2:
        store(aligned(h * HALO, y), own)
        store(aligned((1 - h) * y, HALO), others[0])
    else:
        store(pl.ds(0, HALO), others[0])
        store(pl.ds(HALO, y), own)
        store(pl.ds(HALO + y, HALO), others[1])


PACK = 2 * N + 2 * N * HALO
CUTS = [0, 2 * N + 5 * HALO, 2 * N + 10 * HALO, PACK]


def pack_rows(side, a):
    return pl.ds(2 * N + (side * N + a) * HALO, HALO)


class Pieces:
    def __init__(self, refs):
        self.refs = refs

    def __getitem__(self, rows):
        if len(self.refs) == 1:
            return self.refs[0][rows, :]
        k = max(i for i in range(len(self.refs)) if CUTS[i] <= rows.start)
        return self.refs[k][pl.ds(rows.start - CUTS[k], rows.size), :]


def line_rows(lay, h):
    if lay.sub == 1:
        return []
    if lay.sub == 2:
        return [(lay.own_y - 1) * (1 - h)]
    return [0, lay.own_y - 1]


def line_count(lay):
    return 0 if lay.sub == 1 else 1 if lay.sub == 2 else 2


def own_kernel(lay, raw, z_sq, y_sq, w3, face, w_out, d_out, r_out, *packs):
    rhs, coef = raw.at[0], raw.at[1]
    y, nz = lay.own_y, lay.nz
    parity, h = lay.where()[:2]
    table3 = w3[...]
    for e in range(y // N):
        rows = pl.ds(N * e, N)
        w = [coef[a, rows, :] * table3[a] for a in range(N)]
        dx = even_odd((DM * DM).T, w, 1)
        for a in range(N):
            w_out[a, rows, :] = w[a]
            d_out[a, rows, :] = dx[a]
    hi, lo = split(w_out[...].reshape(N * y, nz))
    dz = z_apply(hi, lo, z_sq[...])
    dy = y_planes(lambda a: w_out[a], list(range(N)), y_sq[...])
    for a in range(N):
        d_out[a] = assemble_yz(d_out[a] + dz[a * y : (a + 1) * y] + dy[a])
        r_out[a] = assemble_yz(rhs[a])
    inner = (N - 1) * (1 - parity)
    face[0] = r_out[inner]
    face[1] = d_out[inner]
    for pack, (first, far) in zip(packs, lay.sent_rows(h)):
        for side, field in ((0, r_out), (1, d_out)):
            for a in range(N):
                pack[pack_rows(side, a), :] = raw[side, a, aligned(first, HALO), :]
                pack[pl.ds(side * N + a, 1), :] = field[a, pl.ds(far, 1), :]


def message_kernel(lay, w, d, r, face, *refs):
    msg, *side_msgs, u_s, d_s, r_s = refs
    y, nz = lay.own_y, lay.nz
    parity, h, start, offset, low, high = lay.where()
    mask = yz_mask(y, nz, h * y, lay.total_y)
    scale = mask.astype(F32) * (1.0 / THETA)
    odd = parity.astype(F32)
    for a in range(N):
        dd, rr = d[a], r[a]
        keep = scale
        if a in (0, N - 1):
            inner = odd if a == 0 else 1.0 - odd
            dd = dd + inner * face[1]
            rr = rr + inner * face[0]
            keep = scale * inner
        d_s[a] = dd
        r_s[a] = rr
        u_s[a] = keep * rr / jnp.where(mask, dd, 1.0)
    col = [jnp.where(parity == 0, float(DM[a, 0]), float(DM[a, N - 1])) for a in range(N)]
    acc = []
    for e in range(y // N):
        rows = pl.ds(N * e, N)
        g = even_odd(DM, [u_s[a, rows, :] for a in range(N)], -1)
        total = None
        for a in range(N):
            term = (w[a, rows, :] * g[a]) * col[a]
            total = term if total is None else total + term
        acc.append(total)
    outer = (N - 1) * parity
    msg[pl.ds(0, y), :] = r[outer]
    msg[pl.ds(y, y), :] = d[outer]
    msg[pl.ds(2 * y, y), :] = w[outer]
    msg[pl.ds(3 * y, y), :] = assemble_yz(jnp.concatenate(acc, axis=0))
    base = PLANES * y
    for row in line_rows(lay, h):
        for field in (r_s, d_s, w):
            for a in range(N):
                msg[pl.ds(base + a, 1), :] = field[a, pl.ds(row, 1), :]
            base += N
    for out, (first, _) in zip(side_msgs, lay.sent_rows(h)):
        for k in range(PLANES):
            out[pl.ds(k * HALO, HALO), :] = msg[aligned(k * y + first, HALO), :]
        lines = base - PLANES * y
        out[pl.ds(PLANES * HALO, lines), :] = msg[pl.ds(PLANES * y, lines), :]
        out[pl.ds(PLANES * HALO + lines, SPARE), :] = jnp.zeros((SPARE, nz), F32)


def flux_x(lay, u_ref, w_ref, first, count, fx):
    for el in range(2):
        for e in range(count // N):
            rows, to = aligned(first + N * e, N), pl.ds(N * e, N)
            u = [u_ref[N * el + a, rows, :] for a in range(N)]
            g = even_odd(DM, u, -1)
            for a in range(N):
                fx[N * el + a, to, :] = w_ref[N * el + a, rows, :] * g[a]


def flux_yz(lay, u_ref, w_ref, planes, first, count, z_d, y_d, fy, fz):
    part, to = aligned(first, count), pl.ds(0, count)
    u = jnp.concatenate([u_ref[p, part, :] for p in planes], axis=0)
    gz = z_apply(*split(u), z_d[...])
    gy = y_planes(lambda p: u_ref[p, part, :], planes, y_d[...])
    for k, p in enumerate(planes):
        w = w_ref[p, part, :]
        fy[p, to, :] = w * gy[p]
        fz[p, to, :] = w * gz[k * count : (k + 1) * count]


def operate(lay, u_ref, w_ref, back, first, count, tables, fx, fy, fz):
    z_d, z_dt, y_d, y_dt = tables
    nz = lay.nz
    middle = list(range(1, 2 * N - 1))
    flux_x(lay, u_ref, w_ref, first, count, fx)
    flux_yz(lay, u_ref, w_ref, middle, first, count, z_d, y_d, fy, fz)
    to, part = pl.ds(0, count), aligned(first, count)
    for el in range(2):
        for e in range(count // N):
            rows, here = aligned(first + N * e, N), pl.ds(N * e, N)
            b = even_odd(DM.T, [fx[N * el + a, here, :] for a in range(N)], -1)
            for a in range(N):
                back[N * el + a, rows, :] = b[a]
    n = len(middle)
    bz = z_apply(*split(fz[pl.ds(1, n), to, :].reshape(n * count, nz)), z_dt[...])
    by = y_planes(lambda p: fy[p, to, :], middle, y_dt[...])
    for p in middle:
        back[p, part, :] = back[p, part, :] + by[p] + bz[(p - 1) * count : p * count]


def smooth_start(lay, d, r, inv, u, first, count, start):
    part = aligned(first, count)
    mask = yz_mask(count, lay.nz, start + first, lay.total_y)
    inside = mask.astype(F32)
    zero = jnp.zeros((count, lay.nz), F32)
    for p in range(2 * N):
        if p in (0, 2 * N - 1):
            u[p, part, :] = zero
        else:
            i = inside / jnp.where(mask, d[p, part, :], 1.0)
            inv[p, part, :] = i
            u[p, part, :] = i * r[p, part, :] * (1.0 / THETA)


def sum_middle(fields, first, count):
    part = aligned(first, count)
    for s in fields:
        both = s[N - 1, part, :] + s[N, part, :]
        s[N - 1, part, :] = both
        s[N, part, :] = both


def element_sums(lay, base, parity, first, count, source, tables, outs):
    z_sq, y_sq, w3 = tables
    w_out, rhs_out, d_s, r_s, lin = outs[:5]
    nz = lay.nz
    part = aligned(first, count)
    for side, target in ((0, rhs_out), (1, w_out)):
        for a in range(N):
            target[base + a, part, :] = source(side, a)
    table3 = w3[...]
    outer = [jnp.where(parity == 0, float(DM[a, 0]), float(DM[a, N - 1])) for a in range(N)]
    for e in range(count // N):
        rows = aligned(first + N * e, N)
        w = [w_out[base + a, rows, :] * table3[a] for a in range(N)]
        dx = even_odd((DM * DM).T, w, 1)
        cx = even_odd(DM.T, [outer[a] * w[a] for a in range(N)], -1)
        for a in range(N):
            w_out[base + a, rows, :] = w[a]
            d_s[base + a, rows, :] = dx[a]
            lin[base + a, rows, :] = cx[a]
    dz = z_apply(*split(w_out[pl.ds(base, N), part, :].reshape(N * count, nz)), z_sq[...])
    dy = y_planes(lambda a: w_out[base + a, part, :], list(range(N)), y_sq[...])
    for a in range(N):
        d_local = d_s[base + a, part, :] + dz[a * count : (a + 1) * count] + dy[a]
        d_s[base + a, part, :] = assemble_yz(d_local)
        r_s[base + a, part, :] = assemble_yz(rhs_out[base + a, part, :])
        lin[base + a, part, :] = assemble_yz(lin[base + a, part, :])


def other_sums(lay, base, parity, h, pieces, tables, outs):
    d_s, r_s = outs[2:4]
    for piece, first, row in zip(pieces, lay.other_starts(h), lay.far_rows(h)):
        source = lambda side, a, piece=piece: piece[pack_rows(side, a)]
        element_sums(lay, base, parity, first, HALO, source, tables, outs)
        for side, target in ((0, r_s), (1, d_s)):
            for a in range(N):
                target[base + a, pl.ds(row, 1), :] = piece[pl.ds(side * N + a, 1)]


ARRAYS = 8


def early_kernel(lay, own, *refs):
    mate, refs = refs[:2], refs[2:]
    z_sq, y_sq, w3 = refs[:3]
    tables, outs, scratch = refs[3:7], refs[7 : 7 + ARRAYS], refs[7 + ARRAYS :]
    w, _, d, r, _, inv, u, back = outs
    parity, h, start, offset, low, high = lay.where()
    own = (own.at[0], own.at[1])
    for base, el, block in ((parity * N, parity, own), ((1 - parity) * N, 1 - parity, mate)):
        source = lambda side, a, block=block: block[side][a]
        element_sums(lay, base, el, offset, lay.own_y, source, (z_sq, y_sq, w3), outs)
    sum_middle((d, r), offset, lay.own_y)
    smooth_start(lay, d, r, inv, u, offset, lay.own_y, start)
    first, count = lay.early_rows(h)
    operate(lay, u, w, back, first, count, tables, *scratch)


def near_kernel(lay, n_other, *refs):
    other, tables = refs[:n_other], refs[n_other : n_other + 3]
    outs = refs[n_other + 3 + ARRAYS :]
    parity, h = lay.where()[:2]
    other_sums(lay, parity * N, parity, h, [Pieces([o]) for o in other], tables, outs)


def deep_kernel(lay, n_other, *refs):
    cuts = len(CUTS) - 1
    mate_other = [Pieces(refs[cuts * k : cuts * (k + 1)]) for k in range(n_other)]
    refs = refs[cuts * n_other :]
    z_sq, y_sq, w3 = refs[:3]
    tables = refs[3:7]
    refs = refs[7 + ARRAYS :]
    outs, sec_out, ends = refs[:ARRAYS], refs[ARRAYS], refs[ARRAYS + 1]
    scratch = refs[ARRAYS + 2 :]
    w, _, d, r, lin, inv, u, back = outs
    last = 2 * N - 1
    parity, h, start, offset, low, high = lay.where()
    other_sums(lay, (1 - parity) * N, 1 - parity, h, mate_other, (z_sq, y_sq, w3), outs)
    for first in lay.other_starts(h):
        sum_middle((d, r), first, HALO)
    for begin in lay.interfaces(h):
        above, below = pl.ds(begin - 1, 1), pl.ds(begin, 1)
        for s in (d, r, lin):
            for p in range(2 * N):
                both = s[p, above, :] + s[p, below, :]
                s[p, above, :] = both
                s[p, below, :] = both
    for side, p in ((0, 0), (1, last)):
        ends[side, 0] = r[p]
        ends[side, 1] = d[p]
    for first in lay.late_starts(h):
        smooth_start(lay, d, r, inv, u, first, HALO + N, start)
        operate(lay, u, w, back, first, HALO + N, tables, *scratch)
    for p in range(1, last):
        back[p] = assemble_yz(back[p])
    sum_middle((back,), 0, lay.ny)
    for p in range(2 * N):
        if p in (0, last):
            sec_out[p] = assemble_yz(back[p])
        else:
            i = (2.0 * RHO1 / DELTA) * inv[p]
            lin[p] = -i * lin[p]
            sec_out[p] = (1.0 + RHO1 * RHO0) * u[p] + i * (r[p] - back[p])


def coarse_tables_kernel(lay, w_ref, rhs_ref, my, mz, ry, rz, g_out, r_out):
    ny, nz, cr = lay.ny, lay.nz, lay.cr
    lhs = []
    for el in range(2):
        for m in MASS:
            total = None
            for a in range(N):
                term = float(m[a]) * w_ref[N * el + a]
                total = term if total is None else total + term
            lhs.append(total)
    along_z = z_apply(*split(jnp.concatenate(lhs, axis=0)), mz[...])
    for el in range(2):
        mom = {}
        for alpha in range(3):
            at = (3 * el + alpha) * ny
            block = y_apply(along_z[at : at + ny], my[...])
            for beta in range(3):
                for gamma in range(3):
                    mom[alpha, beta, gamma] = block[
                        beta * cr : (beta + 1) * cr, gamma * nz : (gamma + 1) * nz
                    ]
        x_sum, y_sum, z_sum = {}, {}, {}
        for i in range(3):
            for j in range(3):
                x_sum[i, j] = mom[0, i, j] + 2.0 * mom[1, i, j] + mom[2, i, j]
                y_sum[i, j] = mom[i, 0, j] + 2.0 * mom[i, 1, j] + mom[i, 2, j]
                z_sum[i, j] = mom[i, j, 0] + 2.0 * mom[i, j, 1] + mom[i, j, 2]
        sign = (1.0, -1.0, 1.0)
        for alpha in range(3):
            for beta in range(3):
                for gamma in range(3):
                    g_out[el, 9 * alpha + 3 * beta + gamma] = 0.25 * (
                        sign[alpha] * x_sum[beta, gamma]
                        + sign[beta] * y_sum[alpha, gamma]
                        + sign[gamma] * z_sum[alpha, beta]
                    )
    sums = []
    for el in range(2):
        for i in range(2):
            total = None
            for a in range(N):
                term = float(RHO[a, i]) * rhs_ref[N * el + a]
                total = term if total is None else total + term
            sums.append(total)
    part = y_apply(jnp.concatenate(sums, axis=1), ry[...])
    rows = jnp.concatenate([part[:, k * nz : (k + 1) * nz] for k in range(4)], axis=0)
    full = z_apply(*split(rows), rz[...])
    for k in range(4):
        r_out[k] = full[k * cr : (k + 1) * cr]


def pair_index(i, j):
    return i + j


def shifted(c, q, r):
    if q:
        c = pltpu.roll(c, c.shape[0] - 1, 0)
    if r:
        c = pltpu.roll(c, c.shape[1] - 1, 1)
    return c


def scatter(parts):
    cr, nz = parts[0, 0].shape
    first = parts[0, 0] + pltpu.roll(parts[0, 1], 1, 1)
    second = parts[1, 0] + pltpu.roll(parts[1, 1], 1, 1)
    return first + pltpu.roll(second, 1, 0)


def gathered(c):
    return {(q, r): shifted(c, q, r) for q in range(2) for r in range(2)}


def face_apply(entry, c, out=None):
    out = {} if out is None else out
    for j in range(2):
        for k in range(2):
            for q in range(2):
                for r in range(2):
                    term = entry(pair_index(j, q), pair_index(k, r)) * c[q, r]
                    out[j, k] = term if (j, k) not in out else out[j, k] + term
    return out


def coarse_diag(entry):
    return scatter({(j, k): entry(2 * j, 2 * k) for j in range(2) for k in range(2)})


def coarse_mask(lay, start):
    row = lax.broadcasted_iota(jnp.int32, (lay.cr, lay.nz), 0) + lax.div(start, N)
    lane = lax.broadcasted_iota(jnp.int32, (lay.cr, lay.nz), 1)
    return (row > 0) & (row < lay.total_y // N) & (lane > 0) & (lane < lay.ez)


def unpack_sides(lay, pieces, mate_pieces, line, parity, h, start, win):
    y, nz = lay.own_y, lay.nz
    for side, group in ((parity, pieces), (1 - parity, mate_pieces)):
        for k in range(PLANES):

            def put(rows, value):
                win[side, k, rows, :] = value

            others = [g[pl.ds(k * HALO, HALO), :] for g in group[1:]]
            gather_window(lay, group[0][pl.ds(k * y, y), :], others, h, put)
    is_even = parity == 0
    lane = lax.broadcasted_iota(jnp.int32, (N, nz), 1)
    node = lax.broadcasted_iota(jnp.int32, (N, nz), 0)
    lane_in = (lane > 0) & (lane < nz - 1)
    flank = lax.broadcasted_iota(jnp.int32, (1, nz), 1)
    last = ((flank % N == N - 1) & (flank < nz - 1)).astype(F32)
    first = ((flank % N == 0) & (flank > 0)).astype(F32)
    for b, begin in enumerate(lay.interfaces(h), 1):
        above, below = pl.ds(begin - 1, 1), pl.ds(begin, 1)
        for side in range(2):
            for k in range(2):
                both = win[side, k, above, :] + win[side, k, below, :]
                win[side, k, above, :] = both
                win[side, k, below, :] = both
        for side in range(2):
            outer = N - 1 if side == 0 else 0

            def field(k):
                def of(group):
                    own_lines, other_lines = PLANES * y + k * N, PLANES * HALO + k * N
                    if lay.sub == 2:
                        mine, theirs = own_lines, other_lines
                        near = group[1]
                    else:
                        mine = own_lines + 3 * N * (b - 1)
                        theirs = other_lines + 3 * N * (2 - b)
                        near = group[b]
                    return group[0][pl.ds(mine, N), :] + near[pl.ds(theirs, N), :]
                mine, theirs = of(pieces), of(mate_pieces)
                if side == 0:
                    return jnp.where(is_even, mine, theirs)
                return jnp.where(is_even, theirs, mine)

            r, d, w = field(0), field(1), field(2)
            row = start + begin
            ok = lane_in & (node != outer) & (row > 0) & (row < lay.total_y)
            u = jnp.where(ok, r / jnp.where(ok, d, 1.0) * (1.0 / THETA), 0.0)
            g = None
            for a in range(N):
                term = line[a] * u[a : a + 1]
                g = term if g is None else g + term
            total = jnp.sum(line[N + side] * (w * g), axis=0, keepdims=True)
            total = total + last * pltpu.roll(total, nz - 1, 1) + first * pltpu.roll(total, 1, 1)
            win[side, 3, above, :] = total
            win[side, 3, below, :] = total


def second_kernel(lay, n_pieces, *refs):
    pieces, mate_pieces = refs[:n_pieces], refs[n_pieces : 2 * n_pieces]
    w_ref, sec_in, lin_in, ends, g_ref, r_ref = refs[2 * n_pieces : 2 * n_pieces + 6]
    refs = refs[2 * n_pieces + 6 :]
    z_d, z_dt, z_sq, y_d, y_dt, y_sq, ry, rz, line = refs[:9]
    out, msg, state = refs[9:12]
    win, sec, fx, fy, fz = refs[12:]
    ny, nz, cr = lay.ny, lay.nz, lay.cr
    last = 2 * N - 1
    parity, h, start, offset, low, high = lay.where()
    mask = yz_mask(ny, nz, start, lay.total_y)
    inside = mask.astype(F32)
    is_even = parity == 0
    unpack_sides(lay, pieces, mate_pieces, line, parity, h, start, win)
    flags = (low, high)
    inv, res, u = [], [], []
    for side in range(2):
        valid = inside * flags[side]
        inv.append(valid / jnp.where(mask, ends[side, 1] + win[side, 1], 1.0))
        res.append(valid * (ends[side, 0] + win[side, 0]))
        u.append(inv[side] * res[side] * (1.0 / THETA))
    for p in range(1, last):
        value = sec_in[p]
        if p <= N:
            value = value + lin_in[min(p, N - 1)] * u[0]
        if p >= N - 1:
            value = value + lin_in[max(p, N)] * u[1]
        sec[p] = value
    flux_yz(lay, sec, w_ref, list(range(1, last)), 0, ny, z_d, y_d, fy, fz)
    weights = [w_ref[0] + win[0, 2], w_ref[last] + win[1, 2]]
    hi, lo = split(jnp.concatenate(u, axis=0))
    gz = z_apply(hi, lo, z_d[...])
    gy = y_apply(jnp.concatenate(u, axis=1), y_d[...])
    weight_z = jnp.concatenate(weights, axis=0)
    weight_y = jnp.concatenate(weights, axis=1)
    bz = z_apply(*split(weight_z * gz), z_dt[...])
    by = y_apply(weight_y * gy, y_dt[...])
    dz = z_apply(*split(jnp.concatenate([win[0, 2], win[1, 2]], axis=0)), z_sq[...])
    dy = y_planes(lambda side: win[side, 2], [0, 1], y_sq[...])
    dx = [
        win[side, 1] - assemble_yz(dz[side * ny : (side + 1) * ny] + dy[side]) for side in range(2)
    ]
    for side, p in ((0, 0), (1, last)):
        plane = assemble_yz(bz[side * ny : (side + 1) * ny] + by[:, side * nz : (side + 1) * nz])
        plane = plane + sec_in[p] + win[side, 3] + (lin_in[p] + dx[side]) * u[side]
        res_one = res[side] - inside * plane
        sec[p] = (1.0 + RHO1 * RHO0) * u[side] + (2.0 * RHO1 / DELTA) * inv[side] * res_one
    out[...] = sec[pl.ds(parity * N, N), pl.ds(pl.multiple_of(offset, N), lay.own_y), :]
    flux_yz(lay, sec, w_ref, [0, last], 0, ny, z_d, y_d, fy, fz)
    flux_x(lay, sec, w_ref, 0, ny, fx)
    sums = []
    for f, weight in ((fx, DRHO), (fy, RHO), (fz, RHO)):
        lanes = []
        for el in range(2):
            for i in range(2):
                total = None
                for a in range(N):
                    term = float(weight[a, i]) * f[N * el + a]
                    total = term if total is None else total + term
                lanes.append(total)
        sums.append(jnp.concatenate(lanes, axis=1))
    data = jnp.concatenate(sums, axis=0)
    hi = data.astype(BF16).astype(F32)
    parts = jnp.concatenate([hi, data - hi], axis=1).astype(BF16)
    both = dot(ry[...].astype(BF16), parts)
    both = both[: 2 * cr, : 4 * nz] + both[2 * cr :, : 4 * nz] + both[: 2 * cr, 4 * nz :]
    rows = [
        jnp.concatenate([v[:, k * nz : (k + 1) * nz] for v in (both[:cr], both[cr:])], axis=1)
        for k in range(4)
    ]
    full = z_apply(*split(jnp.concatenate(rows, axis=0)), rz[...])
    r = {}
    for el in range(2):
        for i in range(2):
            k = 2 * el + i
            r[el, i] = r_ref[k] - full[k * cr : (k + 1) * cr]
    planes = [r[0, 0], r[0, 1] + r[1, 0], r[1, 1]]
    cmask = coarse_mask(lay, start)

    def entry(el, alpha):
        return lambda beta, gamma: g_ref[el, 9 * alpha + 3 * beta + gamma]

    d = [
        coarse_diag(entry(0, 0)),
        coarse_diag(entry(0, 2)) + coarse_diag(entry(1, 0)),
        coarse_diag(entry(1, 2)),
    ]
    cin = cmask.astype(F32)
    mid = (2.0 / 3.0) * cin * planes[1] / jnp.where(cmask, d[1], 1.0)
    c = gathered(mid)
    g_low = scatter(face_apply(entry(0, 1), c))
    g_high = scatter(face_apply(entry(1, 1), c))
    g_mid = scatter(face_apply(entry(1, 0), c, face_apply(entry(0, 2), c)))
    state[0] = planes[0]
    state[1] = planes[1]
    state[2] = planes[2]
    state[3] = d[0]
    state[4] = d[1]
    state[5] = d[2]
    state[6] = g_low
    state[7] = g_mid
    state[8] = g_high
    state[9] = mid
    send = [
        jnp.where(is_even, planes[0], planes[2]),
        jnp.where(is_even, d[0], d[2]),
        jnp.where(is_even, g_low, g_high),
    ]
    send += [jnp.where(is_even, g_ref[0, k], g_ref[1, 18 + k]) for k in range(9)]
    for k in range(3):
        packed = send[4 * k]
        for q in range(1, 4):
            packed = packed + pltpu.roll(send[4 * k + q], q * (nz // 4), 1)
        msg[k] = packed


def third_kernel(lay, *refs):
    own_msg, mate_msg, sec, state, g_ref, py, pz, out, coarse = refs
    ny, nz, cr = lay.ny, lay.nz, lay.cr
    parity, h, start, offset, low, high = lay.where()
    is_even = parity == 0
    cmask = coarse_mask(lay, start)
    cin = cmask.astype(F32)
    lo_msg, hi_msg = [], []
    for k in range(3):
        mine, theirs = own_msg[k], mate_msg[k]
        for target, packed in (
            (lo_msg, jnp.where(is_even, mine, theirs)),
            (hi_msg, jnp.where(is_even, theirs, mine)),
        ):
            target.append(packed)
            for q in range(1, 4):
                target.append(pltpu.roll(packed, nz - q * (nz // 4), 1))

    def entry(el, alpha):
        return lambda beta, gamma: g_ref[el, 9 * alpha + 3 * beta + gamma]

    def outer(at, m, flag, el, alpha):
        rhs = cin * flag * (state[at] + m[0])
        d = jnp.where(cmask, state[3 + at] + m[1], 1.0)
        one = (2.0 / 3.0) * rhs / d
        c = gathered(one)
        here = lambda beta, gamma: g_ref[el, 9 * alpha + 3 * beta + gamma] + m[3 + 3 * beta + gamma]
        image = scatter(face_apply(here, c)) + state[6 + at] + m[2]
        cross = face_apply(entry(el, 1), c)
        solution = one + (2.0 / 3.0) * (rhs - cin * flag * image) / d
        return solution, cross

    c_low, cross_low = outer(0, lo_msg, low, 0, 0)
    c_high, cross_high = outer(2, hi_msg, high, 1, 2)
    cross = scatter({k: cross_low[k] + cross_high[k] for k in cross_low})
    rhs = cin * state[1]
    d = jnp.where(cmask, state[4], 1.0)
    c_mid = state[9] + (2.0 / 3.0) * (rhs - cin * (state[7] + cross)) / d
    left = jnp.where(is_even, c_low, c_mid)
    right = jnp.where(is_even, c_mid, c_high)
    both = jnp.concatenate([left, right], axis=0)
    full = z_apply(*split(both), pz[...])
    y = lay.own_y
    mask = yz_mask(y, nz, start + offset, lay.total_y).astype(F32)
    weight = [jnp.broadcast_to(py[i], (N, nz)) for i in range(2)]
    q = []
    for side in range(2):
        rows = full[side * cr : (side + 1) * cr]
        if lay.sub > 1:
            rows = pltpu.roll(rows, cr - lax.div(offset, N), 0)
        blocks = []
        for e in range(y // N):
            at = [rows[e + i : e + i + 1] for i in range(2)]
            blocks.append(weight[0] * at[0][:, :nz] + weight[1] * at[1][:, :nz])
            for i in range(2):
                coarse[side, pl.ds(2 * e + i, 1), :] = at[i][:, nz : nz + nz // 4]
        q.append(mask * jnp.concatenate(blocks, axis=0))
    q_left, q_right = q
    first_flag = jnp.where(is_even, low, 1.0)
    last_flag = jnp.where(is_even, 1.0, high)
    for a in range(N):
        add = float(INTERP[a, 0]) * q_left + float(INTERP[a, 1]) * q_right
        if a == 0:
            add = first_flag * add
        if a == N - 1:
            add = last_flag * add
        out[a] = sec[a] + add


def run(kernel, args, outs, scratch=(), aliases={}):
    return pl.pallas_call(
        kernel,
        out_shape=[jax.ShapeDtypeStruct(o, F32) for o in outs],
        in_specs=[pl.BlockSpec(memory_space=pltpu.VMEM)] * len(args),
        out_specs=[pl.BlockSpec(memory_space=pltpu.VMEM)] * len(outs),
        scratch_shapes=[pltpu.VMEM(s, F32) for s in scratch],
        compiler_params=pltpu.CompilerParams(vmem_limit_bytes=VMEM_LIMIT),
        input_output_aliases=aliases,
        cost_estimate=pl.CostEstimate(flops=1, bytes_accessed=1, transcendentals=0),
    )(*args)


def swap_pairs(count, first):
    pairs = []
    for i in range(first, count - 1, 2):
        pairs += [(i, i + 1), (i + 1, i)]
    return pairs


def chip_pairs(dom, sub, shift):
    pairs = []
    for a, b in swap_pairs(dom, 1):
        for q in range(sub):
            to = (q + shift) % sub if sub == 2 else q + shift
            if 0 <= to < sub:
                pairs.append((a * sub + q, b * sub + to))
    for end in (0, dom - 1):
        pairs += [(end * sub + a, end * sub + b) for a, b in swap_pairs(sub, 0)]
    return pairs


def shards(dom, sub, rhs_local, coefficient):
    size_x, own_y, nz = rhs_local.shape
    assert size_x == N and dom % 2 == 0 and (sub == 1 or own_y > HALO)
    lay = Layout(own_y, nz, dom, sub)
    ny, cr = lay.ny, lay.cr
    t = {k: jnp.asarray(v) for k, v in make_tables(ny, nz, own_y).items()}
    pick = lambda *names: [t[k] for k in names]
    even = lambda v: lax.ppermute(v, "dom", swap_pairs(dom, 0))
    odd = lambda v, k=0: lax.ppermute(v, ("dom", "sub"), chip_pairs(dom, sub, k))
    block = (N, own_y, nz)
    raw = jnp.stack([rhs_local, coefficient])
    n_other = 0 if sub == 1 else 1 if sub == 2 else 2
    face, w, d, r, *packs = run(
        functools.partial(own_kernel, lay),
        [raw, t["z_sq"], t["y_sq", own_y // N], t["w3"]],
        [(2, own_y, nz), block, block, block]
        + [(PACK, nz)] * n_other,
    )
    mate_face = even(face)
    if sub == 1:
        steps = []
    elif sub == 2:
        steps = [[(0, 1), (1, 0)]]
    else:
        up = [(i, i + 1) for i in range(sub - 1)]
        steps = [up, [(b, a) for a, b in up]]
    others = [lax.ppermute(pack, "sub", step) for pack, step in zip(packs, steps)]
    raw_later = lax.optimization_barrier((raw, face))[0]
    mate = [even(raw_later[side]) for side in range(2)]
    lines = 3 * N * line_count(lay)
    msgs = run(
        functools.partial(message_kernel, lay),
        [w, d, r, mate_face],
        [(PLANES * own_y + lines, nz)] + [(PLANES * HALO + lines + SPARE, nz)] * n_other,
        [block] * 3,
    )
    shifts = [0] if sub == 1 else [0, 1] if sub == 2 else [0, 1, -1]
    pieces = [odd(msg, k) for msg, k in zip(msgs, shifts)]
    pair = (2 * N, ny, nz)
    count = lay.early_rows(0)[1] // N
    arrays = run(
        functools.partial(early_kernel, lay),
        [raw, *mate, t["z_sq"], t["y_sq", own_y // N], t["w3"]]
        + [t["z_d"], t["z_dt"], t["y_d", count], t["y_dt", count]],
        [pair] * ARRAYS,
        [(2 * N, count * N, nz)] * 3,
    )
    others, arrays = lax.optimization_barrier((others, arrays))
    mate_others = [even(o[a:b]) for o in others for a, b in zip(CUTS, CUTS[1:])]
    arrays = run(
        functools.partial(near_kernel, lay, n_other),
        [*others, t["z_sq"], t["y_sq", HALO // N], t["w3"], *arrays],
        [pair] * ARRAYS,
        (),
        {n_other + 3 + k: k for k in range(ARRAYS)},
    )
    pieces[0], arrays = lax.optimization_barrier((pieces[0], arrays))
    late = lambda *names: [t[k, HALO // N + 1] for k in names]
    sums = [t["z_sq"], t["y_sq", HALO // N], t["w3"]]
    w, rhs, _, _, lin, _, _, _, sec, ends = run(
        functools.partial(deep_kernel, lay, n_other),
        [*mate_others, *sums, t["z_d"], t["z_dt"], *late("y_d", "y_dt"), *arrays],
        [pair] * (ARRAYS + 1) + [(2, 2, ny, nz)],
        [(2 * N, HALO + N, nz)] * 3,
        {len(mate_others) + 7 + k: k for k in range(ARRAYS)},
    )
    later, sec = lax.optimization_barrier((pieces[1:], sec))
    pieces = pieces[:1] + later
    mate_pieces = [even(p) for p in pieces]
    g, r = run(
        functools.partial(coarse_tables_kernel, lay),
        [w, rhs] + pick("my", "mz", "ry_one", "rz_one"),
        [(2, 27, cr, nz), (4, cr, nz)],
    )
    sec, msg, state = run(
        functools.partial(second_kernel, lay, len(pieces)),
        [*pieces, *mate_pieces, w, sec, lin, ends, g, r]
        + pick("z_d", "z_dt", "z_sq", "y_d", "y_dt", ("y_sq", lay.ey), "ry", "rz", "line"),
        [block, (3, cr, nz), (10, cr, nz)],
        [(2, PLANES, ny, nz)] + [pair] * 4,
    )
    from_odd = odd(msg)
    from_mate = even(from_odd)
    return tuple(
        run(
            functools.partial(third_kernel, lay),
            [from_odd, from_mate, sec, state, g] + pick("py", "pz"),
            [block, (size_x // 4, own_y // 4, nz // 4)],
        )
    )


def solution(mesh):
    dom, sub = mesh.shape["dom"], mesh.shape["sub"]
    return jax.shard_map(
        functools.partial(shards, dom, sub),
        mesh=mesh,
        in_specs=(P("dom", "sub", None), P("dom", "sub", None)),
        out_specs=(P("dom", "sub", None), P("dom", "sub", None)),
        check_vma=False,
    )
```

```python
import functools

import jax
import jax.numpy as jnp
import numpy as np
from jax import lax
from jax.experimental import pallas as pl
from jax.experimental.pallas import tpu as pltpu
from jax.sharding import PartitionSpec as P

N = 8
SPARE = 4 * N
PLANES = 4
HALO = 3 * N
THETA = 1.1
DELTA = 0.9
SIGMA = THETA / DELTA
RHO0 = 1.0 / SIGMA
RHO1 = 1.0 / (2.0 * SIGMA - RHO0)
LANES = 128
F32 = jnp.float32
BF16 = jnp.bfloat16
VMEM_LIMIT = 48 * 1024 * 1024


def legendre_value(points, degree):
    previous = np.ones(points.shape)
    current = points.copy()
    for level in range(1, degree):
        following = ((2 * level + 1) * points * current - level * previous) / (level + 1)
        previous = current
        current = following
    return current


def tables():
    degree = 7
    points = np.array(
        [
            -1.0,
            -0.8717401485096066,
            -0.5917001814331423,
            -0.2092992179024789,
            0.2092992179024789,
            0.5917001814331423,
            0.8717401485096066,
            1.0,
        ]
    )
    values = legendre_value(points, degree)
    weights = 2.0 / (degree * (degree + 1) * values**2)
    derivative = np.zeros((8, 8))
    for row_at in range(8):
        for col_at in range(8):
            if row_at != col_at:
                derivative[row_at, col_at] = values[row_at] / (
                    values[col_at] * (points[row_at] - points[col_at])
                )
    derivative[0, 0] = -degree * (degree + 1) / 4.0
    derivative[7, 7] = degree * (degree + 1) / 4.0
    interp = np.stack([(1.0 - points) / 2.0, (1.0 + points) / 2.0], axis=1)
    return derivative, weights, interp


DM, WEIGHTS, INTERP = tables()
MULT = np.array([2.0] + [1.0] * 6 + [2.0])
RHO = MULT[:, None] * INTERP
DRHO = DM @ RHO


def blockdiag(block, count):
    return np.kron(np.eye(count), block)


def hi_lo(matrix):
    hi = matrix.astype(jnp.bfloat16)
    lo = (matrix - hi.astype(np.float64)).astype(jnp.bfloat16)
    return hi, lo


def right_table(matrix):
    hi, lo = hi_lo(matrix)
    full = np.concatenate([np.concatenate([hi, hi]), np.concatenate([lo, 0 * lo])], axis=1)
    return np.stack(np.split(full, full.shape[1] // LANES, axis=1))


def left_table(matrix):
    hi, lo = hi_lo(matrix)
    return np.concatenate([hi, hi, lo], axis=1).astype(np.float32)


def vertex_table(per_node, elements, columns, count=8):
    out = np.zeros((count * elements, columns))
    for e in range(elements):
        for i in range(2):
            out[count * e : count * (e + 1), e + i] += per_node[:, i]
    return out


def moment_table(per_node, elements, columns):
    out = np.zeros((8 * elements, columns))
    for e in range(elements):
        out[8 * e : 8 * e + 8, e] = per_node
    return out


PAIRS = [(0, 0), (0, 1), (1, 1)]
MASS = [INTERP[:, i] * INTERP[:, j] for i, j in PAIRS]


def round_up(value, to):
    return -(-value // to) * to


def make_tables(ny, nz, own_y):
    ey, ez = ny // N, nz // N
    cr = round_up(ey + 1, 8)
    t = {}
    t["z_d"] = right_table(blockdiag(DM, ez).T)
    t["z_dt"] = right_table(blockdiag(DM, ez))
    t["z_sq"] = right_table(blockdiag(DM * DM, ez))
    t["y_d"] = left_table(blockdiag(DM, ey))
    t["y_dt"] = left_table(blockdiag(DM, ey).T)
    for count in [*range(1, own_y // N + 1), ey]:
        t["y_sq", count] = left_table(blockdiag(DM * DM, count).T)
        t["y_d", count] = left_table(blockdiag(DM, count))
        t["y_dt", count] = left_table(blockdiag(DM, count).T)
    py = vertex_table(RHO, ey, cr)
    dpy = blockdiag(DM, ey) @ py
    pz = vertex_table(RHO, ez, nz)
    dpz = blockdiag(DM, ez) @ pz
    zero = np.zeros_like(py)
    ry = np.concatenate([np.concatenate([py, dpy, zero]), np.concatenate([zero, zero, py])], axis=1)
    t["ry"] = np.concatenate(hi_lo(ry.T), axis=0).astype(np.float32)
    t["ry_one"] = left_table(py.T)
    t["rz"] = right_table(np.concatenate([pz, dpz], axis=0))
    t["rz_one"] = right_table(pz)
    t["my"] = left_table(np.concatenate([moment_table(m, ey, cr) for m in MASS], axis=1).T)
    t["mz"] = right_table(np.concatenate([moment_table(m, ez, nz) for m in MASS], axis=1))
    t["py"] = np.broadcast_to(INTERP.T[:, :, None], (2, N, nz)).astype(np.float32)
    pz = vertex_table(INTERP, ez, nz).T
    sz = vertex_table(np.eye(2), ez, nz, 2).T
    t["pz"] = right_table(np.concatenate([pz, sz], axis=1))
    cols = np.concatenate([DM.T, DM.T[[N - 1]], DM.T[[0]]], axis=0)
    t["line"] = np.broadcast_to(cols[:, :, None], (N + 2, N, nz)).astype(np.float32)
    w3 = WEIGHTS[:, None, None] * WEIGHTS[None, :, None] * np.ones((1, 1, nz))
    t["w3"] = (w3 * np.tile(WEIGHTS, ez)[None, None, :]).astype(np.float32)
    return t


def even_odd(matrix, values, sign):
    even = [values[b] + values[7 - b] for b in range(4)]
    odd = [values[b] - values[7 - b] for b in range(4)]
    out = [None] * 8
    for a in range(4):
        pe = po = None
        for b in range(4):
            ce = float((matrix[a, b] + matrix[a, 7 - b]) / 2.0)
            co = float((matrix[a, b] - matrix[a, 7 - b]) / 2.0)
            te = ce * even[b]
            to = co * odd[b]
            pe = te if pe is None else pe + te
            po = to if po is None else po + to
        out[a] = pe + po
        out[7 - a] = pe - po if sign > 0 else po - pe
    return out


def split(x):
    hi = x.astype(BF16)
    lo = (x - hi.astype(F32)).astype(BF16)
    return hi, lo


def dot(a, b):
    return jnp.dot(a, b, preferred_element_type=F32)


def z_apply(hi, lo, table):
    table = jnp.concatenate([table[k] for k in range(table.shape[0])], axis=1)
    both = dot(jnp.concatenate([hi, lo], axis=1), table)
    half = both.shape[1] // 2
    return both[:, :half] + both[:, half:]


def y_apply(x, table):
    hi = x.astype(BF16).astype(F32)
    parts = jnp.concatenate([hi, x - hi, hi], axis=0).astype(BF16)
    return dot(table.astype(BF16), parts)


def y_planes(get, planes, table):
    table = table.astype(BF16)
    out = {}
    for p, q in zip(planes[::2], planes[1::2]):
        both = y_apply(jnp.concatenate([get(p), get(q)], axis=1), table)
        nz = both.shape[1] // 2
        out[p], out[q] = both[:, :nz], both[:, nz:]
    return out


def assemble_yz(v):
    ny, nz = v.shape
    row = lax.broadcasted_iota(jnp.int32, (N, nz), 0)
    lane = lax.broadcasted_iota(jnp.int32, (ny, nz), 1)
    is_top = row == 0
    flip = (N - 1) - row
    blocks = [v[N * e : N * e + N] for e in range(ny // N)]
    top = (row == N - 1).astype(F32)
    bottom = (row == 0).astype(F32)
    out = []
    for e, b in enumerate(blocks):
        if len(blocks) == 1:
            out.append(b)
            continue
        if e == 0:
            near, mask = blocks[1], top
        elif e + 1 == len(blocks):
            near, mask = blocks[e - 1], bottom
        else:
            near, mask = jnp.where(is_top, blocks[e + 1], blocks[e - 1]), top + bottom
        out.append(b + mask * jnp.take_along_axis(near, flip, axis=0))
    v = jnp.concatenate(out, axis=0)
    last = (lane % N == N - 1) & (lane < nz - 1)
    first = (lane % N == 0) & (lane > 0)
    other = lane + jnp.where(last, 1, 0) - jnp.where(first, 1, 0)
    mask = (last | first).astype(F32)
    return v + mask * jnp.take_along_axis(v, other, axis=1)


def yz_mask(ny, nz, start, total):
    row = lax.broadcasted_iota(jnp.int32, (ny, nz), 0) + start
    lane = lax.broadcasted_iota(jnp.int32, (ny, nz), 1)
    return (row > 0) & (row < total - 1) & (lane > 0) & (lane < nz - 1)


class Layout:
    def __init__(self, own_y, nz, dom, sub):
        self.own_y, self.nz, self.dom, self.sub = own_y, nz, dom, sub
        self.blocks = min(sub, 3)
        self.ny = own_y + HALO * (self.blocks - 1)
        self.total_y = own_y * sub
        self.ey, self.ez = self.ny // N, nz // N
        self.cr = round_up(self.ey + 1, 8)

    def where(self):
        d = lax.axis_index("dom")
        h = lax.axis_index("sub")
        parity = lax.rem(d, 2)
        pair = lax.div(d, 2)
        if self.sub == 1:
            start, offset = 0, 0
        elif self.sub == 2:
            start, offset = h * (self.own_y - HALO), h * HALO
        else:
            start, offset = h * self.own_y - HALO, HALO
        low = (pair > 0).astype(F32)
        high = (pair < self.dom // 2 - 1).astype(F32)
        return parity, h, start, offset, low, high

    def sent_rows(self, h):
        down = self.own_y - HALO
        if self.sub == 1:
            return []
        if self.sub == 2:
            return [((1 - h) * down, (down, HALO - 1))]
        return [(down, down), (0, HALO - 1)]

    def far_rows(self, h):
        if self.sub == 1:
            return []
        if self.sub == 2:
            return [(self.ny - 1, 0)]
        return [0, self.ny - 1]

    def other_starts(self, h):
        if self.sub == 1:
            return []
        if self.sub == 2:
            return [(1 - h) * self.own_y]
        return [0, HALO + self.own_y]

    def early_rows(self, h):
        if self.sub == 1:
            return 0, self.own_y
        if self.sub == 2:
            return h * (HALO + N), self.own_y - N
        return HALO + N, self.own_y - 2 * N

    def late_starts(self, h):
        if self.sub == 1:
            return []
        if self.sub == 2:
            return [(1 - h) * (self.own_y - N)]
        return [0, self.own_y + HALO - N]

    def interfaces(self, h):
        if self.sub == 1:
            return []
        if self.sub == 2:
            return [self.own_y - h * (self.own_y - HALO)]
        return [HALO, HALO + self.own_y]


def aligned(start, size):
    return pl.ds(start if isinstance(start, int) else pl.multiple_of(start, N), size)


def gather_window(lay, own, others, h, store):
    y = lay.own_y
    if lay.sub == 1:
        store(pl.ds(0, y), own)
    elif lay.sub == 2:
        store(aligned(h * HALO, y), own)
        store(aligned((1 - h) * y, HALO), others[0])
    else:
        store(pl.ds(0, HALO), others[0])
        store(pl.ds(HALO, y), own)
        store(pl.ds(HALO + y, HALO), others[1])


PACK = 2 * N + 2 * N * HALO
CUTS = [0, 2 * N + 5 * HALO, 2 * N + 10 * HALO, PACK]


def pack_rows(side, a):
    return pl.ds(2 * N + (side * N + a) * HALO, HALO)


class Pieces:
    def __init__(self, refs):
        self.refs = refs

    def __getitem__(self, rows):
        if len(self.refs) == 1:
            return self.refs[0][rows, :]
        k = max(i for i in range(len(self.refs)) if CUTS[i] <= rows.start)
        return self.refs[k][pl.ds(rows.start - CUTS[k], rows.size), :]


def line_rows(lay, h):
    if lay.sub == 1:
        return []
    if lay.sub == 2:
        return [(lay.own_y - 1, 0)]
    return [0, lay.own_y - 1]


def load_row(field, a, row, h):
    if isinstance(row, int):
        return field[a, pl.ds(row, 1), :]
    first, second = (field[a, pl.ds(r, 1), :] for r in row)
    return jnp.where(h == 0, first, second)


def store_row(field, a, row, h, value):
    if isinstance(row, int):
        field[a, pl.ds(row, 1), :] = value
        return
    for k, r in enumerate(row):
        field[a, pl.ds(r, 1), :] = jnp.where(h == k, value, field[a, pl.ds(r, 1), :])


def line_count(lay):
    return 0 if lay.sub == 1 else 1 if lay.sub == 2 else 2


def own_kernel(lay, raw, z_sq, y_sq, w3, face, w_out, d_out, r_out, *packs):
    rhs, coef = raw.at[0], raw.at[1]
    y, nz = lay.own_y, lay.nz
    parity, h = lay.where()[:2]
    table3 = w3[...]
    for e in range(y // N):
        rows = pl.ds(N * e, N)
        w = [coef[a, rows, :] * table3[a] for a in range(N)]
        dx = even_odd((DM * DM).T, w, 1)
        for a in range(N):
            w_out[a, rows, :] = w[a]
            d_out[a, rows, :] = dx[a]
    hi, lo = split(w_out[...].reshape(N * y, nz))
    dz = z_apply(hi, lo, z_sq[...])
    dy = y_planes(lambda a: w_out[a], list(range(N)), y_sq[...])
    for a in range(N):
        d_out[a] = assemble_yz(d_out[a] + dz[a * y : (a + 1) * y] + dy[a])
        r_out[a] = assemble_yz(rhs[a])
    inner = (N - 1) * (1 - parity)
    face[0] = r_out[inner]
    face[1] = d_out[inner]
    for pack, (first, far) in zip(packs, lay.sent_rows(h)):
        for side, field in ((0, r_out), (1, d_out)):
            for a in range(N):
                pack[pack_rows(side, a), :] = raw[side, a, aligned(first, HALO), :]
                pack[pl.ds(side * N + a, 1), :] = load_row(field, a, far, h)


def message_kernel(lay, w, d, r, face, *refs):
    msg, *side_msgs, u_s, d_s, r_s = refs
    y, nz = lay.own_y, lay.nz
    parity, h, start, offset, low, high = lay.where()
    mask = yz_mask(y, nz, h * y, lay.total_y)
    scale = mask.astype(F32) * (1.0 / THETA)
    odd = parity.astype(F32)
    for a in range(N):
        dd, rr = d[a], r[a]
        keep = scale
        if a in (0, N - 1):
            inner = odd if a == 0 else 1.0 - odd
            dd = dd + inner * face[1]
            rr = rr + inner * face[0]
            keep = scale * inner
        d_s[a] = dd
        r_s[a] = rr
        u_s[a] = keep * rr / jnp.where(mask, dd, 1.0)
    col = [jnp.where(parity == 0, float(DM[a, 0]), float(DM[a, N - 1])) for a in range(N)]
    acc = []
    for e in range(y // N):
        rows = pl.ds(N * e, N)
        g = even_odd(DM, [u_s[a, rows, :] for a in range(N)], -1)
        total = None
        for a in range(N):
            term = (w[a, rows, :] * g[a]) * col[a]
            total = term if total is None else total + term
        acc.append(total)
    outer = (N - 1) * parity
    msg[pl.ds(0, y), :] = r[outer]
    msg[pl.ds(y, y), :] = d[outer]
    msg[pl.ds(2 * y, y), :] = w[outer]
    msg[pl.ds(3 * y, y), :] = assemble_yz(jnp.concatenate(acc, axis=0))
    base = PLANES * y
    for row in line_rows(lay, h):
        for field in (r_s, d_s, w):
            for a in range(N):
                msg[pl.ds(base + a, 1), :] = load_row(field, a, row, h)
            base += N
    for out, (first, _) in zip(side_msgs, lay.sent_rows(h)):
        for k in range(PLANES):
            out[pl.ds(k * HALO, HALO), :] = msg[aligned(k * y + first, HALO), :]
        lines = base - PLANES * y
        out[pl.ds(PLANES * HALO, lines), :] = msg[pl.ds(PLANES * y, lines), :]
        out[pl.ds(PLANES * HALO + lines, SPARE), :] = jnp.zeros((SPARE, nz), F32)


def flux_x(lay, u_ref, w_ref, first, count, fx):
    for el in range(2):
        for e in range(count // N):
            rows, to = aligned(first + N * e, N), pl.ds(N * e, N)
            u = [u_ref[N * el + a, rows, :] for a in range(N)]
            g = even_odd(DM, u, -1)
            for a in range(N):
                fx[N * el + a, to, :] = w_ref[N * el + a, rows, :] * g[a]


def flux_yz(lay, u_ref, w_ref, planes, first, count, z_d, y_d, fy, fz):
    part, to = aligned(first, count), pl.ds(0, count)
    u = jnp.concatenate([u_ref[p, part, :] for p in planes], axis=0)
    gz = z_apply(*split(u), z_d[...])
    gy = y_planes(lambda p: u_ref[p, part, :], planes, y_d[...])
    for k, p in enumerate(planes):
        w = w_ref[p, part, :]
        fy[p, to, :] = w * gy[p]
        fz[p, to, :] = w * gz[k * count : (k + 1) * count]


def operate(lay, u_ref, w_ref, back, first, count, tables, fx, fy, fz):
    z_d, z_dt, y_d, y_dt = tables
    nz = lay.nz
    middle = list(range(1, 2 * N - 1))
    flux_x(lay, u_ref, w_ref, first, count, fx)
    flux_yz(lay, u_ref, w_ref, middle, first, count, z_d, y_d, fy, fz)
    to, part = pl.ds(0, count), aligned(first, count)
    for el in range(2):
        for e in range(count // N):
            rows, here = aligned(first + N * e, N), pl.ds(N * e, N)
            b = even_odd(DM.T, [fx[N * el + a, here, :] for a in range(N)], -1)
            for a in range(N):
                back[N * el + a, rows, :] = b[a]
    n = len(middle)
    bz = z_apply(*split(fz[pl.ds(1, n), to, :].reshape(n * count, nz)), z_dt[...])
    by = y_planes(lambda p: fy[p, to, :], middle, y_dt[...])
    for p in middle:
        back[p, part, :] = back[p, part, :] + by[p] + bz[(p - 1) * count : p * count]


def smooth_start(lay, d, r, inv, u, first, count, start):
    part = aligned(first, count)
    mask = yz_mask(count, lay.nz, start + first, lay.total_y)
    inside = mask.astype(F32)
    zero = jnp.zeros((count, lay.nz), F32)
    for p in range(2 * N):
        if p in (0, 2 * N - 1):
            u[p, part, :] = zero
        else:
            i = inside / jnp.where(mask, d[p, part, :], 1.0)
            inv[p, part, :] = i
            u[p, part, :] = i * r[p, part, :] * (1.0 / THETA)


def sum_middle(fields, first, count):
    part = aligned(first, count)
    for s in fields:
        both = s[N - 1, part, :] + s[N, part, :]
        s[N - 1, part, :] = both
        s[N, part, :] = both


def element_sums(lay, base, parity, first, count, source, tables, outs):
    z_sq, y_sq, w3 = tables
    w_out, rhs_out, d_s, r_s, lin = outs[:5]
    nz = lay.nz
    part = aligned(first, count)
    for side, target in ((0, rhs_out), (1, w_out)):
        for a in range(N):
            target[base + a, part, :] = source(side, a)
    table3 = w3[...]
    outer = [jnp.where(parity == 0, float(DM[a, 0]), float(DM[a, N - 1])) for a in range(N)]
    for e in range(count // N):
        rows = aligned(first + N * e, N)
        w = [w_out[base + a, rows, :] * table3[a] for a in range(N)]
        dx = even_odd((DM * DM).T, w, 1)
        cx = even_odd(DM.T, [outer[a] * w[a] for a in range(N)], -1)
        for a in range(N):
            w_out[base + a, rows, :] = w[a]
            d_s[base + a, rows, :] = dx[a]
            lin[base + a, rows, :] = cx[a]
    dz = z_apply(*split(w_out[pl.ds(base, N), part, :].reshape(N * count, nz)), z_sq[...])
    dy = y_planes(lambda a: w_out[base + a, part, :], list(range(N)), y_sq[...])
    for a in range(N):
        d_local = d_s[base + a, part, :] + dz[a * count : (a + 1) * count] + dy[a]
        d_s[base + a, part, :] = assemble_yz(d_local)
        r_s[base + a, part, :] = assemble_yz(rhs_out[base + a, part, :])
        lin[base + a, part, :] = assemble_yz(lin[base + a, part, :])


def other_sums(lay, base, parity, h, pieces, tables, outs):
    d_s, r_s = outs[2:4]
    for piece, first, row in zip(pieces, lay.other_starts(h), lay.far_rows(h)):
        source = lambda side, a, piece=piece: piece[pack_rows(side, a)]
        element_sums(lay, base, parity, first, HALO, source, tables, outs)
        for side, target in ((0, r_s), (1, d_s)):
            for a in range(N):
                store_row(target, base + a, row, h, piece[pl.ds(side * N + a, 1)])


ARRAYS = 8


def early_kernel(lay, own, *refs):
    mate, refs = refs[:2], refs[2:]
    z_sq, y_sq, w3 = refs[:3]
    tables, outs, scratch = refs[3:7], refs[7 : 7 + ARRAYS], refs[7 + ARRAYS :]
    w, _, d, r, _, inv, u, back = outs
    parity, h, start, offset, low, high = lay.where()
    own = (own.at[0], own.at[1])
    for base, el, block in ((parity * N, parity, own), ((1 - parity) * N, 1 - parity, mate)):
        source = lambda side, a, block=block: block[side][a]
        element_sums(lay, base, el, offset, lay.own_y, source, (z_sq, y_sq, w3), outs)
    sum_middle((d, r), offset, lay.own_y)
    smooth_start(lay, d, r, inv, u, offset, lay.own_y, start)
    first, count = lay.early_rows(h)
    operate(lay, u, w, back, first, count, tables, *scratch)


def near_kernel(lay, n_other, *refs):
    other, tables = refs[:n_other], refs[n_other : n_other + 3]
    outs = refs[n_other + 3 + ARRAYS :]
    parity, h = lay.where()[:2]
    other_sums(lay, parity * N, parity, h, [Pieces([o]) for o in other], tables, outs)


def deep_kernel(lay, n_other, *refs):
    cuts = len(CUTS) - 1
    mate_other = [Pieces(refs[cuts * k : cuts * (k + 1)]) for k in range(n_other)]
    refs = refs[cuts * n_other :]
    z_sq, y_sq, w3 = refs[:3]
    tables = refs[3:7]
    refs = refs[7 + ARRAYS :]
    outs, sec_out, ends = refs[:ARRAYS], refs[ARRAYS], refs[ARRAYS + 1]
    scratch = refs[ARRAYS + 2 :]
    w, _, d, r, lin, inv, u, back = outs
    last = 2 * N - 1
    parity, h, start, offset, low, high = lay.where()
    other_sums(lay, (1 - parity) * N, 1 - parity, h, mate_other, (z_sq, y_sq, w3), outs)
    for first in lay.other_starts(h):
        sum_middle((d, r), first, HALO)
    for begin in lay.interfaces(h):
        above, below = pl.ds(begin - 1, 1), pl.ds(begin, 1)
        for s in (d, r, lin):
            for p in range(2 * N):
                both = s[p, above, :] + s[p, below, :]
                s[p, above, :] = both
                s[p, below, :] = both
    for side, p in ((0, 0), (1, last)):
        ends[side, 0] = r[p]
        ends[side, 1] = d[p]
    for first in lay.late_starts(h):
        smooth_start(lay, d, r, inv, u, first, HALO + N, start)
        operate(lay, u, w, back, first, HALO + N, tables, *scratch)
    for p in range(1, last):
        back[p] = assemble_yz(back[p])
    sum_middle((back,), 0, lay.ny)
    for p in range(2 * N):
        if p in (0, last):
            sec_out[p] = assemble_yz(back[p])
        else:
            i = (2.0 * RHO1 / DELTA) * inv[p]
            lin[p] = -i * lin[p]
            sec_out[p] = (1.0 + RHO1 * RHO0) * u[p] + i * (r[p] - back[p])


def coarse_tables_kernel(lay, w_ref, rhs_ref, my, mz, ry, rz, g_out, r_out):
    ny, nz, cr = lay.ny, lay.nz, lay.cr
    lhs = []
    for el in range(2):
        for m in MASS:
            total = None
            for a in range(N):
                term = float(m[a]) * w_ref[N * el + a]
                total = term if total is None else total + term
            lhs.append(total)
    along_z = z_apply(*split(jnp.concatenate(lhs, axis=0)), mz[...])
    for el in range(2):
        mom = {}
        for alpha in range(3):
            at = (3 * el + alpha) * ny
            block = y_apply(along_z[at : at + ny], my[...])
            for beta in range(3):
                for gamma in range(3):
                    mom[alpha, beta, gamma] = block[
                        beta * cr : (beta + 1) * cr, gamma * nz : (gamma + 1) * nz
                    ]
        x_sum, y_sum, z_sum = {}, {}, {}
        for i in range(3):
            for j in range(3):
                x_sum[i, j] = mom[0, i, j] + 2.0 * mom[1, i, j] + mom[2, i, j]
                y_sum[i, j] = mom[i, 0, j] + 2.0 * mom[i, 1, j] + mom[i, 2, j]
                z_sum[i, j] = mom[i, j, 0] + 2.0 * mom[i, j, 1] + mom[i, j, 2]
        sign = (1.0, -1.0, 1.0)
        for alpha in range(3):
            for beta in range(3):
                for gamma in range(3):
                    g_out[el, 9 * alpha + 3 * beta + gamma] = 0.25 * (
                        sign[alpha] * x_sum[beta, gamma]
                        + sign[beta] * y_sum[alpha, gamma]
                        + sign[gamma] * z_sum[alpha, beta]
                    )
    sums = []
    for el in range(2):
        for i in range(2):
            total = None
            for a in range(N):
                term = float(RHO[a, i]) * rhs_ref[N * el + a]
                total = term if total is None else total + term
            sums.append(total)
    part = y_apply(jnp.concatenate(sums, axis=1), ry[...])
    rows = jnp.concatenate([part[:, k * nz : (k + 1) * nz] for k in range(4)], axis=0)
    full = z_apply(*split(rows), rz[...])
    for k in range(4):
        r_out[k] = full[k * cr : (k + 1) * cr]


def pair_index(i, j):
    return i + j


def shifted(c, q, r):
    if q:
        c = pltpu.roll(c, c.shape[0] - 1, 0)
    if r:
        c = pltpu.roll(c, c.shape[1] - 1, 1)
    return c


def scatter(parts):
    cr, nz = parts[0, 0].shape
    first = parts[0, 0] + pltpu.roll(parts[0, 1], 1, 1)
    second = parts[1, 0] + pltpu.roll(parts[1, 1], 1, 1)
    return first + pltpu.roll(second, 1, 0)


def gathered(c):
    return {(q, r): shifted(c, q, r) for q in range(2) for r in range(2)}


def face_apply(entry, c, out=None):
    out = {} if out is None else out
    for j in range(2):
        for k in range(2):
            for q in range(2):
                for r in range(2):
                    term = entry(pair_index(j, q), pair_index(k, r)) * c[q, r]
                    out[j, k] = term if (j, k) not in out else out[j, k] + term
    return out


def coarse_diag(entry):
    return scatter({(j, k): entry(2 * j, 2 * k) for j in range(2) for k in range(2)})


def coarse_mask(lay, start):
    row = lax.broadcasted_iota(jnp.int32, (lay.cr, lay.nz), 0) + lax.div(start, N)
    lane = lax.broadcasted_iota(jnp.int32, (lay.cr, lay.nz), 1)
    return (row > 0) & (row < lay.total_y // N) & (lane > 0) & (lane < lay.ez)


def unpack_sides(lay, pieces, mate_pieces, line, parity, h, start, win):
    y, nz = lay.own_y, lay.nz
    for side, group in ((parity, pieces), (1 - parity, mate_pieces)):
        for k in range(PLANES):

            def put(rows, value):
                win[side, k, rows, :] = value

            others = [g[pl.ds(k * HALO, HALO), :] for g in group[1:]]
            gather_window(lay, group[0][pl.ds(k * y, y), :], others, h, put)
    is_even = parity == 0
    lane = lax.broadcasted_iota(jnp.int32, (N, nz), 1)
    node = lax.broadcasted_iota(jnp.int32, (N, nz), 0)
    lane_in = (lane > 0) & (lane < nz - 1)
    flank = lax.broadcasted_iota(jnp.int32, (1, nz), 1)
    last = ((flank % N == N - 1) & (flank < nz - 1)).astype(F32)
    first = ((flank % N == 0) & (flank > 0)).astype(F32)
    for b, begin in enumerate(lay.interfaces(h), 1):
        above, below = pl.ds(begin - 1, 1), pl.ds(begin, 1)
        for side in range(2):
            for k in range(2):
                both = win[side, k, above, :] + win[side, k, below, :]
                win[side, k, above, :] = both
                win[side, k, below, :] = both
        for side in range(2):
            outer = N - 1 if side == 0 else 0

            def field(k):
                def of(group):
                    own_lines, other_lines = PLANES * y + k * N, PLANES * HALO + k * N
                    if lay.sub == 2:
                        mine, theirs = own_lines, other_lines
                        near = group[1]
                    else:
                        mine = own_lines + 3 * N * (b - 1)
                        theirs = other_lines + 3 * N * (2 - b)
                        near = group[b]
                    return group[0][pl.ds(mine, N), :] + near[pl.ds(theirs, N), :]
                mine, theirs = of(pieces), of(mate_pieces)
                if side == 0:
                    return jnp.where(is_even, mine, theirs)
                return jnp.where(is_even, theirs, mine)

            r, d, w = field(0), field(1), field(2)
            row = start + begin
            ok = lane_in & (node != outer) & (row > 0) & (row < lay.total_y)
            u = jnp.where(ok, r / jnp.where(ok, d, 1.0) * (1.0 / THETA), 0.0)
            g = None
            for a in range(N):
                term = line[a] * u[a : a + 1]
                g = term if g is None else g + term
            total = jnp.sum(line[N + side] * (w * g), axis=0, keepdims=True)
            total = total + last * pltpu.roll(total, nz - 1, 1) + first * pltpu.roll(total, 1, 1)
            win[side, 3, above, :] = total
            win[side, 3, below, :] = total


def second_kernel(lay, n_pieces, *refs):
    pieces, mate_pieces = refs[:n_pieces], refs[n_pieces : 2 * n_pieces]
    w_ref, sec_in, lin_in, ends, g_ref, r_ref = refs[2 * n_pieces : 2 * n_pieces + 6]
    refs = refs[2 * n_pieces + 6 :]
    z_d, z_dt, z_sq, y_d, y_dt, y_sq, ry, rz, line = refs[:9]
    out, msg, state = refs[9:12]
    win, sec, fx, fy, fz = refs[12:]
    ny, nz, cr = lay.ny, lay.nz, lay.cr
    last = 2 * N - 1
    parity, h, start, offset, low, high = lay.where()
    mask = yz_mask(ny, nz, start, lay.total_y)
    inside = mask.astype(F32)
    is_even = parity == 0
    unpack_sides(lay, pieces, mate_pieces, line, parity, h, start, win)
    flags = (low, high)
    inv, res, u = [], [], []
    for side in range(2):
        valid = inside * flags[side]
        inv.append(valid / jnp.where(mask, ends[side, 1] + win[side, 1], 1.0))
        res.append(valid * (ends[side, 0] + win[side, 0]))
        u.append(inv[side] * res[side] * (1.0 / THETA))
    for p in range(1, last):
        value = sec_in[p]
        if p <= N:
            value = value + lin_in[min(p, N - 1)] * u[0]
        if p >= N - 1:
            value = value + lin_in[max(p, N)] * u[1]
        sec[p] = value
    flux_yz(lay, sec, w_ref, list(range(1, last)), 0, ny, z_d, y_d, fy, fz)
    weights = [w_ref[0] + win[0, 2], w_ref[last] + win[1, 2]]
    hi, lo = split(jnp.concatenate(u, axis=0))
    gz = z_apply(hi, lo, z_d[...])
    gy = y_apply(jnp.concatenate(u, axis=1), y_d[...])
    weight_z = jnp.concatenate(weights, axis=0)
    weight_y = jnp.concatenate(weights, axis=1)
    bz = z_apply(*split(weight_z * gz), z_dt[...])
    by = y_apply(weight_y * gy, y_dt[...])
    dz = z_apply(*split(jnp.concatenate([win[0, 2], win[1, 2]], axis=0)), z_sq[...])
    dy = y_planes(lambda side: win[side, 2], [0, 1], y_sq[...])
    dx = [
        win[side, 1] - assemble_yz(dz[side * ny : (side + 1) * ny] + dy[side]) for side in range(2)
    ]
    for side, p in ((0, 0), (1, last)):
        plane = assemble_yz(bz[side * ny : (side + 1) * ny] + by[:, side * nz : (side + 1) * nz])
        plane = plane + sec_in[p] + win[side, 3] + (lin_in[p] + dx[side]) * u[side]
        res_one = res[side] - inside * plane
        sec[p] = (1.0 + RHO1 * RHO0) * u[side] + (2.0 * RHO1 / DELTA) * inv[side] * res_one
    out[...] = sec[pl.ds(parity * N, N), pl.ds(pl.multiple_of(offset, N), lay.own_y), :]
    flux_yz(lay, sec, w_ref, [0, last], 0, ny, z_d, y_d, fy, fz)
    flux_x(lay, sec, w_ref, 0, ny, fx)
    sums = []
    for f, weight in ((fx, DRHO), (fy, RHO), (fz, RHO)):
        lanes = []
        for el in range(2):
            for i in range(2):
                total = None
                for a in range(N):
                    term = float(weight[a, i]) * f[N * el + a]
                    total = term if total is None else total + term
                lanes.append(total)
        sums.append(jnp.concatenate(lanes, axis=1))
    data = jnp.concatenate(sums, axis=0)
    hi = data.astype(BF16).astype(F32)
    parts = jnp.concatenate([hi, data - hi], axis=1).astype(BF16)
    both = dot(ry[...].astype(BF16), parts)
    both = both[: 2 * cr, : 4 * nz] + both[2 * cr :, : 4 * nz] + both[: 2 * cr, 4 * nz :]
    rows = [
        jnp.concatenate([v[:, k * nz : (k + 1) * nz] for v in (both[:cr], both[cr:])], axis=1)
        for k in range(4)
    ]
    full = z_apply(*split(jnp.concatenate(rows, axis=0)), rz[...])
    r = {}
    for el in range(2):
        for i in range(2):
            k = 2 * el + i
            r[el, i] = r_ref[k] - full[k * cr : (k + 1) * cr]
    planes = [r[0, 0], r[0, 1] + r[1, 0], r[1, 1]]
    cmask = coarse_mask(lay, start)

    def entry(el, alpha):
        return lambda beta, gamma: g_ref[el, 9 * alpha + 3 * beta + gamma]

    d = [
        coarse_diag(entry(0, 0)),
        coarse_diag(entry(0, 2)) + coarse_diag(entry(1, 0)),
        coarse_diag(entry(1, 2)),
    ]
    cin = cmask.astype(F32)
    mid = (2.0 / 3.0) * cin * planes[1] / jnp.where(cmask, d[1], 1.0)
    c = gathered(mid)
    g_low = scatter(face_apply(entry(0, 1), c))
    g_high = scatter(face_apply(entry(1, 1), c))
    g_mid = scatter(face_apply(entry(1, 0), c, face_apply(entry(0, 2), c)))
    state[0] = planes[0]
    state[1] = planes[1]
    state[2] = planes[2]
    state[3] = d[0]
    state[4] = d[1]
    state[5] = d[2]
    state[6] = g_low
    state[7] = g_mid
    state[8] = g_high
    state[9] = mid
    send = [
        jnp.where(is_even, planes[0], planes[2]),
        jnp.where(is_even, d[0], d[2]),
        jnp.where(is_even, g_low, g_high),
    ]
    send += [jnp.where(is_even, g_ref[0, k], g_ref[1, 18 + k]) for k in range(9)]
    for k in range(3):
        packed = send[4 * k]
        for q in range(1, 4):
            packed = packed + pltpu.roll(send[4 * k + q], q * (nz // 4), 1)
        msg[k] = packed


def third_kernel(lay, *refs):
    own_msg, mate_msg, sec, state, g_ref, py, pz, out, coarse = refs
    ny, nz, cr = lay.ny, lay.nz, lay.cr
    parity, h, start, offset, low, high = lay.where()
    is_even = parity == 0
    cmask = coarse_mask(lay, start)
    cin = cmask.astype(F32)
    lo_msg, hi_msg = [], []
    for k in range(3):
        mine, theirs = own_msg[k], mate_msg[k]
        for target, packed in (
            (lo_msg, jnp.where(is_even, mine, theirs)),
            (hi_msg, jnp.where(is_even, theirs, mine)),
        ):
            target.append(packed)
            for q in range(1, 4):
                target.append(pltpu.roll(packed, nz - q * (nz // 4), 1))

    def entry(el, alpha):
        return lambda beta, gamma: g_ref[el, 9 * alpha + 3 * beta + gamma]

    def outer(at, m, flag, el, alpha):
        rhs = cin * flag * (state[at] + m[0])
        d = jnp.where(cmask, state[3 + at] + m[1], 1.0)
        one = (2.0 / 3.0) * rhs / d
        c = gathered(one)
        here = lambda beta, gamma: g_ref[el, 9 * alpha + 3 * beta + gamma] + m[3 + 3 * beta + gamma]
        image = scatter(face_apply(here, c)) + state[6 + at] + m[2]
        cross = face_apply(entry(el, 1), c)
        solution = one + (2.0 / 3.0) * (rhs - cin * flag * image) / d
        return solution, cross

    c_low, cross_low = outer(0, lo_msg, low, 0, 0)
    c_high, cross_high = outer(2, hi_msg, high, 1, 2)
    cross = scatter({k: cross_low[k] + cross_high[k] for k in cross_low})
    rhs = cin * state[1]
    d = jnp.where(cmask, state[4], 1.0)
    c_mid = state[9] + (2.0 / 3.0) * (rhs - cin * (state[7] + cross)) / d
    left = jnp.where(is_even, c_low, c_mid)
    right = jnp.where(is_even, c_mid, c_high)
    both = jnp.concatenate([left, right], axis=0)
    full = z_apply(*split(both), pz[...])
    y = lay.own_y
    mask = yz_mask(y, nz, start + offset, lay.total_y).astype(F32)
    weight = [jnp.broadcast_to(py[i], (N, nz)) for i in range(2)]
    q = []
    for side in range(2):
        rows = full[side * cr : (side + 1) * cr]
        if lay.sub > 1:
            rows = pltpu.roll(rows, cr - lax.div(offset, N), 0)
        blocks = []
        for e in range(y // N):
            at = [rows[e + i : e + i + 1] for i in range(2)]
            blocks.append(weight[0] * at[0][:, :nz] + weight[1] * at[1][:, :nz])
            for i in range(2):
                coarse[side, pl.ds(2 * e + i, 1), :] = at[i][:, nz : nz + nz // 4]
        q.append(mask * jnp.concatenate(blocks, axis=0))
    q_left, q_right = q
    first_flag = jnp.where(is_even, low, 1.0)
    last_flag = jnp.where(is_even, 1.0, high)
    for a in range(N):
        add = float(INTERP[a, 0]) * q_left + float(INTERP[a, 1]) * q_right
        if a == 0:
            add = first_flag * add
        if a == N - 1:
            add = last_flag * add
        out[a] = sec[a] + add


def run(kernel, args, outs, scratch=(), aliases={}):
    return pl.pallas_call(
        kernel,
        out_shape=[jax.ShapeDtypeStruct(o, F32) for o in outs],
        in_specs=[pl.BlockSpec(memory_space=pltpu.VMEM)] * len(args),
        out_specs=[pl.BlockSpec(memory_space=pltpu.VMEM)] * len(outs),
        scratch_shapes=[pltpu.VMEM(s, F32) for s in scratch],
        compiler_params=pltpu.CompilerParams(vmem_limit_bytes=VMEM_LIMIT),
        input_output_aliases=aliases,
        cost_estimate=pl.CostEstimate(flops=1, bytes_accessed=1, transcendentals=0),
    )(*args)


def swap_pairs(count, first):
    pairs = []
    for i in range(first, count - 1, 2):
        pairs += [(i, i + 1), (i + 1, i)]
    return pairs


def chip_pairs(dom, sub, shift):
    pairs = []
    for a, b in swap_pairs(dom, 1):
        for q in range(sub):
            to = (q + shift) % sub if sub == 2 else q + shift
            if 0 <= to < sub:
                pairs.append((a * sub + q, b * sub + to))
    for end in (0, dom - 1):
        pairs += [(end * sub + a, end * sub + b) for a, b in swap_pairs(sub, 0)]
    return pairs


def shards(dom, sub, rhs_local, coefficient):
    size_x, own_y, nz = rhs_local.shape
    assert size_x == N and dom % 2 == 0 and (sub == 1 or own_y > HALO)
    lay = Layout(own_y, nz, dom, sub)
    ny, cr = lay.ny, lay.cr
    t = {k: jnp.asarray(v) for k, v in make_tables(ny, nz, own_y).items()}
    pick = lambda *names: [t[k] for k in names]
    even = lambda v: lax.ppermute(v, "dom", swap_pairs(dom, 0))
    odd = lambda v, k=0: lax.ppermute(v, ("dom", "sub"), chip_pairs(dom, sub, k))
    block = (N, own_y, nz)
    raw = jnp.stack([rhs_local, coefficient])
    n_other = 0 if sub == 1 else 1 if sub == 2 else 2
    face, w, d, r, *packs = run(
        functools.partial(own_kernel, lay),
        [raw, t["z_sq"], t["y_sq", own_y // N], t["w3"]],
        [(2, own_y, nz), block, block, block]
        + [(PACK, nz)] * n_other,
    )
    mate_face = even(face)
    if sub == 1:
        steps = []
    elif sub == 2:
        steps = [[(0, 1), (1, 0)]]
    else:
        up = [(i, i + 1) for i in range(sub - 1)]
        steps = [up, [(b, a) for a, b in up]]
    others = [lax.ppermute(pack, "sub", step) for pack, step in zip(packs, steps)]
    raw_later = lax.optimization_barrier((raw, face))[0]
    mate = [even(raw_later[side]) for side in range(2)]
    lines = 3 * N * line_count(lay)
    msgs = run(
        functools.partial(message_kernel, lay),
        [w, d, r, mate_face],
        [(PLANES * own_y + lines, nz)] + [(PLANES * HALO + lines + SPARE, nz)] * n_other,
        [block] * 3,
    )
    shifts = [0] if sub == 1 else [0, 1] if sub == 2 else [0, 1, -1]
    pieces = [odd(msg, k) for msg, k in zip(msgs, shifts)]
    pair = (2 * N, ny, nz)
    count = lay.early_rows(0)[1] // N
    arrays = run(
        functools.partial(early_kernel, lay),
        [raw, *mate, t["z_sq"], t["y_sq", own_y // N], t["w3"]]
        + [t["z_d"], t["z_dt"], t["y_d", count], t["y_dt", count]],
        [pair] * ARRAYS,
        [(2 * N, count * N, nz)] * 3,
    )
    others, arrays = lax.optimization_barrier((others, arrays))
    mate_others = [even(o[a:b]) for o in others for a, b in zip(CUTS, CUTS[1:])]
    arrays = run(
        functools.partial(near_kernel, lay, n_other),
        [*others, t["z_sq"], t["y_sq", HALO // N], t["w3"], *arrays],
        [pair] * ARRAYS,
        (),
        {n_other + 3 + k: k for k in range(ARRAYS)},
    )
    pieces[0], arrays = lax.optimization_barrier((pieces[0], arrays))
    late = lambda *names: [t[k, HALO // N + 1] for k in names]
    sums = [t["z_sq"], t["y_sq", HALO // N], t["w3"]]
    w, rhs, _, _, lin, _, _, _, sec, ends = run(
        functools.partial(deep_kernel, lay, n_other),
        [*mate_others, *sums, t["z_d"], t["z_dt"], *late("y_d", "y_dt"), *arrays],
        [pair] * (ARRAYS + 1) + [(2, 2, ny, nz)],
        [(2 * N, HALO + N, nz)] * 3,
        {len(mate_others) + 7 + k: k for k in range(ARRAYS)},
    )
    later, sec = lax.optimization_barrier((pieces[1:], sec))
    pieces = pieces[:1] + later
    mate_pieces = [even(p) for p in pieces]
    g, r = run(
        functools.partial(coarse_tables_kernel, lay),
        [w, rhs] + pick("my", "mz", "ry_one", "rz_one"),
        [(2, 27, cr, nz), (4, cr, nz)],
    )
    sec, msg, state = run(
        functools.partial(second_kernel, lay, len(pieces)),
        [*pieces, *mate_pieces, w, sec, lin, ends, g, r]
        + pick("z_d", "z_dt", "z_sq", "y_d", "y_dt", ("y_sq", lay.ey), "ry", "rz", "line"),
        [block, (3, cr, nz), (10, cr, nz)],
        [(2, PLANES, ny, nz)] + [pair] * 4,
    )
    from_odd = odd(msg)
    from_mate = even(from_odd)
    return tuple(
        run(
            functools.partial(third_kernel, lay),
            [from_odd, from_mate, sec, state, g] + pick("py", "pz"),
            [block, (size_x // 4, own_y // 4, nz // 4)],
        )
    )


def solution(mesh):
    dom, sub = mesh.shape["dom"], mesh.shape["sub"]
    return jax.shard_map(
        functools.partial(shards, dom, sub),
        mesh=mesh,
        in_specs=(P("dom", "sub", None), P("dom", "sub", None)),
        out_specs=(P("dom", "sub", None), P("dom", "sub", None)),
        check_vma=False,
    )
```

```python
import functools

import jax
import jax.numpy as jnp
import numpy as np
from jax import lax
from jax.experimental import pallas as pl
from jax.experimental.pallas import tpu as pltpu
from jax.sharding import PartitionSpec as P

N = 8
SPARE = 4 * N
PLANES = 4
HALO = 3 * N
THETA = 1.1
DELTA = 0.9
SIGMA = THETA / DELTA
RHO0 = 1.0 / SIGMA
RHO1 = 1.0 / (2.0 * SIGMA - RHO0)
LANES = 128
F32 = jnp.float32
BF16 = jnp.bfloat16
VMEM_LIMIT = 48 * 1024 * 1024


def legendre_value(points, degree):
    previous = np.ones(points.shape)
    current = points.copy()
    for level in range(1, degree):
        following = ((2 * level + 1) * points * current - level * previous) / (level + 1)
        previous = current
        current = following
    return current


def tables():
    degree = 7
    points = np.array(
        [
            -1.0,
            -0.8717401485096066,
            -0.5917001814331423,
            -0.2092992179024789,
            0.2092992179024789,
            0.5917001814331423,
            0.8717401485096066,
            1.0,
        ]
    )
    values = legendre_value(points, degree)
    weights = 2.0 / (degree * (degree + 1) * values**2)
    derivative = np.zeros((8, 8))
    for row_at in range(8):
        for col_at in range(8):
            if row_at != col_at:
                derivative[row_at, col_at] = values[row_at] / (
                    values[col_at] * (points[row_at] - points[col_at])
                )
    derivative[0, 0] = -degree * (degree + 1) / 4.0
    derivative[7, 7] = degree * (degree + 1) / 4.0
    interp = np.stack([(1.0 - points) / 2.0, (1.0 + points) / 2.0], axis=1)
    return derivative, weights, interp


DM, WEIGHTS, INTERP = tables()
MULT = np.array([2.0] + [1.0] * 6 + [2.0])
RHO = MULT[:, None] * INTERP
DRHO = DM @ RHO


def blockdiag(block, count):
    return np.kron(np.eye(count), block)


def hi_lo(matrix):
    hi = matrix.astype(jnp.bfloat16)
    lo = (matrix - hi.astype(np.float64)).astype(jnp.bfloat16)
    return hi, lo


def right_table(matrix):
    hi, lo = hi_lo(matrix)
    full = np.concatenate([np.concatenate([hi, hi]), np.concatenate([lo, 0 * lo])], axis=1)
    return np.stack(np.split(full, full.shape[1] // LANES, axis=1))


def left_table(matrix):
    hi, lo = hi_lo(matrix)
    return np.concatenate([hi, hi, lo], axis=1).astype(np.float32)


def vertex_table(per_node, elements, columns, count=8):
    out = np.zeros((count * elements, columns))
    for e in range(elements):
        for i in range(2):
            out[count * e : count * (e + 1), e + i] += per_node[:, i]
    return out


def moment_table(per_node, elements, columns):
    out = np.zeros((8 * elements, columns))
    for e in range(elements):
        out[8 * e : 8 * e + 8, e] = per_node
    return out


PAIRS = [(0, 0), (0, 1), (1, 1)]
MASS = [INTERP[:, i] * INTERP[:, j] for i, j in PAIRS]


def round_up(value, to):
    return -(-value // to) * to


def make_tables(ny, nz, own_y):
    ey, ez = ny // N, nz // N
    cr = round_up(ey + 1, 8)
    t = {}
    t["z_d"] = right_table(blockdiag(DM, ez).T)
    t["z_dt"] = right_table(blockdiag(DM, ez))
    t["z_sq"] = right_table(blockdiag(DM * DM, ez))
    t["y_d"] = left_table(blockdiag(DM, ey))
    t["y_dt"] = left_table(blockdiag(DM, ey).T)
    for count in [*range(1, own_y // N + 1), ey]:
        t["y_sq", count] = left_table(blockdiag(DM * DM, count).T)
        t["y_d", count] = left_table(blockdiag(DM, count))
        t["y_dt", count] = left_table(blockdiag(DM, count).T)
    py = vertex_table(RHO, ey, cr)
    dpy = blockdiag(DM, ey) @ py
    pz = vertex_table(RHO, ez, nz)
    dpz = blockdiag(DM, ez) @ pz
    zero = np.zeros_like(py)
    ry = np.concatenate([np.concatenate([py, dpy, zero]), np.concatenate([zero, zero, py])], axis=1)
    t["ry"] = np.concatenate(hi_lo(ry.T), axis=0).astype(np.float32)
    t["ry_one"] = left_table(py.T)
    t["rz"] = right_table(np.concatenate([pz, dpz], axis=0))
    t["rz_one"] = right_table(pz)
    t["my"] = left_table(np.concatenate([moment_table(m, ey, cr) for m in MASS], axis=1).T)
    t["mz"] = right_table(np.concatenate([moment_table(m, ez, nz) for m in MASS], axis=1))
    t["py"] = np.broadcast_to(INTERP.T[:, :, None], (2, N, nz)).astype(np.float32)
    pz = vertex_table(INTERP, ez, nz).T
    sz = vertex_table(np.eye(2), ez, nz, 2).T
    t["pz"] = right_table(np.concatenate([pz, sz], axis=1))
    cols = np.concatenate([DM.T, DM.T[[N - 1]], DM.T[[0]]], axis=0)
    t["line"] = np.broadcast_to(cols[:, :, None], (N + 2, N, nz)).astype(np.float32)
    w3 = WEIGHTS[:, None, None] * WEIGHTS[None, :, None] * np.ones((1, 1, nz))
    t["w3"] = (w3 * np.tile(WEIGHTS, ez)[None, None, :]).astype(np.float32)
    return t


def even_odd(matrix, values, sign):
    even = [values[b] + values[7 - b] for b in range(4)]
    odd = [values[b] - values[7 - b] for b in range(4)]
    out = [None] * 8
    for a in range(4):
        pe = po = None
        for b in range(4):
            ce = float((matrix[a, b] + matrix[a, 7 - b]) / 2.0)
            co = float((matrix[a, b] - matrix[a, 7 - b]) / 2.0)
            te = ce * even[b]
            to = co * odd[b]
            pe = te if pe is None else pe + te
            po = to if po is None else po + to
        out[a] = pe + po
        out[7 - a] = pe - po if sign > 0 else po - pe
    return out


def split(x):
    hi = x.astype(BF16)
    lo = (x - hi.astype(F32)).astype(BF16)
    return hi, lo


def dot(a, b):
    return jnp.dot(a, b, preferred_element_type=F32)


def z_apply(hi, lo, table):
    table = jnp.concatenate([table[k] for k in range(table.shape[0])], axis=1)
    both = dot(jnp.concatenate([hi, lo], axis=1), table)
    half = both.shape[1] // 2
    return both[:, :half] + both[:, half:]


def y_apply(x, table):
    hi = x.astype(BF16).astype(F32)
    parts = jnp.concatenate([hi, x - hi, hi], axis=0).astype(BF16)
    return dot(table.astype(BF16), parts)


def y_planes(get, planes, table):
    table = table.astype(BF16)
    out = {}
    for p, q in zip(planes[::2], planes[1::2]):
        both = y_apply(jnp.concatenate([get(p), get(q)], axis=1), table)
        nz = both.shape[1] // 2
        out[p], out[q] = both[:, :nz], both[:, nz:]
    return out


def assemble_yz(v):
    ny, nz = v.shape
    row = lax.broadcasted_iota(jnp.int32, (N, nz), 0)
    lane = lax.broadcasted_iota(jnp.int32, (ny, nz), 1)
    is_top = row == 0
    flip = (N - 1) - row
    blocks = [v[N * e : N * e + N] for e in range(ny // N)]
    top = (row == N - 1).astype(F32)
    bottom = (row == 0).astype(F32)
    out = []
    for e, b in enumerate(blocks):
        if len(blocks) == 1:
            out.append(b)
            continue
        if e == 0:
            near, mask = blocks[1], top
        elif e + 1 == len(blocks):
            near, mask = blocks[e - 1], bottom
        else:
            near, mask = jnp.where(is_top, blocks[e + 1], blocks[e - 1]), top + bottom
        out.append(b + mask * jnp.take_along_axis(near, flip, axis=0))
    v = jnp.concatenate(out, axis=0)
    last = (lane % N == N - 1) & (lane < nz - 1)
    first = (lane % N == 0) & (lane > 0)
    other = lane + jnp.where(last, 1, 0) - jnp.where(first, 1, 0)
    mask = (last | first).astype(F32)
    return v + mask * jnp.take_along_axis(v, other, axis=1)


def yz_mask(ny, nz, start, total):
    row = lax.broadcasted_iota(jnp.int32, (ny, nz), 0) + start
    lane = lax.broadcasted_iota(jnp.int32, (ny, nz), 1)
    return (row > 0) & (row < total - 1) & (lane > 0) & (lane < nz - 1)


class Layout:
    def __init__(self, own_y, nz, dom, sub):
        self.own_y, self.nz, self.dom, self.sub = own_y, nz, dom, sub
        self.blocks = min(sub, 3)
        self.ny = own_y + HALO * (self.blocks - 1)
        self.total_y = own_y * sub
        self.ey, self.ez = self.ny // N, nz // N
        self.cr = round_up(self.ey + 1, 8)

    def where(self):
        d = lax.axis_index("dom")
        h = lax.axis_index("sub")
        parity = lax.rem(d, 2)
        pair = lax.div(d, 2)
        if self.sub == 1:
            start, offset = 0, 0
        elif self.sub == 2:
            start, offset = h * (self.own_y - HALO), h * HALO
        else:
            start, offset = h * self.own_y - HALO, HALO
        low = (pair > 0).astype(F32)
        high = (pair < self.dom // 2 - 1).astype(F32)
        return parity, h, start, offset, low, high

    def sent_rows(self, h):
        down = self.own_y - HALO
        if self.sub == 1:
            return []
        if self.sub == 2:
            return [((1 - h) * down, (down, HALO - 1))]
        return [(down, down), (0, HALO - 1)]

    def far_rows(self, h):
        if self.sub == 1:
            return []
        if self.sub == 2:
            return [(self.ny - 1, 0)]
        return [0, self.ny - 1]

    def other_starts(self, h):
        if self.sub == 1:
            return []
        if self.sub == 2:
            return [(1 - h) * self.own_y]
        return [0, HALO + self.own_y]

    def early_rows(self, h):
        if self.sub == 1:
            return 0, self.own_y
        if self.sub == 2:
            return h * (HALO + N), self.own_y - N
        return HALO + N, self.own_y - 2 * N

    def late_starts(self, h):
        if self.sub == 1:
            return []
        if self.sub == 2:
            return [(1 - h) * (self.own_y - N)]
        size = HALO + N
        return [*range(0, self.ny - size, size), self.ny - size]

    def interfaces(self, h):
        if self.sub == 1:
            return []
        if self.sub == 2:
            return [self.own_y - h * (self.own_y - HALO)]
        return [HALO, HALO + self.own_y]


def aligned(start, size):
    return pl.ds(start if isinstance(start, int) else pl.multiple_of(start, N), size)


def gather_window(lay, own, others, h, store):
    y = lay.own_y
    if lay.sub == 1:
        store(pl.ds(0, y), own)
    elif lay.sub == 2:
        store(aligned(h * HALO, y), own)
        store(aligned((1 - h) * y, HALO), others[0])
    else:
        store(pl.ds(0, HALO), others[0])
        store(pl.ds(HALO, y), own)
        store(pl.ds(HALO + y, HALO), others[1])


PACK = 2 * N + 2 * N * HALO
CUTS = [0, 2 * N + 5 * HALO, 2 * N + 10 * HALO, PACK]


def pack_rows(side, a):
    return pl.ds(2 * N + (side * N + a) * HALO, HALO)


class Pieces:
    def __init__(self, refs):
        self.refs = refs

    def __getitem__(self, rows):
        if len(self.refs) == 1:
            return self.refs[0][rows, :]
        k = max(i for i in range(len(self.refs)) if CUTS[i] <= rows.start)
        return self.refs[k][pl.ds(rows.start - CUTS[k], rows.size), :]


def line_rows(lay, h):
    if lay.sub == 1:
        return []
    if lay.sub == 2:
        return [(lay.own_y - 1, 0)]
    return [0, lay.own_y - 1]


def load_row(field, a, row, h):
    if isinstance(row, int):
        return field[a, pl.ds(row, 1), :]
    first, second = (field[a, pl.ds(r, 1), :] for r in row)
    return jnp.where(h == 0, first, second)


def store_row(field, a, row, h, value):
    if isinstance(row, int):
        field[a, pl.ds(row, 1), :] = value
        return
    for k, r in enumerate(row):
        field[a, pl.ds(r, 1), :] = jnp.where(h == k, value, field[a, pl.ds(r, 1), :])


def line_count(lay):
    return 0 if lay.sub == 1 else 1 if lay.sub == 2 else 2


def own_kernel(lay, raw, z_sq, y_sq, w3, face, w_out, d_out, r_out, *packs):
    rhs, coef = raw.at[0], raw.at[1]
    y, nz = lay.own_y, lay.nz
    parity, h = lay.where()[:2]
    table3 = w3[...]
    for e in range(y // N):
        rows = pl.ds(N * e, N)
        w = [coef[a, rows, :] * table3[a] for a in range(N)]
        dx = even_odd((DM * DM).T, w, 1)
        for a in range(N):
            w_out[a, rows, :] = w[a]
            d_out[a, rows, :] = dx[a]
    hi, lo = split(w_out[...].reshape(N * y, nz))
    dz = z_apply(hi, lo, z_sq[...])
    dy = y_planes(lambda a: w_out[a], list(range(N)), y_sq[...])
    for a in range(N):
        d_out[a] = assemble_yz(d_out[a] + dz[a * y : (a + 1) * y] + dy[a])
        r_out[a] = assemble_yz(rhs[a])
    inner = (N - 1) * (1 - parity)
    face[0] = r_out[inner]
    face[1] = d_out[inner]
    for pack, (first, far) in zip(packs, lay.sent_rows(h)):
        for side, field in ((0, r_out), (1, d_out)):
            for a in range(N):
                pack[pack_rows(side, a), :] = raw[side, a, aligned(first, HALO), :]
                pack[pl.ds(side * N + a, 1), :] = load_row(field, a, far, h)


def message_kernel(lay, w, d, r, face, *refs):
    msg, *side_msgs, u_s, d_s, r_s = refs
    y, nz = lay.own_y, lay.nz
    parity, h, start, offset, low, high = lay.where()
    mask = yz_mask(y, nz, h * y, lay.total_y)
    scale = mask.astype(F32) * (1.0 / THETA)
    odd = parity.astype(F32)
    for a in range(N):
        dd, rr = d[a], r[a]
        keep = scale
        if a in (0, N - 1):
            inner = odd if a == 0 else 1.0 - odd
            dd = dd + inner * face[1]
            rr = rr + inner * face[0]
            keep = scale * inner
        d_s[a] = dd
        r_s[a] = rr
        u_s[a] = keep * rr / jnp.where(mask, dd, 1.0)
    col = [jnp.where(parity == 0, float(DM[a, 0]), float(DM[a, N - 1])) for a in range(N)]
    acc = []
    for e in range(y // N):
        rows = pl.ds(N * e, N)
        g = even_odd(DM, [u_s[a, rows, :] for a in range(N)], -1)
        total = None
        for a in range(N):
            term = (w[a, rows, :] * g[a]) * col[a]
            total = term if total is None else total + term
        acc.append(total)
    outer = (N - 1) * parity
    msg[pl.ds(0, y), :] = r[outer]
    msg[pl.ds(y, y), :] = d[outer]
    msg[pl.ds(2 * y, y), :] = w[outer]
    msg[pl.ds(3 * y, y), :] = assemble_yz(jnp.concatenate(acc, axis=0))
    base = PLANES * y
    for row in line_rows(lay, h):
        for field in (r_s, d_s, w):
            for a in range(N):
                msg[pl.ds(base + a, 1), :] = load_row(field, a, row, h)
            base += N
    for out, (first, _) in zip(side_msgs, lay.sent_rows(h)):
        for k in range(PLANES):
            out[pl.ds(k * HALO, HALO), :] = msg[aligned(k * y + first, HALO), :]
        lines = base - PLANES * y
        out[pl.ds(PLANES * HALO, lines), :] = msg[pl.ds(PLANES * y, lines), :]
        out[pl.ds(PLANES * HALO + lines, SPARE), :] = jnp.zeros((SPARE, nz), F32)


def flux_x(lay, u_ref, w_ref, first, count, fx):
    for el in range(2):
        for e in range(count // N):
            rows, to = aligned(first + N * e, N), pl.ds(N * e, N)
            u = [u_ref[N * el + a, rows, :] for a in range(N)]
            g = even_odd(DM, u, -1)
            for a in range(N):
                fx[N * el + a, to, :] = w_ref[N * el + a, rows, :] * g[a]


def flux_yz(lay, u_ref, w_ref, planes, first, count, z_d, y_d, fy, fz):
    part, to = aligned(first, count), pl.ds(0, count)
    u = jnp.concatenate([u_ref[p, part, :] for p in planes], axis=0)
    gz = z_apply(*split(u), z_d[...])
    gy = y_planes(lambda p: u_ref[p, part, :], planes, y_d[...])
    for k, p in enumerate(planes):
        w = w_ref[p, part, :]
        fy[p, to, :] = w * gy[p]
        fz[p, to, :] = w * gz[k * count : (k + 1) * count]


def operate(lay, u_ref, w_ref, back, first, count, tables, fx, fy, fz):
    z_d, z_dt, y_d, y_dt = tables
    nz = lay.nz
    middle = list(range(1, 2 * N - 1))
    flux_x(lay, u_ref, w_ref, first, count, fx)
    flux_yz(lay, u_ref, w_ref, middle, first, count, z_d, y_d, fy, fz)
    to, part = pl.ds(0, count), aligned(first, count)
    for el in range(2):
        for e in range(count // N):
            rows, here = aligned(first + N * e, N), pl.ds(N * e, N)
            b = even_odd(DM.T, [fx[N * el + a, here, :] for a in range(N)], -1)
            for a in range(N):
                back[N * el + a, rows, :] = b[a]
    n = len(middle)
    bz = z_apply(*split(fz[pl.ds(1, n), to, :].reshape(n * count, nz)), z_dt[...])
    by = y_planes(lambda p: fy[p, to, :], middle, y_dt[...])
    for p in middle:
        back[p, part, :] = back[p, part, :] + by[p] + bz[(p - 1) * count : p * count]


def smooth_start(lay, d, r, inv, u, first, count, start):
    part = aligned(first, count)
    mask = yz_mask(count, lay.nz, start + first, lay.total_y)
    inside = mask.astype(F32)
    zero = jnp.zeros((count, lay.nz), F32)
    for p in range(2 * N):
        if p in (0, 2 * N - 1):
            u[p, part, :] = zero
        else:
            i = inside / jnp.where(mask, d[p, part, :], 1.0)
            inv[p, part, :] = i
            u[p, part, :] = i * r[p, part, :] * (1.0 / THETA)


def sum_middle(fields, first, count):
    part = aligned(first, count)
    for s in fields:
        both = s[N - 1, part, :] + s[N, part, :]
        s[N - 1, part, :] = both
        s[N, part, :] = both


def element_sums(lay, base, parity, first, count, source, tables, outs):
    z_sq, y_sq, w3 = tables
    w_out, rhs_out, d_s, r_s, lin = outs[:5]
    nz = lay.nz
    part = aligned(first, count)
    for side, target in ((0, rhs_out), (1, w_out)):
        for a in range(N):
            target[base + a, part, :] = source(side, a)
    table3 = w3[...]
    outer = [jnp.where(parity == 0, float(DM[a, 0]), float(DM[a, N - 1])) for a in range(N)]
    for e in range(count // N):
        rows = aligned(first + N * e, N)
        w = [w_out[base + a, rows, :] * table3[a] for a in range(N)]
        dx = even_odd((DM * DM).T, w, 1)
        cx = even_odd(DM.T, [outer[a] * w[a] for a in range(N)], -1)
        for a in range(N):
            w_out[base + a, rows, :] = w[a]
            d_s[base + a, rows, :] = dx[a]
            lin[base + a, rows, :] = cx[a]
    dz = z_apply(*split(w_out[pl.ds(base, N), part, :].reshape(N * count, nz)), z_sq[...])
    dy = y_planes(lambda a: w_out[base + a, part, :], list(range(N)), y_sq[...])
    for a in range(N):
        d_local = d_s[base + a, part, :] + dz[a * count : (a + 1) * count] + dy[a]
        d_s[base + a, part, :] = assemble_yz(d_local)
        r_s[base + a, part, :] = assemble_yz(rhs_out[base + a, part, :])
        lin[base + a, part, :] = assemble_yz(lin[base + a, part, :])


def other_sums(lay, base, parity, h, pieces, tables, outs):
    d_s, r_s = outs[2:4]
    for piece, first, row in zip(pieces, lay.other_starts(h), lay.far_rows(h)):
        source = lambda side, a, piece=piece: piece[pack_rows(side, a)]
        element_sums(lay, base, parity, first, HALO, source, tables, outs)
        for side, target in ((0, r_s), (1, d_s)):
            for a in range(N):
                store_row(target, base + a, row, h, piece[pl.ds(side * N + a, 1)])


ARRAYS = 8


def early_kernel(lay, own, *refs):
    mate, refs = refs[:2], refs[2:]
    z_sq, y_sq, w3 = refs[:3]
    tables, outs, scratch = refs[3:7], refs[7 : 7 + ARRAYS], refs[7 + ARRAYS :]
    w, _, d, r, _, inv, u, back = outs
    parity, h, start, offset, low, high = lay.where()
    own = (own.at[0], own.at[1])
    for base, el, block in ((parity * N, parity, own), ((1 - parity) * N, 1 - parity, mate)):
        source = lambda side, a, block=block: block[side][a]
        element_sums(lay, base, el, offset, lay.own_y, source, (z_sq, y_sq, w3), outs)
    sum_middle((d, r), offset, lay.own_y)
    smooth_start(lay, d, r, inv, u, offset, lay.own_y, start)
    first, count = lay.early_rows(h)
    operate(lay, u, w, back, first, count, tables, *scratch)


def near_kernel(lay, n_other, *refs):
    other, tables = refs[:n_other], refs[n_other : n_other + 3]
    outs = refs[n_other + 3 + ARRAYS :]
    parity, h = lay.where()[:2]
    other_sums(lay, parity * N, parity, h, [Pieces([o]) for o in other], tables, outs)


def deep_kernel(lay, n_other, *refs):
    cuts = len(CUTS) - 1
    mate_other = [Pieces(refs[cuts * k : cuts * (k + 1)]) for k in range(n_other)]
    refs = refs[cuts * n_other :]
    z_sq, y_sq, w3 = refs[:3]
    tables = refs[3:7]
    refs = refs[7 + ARRAYS :]
    outs, sec_out, ends = refs[:ARRAYS], refs[ARRAYS], refs[ARRAYS + 1]
    scratch = refs[ARRAYS + 2 :]
    w, _, d, r, lin, inv, u, back = outs
    last = 2 * N - 1
    parity, h, start, offset, low, high = lay.where()
    other_sums(lay, (1 - parity) * N, 1 - parity, h, mate_other, (z_sq, y_sq, w3), outs)
    for first in lay.other_starts(h):
        sum_middle((d, r), first, HALO)
    for begin in lay.interfaces(h):
        above, below = pl.ds(begin - 1, 1), pl.ds(begin, 1)
        for s in (d, r, lin):
            for p in range(2 * N):
                both = s[p, above, :] + s[p, below, :]
                s[p, above, :] = both
                s[p, below, :] = both
    for side, p in ((0, 0), (1, last)):
        ends[side, 0] = r[p]
        ends[side, 1] = d[p]
    for first in lay.late_starts(h):
        smooth_start(lay, d, r, inv, u, first, HALO + N, start)
        operate(lay, u, w, back, first, HALO + N, tables, *scratch)
    for p in range(1, last):
        back[p] = assemble_yz(back[p])
    sum_middle((back,), 0, lay.ny)
    for p in range(2 * N):
        if p in (0, last):
            sec_out[p] = assemble_yz(back[p])
        else:
            i = (2.0 * RHO1 / DELTA) * inv[p]
            lin[p] = -i * lin[p]
            sec_out[p] = (1.0 + RHO1 * RHO0) * u[p] + i * (r[p] - back[p])


def coarse_tables_kernel(lay, w_ref, rhs_ref, my, mz, ry, rz, g_out, r_out):
    ny, nz, cr = lay.ny, lay.nz, lay.cr
    lhs = []
    for el in range(2):
        for m in MASS:
            total = None
            for a in range(N):
                term = float(m[a]) * w_ref[N * el + a]
                total = term if total is None else total + term
            lhs.append(total)
    along_z = z_apply(*split(jnp.concatenate(lhs, axis=0)), mz[...])
    for el in range(2):
        mom = {}
        for alpha in range(3):
            at = (3 * el + alpha) * ny
            block = y_apply(along_z[at : at + ny], my[...])
            for beta in range(3):
                for gamma in range(3):
                    mom[alpha, beta, gamma] = block[
                        beta * cr : (beta + 1) * cr, gamma * nz : (gamma + 1) * nz
                    ]
        x_sum, y_sum, z_sum = {}, {}, {}
        for i in range(3):
            for j in range(3):
                x_sum[i, j] = mom[0, i, j] + 2.0 * mom[1, i, j] + mom[2, i, j]
                y_sum[i, j] = mom[i, 0, j] + 2.0 * mom[i, 1, j] + mom[i, 2, j]
                z_sum[i, j] = mom[i, j, 0] + 2.0 * mom[i, j, 1] + mom[i, j, 2]
        sign = (1.0, -1.0, 1.0)
        for alpha in range(3):
            for beta in range(3):
                for gamma in range(3):
                    g_out[el, 9 * alpha + 3 * beta + gamma] = 0.25 * (
                        sign[alpha] * x_sum[beta, gamma]
                        + sign[beta] * y_sum[alpha, gamma]
                        + sign[gamma] * z_sum[alpha, beta]
                    )
    sums = []
    for el in range(2):
        for i in range(2):
            total = None
            for a in range(N):
                term = float(RHO[a, i]) * rhs_ref[N * el + a]
                total = term if total is None else total + term
            sums.append(total)
    part = y_apply(jnp.concatenate(sums, axis=1), ry[...])
    rows = jnp.concatenate([part[:, k * nz : (k + 1) * nz] for k in range(4)], axis=0)
    full = z_apply(*split(rows), rz[...])
    for k in range(4):
        r_out[k] = full[k * cr : (k + 1) * cr]


def pair_index(i, j):
    return i + j


def shifted(c, q, r):
    if q:
        c = pltpu.roll(c, c.shape[0] - 1, 0)
    if r:
        c = pltpu.roll(c, c.shape[1] - 1, 1)
    return c


def scatter(parts):
    cr, nz = parts[0, 0].shape
    first = parts[0, 0] + pltpu.roll(parts[0, 1], 1, 1)
    second = parts[1, 0] + pltpu.roll(parts[1, 1], 1, 1)
    return first + pltpu.roll(second, 1, 0)


def gathered(c):
    return {(q, r): shifted(c, q, r) for q in range(2) for r in range(2)}


def face_apply(entry, c, out=None):
    out = {} if out is None else out
    for j in range(2):
        for k in range(2):
            for q in range(2):
                for r in range(2):
                    term = entry(pair_index(j, q), pair_index(k, r)) * c[q, r]
                    out[j, k] = term if (j, k) not in out else out[j, k] + term
    return out


def coarse_diag(entry):
    return scatter({(j, k): entry(2 * j, 2 * k) for j in range(2) for k in range(2)})


def coarse_mask(lay, start):
    row = lax.broadcasted_iota(jnp.int32, (lay.cr, lay.nz), 0) + lax.div(start, N)
    lane = lax.broadcasted_iota(jnp.int32, (lay.cr, lay.nz), 1)
    return (row > 0) & (row < lay.total_y // N) & (lane > 0) & (lane < lay.ez)


def unpack_sides(lay, pieces, mate_pieces, line, parity, h, start, win):
    y, nz = lay.own_y, lay.nz
    for side, group in ((parity, pieces), (1 - parity, mate_pieces)):
        for k in range(PLANES):

            def put(rows, value):
                win[side, k, rows, :] = value

            others = [g[pl.ds(k * HALO, HALO), :] for g in group[1:]]
            gather_window(lay, group[0][pl.ds(k * y, y), :], others, h, put)
    is_even = parity == 0
    lane = lax.broadcasted_iota(jnp.int32, (N, nz), 1)
    node = lax.broadcasted_iota(jnp.int32, (N, nz), 0)
    lane_in = (lane > 0) & (lane < nz - 1)
    flank = lax.broadcasted_iota(jnp.int32, (1, nz), 1)
    last = ((flank % N == N - 1) & (flank < nz - 1)).astype(F32)
    first = ((flank % N == 0) & (flank > 0)).astype(F32)
    for b, begin in enumerate(lay.interfaces(h), 1):
        above, below = pl.ds(begin - 1, 1), pl.ds(begin, 1)
        for side in range(2):
            for k in range(2):
                both = win[side, k, above, :] + win[side, k, below, :]
                win[side, k, above, :] = both
                win[side, k, below, :] = both
        for side in range(2):
            outer = N - 1 if side == 0 else 0

            def field(k):
                def of(group):
                    own_lines, other_lines = PLANES * y + k * N, PLANES * HALO + k * N
                    if lay.sub == 2:
                        mine, theirs = own_lines, other_lines
                        near = group[1]
                    else:
                        mine = own_lines + 3 * N * (b - 1)
                        theirs = other_lines + 3 * N * (2 - b)
                        near = group[b]
                    return group[0][pl.ds(mine, N), :] + near[pl.ds(theirs, N), :]
                mine, theirs = of(pieces), of(mate_pieces)
                if side == 0:
                    return jnp.where(is_even, mine, theirs)
                return jnp.where(is_even, theirs, mine)

            r, d, w = field(0), field(1), field(2)
            row = start + begin
            ok = lane_in & (node != outer) & (row > 0) & (row < lay.total_y)
            u = jnp.where(ok, r / jnp.where(ok, d, 1.0) * (1.0 / THETA), 0.0)
            g = None
            for a in range(N):
                term = line[a] * u[a : a + 1]
                g = term if g is None else g + term
            total = jnp.sum(line[N + side] * (w * g), axis=0, keepdims=True)
            total = total + last * pltpu.roll(total, nz - 1, 1) + first * pltpu.roll(total, 1, 1)
            win[side, 3, above, :] = total
            win[side, 3, below, :] = total


def second_kernel(lay, n_pieces, *refs):
    pieces, mate_pieces = refs[:n_pieces], refs[n_pieces : 2 * n_pieces]
    w_ref, sec_in, lin_in, ends, g_ref, r_ref = refs[2 * n_pieces : 2 * n_pieces + 6]
    refs = refs[2 * n_pieces + 6 :]
    z_d, z_dt, z_sq, y_d, y_dt, y_sq, ry, rz, line = refs[:9]
    out, msg, state = refs[9:12]
    win, sec, fx, fy, fz = refs[12:]
    ny, nz, cr = lay.ny, lay.nz, lay.cr
    last = 2 * N - 1
    parity, h, start, offset, low, high = lay.where()
    mask = yz_mask(ny, nz, start, lay.total_y)
    inside = mask.astype(F32)
    is_even = parity == 0
    unpack_sides(lay, pieces, mate_pieces, line, parity, h, start, win)
    flags = (low, high)
    inv, res, u = [], [], []
    for side in range(2):
        valid = inside * flags[side]
        inv.append(valid / jnp.where(mask, ends[side, 1] + win[side, 1], 1.0))
        res.append(valid * (ends[side, 0] + win[side, 0]))
        u.append(inv[side] * res[side] * (1.0 / THETA))
    for p in range(1, last):
        value = sec_in[p]
        if p <= N:
            value = value + lin_in[min(p, N - 1)] * u[0]
        if p >= N - 1:
            value = value + lin_in[max(p, N)] * u[1]
        sec[p] = value
    flux_yz(lay, sec, w_ref, list(range(1, last)), 0, ny, z_d, y_d, fy, fz)
    weights = [w_ref[0] + win[0, 2], w_ref[last] + win[1, 2]]
    hi, lo = split(jnp.concatenate(u, axis=0))
    gz = z_apply(hi, lo, z_d[...])
    gy = y_apply(jnp.concatenate(u, axis=1), y_d[...])
    weight_z = jnp.concatenate(weights, axis=0)
    weight_y = jnp.concatenate(weights, axis=1)
    bz = z_apply(*split(weight_z * gz), z_dt[...])
    by = y_apply(weight_y * gy, y_dt[...])
    dz = z_apply(*split(jnp.concatenate([win[0, 2], win[1, 2]], axis=0)), z_sq[...])
    dy = y_planes(lambda side: win[side, 2], [0, 1], y_sq[...])
    dx = [
        win[side, 1] - assemble_yz(dz[side * ny : (side + 1) * ny] + dy[side]) for side in range(2)
    ]
    for side, p in ((0, 0), (1, last)):
        plane = assemble_yz(bz[side * ny : (side + 1) * ny] + by[:, side * nz : (side + 1) * nz])
        plane = plane + sec_in[p] + win[side, 3] + (lin_in[p] + dx[side]) * u[side]
        res_one = res[side] - inside * plane
        sec[p] = (1.0 + RHO1 * RHO0) * u[side] + (2.0 * RHO1 / DELTA) * inv[side] * res_one
    out[...] = sec[pl.ds(parity * N, N), pl.ds(pl.multiple_of(offset, N), lay.own_y), :]
    flux_yz(lay, sec, w_ref, [0, last], 0, ny, z_d, y_d, fy, fz)
    flux_x(lay, sec, w_ref, 0, ny, fx)
    sums = []
    for f, weight in ((fx, DRHO), (fy, RHO), (fz, RHO)):
        lanes = []
        for el in range(2):
            for i in range(2):
                total = None
                for a in range(N):
                    term = float(weight[a, i]) * f[N * el + a]
                    total = term if total is None else total + term
                lanes.append(total)
        sums.append(jnp.concatenate(lanes, axis=1))
    data = jnp.concatenate(sums, axis=0)
    hi = data.astype(BF16).astype(F32)
    parts = jnp.concatenate([hi, data - hi], axis=1).astype(BF16)
    both = dot(ry[...].astype(BF16), parts)
    both = both[: 2 * cr, : 4 * nz] + both[2 * cr :, : 4 * nz] + both[: 2 * cr, 4 * nz :]
    rows = [
        jnp.concatenate([v[:, k * nz : (k + 1) * nz] for v in (both[:cr], both[cr:])], axis=1)
        for k in range(4)
    ]
    full = z_apply(*split(jnp.concatenate(rows, axis=0)), rz[...])
    r = {}
    for el in range(2):
        for i in range(2):
            k = 2 * el + i
            r[el, i] = r_ref[k] - full[k * cr : (k + 1) * cr]
    planes = [r[0, 0], r[0, 1] + r[1, 0], r[1, 1]]
    cmask = coarse_mask(lay, start)

    def entry(el, alpha):
        return lambda beta, gamma: g_ref[el, 9 * alpha + 3 * beta + gamma]

    d = [
        coarse_diag(entry(0, 0)),
        coarse_diag(entry(0, 2)) + coarse_diag(entry(1, 0)),
        coarse_diag(entry(1, 2)),
    ]
    cin = cmask.astype(F32)
    mid = (2.0 / 3.0) * cin * planes[1] / jnp.where(cmask, d[1], 1.0)
    c = gathered(mid)
    g_low = scatter(face_apply(entry(0, 1), c))
    g_high = scatter(face_apply(entry(1, 1), c))
    g_mid = scatter(face_apply(entry(1, 0), c, face_apply(entry(0, 2), c)))
    state[0] = planes[0]
    state[1] = planes[1]
    state[2] = planes[2]
    state[3] = d[0]
    state[4] = d[1]
    state[5] = d[2]
    state[6] = g_low
    state[7] = g_mid
    state[8] = g_high
    state[9] = mid
    send = [
        jnp.where(is_even, planes[0], planes[2]),
        jnp.where(is_even, d[0], d[2]),
        jnp.where(is_even, g_low, g_high),
    ]
    send += [jnp.where(is_even, g_ref[0, k], g_ref[1, 18 + k]) for k in range(9)]
    for k in range(3):
        packed = send[4 * k]
        for q in range(1, 4):
            packed = packed + pltpu.roll(send[4 * k + q], q * (nz // 4), 1)
        msg[k] = packed


def third_kernel(lay, *refs):
    own_msg, mate_msg, sec, state, g_ref, py, pz, out, coarse = refs
    ny, nz, cr = lay.ny, lay.nz, lay.cr
    parity, h, start, offset, low, high = lay.where()
    is_even = parity == 0
    cmask = coarse_mask(lay, start)
    cin = cmask.astype(F32)
    lo_msg, hi_msg = [], []
    for k in range(3):
        mine, theirs = own_msg[k], mate_msg[k]
        for target, packed in (
            (lo_msg, jnp.where(is_even, mine, theirs)),
            (hi_msg, jnp.where(is_even, theirs, mine)),
        ):
            target.append(packed)
            for q in range(1, 4):
                target.append(pltpu.roll(packed, nz - q * (nz // 4), 1))

    def entry(el, alpha):
        return lambda beta, gamma: g_ref[el, 9 * alpha + 3 * beta + gamma]

    def outer(at, m, flag, el, alpha):
        rhs = cin * flag * (state[at] + m[0])
        d = jnp.where(cmask, state[3 + at] + m[1], 1.0)
        one = (2.0 / 3.0) * rhs / d
        c = gathered(one)
        here = lambda beta, gamma: g_ref[el, 9 * alpha + 3 * beta + gamma] + m[3 + 3 * beta + gamma]
        image = scatter(face_apply(here, c)) + state[6 + at] + m[2]
        cross = face_apply(entry(el, 1), c)
        solution = one + (2.0 / 3.0) * (rhs - cin * flag * image) / d
        return solution, cross

    c_low, cross_low = outer(0, lo_msg, low, 0, 0)
    c_high, cross_high = outer(2, hi_msg, high, 1, 2)
    cross = scatter({k: cross_low[k] + cross_high[k] for k in cross_low})
    rhs = cin * state[1]
    d = jnp.where(cmask, state[4], 1.0)
    c_mid = state[9] + (2.0 / 3.0) * (rhs - cin * (state[7] + cross)) / d
    left = jnp.where(is_even, c_low, c_mid)
    right = jnp.where(is_even, c_mid, c_high)
    both = jnp.concatenate([left, right], axis=0)
    full = z_apply(*split(both), pz[...])
    y = lay.own_y
    mask = yz_mask(y, nz, start + offset, lay.total_y).astype(F32)
    weight = [jnp.broadcast_to(py[i], (N, nz)) for i in range(2)]
    q = []
    for side in range(2):
        rows = full[side * cr : (side + 1) * cr]
        if lay.sub > 1:
            rows = pltpu.roll(rows, cr - lax.div(offset, N), 0)
        blocks = []
        for e in range(y // N):
            at = [rows[e + i : e + i + 1] for i in range(2)]
            blocks.append(weight[0] * at[0][:, :nz] + weight[1] * at[1][:, :nz])
            for i in range(2):
                coarse[side, pl.ds(2 * e + i, 1), :] = at[i][:, nz : nz + nz // 4]
        q.append(mask * jnp.concatenate(blocks, axis=0))
    q_left, q_right = q
    first_flag = jnp.where(is_even, low, 1.0)
    last_flag = jnp.where(is_even, 1.0, high)
    for a in range(N):
        add = float(INTERP[a, 0]) * q_left + float(INTERP[a, 1]) * q_right
        if a == 0:
            add = first_flag * add
        if a == N - 1:
            add = last_flag * add
        out[a] = sec[a] + add


def run(kernel, args, outs, scratch=(), aliases={}):
    return pl.pallas_call(
        kernel,
        out_shape=[jax.ShapeDtypeStruct(o, F32) for o in outs],
        in_specs=[pl.BlockSpec(memory_space=pltpu.VMEM)] * len(args),
        out_specs=[pl.BlockSpec(memory_space=pltpu.VMEM)] * len(outs),
        scratch_shapes=[pltpu.VMEM(s, F32) for s in scratch],
        compiler_params=pltpu.CompilerParams(vmem_limit_bytes=VMEM_LIMIT),
        input_output_aliases=aliases,
        cost_estimate=pl.CostEstimate(flops=1, bytes_accessed=1, transcendentals=0),
    )(*args)


def swap_pairs(count, first):
    pairs = []
    for i in range(first, count - 1, 2):
        pairs += [(i, i + 1), (i + 1, i)]
    return pairs


def chip_pairs(dom, sub, shift):
    pairs = []
    for a, b in swap_pairs(dom, 1):
        for q in range(sub):
            to = (q + shift) % sub if sub == 2 else q + shift
            if 0 <= to < sub:
                pairs.append((a * sub + q, b * sub + to))
    for end in (0, dom - 1):
        pairs += [(end * sub + a, end * sub + b) for a, b in swap_pairs(sub, 0)]
    return pairs


def shards(dom, sub, rhs_local, coefficient):
    size_x, own_y, nz = rhs_local.shape
    assert size_x == N and dom % 2 == 0 and (sub == 1 or own_y > HALO)
    lay = Layout(own_y, nz, dom, sub)
    ny, cr = lay.ny, lay.cr
    t = {k: jnp.asarray(v) for k, v in make_tables(ny, nz, own_y).items()}
    pick = lambda *names: [t[k] for k in names]
    even = lambda v: lax.ppermute(v, "dom", swap_pairs(dom, 0))
    odd = lambda v, k=0: lax.ppermute(v, ("dom", "sub"), chip_pairs(dom, sub, k))
    block = (N, own_y, nz)
    raw = jnp.stack([rhs_local, coefficient])
    n_other = 0 if sub == 1 else 1 if sub == 2 else 2
    face, w, d, r, *packs = run(
        functools.partial(own_kernel, lay),
        [raw, t["z_sq"], t["y_sq", own_y // N], t["w3"]],
        [(2, own_y, nz), block, block, block]
        + [(PACK, nz)] * n_other,
    )
    mate_face = even(face)
    if sub == 1:
        steps = []
    elif sub == 2:
        steps = [[(0, 1), (1, 0)]]
    else:
        up = [(i, i + 1) for i in range(sub - 1)]
        steps = [up, [(b, a) for a, b in up]]
    others = [lax.ppermute(pack, "sub", step) for pack, step in zip(packs, steps)]
    raw_later = lax.optimization_barrier((raw, face))[0]
    mate = [even(raw_later[side]) for side in range(2)]
    lines = 3 * N * line_count(lay)
    msgs = run(
        functools.partial(message_kernel, lay),
        [w, d, r, mate_face],
        [(PLANES * own_y + lines, nz)] + [(PLANES * HALO + lines + SPARE, nz)] * n_other,
        [block] * 3,
    )
    shifts = [0] if sub == 1 else [0, 1] if sub == 2 else [0, 1, -1]
    pieces = [odd(msg, k) for msg, k in zip(msgs, shifts)]
    pair = (2 * N, ny, nz)
    count = lay.early_rows(0)[1] // N
    arrays = run(
        functools.partial(early_kernel, lay),
        [raw, *mate, t["z_sq"], t["y_sq", own_y // N], t["w3"]]
        + [t["z_d"], t["z_dt"], t["y_d", count], t["y_dt", count]],
        [pair] * ARRAYS,
        [(2 * N, count * N, nz)] * 3,
    )
    others, arrays = lax.optimization_barrier((others, arrays))
    mate_others = [even(o[a:b]) for o in others for a, b in zip(CUTS, CUTS[1:])]
    arrays = run(
        functools.partial(near_kernel, lay, n_other),
        [*others, t["z_sq"], t["y_sq", HALO // N], t["w3"], *arrays],
        [pair] * ARRAYS,
        (),
        {n_other + 3 + k: k for k in range(ARRAYS)},
    )
    pieces[0], arrays = lax.optimization_barrier((pieces[0], arrays))
    late = lambda *names: [t[k, HALO // N + 1] for k in names]
    sums = [t["z_sq"], t["y_sq", HALO // N], t["w3"]]
    w, rhs, _, _, lin, _, _, _, sec, ends = run(
        functools.partial(deep_kernel, lay, n_other),
        [*mate_others, *sums, t["z_d"], t["z_dt"], *late("y_d", "y_dt"), *arrays],
        [pair] * (ARRAYS + 1) + [(2, 2, ny, nz)],
        [(2 * N, HALO + N, nz)] * 3,
        {len(mate_others) + 7 + k: k for k in range(ARRAYS)},
    )
    later, sec = lax.optimization_barrier((pieces[1:], sec))
    pieces = pieces[:1] + later
    mate_pieces = [even(p) for p in pieces]
    g, r = run(
        functools.partial(coarse_tables_kernel, lay),
        [w, rhs] + pick("my", "mz", "ry_one", "rz_one"),
        [(2, 27, cr, nz), (4, cr, nz)],
    )
    sec, msg, state = run(
        functools.partial(second_kernel, lay, len(pieces)),
        [*pieces, *mate_pieces, w, sec, lin, ends, g, r]
        + pick("z_d", "z_dt", "z_sq", "y_d", "y_dt", ("y_sq", lay.ey), "ry", "rz", "line"),
        [block, (3, cr, nz), (10, cr, nz)],
        [(2, PLANES, ny, nz)] + [pair] * 4,
    )
    from_odd = odd(msg)
    from_mate = even(from_odd)
    return tuple(
        run(
            functools.partial(third_kernel, lay),
            [from_odd, from_mate, sec, state, g] + pick("py", "pz"),
            [block, (size_x // 4, own_y // 4, nz // 4)],
        )
    )


def solution(mesh):
    dom, sub = mesh.shape["dom"], mesh.shape["sub"]
    return jax.shard_map(
        functools.partial(shards, dom, sub),
        mesh=mesh,
        in_specs=(P("dom", "sub", None), P("dom", "sub", None)),
        out_specs=(P("dom", "sub", None), P("dom", "sub", None)),
        check_vma=False,
    )
```

```python
import functools

import jax
import jax.numpy as jnp
import numpy as np
from jax import lax
from jax.experimental import pallas as pl
from jax.experimental.pallas import tpu as pltpu
from jax.sharding import PartitionSpec as P

N = 8
SPARE = 4 * N
PLANES = 4
HALO = 3 * N
THETA = 1.1
DELTA = 0.9
SIGMA = THETA / DELTA
RHO0 = 1.0 / SIGMA
RHO1 = 1.0 / (2.0 * SIGMA - RHO0)
LANES = 128
F32 = jnp.float32
BF16 = jnp.bfloat16
VMEM_LIMIT = 24 * 1024 * 1024


def legendre_value(points, degree):
    previous = np.ones(points.shape)
    current = points.copy()
    for level in range(1, degree):
        following = ((2 * level + 1) * points * current - level * previous) / (level + 1)
        previous = current
        current = following
    return current


def tables():
    degree = 7
    points = np.array(
        [
            -1.0,
            -0.8717401485096066,
            -0.5917001814331423,
            -0.2092992179024789,
            0.2092992179024789,
            0.5917001814331423,
            0.8717401485096066,
            1.0,
        ]
    )
    values = legendre_value(points, degree)
    weights = 2.0 / (degree * (degree + 1) * values**2)
    derivative = np.zeros((8, 8))
    for row_at in range(8):
        for col_at in range(8):
            if row_at != col_at:
                derivative[row_at, col_at] = values[row_at] / (
                    values[col_at] * (points[row_at] - points[col_at])
                )
    derivative[0, 0] = -degree * (degree + 1) / 4.0
    derivative[7, 7] = degree * (degree + 1) / 4.0
    interp = np.stack([(1.0 - points) / 2.0, (1.0 + points) / 2.0], axis=1)
    return derivative, weights, interp


DM, WEIGHTS, INTERP = tables()
MULT = np.array([2.0] + [1.0] * 6 + [2.0])
RHO = MULT[:, None] * INTERP
DRHO = DM @ RHO


def blockdiag(block, count):
    return np.kron(np.eye(count), block)


def hi_lo(matrix):
    hi = matrix.astype(jnp.bfloat16)
    lo = (matrix - hi.astype(np.float64)).astype(jnp.bfloat16)
    return hi, lo


def right_table(matrix):
    hi, lo = hi_lo(matrix)
    full = np.concatenate([np.concatenate([hi, hi]), np.concatenate([lo, 0 * lo])], axis=1)
    return np.stack(np.split(full, full.shape[1] // LANES, axis=1))


def left_table(matrix):
    hi, lo = hi_lo(matrix)
    return np.concatenate([hi, hi, lo], axis=1).astype(np.float32)


def vertex_table(per_node, elements, columns, count=8):
    out = np.zeros((count * elements, columns))
    for e in range(elements):
        for i in range(2):
            out[count * e : count * (e + 1), e + i] += per_node[:, i]
    return out


def moment_table(per_node, elements, columns):
    out = np.zeros((8 * elements, columns))
    for e in range(elements):
        out[8 * e : 8 * e + 8, e] = per_node
    return out


PAIRS = [(0, 0), (0, 1), (1, 1)]
MASS = [INTERP[:, i] * INTERP[:, j] for i, j in PAIRS]


def round_up(value, to):
    return -(-value // to) * to


def make_tables(ny, nz, own_y):
    ey, ez = ny // N, nz // N
    cr = round_up(ey + 1, 8)
    t = {}
    t["z_d"] = right_table(blockdiag(DM, ez).T)
    t["z_dt"] = right_table(blockdiag(DM, ez))
    t["z_sq"] = right_table(blockdiag(DM * DM, ez))
    t["y_d"] = left_table(blockdiag(DM, ey))
    t["y_dt"] = left_table(blockdiag(DM, ey).T)
    for count in [*range(1, own_y // N + 1), ey]:
        t["y_sq", count] = left_table(blockdiag(DM * DM, count).T)
        t["y_d", count] = left_table(blockdiag(DM, count))
        t["y_dt", count] = left_table(blockdiag(DM, count).T)
    py = vertex_table(RHO, ey, cr)
    dpy = blockdiag(DM, ey) @ py
    pz = vertex_table(RHO, ez, nz)
    dpz = blockdiag(DM, ez) @ pz
    zero = np.zeros_like(py)
    ry = np.concatenate([np.concatenate([py, dpy, zero]), np.concatenate([zero, zero, py])], axis=1)
    t["ry"] = np.concatenate(hi_lo(ry.T), axis=0).astype(np.float32)
    t["ry_one"] = left_table(py.T)
    t["rz"] = right_table(np.concatenate([pz, dpz], axis=0))
    t["rz_one"] = right_table(pz)
    t["my"] = left_table(np.concatenate([moment_table(m, ey, cr) for m in MASS], axis=1).T)
    t["mz"] = right_table(np.concatenate([moment_table(m, ez, nz) for m in MASS], axis=1))
    t["py"] = np.broadcast_to(INTERP.T[:, :, None], (2, N, nz)).astype(np.float32)
    pz = vertex_table(INTERP, ez, nz).T
    sz = vertex_table(np.eye(2), ez, nz, 2).T
    t["pz"] = right_table(np.concatenate([pz, sz], axis=1))
    cols = np.concatenate([DM.T, DM.T[[N - 1]], DM.T[[0]]], axis=0)
    t["line"] = np.broadcast_to(cols[:, :, None], (N + 2, N, nz)).astype(np.float32)
    w3 = WEIGHTS[:, None, None] * WEIGHTS[None, :, None] * np.ones((1, 1, nz))
    t["w3"] = (w3 * np.tile(WEIGHTS, ez)[None, None, :]).astype(np.float32)
    return t


def even_odd(matrix, values, sign):
    even = [values[b] + values[7 - b] for b in range(4)]
    odd = [values[b] - values[7 - b] for b in range(4)]
    out = [None] * 8
    for a in range(4):
        pe = po = None
        for b in range(4):
            ce = float((matrix[a, b] + matrix[a, 7 - b]) / 2.0)
            co = float((matrix[a, b] - matrix[a, 7 - b]) / 2.0)
            te = ce * even[b]
            to = co * odd[b]
            pe = te if pe is None else pe + te
            po = to if po is None else po + to
        out[a] = pe + po
        out[7 - a] = pe - po if sign > 0 else po - pe
    return out


def split(x):
    hi = x.astype(BF16)
    lo = (x - hi.astype(F32)).astype(BF16)
    return hi, lo


def dot(a, b):
    return jnp.dot(a, b, preferred_element_type=F32)


def z_apply(hi, lo, table):
    table = jnp.concatenate([table[k] for k in range(table.shape[0])], axis=1)
    both = dot(jnp.concatenate([hi, lo], axis=1), table)
    half = both.shape[1] // 2
    return both[:, :half] + both[:, half:]


def y_apply(x, table):
    hi = x.astype(BF16).astype(F32)
    parts = jnp.concatenate([hi, x - hi, hi], axis=0).astype(BF16)
    return dot(table.astype(BF16), parts)


def y_planes(get, planes, table):
    table = table.astype(BF16)
    out = {}
    for p, q in zip(planes[::2], planes[1::2]):
        both = y_apply(jnp.concatenate([get(p), get(q)], axis=1), table)
        nz = both.shape[1] // 2
        out[p], out[q] = both[:, :nz], both[:, nz:]
    return out


def assemble_yz(v):
    ny, nz = v.shape
    row = lax.broadcasted_iota(jnp.int32, (N, nz), 0)
    lane = lax.broadcasted_iota(jnp.int32, (ny, nz), 1)
    is_top = row == 0
    flip = (N - 1) - row
    blocks = [v[N * e : N * e + N] for e in range(ny // N)]
    top = (row == N - 1).astype(F32)
    bottom = (row == 0).astype(F32)
    out = []
    for e, b in enumerate(blocks):
        if len(blocks) == 1:
            out.append(b)
            continue
        if e == 0:
            near, mask = blocks[1], top
        elif e + 1 == len(blocks):
            near, mask = blocks[e - 1], bottom
        else:
            near, mask = jnp.where(is_top, blocks[e + 1], blocks[e - 1]), top + bottom
        out.append(b + mask * jnp.take_along_axis(near, flip, axis=0))
    v = jnp.concatenate(out, axis=0)
    last = (lane % N == N - 1) & (lane < nz - 1)
    first = (lane % N == 0) & (lane > 0)
    other = lane + jnp.where(last, 1, 0) - jnp.where(first, 1, 0)
    mask = (last | first).astype(F32)
    return v + mask * jnp.take_along_axis(v, other, axis=1)


def yz_mask(ny, nz, start, total):
    row = lax.broadcasted_iota(jnp.int32, (ny, nz), 0) + start
    lane = lax.broadcasted_iota(jnp.int32, (ny, nz), 1)
    return (row > 0) & (row < total - 1) & (lane > 0) & (lane < nz - 1)


class Layout:
    def __init__(self, own_y, nz, dom, sub):
        self.own_y, self.nz, self.dom, self.sub = own_y, nz, dom, sub
        self.blocks = min(sub, 3)
        self.ny = own_y + HALO * (self.blocks - 1)
        self.total_y = own_y * sub
        self.ey, self.ez = self.ny // N, nz // N
        self.cr = round_up(self.ey + 1, 8)

    def where(self):
        d = lax.axis_index("dom")
        h = lax.axis_index("sub")
        parity = lax.rem(d, 2)
        pair = lax.div(d, 2)
        if self.sub == 1:
            start, offset = 0, 0
        elif self.sub == 2:
            start, offset = h * (self.own_y - HALO), h * HALO
        else:
            start, offset = h * self.own_y - HALO, HALO
        low = (pair > 0).astype(F32)
        high = (pair < self.dom // 2 - 1).astype(F32)
        return parity, h, start, offset, low, high

    def sent_rows(self, h):
        down = self.own_y - HALO
        if self.sub == 1:
            return []
        if self.sub == 2:
            return [((1 - h) * down, (down, HALO - 1))]
        return [(down, down), (0, HALO - 1)]

    def far_rows(self, h):
        if self.sub == 1:
            return []
        if self.sub == 2:
            return [(self.ny - 1, 0)]
        return [0, self.ny - 1]

    def other_starts(self, h):
        if self.sub == 1:
            return []
        if self.sub == 2:
            return [(1 - h) * self.own_y]
        return [0, HALO + self.own_y]

    def early_rows(self, h):
        if self.sub == 1:
            return 0, self.own_y
        if self.sub == 2:
            return h * (HALO + N), self.own_y - N
        return HALO + N, self.own_y - 2 * N

    def late_starts(self, h):
        if self.sub == 1:
            return []
        if self.sub == 2:
            return [(1 - h) * (self.own_y - N)]
        size = HALO + N
        return [*range(0, self.ny - size, size), self.ny - size]

    def interfaces(self, h):
        if self.sub == 1:
            return []
        if self.sub == 2:
            return [self.own_y - h * (self.own_y - HALO)]
        return [HALO, HALO + self.own_y]


def aligned(start, size):
    return pl.ds(start if isinstance(start, int) else pl.multiple_of(start, N), size)


def gather_window(lay, own, others, h, store):
    y = lay.own_y
    if lay.sub == 1:
        store(pl.ds(0, y), own)
    elif lay.sub == 2:
        store(aligned(h * HALO, y), own)
        store(aligned((1 - h) * y, HALO), others[0])
    else:
        store(pl.ds(0, HALO), others[0])
        store(pl.ds(HALO, y), own)
        store(pl.ds(HALO + y, HALO), others[1])


PACK = 2 * N + 2 * N * HALO
CUTS = [0, 2 * N + 5 * HALO, 2 * N + 10 * HALO, PACK]


def pack_rows(side, a):
    return pl.ds(2 * N + (side * N + a) * HALO, HALO)


class Pieces:
    def __init__(self, refs):
        self.refs = refs

    def __getitem__(self, rows):
        if len(self.refs) == 1:
            return self.refs[0][rows, :]
        k = max(i for i in range(len(self.refs)) if CUTS[i] <= rows.start)
        return self.refs[k][pl.ds(rows.start - CUTS[k], rows.size), :]


def line_rows(lay, h):
    if lay.sub == 1:
        return []
    if lay.sub == 2:
        return [(lay.own_y - 1, 0)]
    return [0, lay.own_y - 1]


def load_row(field, a, row, h):
    if isinstance(row, int):
        return field[a, pl.ds(row, 1), :]
    first, second = (field[a, pl.ds(r, 1), :] for r in row)
    return jnp.where(h == 0, first, second)


def store_row(field, a, row, h, value):
    if isinstance(row, int):
        field[a, pl.ds(row, 1), :] = value
        return
    for k, r in enumerate(row):
        field[a, pl.ds(r, 1), :] = jnp.where(h == k, value, field[a, pl.ds(r, 1), :])


def line_count(lay):
    return 0 if lay.sub == 1 else 1 if lay.sub == 2 else 2


def own_kernel(lay, raw, z_sq, y_sq, w3, face, w_out, d_out, r_out, *packs):
    rhs, coef = raw.at[0], raw.at[1]
    y, nz = lay.own_y, lay.nz
    parity, h = lay.where()[:2]
    table3 = w3[...]
    for e in range(y // N):
        rows = pl.ds(N * e, N)
        w = [coef[a, rows, :] * table3[a] for a in range(N)]
        dx = even_odd((DM * DM).T, w, 1)
        for a in range(N):
            w_out[a, rows, :] = w[a]
            d_out[a, rows, :] = dx[a]
    hi, lo = split(w_out[...].reshape(N * y, nz))
    dz = z_apply(hi, lo, z_sq[...])
    dy = y_planes(lambda a: w_out[a], list(range(N)), y_sq[...])
    for a in range(N):
        d_out[a] = assemble_yz(d_out[a] + dz[a * y : (a + 1) * y] + dy[a])
        r_out[a] = assemble_yz(rhs[a])
    inner = (N - 1) * (1 - parity)
    face[0] = r_out[inner]
    face[1] = d_out[inner]
    for pack, (first, far) in zip(packs, lay.sent_rows(h)):
        for side, field in ((0, r_out), (1, d_out)):
            for a in range(N):
                pack[pack_rows(side, a), :] = raw[side, a, aligned(first, HALO), :]
                pack[pl.ds(side * N + a, 1), :] = load_row(field, a, far, h)


def message_kernel(lay, w, d, r, face, *refs):
    msg, *side_msgs, u_s, d_s, r_s = refs
    y, nz = lay.own_y, lay.nz
    parity, h, start, offset, low, high = lay.where()
    mask = yz_mask(y, nz, h * y, lay.total_y)
    scale = mask.astype(F32) * (1.0 / THETA)
    odd = parity.astype(F32)
    for a in range(N):
        dd, rr = d[a], r[a]
        keep = scale
        if a in (0, N - 1):
            inner = odd if a == 0 else 1.0 - odd
            dd = dd + inner * face[1]
            rr = rr + inner * face[0]
            keep = scale * inner
        d_s[a] = dd
        r_s[a] = rr
        u_s[a] = keep * rr / jnp.where(mask, dd, 1.0)
    col = [jnp.where(parity == 0, float(DM[a, 0]), float(DM[a, N - 1])) for a in range(N)]
    acc = []
    for e in range(y // N):
        rows = pl.ds(N * e, N)
        g = even_odd(DM, [u_s[a, rows, :] for a in range(N)], -1)
        total = None
        for a in range(N):
            term = (w[a, rows, :] * g[a]) * col[a]
            total = term if total is None else total + term
        acc.append(total)
    outer = (N - 1) * parity
    msg[pl.ds(0, y), :] = r[outer]
    msg[pl.ds(y, y), :] = d[outer]
    msg[pl.ds(2 * y, y), :] = w[outer]
    msg[pl.ds(3 * y, y), :] = assemble_yz(jnp.concatenate(acc, axis=0))
    base = PLANES * y
    for row in line_rows(lay, h):
        for field in (r_s, d_s, w):
            for a in range(N):
                msg[pl.ds(base + a, 1), :] = load_row(field, a, row, h)
            base += N
    for out, (first, _) in zip(side_msgs, lay.sent_rows(h)):
        for k in range(PLANES):
            out[pl.ds(k * HALO, HALO), :] = msg[aligned(k * y + first, HALO), :]
        lines = base - PLANES * y
        out[pl.ds(PLANES * HALO, lines), :] = msg[pl.ds(PLANES * y, lines), :]
        out[pl.ds(PLANES * HALO + lines, SPARE), :] = jnp.zeros((SPARE, nz), F32)


def flux_x(lay, u_ref, w_ref, first, count, fx):
    for el in range(2):
        for e in range(count // N):
            rows, to = aligned(first + N * e, N), pl.ds(N * e, N)
            u = [u_ref[N * el + a, rows, :] for a in range(N)]
            g = even_odd(DM, u, -1)
            for a in range(N):
                fx[N * el + a, to, :] = w_ref[N * el + a, rows, :] * g[a]


def flux_yz(lay, u_ref, w_ref, planes, first, count, z_d, y_d, fy, fz):
    part, to = aligned(first, count), pl.ds(0, count)
    u = jnp.concatenate([u_ref[p, part, :] for p in planes], axis=0)
    gz = z_apply(*split(u), z_d[...])
    gy = y_planes(lambda p: u_ref[p, part, :], planes, y_d[...])
    for k, p in enumerate(planes):
        w = w_ref[p, part, :]
        fy[p, to, :] = w * gy[p]
        fz[p, to, :] = w * gz[k * count : (k + 1) * count]


def operate(lay, u_ref, w_ref, back, first, count, tables, fx, fy, fz):
    z_d, z_dt, y_d, y_dt = tables
    nz = lay.nz
    middle = list(range(1, 2 * N - 1))
    flux_x(lay, u_ref, w_ref, first, count, fx)
    flux_yz(lay, u_ref, w_ref, middle, first, count, z_d, y_d, fy, fz)
    to, part = pl.ds(0, count), aligned(first, count)
    for el in range(2):
        for e in range(count // N):
            rows, here = aligned(first + N * e, N), pl.ds(N * e, N)
            b = even_odd(DM.T, [fx[N * el + a, here, :] for a in range(N)], -1)
            for a in range(N):
                back[N * el + a, rows, :] = b[a]
    n = len(middle)
    bz = z_apply(*split(fz[pl.ds(1, n), to, :].reshape(n * count, nz)), z_dt[...])
    by = y_planes(lambda p: fy[p, to, :], middle, y_dt[...])
    for p in middle:
        back[p, part, :] = back[p, part, :] + by[p] + bz[(p - 1) * count : p * count]


def smooth_start(lay, d, r, inv, u, first, count, start):
    part = aligned(first, count)
    mask = yz_mask(count, lay.nz, start + first, lay.total_y)
    inside = mask.astype(F32)
    zero = jnp.zeros((count, lay.nz), F32)
    for p in range(2 * N):
        if p in (0, 2 * N - 1):
            u[p, part, :] = zero
        else:
            i = inside / jnp.where(mask, d[p, part, :], 1.0)
            inv[p, part, :] = i
            u[p, part, :] = i * r[p, part, :] * (1.0 / THETA)


def sum_middle(fields, first, count):
    part = aligned(first, count)
    for s in fields:
        both = s[N - 1, part, :] + s[N, part, :]
        s[N - 1, part, :] = both
        s[N, part, :] = both


def element_sums(lay, base, parity, first, count, source, tables, outs):
    z_sq, y_sq, w3 = tables
    w_out, rhs_out, d_s, r_s, lin = outs[:5]
    nz = lay.nz
    part = aligned(first, count)
    for side, target in ((0, rhs_out), (1, w_out)):
        for a in range(N):
            target[base + a, part, :] = source(side, a)
    table3 = w3[...]
    outer = [jnp.where(parity == 0, float(DM[a, 0]), float(DM[a, N - 1])) for a in range(N)]
    for e in range(count // N):
        rows = aligned(first + N * e, N)
        w = [w_out[base + a, rows, :] * table3[a] for a in range(N)]
        dx = even_odd((DM * DM).T, w, 1)
        cx = even_odd(DM.T, [outer[a] * w[a] for a in range(N)], -1)
        for a in range(N):
            w_out[base + a, rows, :] = w[a]
            d_s[base + a, rows, :] = dx[a]
            lin[base + a, rows, :] = cx[a]
    dz = z_apply(*split(w_out[pl.ds(base, N), part, :].reshape(N * count, nz)), z_sq[...])
    dy = y_planes(lambda a: w_out[base + a, part, :], list(range(N)), y_sq[...])
    for a in range(N):
        d_local = d_s[base + a, part, :] + dz[a * count : (a + 1) * count] + dy[a]
        d_s[base + a, part, :] = assemble_yz(d_local)
        r_s[base + a, part, :] = assemble_yz(rhs_out[base + a, part, :])
        lin[base + a, part, :] = assemble_yz(lin[base + a, part, :])


def other_sums(lay, base, parity, h, pieces, tables, outs):
    d_s, r_s = outs[2:4]
    for piece, first, row in zip(pieces, lay.other_starts(h), lay.far_rows(h)):
        source = lambda side, a, piece=piece: piece[pack_rows(side, a)]
        element_sums(lay, base, parity, first, HALO, source, tables, outs)
        for side, target in ((0, r_s), (1, d_s)):
            for a in range(N):
                store_row(target, base + a, row, h, piece[pl.ds(side * N + a, 1)])


ARRAYS = 8


def early_kernel(lay, own, *refs):
    mate, refs = refs[:2], refs[2:]
    z_sq, y_sq, w3 = refs[:3]
    tables, outs, scratch = refs[3:7], refs[7 : 7 + ARRAYS], refs[7 + ARRAYS :]
    w, _, d, r, _, inv, u, back = outs
    parity, h, start, offset, low, high = lay.where()
    own = (own.at[0], own.at[1])
    for base, el, block in ((parity * N, parity, own), ((1 - parity) * N, 1 - parity, mate)):
        source = lambda side, a, block=block: block[side][a]
        element_sums(lay, base, el, offset, lay.own_y, source, (z_sq, y_sq, w3), outs)
    sum_middle((d, r), offset, lay.own_y)
    smooth_start(lay, d, r, inv, u, offset, lay.own_y, start)
    first, count = lay.early_rows(h)
    operate(lay, u, w, back, first, count, tables, *scratch)


def near_kernel(lay, n_other, *refs):
    other, tables = refs[:n_other], refs[n_other : n_other + 3]
    outs = refs[n_other + 3 + ARRAYS :]
    parity, h = lay.where()[:2]
    other_sums(lay, parity * N, parity, h, [Pieces([o]) for o in other], tables, outs)


def deep_kernel(lay, n_other, *refs):
    cuts = len(CUTS) - 1
    mate_other = [Pieces(refs[cuts * k : cuts * (k + 1)]) for k in range(n_other)]
    refs = refs[cuts * n_other :]
    z_sq, y_sq, w3 = refs[:3]
    tables = refs[3:7]
    refs = refs[7 + ARRAYS :]
    outs, sec_out, ends = refs[:ARRAYS], refs[ARRAYS], refs[ARRAYS + 1]
    scratch = refs[ARRAYS + 2 :]
    w, _, d, r, lin, inv, u, back = outs
    last = 2 * N - 1
    parity, h, start, offset, low, high = lay.where()
    other_sums(lay, (1 - parity) * N, 1 - parity, h, mate_other, (z_sq, y_sq, w3), outs)
    for first in lay.other_starts(h):
        sum_middle((d, r), first, HALO)
    for begin in lay.interfaces(h):
        above, below = pl.ds(begin - 1, 1), pl.ds(begin, 1)
        for s in (d, r, lin):
            for p in range(2 * N):
                both = s[p, above, :] + s[p, below, :]
                s[p, above, :] = both
                s[p, below, :] = both
    for side, p in ((0, 0), (1, last)):
        ends[side, 0] = r[p]
        ends[side, 1] = d[p]
    for first in lay.late_starts(h):
        smooth_start(lay, d, r, inv, u, first, HALO + N, start)
        operate(lay, u, w, back, first, HALO + N, tables, *scratch)
    for p in range(1, last):
        back[p] = assemble_yz(back[p])
    sum_middle((back,), 0, lay.ny)
    for p in range(2 * N):
        if p in (0, last):
            sec_out[p] = assemble_yz(back[p])
        else:
            i = (2.0 * RHO1 / DELTA) * inv[p]
            lin[p] = -i * lin[p]
            sec_out[p] = (1.0 + RHO1 * RHO0) * u[p] + i * (r[p] - back[p])


def coarse_tables_kernel(lay, w_ref, rhs_ref, my, mz, ry, rz, g_out, r_out):
    ny, nz, cr = lay.ny, lay.nz, lay.cr
    lhs = []
    for el in range(2):
        for m in MASS:
            total = None
            for a in range(N):
                term = float(m[a]) * w_ref[N * el + a]
                total = term if total is None else total + term
            lhs.append(total)
    along_z = z_apply(*split(jnp.concatenate(lhs, axis=0)), mz[...])
    for el in range(2):
        mom = {}
        for alpha in range(3):
            at = (3 * el + alpha) * ny
            block = y_apply(along_z[at : at + ny], my[...])
            for beta in range(3):
                for gamma in range(3):
                    mom[alpha, beta, gamma] = block[
                        beta * cr : (beta + 1) * cr, gamma * nz : (gamma + 1) * nz
                    ]
        x_sum, y_sum, z_sum = {}, {}, {}
        for i in range(3):
            for j in range(3):
                x_sum[i, j] = mom[0, i, j] + 2.0 * mom[1, i, j] + mom[2, i, j]
                y_sum[i, j] = mom[i, 0, j] + 2.0 * mom[i, 1, j] + mom[i, 2, j]
                z_sum[i, j] = mom[i, j, 0] + 2.0 * mom[i, j, 1] + mom[i, j, 2]
        sign = (1.0, -1.0, 1.0)
        for alpha in range(3):
            for beta in range(3):
                for gamma in range(3):
                    g_out[el, 9 * alpha + 3 * beta + gamma] = 0.25 * (
                        sign[alpha] * x_sum[beta, gamma]
                        + sign[beta] * y_sum[alpha, gamma]
                        + sign[gamma] * z_sum[alpha, beta]
                    )
    sums = []
    for el in range(2):
        for i in range(2):
            total = None
            for a in range(N):
                term = float(RHO[a, i]) * rhs_ref[N * el + a]
                total = term if total is None else total + term
            sums.append(total)
    part = y_apply(jnp.concatenate(sums, axis=1), ry[...])
    rows = jnp.concatenate([part[:, k * nz : (k + 1) * nz] for k in range(4)], axis=0)
    full = z_apply(*split(rows), rz[...])
    for k in range(4):
        r_out[k] = full[k * cr : (k + 1) * cr]


def pair_index(i, j):
    return i + j


def shifted(c, q, r):
    if q:
        c = pltpu.roll(c, c.shape[0] - 1, 0)
    if r:
        c = pltpu.roll(c, c.shape[1] - 1, 1)
    return c


def scatter(parts):
    cr, nz = parts[0, 0].shape
    first = parts[0, 0] + pltpu.roll(parts[0, 1], 1, 1)
    second = parts[1, 0] + pltpu.roll(parts[1, 1], 1, 1)
    return first + pltpu.roll(second, 1, 0)


def gathered(c):
    return {(q, r): shifted(c, q, r) for q in range(2) for r in range(2)}


def face_apply(entry, c, out=None):
    out = {} if out is None else out
    for j in range(2):
        for k in range(2):
            for q in range(2):
                for r in range(2):
                    term = entry(pair_index(j, q), pair_index(k, r)) * c[q, r]
                    out[j, k] = term if (j, k) not in out else out[j, k] + term
    return out


def coarse_diag(entry):
    return scatter({(j, k): entry(2 * j, 2 * k) for j in range(2) for k in range(2)})


def coarse_mask(lay, start):
    row = lax.broadcasted_iota(jnp.int32, (lay.cr, lay.nz), 0) + lax.div(start, N)
    lane = lax.broadcasted_iota(jnp.int32, (lay.cr, lay.nz), 1)
    return (row > 0) & (row < lay.total_y // N) & (lane > 0) & (lane < lay.ez)


def unpack_sides(lay, pieces, mate_pieces, line, parity, h, start, win):
    y, nz = lay.own_y, lay.nz
    for side, group in ((parity, pieces), (1 - parity, mate_pieces)):
        for k in range(PLANES):

            def put(rows, value):
                win[side, k, rows, :] = value

            others = [g[pl.ds(k * HALO, HALO), :] for g in group[1:]]
            gather_window(lay, group[0][pl.ds(k * y, y), :], others, h, put)
    is_even = parity == 0
    lane = lax.broadcasted_iota(jnp.int32, (N, nz), 1)
    node = lax.broadcasted_iota(jnp.int32, (N, nz), 0)
    lane_in = (lane > 0) & (lane < nz - 1)
    flank = lax.broadcasted_iota(jnp.int32, (1, nz), 1)
    last = ((flank % N == N - 1) & (flank < nz - 1)).astype(F32)
    first = ((flank % N == 0) & (flank > 0)).astype(F32)
    for b, begin in enumerate(lay.interfaces(h), 1):
        above, below = pl.ds(begin - 1, 1), pl.ds(begin, 1)
        for side in range(2):
            for k in range(2):
                both = win[side, k, above, :] + win[side, k, below, :]
                win[side, k, above, :] = both
                win[side, k, below, :] = both
        for side in range(2):
            outer = N - 1 if side == 0 else 0

            def field(k):
                def of(group):
                    own_lines, other_lines = PLANES * y + k * N, PLANES * HALO + k * N
                    if lay.sub == 2:
                        mine, theirs = own_lines, other_lines
                        near = group[1]
                    else:
                        mine = own_lines + 3 * N * (b - 1)
                        theirs = other_lines + 3 * N * (2 - b)
                        near = group[b]
                    return group[0][pl.ds(mine, N), :] + near[pl.ds(theirs, N), :]
                mine, theirs = of(pieces), of(mate_pieces)
                if side == 0:
                    return jnp.where(is_even, mine, theirs)
                return jnp.where(is_even, theirs, mine)

            r, d, w = field(0), field(1), field(2)
            row = start + begin
            ok = lane_in & (node != outer) & (row > 0) & (row < lay.total_y)
            u = jnp.where(ok, r / jnp.where(ok, d, 1.0) * (1.0 / THETA), 0.0)
            g = None
            for a in range(N):
                term = line[a] * u[a : a + 1]
                g = term if g is None else g + term
            total = jnp.sum(line[N + side] * (w * g), axis=0, keepdims=True)
            total = total + last * pltpu.roll(total, nz - 1, 1) + first * pltpu.roll(total, 1, 1)
            win[side, 3, above, :] = total
            win[side, 3, below, :] = total


def second_kernel(lay, n_pieces, *refs):
    pieces, mate_pieces = refs[:n_pieces], refs[n_pieces : 2 * n_pieces]
    w_ref, sec_in, lin_in, ends, g_ref, r_ref = refs[2 * n_pieces : 2 * n_pieces + 6]
    refs = refs[2 * n_pieces + 6 :]
    z_d, z_dt, z_sq, y_d, y_dt, y_sq, ry, rz, line = refs[:9]
    out, msg, state = refs[9:12]
    win, sec, fx, fy, fz = refs[12:]
    ny, nz, cr = lay.ny, lay.nz, lay.cr
    last = 2 * N - 1
    parity, h, start, offset, low, high = lay.where()
    mask = yz_mask(ny, nz, start, lay.total_y)
    inside = mask.astype(F32)
    is_even = parity == 0
    unpack_sides(lay, pieces, mate_pieces, line, parity, h, start, win)
    flags = (low, high)
    inv, res, u = [], [], []
    for side in range(2):
        valid = inside * flags[side]
        inv.append(valid / jnp.where(mask, ends[side, 1] + win[side, 1], 1.0))
        res.append(valid * (ends[side, 0] + win[side, 0]))
        u.append(inv[side] * res[side] * (1.0 / THETA))
    for p in range(1, last):
        value = sec_in[p]
        if p <= N:
            value = value + lin_in[min(p, N - 1)] * u[0]
        if p >= N - 1:
            value = value + lin_in[max(p, N)] * u[1]
        sec[p] = value
    flux_yz(lay, sec, w_ref, list(range(1, last)), 0, ny, z_d, y_d, fy, fz)
    weights = [w_ref[0] + win[0, 2], w_ref[last] + win[1, 2]]
    hi, lo = split(jnp.concatenate(u, axis=0))
    gz = z_apply(hi, lo, z_d[...])
    gy = y_apply(jnp.concatenate(u, axis=1), y_d[...])
    weight_z = jnp.concatenate(weights, axis=0)
    weight_y = jnp.concatenate(weights, axis=1)
    bz = z_apply(*split(weight_z * gz), z_dt[...])
    by = y_apply(weight_y * gy, y_dt[...])
    dz = z_apply(*split(jnp.concatenate([win[0, 2], win[1, 2]], axis=0)), z_sq[...])
    dy = y_planes(lambda side: win[side, 2], [0, 1], y_sq[...])
    dx = [
        win[side, 1] - assemble_yz(dz[side * ny : (side + 1) * ny] + dy[side]) for side in range(2)
    ]
    for side, p in ((0, 0), (1, last)):
        plane = assemble_yz(bz[side * ny : (side + 1) * ny] + by[:, side * nz : (side + 1) * nz])
        plane = plane + sec_in[p] + win[side, 3] + (lin_in[p] + dx[side]) * u[side]
        res_one = res[side] - inside * plane
        sec[p] = (1.0 + RHO1 * RHO0) * u[side] + (2.0 * RHO1 / DELTA) * inv[side] * res_one
    out[...] = sec[pl.ds(parity * N, N), pl.ds(pl.multiple_of(offset, N), lay.own_y), :]
    flux_yz(lay, sec, w_ref, [0, last], 0, ny, z_d, y_d, fy, fz)
    flux_x(lay, sec, w_ref, 0, ny, fx)
    sums = []
    for f, weight in ((fx, DRHO), (fy, RHO), (fz, RHO)):
        lanes = []
        for el in range(2):
            for i in range(2):
                total = None
                for a in range(N):
                    term = float(weight[a, i]) * f[N * el + a]
                    total = term if total is None else total + term
                lanes.append(total)
        sums.append(jnp.concatenate(lanes, axis=1))
    data = jnp.concatenate(sums, axis=0)
    hi = data.astype(BF16).astype(F32)
    parts = jnp.concatenate([hi, data - hi], axis=1).astype(BF16)
    both = dot(ry[...].astype(BF16), parts)
    both = both[: 2 * cr, : 4 * nz] + both[2 * cr :, : 4 * nz] + both[: 2 * cr, 4 * nz :]
    rows = [
        jnp.concatenate([v[:, k * nz : (k + 1) * nz] for v in (both[:cr], both[cr:])], axis=1)
        for k in range(4)
    ]
    full = z_apply(*split(jnp.concatenate(rows, axis=0)), rz[...])
    r = {}
    for el in range(2):
        for i in range(2):
            k = 2 * el + i
            r[el, i] = r_ref[k] - full[k * cr : (k + 1) * cr]
    planes = [r[0, 0], r[0, 1] + r[1, 0], r[1, 1]]
    cmask = coarse_mask(lay, start)

    def entry(el, alpha):
        return lambda beta, gamma: g_ref[el, 9 * alpha + 3 * beta + gamma]

    d = [
        coarse_diag(entry(0, 0)),
        coarse_diag(entry(0, 2)) + coarse_diag(entry(1, 0)),
        coarse_diag(entry(1, 2)),
    ]
    cin = cmask.astype(F32)
    mid = (2.0 / 3.0) * cin * planes[1] / jnp.where(cmask, d[1], 1.0)
    c = gathered(mid)
    g_low = scatter(face_apply(entry(0, 1), c))
    g_high = scatter(face_apply(entry(1, 1), c))
    g_mid = scatter(face_apply(entry(1, 0), c, face_apply(entry(0, 2), c)))
    state[0] = planes[0]
    state[1] = planes[1]
    state[2] = planes[2]
    state[3] = d[0]
    state[4] = d[1]
    state[5] = d[2]
    state[6] = g_low
    state[7] = g_mid
    state[8] = g_high
    state[9] = mid
    send = [
        jnp.where(is_even, planes[0], planes[2]),
        jnp.where(is_even, d[0], d[2]),
        jnp.where(is_even, g_low, g_high),
    ]
    send += [jnp.where(is_even, g_ref[0, k], g_ref[1, 18 + k]) for k in range(9)]
    for k in range(3):
        packed = send[4 * k]
        for q in range(1, 4):
            packed = packed + pltpu.roll(send[4 * k + q], q * (nz // 4), 1)
        msg[k] = packed


def third_kernel(lay, *refs):
    own_msg, mate_msg, sec, state, g_ref, py, pz, out, coarse = refs
    ny, nz, cr = lay.ny, lay.nz, lay.cr
    parity, h, start, offset, low, high = lay.where()
    is_even = parity == 0
    cmask = coarse_mask(lay, start)
    cin = cmask.astype(F32)
    lo_msg, hi_msg = [], []
    for k in range(3):
        mine, theirs = own_msg[k], mate_msg[k]
        for target, packed in (
            (lo_msg, jnp.where(is_even, mine, theirs)),
            (hi_msg, jnp.where(is_even, theirs, mine)),
        ):
            target.append(packed)
            for q in range(1, 4):
                target.append(pltpu.roll(packed, nz - q * (nz // 4), 1))

    def entry(el, alpha):
        return lambda beta, gamma: g_ref[el, 9 * alpha + 3 * beta + gamma]

    def outer(at, m, flag, el, alpha):
        rhs = cin * flag * (state[at] + m[0])
        d = jnp.where(cmask, state[3 + at] + m[1], 1.0)
        one = (2.0 / 3.0) * rhs / d
        c = gathered(one)
        here = lambda beta, gamma: g_ref[el, 9 * alpha + 3 * beta + gamma] + m[3 + 3 * beta + gamma]
        image = scatter(face_apply(here, c)) + state[6 + at] + m[2]
        cross = face_apply(entry(el, 1), c)
        solution = one + (2.0 / 3.0) * (rhs - cin * flag * image) / d
        return solution, cross

    c_low, cross_low = outer(0, lo_msg, low, 0, 0)
    c_high, cross_high = outer(2, hi_msg, high, 1, 2)
    cross = scatter({k: cross_low[k] + cross_high[k] for k in cross_low})
    rhs = cin * state[1]
    d = jnp.where(cmask, state[4], 1.0)
    c_mid = state[9] + (2.0 / 3.0) * (rhs - cin * (state[7] + cross)) / d
    left = jnp.where(is_even, c_low, c_mid)
    right = jnp.where(is_even, c_mid, c_high)
    both = jnp.concatenate([left, right], axis=0)
    full = z_apply(*split(both), pz[...])
    y = lay.own_y
    mask = yz_mask(y, nz, start + offset, lay.total_y).astype(F32)
    weight = [jnp.broadcast_to(py[i], (N, nz)) for i in range(2)]
    q = []
    for side in range(2):
        rows = full[side * cr : (side + 1) * cr]
        if lay.sub > 1:
            rows = pltpu.roll(rows, cr - lax.div(offset, N), 0)
        blocks = []
        for e in range(y // N):
            at = [rows[e + i : e + i + 1] for i in range(2)]
            blocks.append(weight[0] * at[0][:, :nz] + weight[1] * at[1][:, :nz])
            for i in range(2):
                coarse[side, pl.ds(2 * e + i, 1), :] = at[i][:, nz : nz + nz // 4]
        q.append(mask * jnp.concatenate(blocks, axis=0))
    q_left, q_right = q
    first_flag = jnp.where(is_even, low, 1.0)
    last_flag = jnp.where(is_even, 1.0, high)
    for a in range(N):
        add = float(INTERP[a, 0]) * q_left + float(INTERP[a, 1]) * q_right
        if a == 0:
            add = first_flag * add
        if a == N - 1:
            add = last_flag * add
        out[a] = sec[a] + add


def run(kernel, args, outs, scratch=(), aliases={}):
    return pl.pallas_call(
        kernel,
        out_shape=[jax.ShapeDtypeStruct(o, F32) for o in outs],
        in_specs=[pl.BlockSpec(memory_space=pltpu.VMEM)] * len(args),
        out_specs=[pl.BlockSpec(memory_space=pltpu.VMEM)] * len(outs),
        scratch_shapes=[pltpu.VMEM(s, F32) for s in scratch],
        compiler_params=pltpu.CompilerParams(vmem_limit_bytes=VMEM_LIMIT),
        input_output_aliases=aliases,
        cost_estimate=pl.CostEstimate(flops=1, bytes_accessed=1, transcendentals=0),
    )(*args)


def swap_pairs(count, first):
    pairs = []
    for i in range(first, count - 1, 2):
        pairs += [(i, i + 1), (i + 1, i)]
    return pairs


def chip_pairs(dom, sub, shift):
    pairs = []
    for a, b in swap_pairs(dom, 1):
        for q in range(sub):
            to = (q + shift) % sub if sub == 2 else q + shift
            if 0 <= to < sub:
                pairs.append((a * sub + q, b * sub + to))
    for end in (0, dom - 1):
        pairs += [(end * sub + a, end * sub + b) for a, b in swap_pairs(sub, 0)]
    return pairs


def shards(dom, sub, rhs_local, coefficient):
    size_x, own_y, nz = rhs_local.shape
    assert size_x == N and dom % 2 == 0 and (sub == 1 or own_y > HALO)
    lay = Layout(own_y, nz, dom, sub)
    ny, cr = lay.ny, lay.cr
    t = {k: jnp.asarray(v) for k, v in make_tables(ny, nz, own_y).items()}
    pick = lambda *names: [t[k] for k in names]
    even = lambda v: lax.ppermute(v, "dom", swap_pairs(dom, 0))
    odd = lambda v, k=0: lax.ppermute(v, ("dom", "sub"), chip_pairs(dom, sub, k))
    block = (N, own_y, nz)
    raw = jnp.stack([rhs_local, coefficient])
    n_other = 0 if sub == 1 else 1 if sub == 2 else 2
    face, w, d, r, *packs = run(
        functools.partial(own_kernel, lay),
        [raw, t["z_sq"], t["y_sq", own_y // N], t["w3"]],
        [(2, own_y, nz), block, block, block]
        + [(PACK, nz)] * n_other,
    )
    mate_face = even(face)
    if sub == 1:
        steps = []
    elif sub == 2:
        steps = [[(0, 1), (1, 0)]]
    else:
        up = [(i, i + 1) for i in range(sub - 1)]
        steps = [up, [(b, a) for a, b in up]]
    others = [lax.ppermute(pack, "sub", step) for pack, step in zip(packs, steps)]
    raw_later = lax.optimization_barrier((raw, face))[0]
    mate = [even(raw_later[side]) for side in range(2)]
    lines = 3 * N * line_count(lay)
    msgs = run(
        functools.partial(message_kernel, lay),
        [w, d, r, mate_face],
        [(PLANES * own_y + lines, nz)] + [(PLANES * HALO + lines + SPARE, nz)] * n_other,
        [block] * 3,
    )
    shifts = [0] if sub == 1 else [0, 1] if sub == 2 else [0, 1, -1]
    pieces = [odd(msg, k) for msg, k in zip(msgs, shifts)]
    pair = (2 * N, ny, nz)
    count = lay.early_rows(0)[1] // N
    arrays = run(
        functools.partial(early_kernel, lay),
        [raw, *mate, t["z_sq"], t["y_sq", own_y // N], t["w3"]]
        + [t["z_d"], t["z_dt"], t["y_d", count], t["y_dt", count]],
        [pair] * ARRAYS,
        [(2 * N, count * N, nz)] * 3,
    )
    others, arrays = lax.optimization_barrier((others, arrays))
    mate_others = [even(o[a:b]) for o in others for a, b in zip(CUTS, CUTS[1:])]
    arrays = run(
        functools.partial(near_kernel, lay, n_other),
        [*others, t["z_sq"], t["y_sq", HALO // N], t["w3"], *arrays],
        [pair] * ARRAYS,
        (),
        {n_other + 3 + k: k for k in range(ARRAYS)},
    )
    pieces[0], arrays = lax.optimization_barrier((pieces[0], arrays))
    late = lambda *names: [t[k, HALO // N + 1] for k in names]
    sums = [t["z_sq"], t["y_sq", HALO // N], t["w3"]]
    w, rhs, _, _, lin, _, _, _, sec, ends = run(
        functools.partial(deep_kernel, lay, n_other),
        [*mate_others, *sums, t["z_d"], t["z_dt"], *late("y_d", "y_dt"), *arrays],
        [pair] * (ARRAYS + 1) + [(2, 2, ny, nz)],
        [(2 * N, HALO + N, nz)] * 3,
        {len(mate_others) + 7 + k: k for k in range(ARRAYS)},
    )
    later, sec = lax.optimization_barrier((pieces[1:], sec))
    pieces = pieces[:1] + later
    mate_pieces = [even(p) for p in pieces]
    g, r = run(
        functools.partial(coarse_tables_kernel, lay),
        [w, rhs] + pick("my", "mz", "ry_one", "rz_one"),
        [(2, 27, cr, nz), (4, cr, nz)],
    )
    sec, msg, state = run(
        functools.partial(second_kernel, lay, len(pieces)),
        [*pieces, *mate_pieces, w, sec, lin, ends, g, r]
        + pick("z_d", "z_dt", "z_sq", "y_d", "y_dt", ("y_sq", lay.ey), "ry", "rz", "line"),
        [block, (3, cr, nz), (10, cr, nz)],
        [(2, PLANES, ny, nz)] + [pair] * 4,
    )
    from_odd = odd(msg)
    from_mate = even(from_odd)
    return tuple(
        run(
            functools.partial(third_kernel, lay),
            [from_odd, from_mate, sec, state, g] + pick("py", "pz"),
            [block, (size_x // 4, own_y // 4, nz // 4)],
        )
    )


def solution(mesh):
    dom, sub = mesh.shape["dom"], mesh.shape["sub"]
    return jax.shard_map(
        functools.partial(shards, dom, sub),
        mesh=mesh,
        in_specs=(P("dom", "sub", None), P("dom", "sub", None)),
        out_specs=(P("dom", "sub", None), P("dom", "sub", None)),
        check_vma=False,
    )
```
